32 devices in a mesh: dp: 8 (over y, x, core), mp: 4 (over z).
Axes of the slice: x: 2, y: 2, z: 4, core: 2. Of those that a mesh axis runs over, the one named last changes fastest.
Arguments:
- tokens: bfloat16 [16384, 768], P(('dp', 'mp')), may hold values from -6 to 6
- cotangent: bfloat16 [16384, 768], P(('dp', 'mp')), may hold values from -6 to 6
- doc_lengths: int32 [8, 3], P('dp'), may hold values from 1 to 1024, 2048 in all within a row
- in_weight: float32 [768, 3, 768], P('dp', None, 'mp'), may hold values from -0.21875 to 0.21875
- out_weight: float32 [768, 768], P('dp', 'mp')
- up_weight: float32 [768, 3072], P('dp', 'mp'), may hold values from -0.21875 to 0.21875
- down_weight: float32 [768, 3072], P('dp', 'mp')
- gains: float32 [768, 2], P('dp')
- channel_weight: float32 [10, 768], P(None, 'mp'), may hold values from -3.6 to 3.6
- filter_in: float32 [33, 64], replicated, may hold values from -1 to 1
- filter_out: float32 [64, 768], P(None, 'mp'), may hold values from -0.0625 to 0.0625
- in_rows: float32 [768], P('dp'), may hold values from 1.13028067e-07 to 7.064254e-07
- in_cols: float32 [3, 768], P(None, 'mp'), may hold values from 1.13028067e-07 to 7.064254e-07
- out_rows: float32 [768], P('dp'), may hold values from 1.13028067e-07 to 7.064254e-07
- out_cols: float32 [768], P('mp'), may hold values from 1.13028067e-07 to 7.064254e-07
- up_rows: float32 [768], P('dp'), may hold values from 1.4128508e-08 to 8.8303177e-08
- up_cols: float32 [3072], P('mp'), may hold values from 1.4128508e-08 to 8.8303177e-08
- down_rows: float32 [768], P('dp'), may hold values from 1.4128508e-08 to 8.8303177e-08
- down_cols: float32 [3072], P('mp'), may hold values from 1.4128508e-08 to 8.8303177e-08
- gain_moment: float32 [768, 2], P('dp'), may hold values from 1.13028067e-07 to 7.064254e-07
- channel_moment: float32 [10, 768], P(None, 'mp'), may hold values from 1.13028067e-07 to 7.064254e-07
- filter_in_moment: float32 [33, 64], replicated, may hold values from 1.4467593e-06 to 5.787037e-06
- filter_out_moment: float32 [64, 768], P(None, 'mp'), may hold values from 9.259259e-06 to 5.787037e-05
Outputs:
- activations: bfloat16 [16384, 768], P(('dp', 'mp'))
- input_grad: bfloat16 [16384, 768], P(('dp', 'mp'))
- grad_norm: float32 [], replicated
- in_grad: float32 [768, 3, 768], P('dp', None, 'mp')
- out_grad: float32 [768, 768], P('dp', 'mp')
- up_grad: float32 [768, 3072], P('dp', 'mp')
- down_grad: float32 [768, 3072], P('dp', 'mp')
- gain_grad: float32 [768, 2], P('dp')
- channel_grad: float32 [10, 768], P(None, 'mp')
- filter_in_grad: float32 [33, 64], replicated
- filter_out_grad: float32 [64, 768], P(None, 'mp')
- in_new: float32 [768, 3, 768], P('dp', None, 'mp')
- out_new: float32 [768, 768], P('dp', 'mp')
- up_new: float32 [768, 3072], P('dp', 'mp')
- down_new: float32 [768, 3072], P('dp', 'mp')
- gain_new: float32 [768, 2], P('dp')
- channel_new: float32 [10, 768], P(None, 'mp')
- filter_in_new: float32 [33, 64], replicated
- filter_out_new: float32 [64, 768], P(None, 'mp')
- in_rows_new: float32 [768], P('dp')
- in_cols_new: float32 [3, 768], P(None, 'mp')
- out_rows_new: float32 [768], P('dp')
- out_cols_new: float32 [768], P('mp')
- up_rows_new: float32 [768], P('dp')
- up_cols_new: float32 [3072], P('mp')
- down_rows_new: float32 [768], P('dp')
- down_cols_new: float32 [3072], P('mp')
- gain_moment_new: float32 [768, 2], P('dp')
- channel_moment_new: float32 [10, 768], P(None, 'mp')
- filter_in_moment_new: float32 [33, 64], replicated
- filter_out_moment_new: float32 [64, 768], P(None, 'mp')
The draws below stay inside these ranges and needn't reach their ends.
Inputs may be any that keep to these rules, and one draw needn't show every extreme that they name: `doc_lengths`: each row's documents fill its 2048 positions in order, and the longest of a row has exactly 1024 tokens.
All inputs are finite; a program needn't handle non-finite values.
Results may differ from the reference program's by a relative error of at most 0.012.
The reference program's roundings to bfloat16 on the way count: a program that leaves them out, or rounds other values in their place, can miss the bound.
Values may be sent and summed in bfloat16 or wider, within the bound.
A program may use at most 320 MiB of HBM per device.

```python
import math
import jax
import jax.numpy as jnp
import numpy as np
from jax import lax

D = 768
FF = 3072
LENGTH = 2048
FEATS = 33
FILTER_WIDTH = 64
SHORT = 3
DOCS = 3
MOST = 1024
ROWS = 8
TOKENS = 16384


def ramp_values(count_values, low_end):
    fraction = jnp.arange(count_values, dtype=jnp.float32) / (count_values - 1)
    return low_end + fraction


def falling_moment(key, extent, axis_pos, base_value, reach_value, jitter_low, jitter_high):
    count_values = extent[axis_pos]
    fraction = jnp.arange(count_values, dtype=jnp.float32) / (count_values - 1)
    profile = 1.0 + reach_value * (1.0 - fraction)
    view = [1] * len(extent)
    view[axis_pos] = count_values
    jitter = jax.random.uniform(key, extent, jnp.float32, jitter_low, jitter_high)
    return base_value * jitter * profile.reshape(tuple(view))


def moment_law(key, extent, axis_pos, base_value):
    return falling_moment(key, extent, axis_pos, base_value, 3.0, 0.85, 1.1)


def draw_out_weight(key, part):
    key = jax.random.fold_in(key, 11)
    values = jax.random.normal(key, (D, D), jnp.float32)
    column_scale = ramp_values(D, 0.5)
    return values * column_scale[None, :] * (1.0 / math.sqrt(D))


def draw_down_weight(key, part):
    key = jax.random.fold_in(key, 12)
    values = jax.random.normal(key, (D, FF), jnp.float32)
    column_scale = ramp_values(FF, 0.5)
    return values * column_scale[None, :] * (1.0 / math.sqrt(FF))


def draw_gains(key, part):
    key = jax.random.fold_in(key, 13)
    jitter = jax.random.uniform(key, (D, 2), jnp.float32, 0.85, 1.15)
    row_scale = ramp_values(D, 0.5)
    return jitter * row_scale[:, None]


def draw_in_rows(key, part):
    key = jax.random.fold_in(key, 21)
    return moment_law(key, (D,), 0, 1.0 / (12 * D * D))


def draw_in_cols(key, part):
    key = jax.random.fold_in(key, 22)
    return moment_law(key, (3, D), 1, 1.0 / (12 * D * D))


def draw_out_rows(key, part):
    key = jax.random.fold_in(key, 23)
    return moment_law(key, (D,), 0, 1.0 / (12 * D * D))


def draw_out_cols(key, part):
    key = jax.random.fold_in(key, 24)
    return moment_law(key, (D,), 0, 1.0 / (12 * D * D))


def draw_up_rows(key, part):
    key = jax.random.fold_in(key, 25)
    return moment_law(key, (D,), 0, 1.0 / (96 * D * D))


def draw_up_cols(key, part):
    key = jax.random.fold_in(key, 26)
    return moment_law(key, (FF,), 0, 1.0 / (96 * D * D))


def draw_down_rows(key, part):
    key = jax.random.fold_in(key, 27)
    return moment_law(key, (D,), 0, 1.0 / (96 * D * D))


def draw_down_cols(key, part):
    key = jax.random.fold_in(key, 28)
    return moment_law(key, (FF,), 0, 1.0 / (96 * D * D))


def draw_gain_moment(key, part):
    key = jax.random.fold_in(key, 29)
    return moment_law(key, (D, 2), 0, 1.0 / (12 * D * D))


def draw_channel_moment(key, part):
    key = jax.random.fold_in(key, 30)
    return moment_law(key, (3 * SHORT + 1, D), 1, 1.0 / (12 * D * D))


def draw_filter_out_moment(key, part):
    key = jax.random.fold_in(key, 31)
    return moment_law(key, (FILTER_WIDTH, D), 1, LENGTH / (300.0 * D * D))


def block_scale(key, shape, split, smallest, largest):
    level = 1.0
    for dim, shards_of in split:
        heights = jax.random.uniform(jax.random.fold_in(jax.random.fold_in(key, 6), dim), (shards_of,), jnp.float32, smallest / len(split), largest / len(split))
        level = level * jnp.repeat(jnp.exp(heights), shape[dim] // shards_of).reshape((-1,) + (1,) * (len(shape) - 1 - dim))
    return level


def length_profile(count, total, most, lean):
    loads = [(1 << 20) // math.isqrt(rank ** lean) + 1 for rank in range(2, count + 1)]
    spare, given = total - most - (count - 1), [1] * (count - 1)
    while spare > 0:
        movable = [i for i in range(count - 1) if given[i] < most]
        whole, remaining = sum([loads[i] for i in movable]), spare
        for i in movable:
            addition = min(most - given[i], max(1, remaining * loads[i] // whole), spare)
            given[i] = given[i] + addition
            spare = spare - addition
    return np.array([most] + given)


def ragged_sizes(key, count, total, limit, slope):
    if count == 2:
        one = jax.random.randint(key, (), max(1, total - limit), min(limit, total - 1) + 1)
        return jnp.stack([one, total - one])
    lengths = jnp.asarray(length_profile(count, total, limit, slope), jnp.int32)
    pairs = (count - 1) // 2
    source_of, receiver = lengths[1:1 + 2 * pairs:2], lengths[2:2 + 2 * pairs:2]
    room = jnp.minimum(source_of - 1, limit - receiver)
    passed = jax.random.randint(jax.random.fold_in(key, 1), (pairs,), 0, 1 << 20) % (room + 1)
    lengths = lengths.at[1:1 + 2 * pairs:2].set(source_of - passed).at[2:2 + 2 * pairs:2].set(receiver + passed)
    return lengths[jax.random.permutation(jax.random.fold_in(key, 2), count)]


def bell_draw(rng, shape, scale, reach, split=(), kind=jnp.bfloat16):
    drawn = scale * jax.random.normal(rng, shape, jnp.float32)
    if split:
        drawn = drawn * block_scale(rng, shape, split, -0.22, 0.18)
    return jnp.clip(drawn, -reach, reach).astype(kind)


def setup_inputs(seed: int = 0) -> dict:
    seeds = jax.random.split(jax.random.key(seed), 24)
    return {
        "tokens": bell_draw(seeds[0], (TOKENS, D), 1.0, 6.0, ((0, 32),)),
        "cotangent": bell_draw(seeds[1], (TOKENS, D), 1.0, 6.0, ((0, 32),)),
        "doc_lengths": jax.vmap(lambda own: ragged_sizes(own, DOCS, LENGTH, MOST, 2))(jax.random.split(seeds[2], ROWS)).reshape((ROWS, DOCS)).astype(jnp.int32),
        "in_weight": bell_draw(seeds[3], (D, 3, D), D ** -0.5, 0.21875, ((0, 8), (2, 4)), jnp.float32),
        "out_weight": draw_out_weight(jax.random.fold_in(seeds[23], 71), 0),
        "up_weight": bell_draw(seeds[5], (D, FF), D ** -0.5, 0.21875, ((0, 8), (1, 4)), jnp.float32),
        "down_weight": draw_down_weight(jax.random.fold_in(seeds[23], 71), 0),
        "gains": draw_gains(jax.random.fold_in(seeds[23], 71), 0),
        "channel_weight": bell_draw(seeds[8], (3 * SHORT + 1, D), 0.6, 3.6, ((1, 4),), jnp.float32),
        "filter_in": bell_draw(seeds[9], (FEATS, FILTER_WIDTH), FEATS ** -0.5, 1.0, (), jnp.float32),
        "filter_out": bell_draw(seeds[10], (FILTER_WIDTH, D), (4 * LENGTH) ** -0.5, 0.0625, ((1, 4),), jnp.float32),
        "in_rows": draw_in_rows(jax.random.fold_in(seeds[23], 71), 0),
        "in_cols": draw_in_cols(jax.random.fold_in(seeds[23], 71), 0),
        "out_rows": draw_out_rows(jax.random.fold_in(seeds[23], 71), 0),
        "out_cols": draw_out_cols(jax.random.fold_in(seeds[23], 71), 0),
        "up_rows": draw_up_rows(jax.random.fold_in(seeds[23], 71), 0),
        "up_cols": draw_up_cols(jax.random.fold_in(seeds[23], 71), 0),
        "down_rows": draw_down_rows(jax.random.fold_in(seeds[23], 71), 0),
        "down_cols": draw_down_cols(jax.random.fold_in(seeds[23], 71), 0),
        "gain_moment": draw_gain_moment(jax.random.fold_in(seeds[23], 71), 0),
        "channel_moment": draw_channel_moment(jax.random.fold_in(seeds[23], 71), 0),
        "filter_in_moment": jnp.clip(jnp.exp(jax.random.uniform(seeds[21], (FEATS, FILTER_WIDTH), jnp.float32, math.log(1.4467592563960352e-06), math.log(5.787037025584141e-06))), 1.4467592563960352e-06, 5.787037025584141e-06),
        "filter_out_moment": draw_filter_out_moment(jax.random.fold_in(seeds[23], 71), 0),
    }


@jax.custom_vjp
def low(v):
    return lax.optimization_barrier(v.astype(jnp.bfloat16)).astype(jnp.float32)

@jax.custom_vjp
def low_back(v):
    return v

def low_keep(v):
    return (low(v), None)

def low_pass(kept, grad):
    return (grad,)

def back_keep(v):
    return (v, None)

def back_low(kept, grad):
    return (low(grad),)
low.defvjp(low_keep, low_pass)
low_back.defvjp(back_keep, back_low)
EPS_NORM = 1e-05
MOMENT_DECAY = 0.5
CLIP_NORM = 1.0
CLIP_STEP = 0.25
STEP_RATE = 2.0
FAST_DECAY = 15.35
SLOW_DECAY = 3.07
FULL_PRECISION = lax.Precision.HIGHEST

def product(left_side, right_side):
    return jnp.dot(left_side, right_side, precision=FULL_PRECISION, preferred_element_type=jnp.float32)

def layer_norm(values, gain_vector):
    centred = values - lax.optimization_barrier(jnp.mean(values, axis=-1, keepdims=True))
    inverse_std = lax.rsqrt(lax.optimization_barrier(jnp.mean(centred * centred, axis=-1, keepdims=True)) + EPS_NORM)
    return centred * inverse_std * gain_vector

def features(length, feature_count):
    step_index = jnp.arange(length, dtype=jnp.int32)
    band_index = jnp.arange(1, (feature_count - 1) // 2 + 1, dtype=jnp.int32)
    phase_angle = (step_index[:, None] * band_index[None, :] % length).astype(jnp.float32) * (2.0 * math.pi / length)
    positions = step_index.astype(jnp.float32) / length
    return (jnp.concatenate([positions[:, None], jnp.cos(phase_angle), jnp.sin(phase_angle)], axis=1), positions)

def implicit_filter(filter_in, filter_out, first_channel, total_channels, feature_table, positions):
    hidden = jnp.sin(product(feature_table, filter_in))
    shaped = product(hidden, filter_out)
    channel = (first_channel + jnp.arange(filter_out.shape[1], dtype=jnp.int32)).astype(jnp.float32)
    decay_rate = FAST_DECAY + (SLOW_DECAY - FAST_DECAY) * channel / (total_channels - 1)
    return shaped * jnp.exp(-positions[:, None] * decay_rate[None, :])

def document_index(doc_lengths, length):
    doc_ends = jnp.cumsum(doc_lengths, axis=-1).astype(jnp.int32)
    step_index = jnp.arange(length, dtype=jnp.int32)
    return lax.optimization_barrier(jnp.sum((step_index[:, None] >= doc_ends[..., None, :]).astype(jnp.int32), axis=-1)).astype(jnp.int32)

def forward(token_values, in_weight, out_weight, up_weight, down_weight, gains, channel_weight, filter_in, filter_out, doc_lengths):
    weight_in = low(in_weight).reshape(D, 3 * D)
    weight_out = low(out_weight)
    weight_up = low(up_weight)
    weight_down = low(down_weight)
    gain_low = low(gains)
    feature_table, positions = features(LENGTH, FEATS)
    filters = implicit_filter(filter_in, filter_out, 0, D, feature_table, positions)
    spectrum = jnp.fft.rfft(filters, n=2 * LENGTH, axis=0)
    conv_taps = channel_weight[:3 * SHORT].reshape(SHORT, 3, D)
    skip_gain = channel_weight[3 * SHORT]

    def one_row(row_inputs):
        row_tokens, row_lengths = row_inputs
        doc_index = document_index(row_lengths, LENGTH)
        normed = low(layer_norm(row_tokens, gain_low[:, 0]))
        stream = low_back(product(normed, weight_in)).reshape(LENGTH, 3, D)
        convolved = conv_taps[0] * stream
        for offset in range(1, SHORT):
            same_doc = (doc_index[offset:] == doc_index[:-offset]).astype(stream.dtype)
            shifted = jnp.concatenate([jnp.zeros((offset, 3, D), stream.dtype), stream[:-offset] * same_doc[:, None, None]], axis=0)
            convolved = convolved + conv_taps[offset] * shifted
        gated_value = convolved[:, 2] * convolved[:, 1]
        result = skip_gain * gated_value
        for document in range(DOCS):
            member = (doc_index == document).astype(gated_value.dtype)[:, None]
            spread = jnp.fft.irfft(spectrum * jnp.fft.rfft(member * gated_value, n=2 * LENGTH, axis=0), n=2 * LENGTH, axis=0)
            result = result + member * spread[:LENGTH]
        mixer_low = low(result * convolved[:, 0])
        residual = row_tokens + low_back(product(mixer_low, weight_out.T))
        second = low(layer_norm(residual, gain_low[:, 1]))
        gate_low = low(jax.nn.gelu(low_back(product(second, weight_up)), approximate=True))
        return residual + product(gate_low, weight_down.T)
    row_values = token_values.reshape(ROWS, LENGTH, D)
    return lax.map(jax.checkpoint(one_row), (row_values, doc_lengths)).reshape(TOKENS, D)

def factored_update(clipped, weight, row_moment, col_moment):
    squared = clipped * clipped
    row_new = MOMENT_DECAY * row_moment + (1.0 - MOMENT_DECAY) * lax.optimization_barrier(jnp.mean(squared, axis=1))
    col_new = MOMENT_DECAY * col_moment + (1.0 - MOMENT_DECAY) * lax.optimization_barrier(jnp.mean(squared, axis=0))
    second = row_new[:, None] * col_new[None, :] / jnp.mean(row_new)
    update = clipped * lax.rsqrt(second)
    update = update / jnp.maximum(1.0, jnp.sqrt(jnp.mean(update * update)) / CLIP_STEP)
    return (weight - STEP_RATE * jnp.sqrt(jnp.mean(weight * weight)) * update, row_new, col_new)

def plain_update(clipped, weight, moment):
    moment_new = MOMENT_DECAY * moment + (1.0 - MOMENT_DECAY) * clipped * clipped
    update = clipped * lax.rsqrt(moment_new)
    update = update / jnp.maximum(1.0, jnp.sqrt(jnp.mean(update * update)) / CLIP_STEP)
    return (weight - STEP_RATE * jnp.sqrt(jnp.mean(weight * weight)) * update, moment_new)

def reference(tokens, cotangent, doc_lengths, in_weight, out_weight, up_weight, down_weight, gains, channel_weight, filter_in, filter_out, in_rows, in_cols, out_rows, out_cols, up_rows, up_cols, down_rows, down_cols, gain_moment, channel_moment, filter_in_moment, filter_out_moment):

    def whole_block(token_values, weight_a, weight_b, weight_c, weight_d, gain_values, channel_values, first_filter, second_filter):
        return forward(token_values, weight_a, weight_b, weight_c, weight_d, gain_values, channel_values, first_filter, second_filter, doc_lengths)
    output, pullback = jax.vjp(whole_block, tokens.astype(jnp.float32), in_weight, out_weight, up_weight, down_weight, gains, channel_weight, filter_in, filter_out)
    gradients = pullback(cotangent.astype(jnp.float32))
    input_grad = gradients[0]
    raw_grads = gradients[1:]
    grad_norm = jnp.sqrt(sum((jnp.sum(gradient * gradient) for gradient in raw_grads)))
    clip_factor = 1.0 / jnp.maximum(1.0, grad_norm / CLIP_NORM)
    in_grad, out_grad, up_grad, down_grad, gain_grad, channel_grad, filter_in_grad, filter_out_grad = [gradient * clip_factor for gradient in raw_grads]
    in_new, in_rows_new, in_cols_new = factored_update(in_grad.reshape(D, 3 * D), in_weight.reshape(D, 3 * D), in_rows, in_cols.reshape(3 * D))
    out_new, out_rows_new, out_cols_new = factored_update(out_grad, out_weight, out_rows, out_cols)
    up_new, up_rows_new, up_cols_new = factored_update(up_grad, up_weight, up_rows, up_cols)
    down_new, down_rows_new, down_cols_new = factored_update(down_grad, down_weight, down_rows, down_cols)
    gain_new, gain_moment_new = plain_update(gain_grad, gains, gain_moment)
    channel_new, channel_moment_new = plain_update(channel_grad, channel_weight, channel_moment)
    filter_in_new, filter_in_moment_new = plain_update(filter_in_grad, filter_in, filter_in_moment)
    filter_out_new, filter_out_moment_new = plain_update(filter_out_grad, filter_out, filter_out_moment)
    return (output.astype(jnp.bfloat16), input_grad.astype(jnp.bfloat16), grad_norm, in_grad, out_grad, up_grad, down_grad, gain_grad, channel_grad, filter_in_grad, filter_out_grad, in_new.reshape(D, 3, D), out_new, up_new, down_new, gain_new, channel_new, filter_in_new, filter_out_new, in_rows_new, in_cols_new.reshape(3, D), out_rows_new, out_cols_new, up_rows_new, up_cols_new, down_rows_new, down_cols_new, gain_moment_new, channel_moment_new, filter_in_moment_new, filter_out_moment_new)
```

```python
import functools
import math

import jax
import jax.numpy as jnp
import ml_dtypes
import numpy as np
from jax import lax
from jax.experimental import pallas as pl
from jax.experimental.pallas import tpu as pltpu
from jax.sharding import PartitionSpec as P

EPS_NORM = 1e-05
MOMENT_DECAY = 0.5
CLIP_NORM = 1.0
CLIP_STEP = 0.25
STEP_RATE = 2.0
FAST_DECAY = 15.35
SLOW_DECAY = 3.07
FULL_PRECISION = lax.Precision.HIGHEST
BF = jnp.bfloat16
F32 = jnp.float32
MESH = pl.DeviceIdType.MESH
BLOCK = 256
EDGE = 16
ROOM = 56 << 20
IN_VMEM = pl.BlockSpec(memory_space=pltpu.VMEM)
IN_HBM = pl.BlockSpec(memory_space=pl.ANY)
IN_SMEM = pl.BlockSpec(memory_space=pltpu.SMEM)


def struct(shape, dtype):
    return jax.ShapeDtypeStruct(tuple(shape), dtype)


def transform_tables(block):
    freq = 2 * np.arange(block)[:, None] + 1
    angle = np.pi * (freq * np.arange(block)[None, :] % (4 * block)) / (2 * block)
    table = np.concatenate([np.cos(angle), -np.sin(angle)], axis=0).astype(np.float32)
    high = table.astype(ml_dtypes.bfloat16)
    low = (table - high.astype(np.float32)).astype(ml_dtypes.bfloat16)
    return high, low, np.ascontiguousarray(high.T), np.ascontiguousarray(low.T)


def mm(left, right):
    return lax.dot_general(left, right, (((1,), (0,)), ((), ())), preferred_element_type=F32)


def split(values):
    high = values.astype(BF)
    return high, (values - high.astype(F32)).astype(BF)


def load_rows(ref, start, count, lead=()):
    odd = lax.rem(start, 8)
    begin = pl.multiple_of(start - odd, 8)
    tile = ref[lead + (pl.ds(begin, count + 8), slice(None))]
    width = tile.shape[-1]
    tile = pltpu.roll(tile.reshape(count // 8 + 1, 8, width), lax.rem(8 - odd, 8), axis=1)
    first = lax.broadcasted_iota(jnp.int32, (count // 8, 8, width), 1) < 8 - odd
    return jnp.where(first, tile[:-1], tile[1:]).reshape(count, width)


def unpack(target, source):
    parts, block, width = source.shape
    half = width // 2
    for part in range(parts):
        target[pl.ds(2 * part * block, block), :] = source[part, :, 0:half].astype(F32)
        target[pl.ds((2 * part + 1) * block, block), :] = source[part, :, half:width].astype(F32)


def pair_rows(index, block, size):
    first = pl.multiple_of(index * size, size)
    return pl.ds(first, size), pl.ds(pl.multiple_of(block + first, size), size)


def signs(size, width, scale):
    odd = lax.broadcasted_iota(jnp.int32, (size, width), 0) % 2
    return jnp.where(odd == 0, scale, -scale).astype(F32)


def filter_spectrum(filter_ref, spectrum, raw, tables, block):
    count = raw.shape[0]
    high, low = tables[0][...], tables[1][...]
    for lag in range(count):
        top, rest = split(filter_ref[pl.ds(lag * block, block), :])
        raw[lag] = mm(high, top) + mm(high, rest) + mm(low, top)
    scale = 1.0 / block

    def body(index, carry):
        re_rows, im_rows = pair_rows(index, block, 8)
        sign = signs(8, raw.shape[2], scale)
        for lag in range(count):
            re, im = raw[lag, re_rows, :] * scale, raw[lag, im_rows, :] * scale
            if lag:
                re = re - sign * raw[lag - 1, im_rows, :]
                im = im + sign * raw[lag - 1, re_rows, :]
            spectrum[lag, re_rows, :] = re
            spectrum[lag, im_rows, :] = im
        return carry

    lax.fori_loop(0, block // 8, body, 0)


def slot_blocks(source, target, tables, start, length, block):
    high, low = tables[0][...], tables[1][...]
    for index in range(target.shape[0]):
        values = load_rows(source, start + index * block, block)
        inside = lax.broadcasted_iota(jnp.int32, values.shape, 0) + index * block < length
        values = jnp.where(inside, values, 0.0).astype(BF)
        target[index] = mm(high, values) + mm(low, values)


def inverse(top, rest, tables):
    high, low = tables[2][...], tables[3][...]
    return mm(high, top) + mm(high, rest) + mm(low, top)


def document_starts(len_ref, count):
    starts, at = [], jnp.int32(0)
    for slot in range(count):
        starts.append(at)
        at = at + len_ref[0, slot]
    return starts


def merge_slots(slots, starts, put, total, block, most):
    for index in range(total // block):
        first = index * block
        merged = None
        for slot, start in enumerate(starts):
            at = jnp.clip(first - start, -block, most) + block
            values = load_rows(slots, at, block, (slot,))
            if merged is None:
                merged = values
            else:
                inside = lax.broadcasted_iota(jnp.int32, values.shape, 0) + first >= start
                merged = jnp.where(inside, values, merged)
        put(index, merged)


def forward_products(spectrum, raw, top, rest, block):
    count = raw.shape[0]

    def body(index, carry):
        re_rows, im_rows = pair_rows(index, block, 16)
        hr = [spectrum[i, re_rows, :] for i in range(count)]
        hi = [spectrum[i, im_rows, :] for i in range(count)]
        xr = [raw[i, re_rows, :] for i in range(count)]
        xi = [raw[i, im_rows, :] for i in range(count)]
        for out in range(count):
            re = hr[0] * xr[out] - hi[0] * xi[out]
            im = hr[0] * xi[out] + hi[0] * xr[out]
            for lag in range(1, out + 1):
                re = re + (hr[lag] * xr[out - lag] - hi[lag] * xi[out - lag])
                im = im + (hr[lag] * xi[out - lag] + hi[lag] * xr[out - lag])
            top[out, re_rows, :], rest[out, re_rows, :] = split(re)
            top[out, im_rows, :], rest[out, im_rows, :] = split(im)
        return carry

    lax.fori_loop(0, block // 16, body, 0)


def backward_products(spectrum, grad, raw, total, top, rest, block, first_slot):
    count = raw.shape[0]

    def body(index, carry):
        re_rows, im_rows = pair_rows(index, block, 16)
        gr = [grad[i, re_rows, :] for i in range(count)]
        gi = [grad[i, im_rows, :] for i in range(count)]
        hr = [spectrum[i, re_rows, :] for i in range(count)]
        hi = [spectrum[i, im_rows, :] for i in range(count)]
        for out in range(count):
            re = hr[0] * gr[out] + hi[0] * gi[out]
            im = hr[0] * gi[out] - hi[0] * gr[out]
            for later in range(out + 1, count):
                lag = later - out
                re = re + (hr[lag] * gr[later] + hi[lag] * gi[later])
                im = im + (hr[lag] * gi[later] - hi[lag] * gr[later])
            top[out, re_rows, :], rest[out, re_rows, :] = split(re)
            top[out, im_rows, :], rest[out, im_rows, :] = split(im)
        xr = [raw[i, re_rows, :] for i in range(count)]
        xi = [raw[i, im_rows, :] for i in range(count)]
        for lag in range(count):
            re = im = None
            for at in range(count - lag):
                a = xr[at] * gr[at + lag] + xi[at] * gi[at + lag]
                b = xr[at] * gi[at + lag] - xi[at] * gr[at + lag]
                re = a if re is None else re + a
                im = b if im is None else im + b
            if not first_slot:
                re = re + total[lag, re_rows, :]
                im = im + total[lag, im_rows, :]
            total[lag, re_rows, :] = re
            total[lag, im_rows, :] = im
        return carry

    lax.fori_loop(0, block // 16, body, 0)


def filter_gradient(total, top, rest, tables, out_ref, block):
    count, width = total.shape[0], total.shape[2]
    scale = 1.0 / block

    def body(index, carry):
        re_rows, im_rows = pair_rows(index, block, 16)
        sign = signs(16, width, 1.0)
        for lag in range(count):
            re, im = total[lag, re_rows, :], total[lag, im_rows, :]
            if lag + 1 < count:
                re = re + sign * total[lag + 1, im_rows, :]
                im = im - sign * total[lag + 1, re_rows, :]
            top[lag, re_rows, :], rest[lag, re_rows, :] = split(re * scale)
            top[lag, im_rows, :], rest[lag, im_rows, :] = split(im * scale)
        return carry

    lax.fori_loop(0, block // 16, body, 0)
    for lag in range(count):
        out_ref[pl.ds(lag * block, block), :] = inverse(top[lag], rest[lag], tables)


def conv_forward_kernel(doc_count, len_ref, x_ref, filter_ref, t0, t1, t2, t3, y_ref, spectrum, full, raw, top, rest, slots):
    tables = (t0, t1, t2, t3)
    parts, block, width = x_ref.shape
    half = width // 2
    count = raw.shape[0]
    filter_spectrum(filter_ref, spectrum, raw, tables, block)
    unpack(full, x_ref)
    starts = document_starts(len_ref, doc_count)
    for slot in range(doc_count):
        slot_blocks(full, raw, tables, starts[slot], len_ref[0, slot], block)
        forward_products(spectrum, raw, top, rest, block)
        for out in range(count):
            slots[slot, pl.ds((1 + out) * block, block), :] = inverse(top[out], rest[out], tables)

    def put(index, values):
        y_ref[index // 2, :, pl.ds((index % 2) * half, half)] = values.astype(y_ref.dtype)

    merge_slots(slots, starts, put, 2 * parts * block, block, count * block)


def conv_forward(x, lengths, filters, tables):
    parts, block, width = x.shape
    half, docs = width // 2, lengths.shape[1]
    count = filters.shape[0] // block
    wide = (count, 2 * block, half)
    return pl.pallas_call(
        functools.partial(conv_forward_kernel, docs),
        name="conv_forward",
        out_shape=(struct(x.shape, BF), struct(wide, F32)),
        in_specs=[IN_SMEM] + [IN_VMEM] * 6,
        out_specs=(IN_VMEM, IN_VMEM),
        scratch_shapes=[
            pltpu.VMEM(((2 * parts + count) * block + 8, half), F32),
            pltpu.VMEM(wide, F32),
            pltpu.VMEM(wide, BF),
            pltpu.VMEM(wide, BF),
            pltpu.VMEM((docs, (count + 2) * block + 8, half), F32),
        ],
        compiler_params=pltpu.CompilerParams(vmem_limit_bytes=ROOM),
    )(lengths, x, filters, *tables)


def conv_backward_kernel(doc_count, len_ref, g_ref, x_ref, spectrum, skip_ref, t0, t1, t2, t3, gw_ref, edge_ref, gf_ref, g_full, x_full, grad, raw, top, rest, total, slots):
    tables = (t0, t1, t2, t3)
    parts, block, width = x_ref.shape
    half = width // 2
    count = raw.shape[0]
    unpack(g_full, g_ref)
    unpack(x_full, x_ref)
    starts = document_starts(len_ref, doc_count)
    for slot in range(doc_count):
        slot_blocks(g_full, grad, tables, starts[slot], len_ref[0, slot], block)
        slot_blocks(x_full, raw, tables, starts[slot], len_ref[0, slot], block)
        backward_products(spectrum, grad, raw, total, top, rest, block, slot == 0)
        for out in range(count):
            slots[slot, pl.ds((1 + out) * block, block), :] = inverse(top[out], rest[out], tables)
    edge_ref[...] = jnp.zeros(edge_ref.shape, edge_ref.dtype)

    def put(index, values):
        gw_ref[index // 2, :, pl.ds((index % 2) * half, half)] = values.astype(gw_ref.dtype)
        if index % 2 == 0 and index:
            own = g_full[pl.ds(index * block, EDGE), :] * skip_ref[...]
            edge_ref[index // 2 - 1, :, 0:half] = (values[0:EDGE] + own).astype(edge_ref.dtype)

    merge_slots(slots, starts, put, 2 * parts * block, block, count * block)
    filter_gradient(total, top, rest, tables, gf_ref, block)


def conv_backward(g, x, lengths, spectrum, skip_gain, tables):
    parts, block, width = x.shape
    half, docs, count = width // 2, lengths.shape[1], spectrum.shape[0]
    wide = (count, 2 * block, half)
    rows = pltpu.VMEM(((2 * parts + count) * block + 8, half), F32)
    return pl.pallas_call(
        functools.partial(conv_backward_kernel, docs),
        name="conv_backward",
        out_shape=(
            struct(x.shape, BF),
            struct((parts, EDGE, -(-half // 128) * 128), BF),
            struct((count * block, half), F32),
        ),
        in_specs=[IN_SMEM] + [IN_VMEM] * 8,
        out_specs=(IN_VMEM,) * 3,
        scratch_shapes=[
            rows,
            rows,
            pltpu.VMEM(wide, F32),
            pltpu.VMEM(wide, F32),
            pltpu.VMEM(wide, BF),
            pltpu.VMEM(wide, BF),
            pltpu.VMEM(wide, F32),
            pltpu.VMEM((docs, (count + 2) * block + 8, half), F32),
        ],
        compiler_params=pltpu.CompilerParams(vmem_limit_bytes=ROOM),
    )(lengths, g, x, spectrum, skip_gain, *tables)


def turned(value, bit):
    return value + bit - 2 * bit * ((value // bit) % 2)


def send(source, target, send_sem, recv_sem, device):
    copy = pltpu.make_async_remote_copy(
        src_ref=source,
        dst_ref=target,
        send_sem=send_sem,
        recv_sem=recv_sem,
        device_id=device,
        device_id_type=MESH,
    )
    copy.start()
    return copy


def greet(peers):
    barrier = pltpu.get_barrier_semaphore()
    for peer in peers:
        pl.semaphore_signal(barrier, inc=1, device_id=peer, device_id_type=MESH)
    pl.semaphore_wait(barrier, len(peers))


def ring(me, count):
    return [lax.rem(me + step, count) for step in range(1, count)]


def dma(*shape):
    return pltpu.SemaphoreType.DMA(shape)


def gather_kernel(chunk_count, *refs):
    chunks, refs = refs[:chunk_count], refs[chunk_count:]
    gains, channel, edges, refs = refs[0], refs[1], refs[2], refs[3:]
    whole, refs = refs[:chunk_count], refs[chunk_count:]
    gains_all, channel_all, edges_all, refs = refs[0], refs[1], refs[2], refs[3:]
    own_sem, z_send, z_recv, p_send, p_recv, s_send, s_recv = refs
    d, m = lax.axis_index("dp"), lax.axis_index("mp")
    dp, mp = lax.axis_size("dp"), lax.axis_size("mp")
    half = mp // 2
    dx, dy, dc = turned(d, 2), turned(d, 4), turned(d, 1)
    dxy = turned(dx, 4)
    greet([(e, m) for e in ring(d, dp)] + [(d, e) for e in ring(m, mp)])
    small = []
    for step, e in enumerate(ring(d, dp)):
        small.append(send(gains, gains_all.at[d], s_send.at[step], s_recv.at[step], (e, m)))
    for step, e in enumerate(ring(m, mp)):
        at = dp + step
        small.append(send(channel, channel_all.at[m], s_send.at[at], s_recv.at[at], (d, e)))
    gains_all[d] = gains[...]
    channel_all[m] = channel[...]
    at = dp + mp

    def edge(index, peer):
        return pltpu.make_async_remote_copy(
            src_ref=edges.at[index],
            dst_ref=edges_all.at[index],
            send_sem=s_send.at[at + index],
            recv_sem=s_recv.at[at + index],
            device_id=(d, peer),
            device_id_type=MESH,
        )

    up, down = lax.rem(m + 1, mp), lax.rem(m + mp - 1, mp)
    to_next, to_before = edge(0, up), edge(1, down)
    to_next.start()
    to_before.start()
    own, z = [], []
    for c in range(chunk_count):
        copy = pltpu.make_async_copy(chunks[c], whole[c].at[m, d], own_sem.at[c])
        copy.start()
        own.append(copy)
        z.append(
            [
                send(chunks[c], whole[c].at[m, d], z_send.at[c, step], z_recv.at[c, step], (d, e))
                for step, e in enumerate(ring(m, mp))
            ]
        )
    low, high = pl.ds(0, half), pl.ds(half, mp - half)
    first, second, last = [None] * chunk_count, [None] * chunk_count, [None] * chunk_count

    def push(c, slot, rows, owner, peer):
        block = whole[c].at[rows, owner]
        return send(block, block, p_send.at[c, slot], p_recv.at[c, slot], (peer, m))

    def stage_one(c):
        own[c].wait()
        for copy in z[c]:
            copy.wait_recv()
        first[c] = [push(c, 0, low, d, dx), push(c, 1, high, d, dy)]
        last[c] = [push(c, 2, pl.ds(0, mp), d, dc)]

    def stage_two(c):
        for copy in first[c]:
            copy.wait_recv()
        second[c] = [
            push(c, 3, low, d, dy),
            push(c, 4, high, d, dx),
            push(c, 5, low, dx, dy),
            push(c, 6, high, dy, dx),
        ]

    def stage_three(c):
        for copy in second[c]:
            copy.wait_recv()
        for slot, owner in enumerate((dx, dy, dxy)):
            last[c].append(push(c, 7 + slot, pl.ds(0, mp), owner, dc))

    for step in range(chunk_count + 3):
        if step < chunk_count:
            stage_one(step)
        if 0 <= step - 1 < chunk_count:
            stage_two(step - 1)
        if 0 <= step - 2 < chunk_count:
            stage_three(step - 2)
    for c in range(chunk_count):
        for copy in z[c] + first[c] + second[c]:
            copy.wait_send()
        for copy in last[c]:
            copy.wait()
    for copy in small:
        copy.wait()
    to_next.wait()
    to_before.wait()


def gather(chunks, gains, channel, edges):
    dp, mp = lax.axis_size("dp"), lax.axis_size("mp")
    count = len(chunks)
    outs = tuple(struct((mp, dp) + c.shape, c.dtype) for c in chunks)
    smalls = (
        struct((dp,) + gains.shape, gains.dtype),
        struct((mp,) + channel.shape, channel.dtype),
        struct(edges.shape, edges.dtype),
    )
    if dp != 8:
        down = [(i, (i + 1) % mp) for i in range(mp)]
        up = [(i, (i - 1) % mp) for i in range(mp)]
        spread = [lax.all_gather(lax.all_gather(c, "dp"), "mp") for c in chunks]
        return (
            *spread,
            lax.all_gather(gains, "dp"),
            lax.all_gather(channel, "mp"),
            jnp.stack([lax.ppermute(edges[0], "mp", down), lax.ppermute(edges[1], "mp", up)]),
        )
    return pl.pallas_call(
        functools.partial(gather_kernel, count),
        name="gather_weights",
        out_shape=outs + smalls,
        in_specs=[IN_VMEM] * (count + 3),
        out_specs=(IN_HBM,) * count + (IN_VMEM,) * 3,
        scratch_shapes=[
            dma(count),
            dma(count, mp - 1),
            dma(count, mp - 1),
            dma(count, 10),
            dma(count, 10),
            dma(dp + mp + 2),
            dma(dp + mp + 2),
        ],
        compiler_params=pltpu.CompilerParams(collective_id=0, has_side_effects=True, vmem_limit_bytes=ROOM),
    )(*chunks, gains, channel, edges)


def exchange_kernel(count, has_edge, *refs):
    sources, refs = refs[: count + has_edge], refs[count + has_edge :]
    targets, refs = refs[: count + has_edge], refs[count + has_edge :]
    send_sem, recv_sem, edge_send, edge_recv = refs
    d, m, mp = lax.axis_index("dp"), lax.axis_index("mp"), lax.axis_size("mp")
    greet([(d, e) for e in ring(m, mp)])
    copies = []
    for step, e in reversed(list(enumerate(ring(m, mp)))):
        for i in range(count):
            copies.append(
                send(sources[i].at[e], targets[i].at[m], send_sem.at[i, step], recv_sem.at[i, step], (d, e))
            )
    if has_edge:
        before = lax.rem(m + mp - 1, mp)
        copies.append(send(sources[count], targets[count], edge_send.at[0], edge_recv.at[0], (d, before)))
    for i in range(count):
        targets[i][m] = sources[i][m]
    for copy in copies:
        copy.wait()


def exchange(arrays, edge, collective_id):
    mp, count = lax.axis_size("mp"), len(arrays)
    inputs = list(arrays) + ([] if edge is None else [edge])
    return pl.pallas_call(
        functools.partial(exchange_kernel, count, int(edge is not None)),
        name="exchange_%d" % collective_id,
        out_shape=tuple(struct(a.shape, a.dtype) for a in inputs),
        in_specs=[IN_VMEM] * len(inputs),
        out_specs=(IN_VMEM,) * len(inputs),
        scratch_shapes=[dma(count, mp - 1), dma(count, mp - 1), dma(1), dma(1)],
        compiler_params=pltpu.CompilerParams(
            collective_id=collective_id, has_side_effects=True, vmem_limit_bytes=ROOM
        ),
    )(*inputs)


def reduce_kernel(count, small_wide, *refs):
    smalls = len(small_wide)
    parts, refs = refs[:count], refs[count:]
    small, refs = refs[:smalls], refs[smalls:]
    totals, refs = refs[:count], refs[count:]
    small_out, refs = refs[:smalls], refs[smalls:]
    own, from_core, from_y2, from_x2, from_x1, from_y1, from_z = [
        refs[i * count : (i + 1) * count] for i in range(7)
    ]
    refs = refs[7 * count :]
    running, from_dp, from_mp = [refs[i * smalls : (i + 1) * smalls] for i in range(3)]
    own_sem, p_send, p_recv, z_send, z_recv, s_send, s_recv = refs[3 * smalls :]
    d, m = lax.axis_index("dp"), lax.axis_index("mp")
    mp = lax.axis_size("mp")
    half = mp // 2
    low, high = pl.ds(0, half), pl.ds(half, mp - half)
    y, x, core = d // 4, (d // 2) % 2, d % 2
    dx, dy, dc = turned(d, 2), turned(d, 4), turned(d, 1)
    greet([(e, m) for e in (dc, dx, dy)] + [(d, e) for e in ring(m, mp)])
    local, pending = [], []

    def push(c, slot, source, target, peer):
        copy = send(source, target, p_send.at[c, slot], p_recv.at[c, slot], (peer, m))
        pending.append(copy)
        return copy

    core_copy = []
    for c in range(count):
        core_copy.append(push(c, 0, parts[c].at[:, :, :, 1 - core], from_core[c], dc))
        copy = pltpu.make_async_copy(parts[c].at[:, :, :, core], own[c], own_sem.at[c])
        copy.start()
        local.append(copy)

    def small_dp(stage, peer):
        if stage == 0:
            for i in range(smalls):
                running[i][0] = small[i][...]
        copies = []
        for i in range(smalls):
            at = i * 8 + stage
            copies.append(send(running[i].at[stage], from_dp[i].at[stage], s_send.at[at], s_recv.at[at], (peer, m)))
        pending.extend(copies)
        return copies

    def small_dp_end(stage, copies):
        for i, copy in enumerate(copies):
            copy.wait_recv()
            running[i][stage + 1] = running[i][stage] + from_dp[i][stage]

    def small_mp():
        copies = []
        for i in range(smalls):
            if small_wide[i]:
                for step, e in enumerate(ring(m, mp)):
                    at = i * 8 + 3 + step
                    copies.append(send(running[i].at[3], from_mp[i].at[m], s_send.at[at], s_recv.at[at], (d, e)))
                from_mp[i][m] = running[i][3]
        pending.extend(copies)
        return copies

    def small_mp_end(copies):
        for copy in copies:
            copy.wait_recv()
        for i in range(smalls):
            if small_wide[i]:
                total = from_mp[i][0]
                for e in range(1, mp):
                    total = total + from_mp[i][e]
                small_out[i][...] = total
            else:
                small_out[i][...] = running[i][3]

    two, one, z = [None] * count, [None] * count, [None] * count

    def stage_core(c):
        local[c].wait()
        core_copy[c].wait_recv()

        def body(i, carry):
            at = (i // 4, (i // 2) % 2, i % 2)
            own[c][at] = own[c][at] + from_core[c][at]
            return carry

        lax.fori_loop(0, mp * 4, body, 0)
        two[c] = [
            push(c, 1, own[c].at[low, 1 - y], from_y2[c], dy),
            push(c, 2, own[c].at[high, :, 1 - x], from_x2[c], dx),
        ]

    def stage_two(c):
        for copy in two[c]:
            copy.wait_recv()

        def body(i, carry):
            a, b = i // 2, i % 2
            own[c][a, y, b] = own[c][a, y, b] + from_y2[c][a, b]
            own[c][half + a, b, x] = own[c][half + a, b, x] + from_x2[c][a, b]
            return carry

        lax.fori_loop(0, half * 2, body, 0)
        one[c] = [
            push(c, 3, own[c].at[low, y, 1 - x], from_x1[c], dx),
            push(c, 4, own[c].at[high, 1 - y, x], from_y1[c], dy),
        ]

    def stage_one(c):
        for copy in one[c]:
            copy.wait_recv()

        def body(a, carry):
            own[c][a, y, x] = own[c][a, y, x] + from_x1[c][a]
            own[c][half + a, y, x] = own[c][half + a, y, x] + from_y1[c][a]
            return carry

        lax.fori_loop(0, half, body, 0)
        z[c] = [
            send(own[c].at[e, y, x], from_z[c].at[step], z_send.at[c, step], z_recv.at[c, step], (d, e))
            for step, e in enumerate(ring(m, mp))
        ]
        pending.extend(z[c])

    def stage_z(c):
        for copy in z[c]:
            copy.wait_recv()
        total = own[c][m, y, x].astype(F32)
        for step in range(mp - 1):
            total = total + from_z[c][step].astype(F32)
        totals[c][...] = total

    tiny = small_dp(0, dc)
    for step in range(count + 3):
        if step < count:
            stage_core(step)
        if 0 <= step - 1 < count:
            stage_two(step - 1)
        if 0 <= step - 2 < count:
            stage_one(step - 2)
        if 0 <= step - 3 < count:
            stage_z(step - 3)
        if step == 0:
            small_dp_end(0, tiny)
            tiny = small_dp(1, dx)
        if step == 1:
            small_dp_end(1, tiny)
            tiny = small_dp(2, dy)
        if step == 2:
            small_dp_end(2, tiny)
            tiny = small_mp()
        if step == 3:
            small_mp_end(tiny)
    for copy in pending:
        copy.wait_send()


def reduce(parts, small, small_wide):
    dp, mp = lax.axis_size("dp"), lax.axis_size("mp")
    count, smalls = len(parts), len(small)
    if dp != 8:
        totals = []
        for part in parts:
            over_mp = lax.psum_scatter(part, "mp", scatter_dimension=0)
            totals.append(lax.psum_scatter(over_mp, "dp", scatter_dimension=0).astype(F32))
        return (
            *totals,
            *[lax.psum(s, ("dp", "mp") if wide else "dp") for s, wide in zip(small, small_wide)],
        )
    half = mp // 2
    rows, width = parts[0].shape[2:]
    block = (rows, width)
    views = [p.reshape((mp, 2, 2, 2) + block) for p in parts]
    scratch = []
    for lead in ((mp, 2, 2), (mp, 2, 2), (half, 2), (mp - half, 2), (half,), (mp - half,), (mp - 1,)):
        scratch += [pltpu.VMEM(lead + block, BF) for _ in range(count)]
    scratch += [pltpu.VMEM((4,) + s.shape, F32) for s in small]
    scratch += [pltpu.VMEM((3,) + s.shape, F32) for s in small]
    scratch += [pltpu.VMEM((mp,) + s.shape, F32) for s in small]
    return pl.pallas_call(
        functools.partial(reduce_kernel, count, small_wide),
        name="reduce_gradients",
        out_shape=tuple(struct(block, F32) for _ in parts) + tuple(struct(s.shape, F32) for s in small),
        in_specs=[IN_HBM] * count + [IN_VMEM] * smalls,
        out_specs=(IN_VMEM,) * (count + smalls),
        scratch_shapes=scratch
        + [
            dma(count),
            dma(count, 5),
            dma(count, 5),
            dma(count, mp - 1),
            dma(count, mp - 1),
            dma(8 * smalls),
            dma(8 * smalls),
        ],
        compiler_params=pltpu.CompilerParams(collective_id=1, has_side_effects=True, vmem_limit_bytes=ROOM),
    )(*views, *small)


def spread_sum(block, slots, send_sem, recv_sem, axis, first):
    d, m = lax.axis_index("dp"), lax.axis_index("mp")
    count = lax.axis_size(axis)
    me = d if axis == "dp" else m
    copies = []
    for step, e in enumerate(ring(me, count)):
        peer = (e, m) if axis == "dp" else (d, e)
        copies.append(send(block, slots.at[me], send_sem.at[first + step], recv_sem.at[first + step], peer))
    slots[me] = block[...]
    for copy in copies:
        copy.wait()
    total = slots[0]
    for e in range(1, count):
        total = total + slots[e]
    return total


def total_of(values):
    return jnp.sum(jnp.sum(values, axis=1, keepdims=True), axis=0, keepdims=True)


def lanes_of(items):
    lane = lax.broadcasted_iota(jnp.int32, (1, 128), 1)
    row = jnp.zeros((1, 128), F32)
    for index, item in enumerate(items):
        row = row + jnp.where(lane == index, item, 0.0)
    return row


def update_kernel(
    g0, g1, g2, w0, w1, w2, rows, cols, gain_sum, gain, gain_mom, chan_sum, chan, chan_mom,
    fin_sum, fin, fin_mom, fout_sum, fout, fout_mom,
    norm_out, c0, c1, c2, n0, n1, n2, rows_out, cols_out, gain_g, gain_n, gain_m,
    chan_g, chan_n, chan_m, fin_g, fin_n, fin_m, fout_g, fout_n, fout_m,
    turn, mp_block, dp_block, mp_slots, dp_slots, last_block, mp_last, dp_last, send_sem, recv_sem,
):
    d, m = lax.axis_index("dp"), lax.axis_index("mp")
    dp, mp = lax.axis_size("dp"), lax.axis_size("mp")
    size, width = g0.shape
    in_width = 3 * (width // 4)
    greet([(e, m) for e in ring(d, dp)] + [(d, e) for e in ring(m, mp)])
    is_in = lax.broadcasted_iota(jnp.int32, (size, width), 1) < in_width

    def four(v0, v1, v2, reduce_fn):
        return [
            reduce_fn(jnp.where(is_in, v0, 0.0)),
            reduce_fn(jnp.where(is_in, 0.0, v0)),
            reduce_fn(v1),
            reduce_fn(v2),
        ]

    def row_sum(v):
        return jnp.sum(v, axis=1, keepdims=True)

    def col_sum(v):
        return jnp.sum(v, axis=0, keepdims=True)

    s0, s1, s2 = g0[...] * g0[...], g1[...] * g1[...], g2[...] * g2[...]
    lane = lax.broadcasted_iota(jnp.int32, (size, 128), 1)
    row_parts = four(s0, s1, s2, row_sum)
    packed = jnp.zeros((size, 128), F32)
    for index, part in enumerate(row_parts):
        packed = packed + jnp.where(lane == index, part, 0.0)
    turn[...] = jnp.zeros(turn.shape, F32)
    dp_block[...] = jnp.zeros(dp_block.shape, F32)
    turn[pl.ds(0, size), :] = packed
    mp_block[pl.ds(0, 8), :] = jnp.transpose(turn[...])[0:8]
    old = rows[...]
    old_parts = [total_of(old[:, i : i + 1]) / mp for i in range(4)]
    weight_parts = four(w0[...] * w0[...], w1[...] * w1[...], w2[...] * w2[...], total_of)
    scalars = (
        [total_of(p) for p in row_parts]
        + old_parts
        + weight_parts
        + [
            total_of(gain[...] * gain[...]) / mp,
            total_of(chan[...] * chan[...]) / dp,
            total_of(fout[...] * fout[...]) / dp,
            total_of(fout_sum[...] * fout_sum[...]) / dp,
        ]
    )
    mp_block[pl.ds(8, 8), :] = jnp.broadcast_to(lanes_of(scalars), (8, 128))
    over_mp = spread_sum(mp_block, mp_slots, send_sem, recv_sem, "mp", 0)
    pieces = width // 128
    for index, values in enumerate((s0, s1, s2)):
        sums = col_sum(values)
        for piece in range(pieces):
            dp_block[pl.ds(index * pieces + piece, 1), :] = sums[:, piece * 128 : (piece + 1) * 128]
    dp_block[pl.ds(3 * pieces, 1), :] = over_mp[8:9]
    over_dp = spread_sum(dp_block, dp_slots, send_sem, recv_sem, "dp", mp)
    turn[pl.ds(0, 8), :] = over_mp[0:8]
    row_totals = jnp.transpose(turn[...])[0:size]
    shared = over_dp[3 * pieces : 3 * pieces + 1]

    def scalar(index):
        return shared[:, index : index + 1]

    gains_sq = total_of(jnp.sum(gain_sum[...] * gain_sum[...], axis=0))
    chan_sq = total_of(jnp.sum(chan_sum[...] * chan_sum[...], axis=0))
    fin_sq = total_of(fin_sum[...] * fin_sum[...])
    norm = jnp.sqrt(
        scalar(0) + scalar(1) + scalar(2) + scalar(3) + gains_sq + chan_sq + scalar(15) + fin_sq
    )
    norm_out[...] = norm
    clip = 1.0 / jnp.maximum(1.0, norm / CLIP_NORM)
    square = clip * clip
    fresh = 1.0 - MOMENT_DECAY
    all_rows = size * dp
    wide = [in_width * mp, (width - in_width) * mp, width * mp, width * mp]
    ratio = []
    lane4 = lax.broadcasted_iota(jnp.int32, (size, 4), 1)
    fresh_rows = jnp.zeros((size, 4), F32)
    for index in range(4):
        row_new = (
            MOMENT_DECAY * old[:, index : index + 1]
            + fresh * square * row_totals[:, index : index + 1] / wide[index]
        )
        mean = MOMENT_DECAY * scalar(4 + index) / all_rows + fresh * square * scalar(index) / (
            all_rows * wide[index]
        )
        ratio.append(row_new / mean)
        fresh_rows = fresh_rows + jnp.where(lane4 == index, row_new, 0.0)
    rows_out[...] = fresh_rows
    for index in range(3):
        for piece in range(pieces):
            at = pl.ds(piece * 128, 128)
            row = index * pieces + piece
            cols_out[pl.ds(index, 1), at] = (
                MOMENT_DECAY * cols[pl.ds(index, 1), at]
                + fresh * square * over_dp[row : row + 1] / all_rows
            )
    first_ratio = jnp.where(is_in, ratio[0], ratio[1])
    steps = []
    for grad, out, factor, index in ((g0, c0, first_ratio, 0), (g1, c1, ratio[2], 1), (g2, c2, ratio[3], 2)):
        clipped = grad[...] * clip
        out[...] = clipped
        steps.append(clipped * lax.rsqrt(factor * cols_out[pl.ds(index, 1), :]))
    u0, u1, u2 = steps

    def plain(clipped, moment, grad_out, moment_out):
        fresh_moment = MOMENT_DECAY * moment + fresh * clipped * clipped
        grad_out[...] = clipped
        moment_out[...] = fresh_moment
        return clipped * lax.rsqrt(fresh_moment)

    own_gain = gain_sum[0]
    for e in range(1, dp):
        own_gain = jnp.where(d == e, gain_sum[e], own_gain)
    own_chan = chan_sum[0]
    for e in range(1, mp):
        own_chan = jnp.where(m == e, chan_sum[e], own_chan)
    u_gain = plain(own_gain * clip, gain_mom[...], gain_g, gain_m)
    u_chan = plain(own_chan * clip, chan_mom[...], chan_g, chan_m)
    u_fin = plain(fin_sum[...] * clip, fin_mom[...], fin_g, fin_m)
    u_fout = plain(fout_sum[...] * clip, fout_mom[...], fout_g, fout_m)
    step_parts = four(u0 * u0, u1 * u1, u2 * u2, total_of) + [
        total_of(u_gain * u_gain) / mp,
        total_of(u_chan * u_chan) / dp,
        total_of(u_fout * u_fout) / dp,
    ]
    last_block[...] = jnp.broadcast_to(lanes_of(step_parts), (8, 128))
    half_way = spread_sum(last_block, mp_last, send_sem, recv_sem, "mp", mp + dp)
    mp_block[pl.ds(0, 8), :] = half_way
    step_sums = spread_sum(mp_block.at[pl.ds(0, 8)], dp_last, send_sem, recv_sem, "dp", 2 * mp + dp)[0:1]

    def factors(step_total, weight_total, entries):
        shrink = 1.0 / jnp.maximum(1.0, jnp.sqrt(step_total / entries) / CLIP_STEP)
        return STEP_RATE * jnp.sqrt(weight_total / entries) * shrink

    def step_sum(index):
        return step_sums[:, index : index + 1]

    rate = [factors(step_sum(i), scalar(8 + i), all_rows * wide[i]) for i in range(4)]
    n0[...] = w0[...] - jnp.where(is_in, rate[0], rate[1]) * u0
    n1[...] = w1[...] - rate[2] * u1
    n2[...] = w2[...] - rate[3] * u2
    gain_n[...] = gain[...] - factors(step_sum(4), scalar(12), 2 * all_rows) * u_gain
    chan_n[...] = chan[...] - factors(step_sum(5), scalar(13), chan.shape[0] * chan.shape[1] * mp) * u_chan
    fout_n[...] = fout[...] - factors(step_sum(6), scalar(14), fout.shape[0] * fout.shape[1] * mp) * u_fout
    fin_count = fin.shape[0] * fin.shape[1]
    fin_rate = factors(total_of(u_fin * u_fin), total_of(fin[...] * fin[...]), fin_count)
    fin_n[...] = fin[...] - fin_rate * u_fin


def update(grads, weights, rows, cols, gain, chan, fin, fout):
    dp, mp = lax.axis_size("dp"), lax.axis_size("mp")
    big = struct(grads[0].shape, F32)
    small = [struct(v[1].shape, F32) for v in (gain, chan, fin, fout) for _ in range(3)]
    outs = (struct((1, 1), F32),) + (big,) * 6 + (struct(rows.shape, F32), struct(cols.shape, F32), *small)
    inputs = [*grads, *weights, rows, cols, *gain, *chan, *fin, *fout]
    pieces = 3 * grads[0].shape[1] // 128 + 1
    tall = -(-pieces // 8) * 8
    sems = 2 * (dp + mp)
    return pl.pallas_call(
        update_kernel,
        name="clip_and_update",
        out_shape=outs,
        in_specs=[IN_VMEM] * len(inputs),
        out_specs=(IN_VMEM,) * len(outs),
        scratch_shapes=[
            pltpu.VMEM((128, 128), F32),
            pltpu.VMEM((16, 128), F32),
            pltpu.VMEM((tall, 128), F32),
            pltpu.VMEM((mp, 16, 128), F32),
            pltpu.VMEM((dp, tall, 128), F32),
            pltpu.VMEM((8, 128), F32),
            pltpu.VMEM((mp, 8, 128), F32),
            pltpu.VMEM((dp, 8, 128), F32),
            dma(sems),
            dma(sems),
        ],
        compiler_params=pltpu.CompilerParams(collective_id=2, has_side_effects=True, vmem_limit_bytes=ROOM),
    )(*inputs)


def features(length, feature_count, count):
    step = np.arange(count)
    band = np.arange(1, (feature_count - 1) // 2 + 1)
    phase = ((step[:, None] * band[None, :]) % length).astype(np.float32) * np.float32(2.0 * math.pi / length)
    position = (step / length).astype(np.float32)
    table = np.concatenate([position[:, None], np.cos(phase), np.sin(phase)], axis=1)
    return table.astype(np.float32), position


def product(left, right):
    return jnp.dot(left, right, precision=FULL_PRECISION, preferred_element_type=F32)


def norm_parts(values):
    centred = values - jnp.mean(values, axis=-1, keepdims=True)
    inverse_std = lax.rsqrt(jnp.mean(centred * centred, axis=-1, keepdims=True) + EPS_NORM)
    return centred * inverse_std, inverse_std


def norm_back(grad, gain, normed, inverse_std):
    scaled = grad * gain
    mean = jnp.mean(scaled, axis=-1, keepdims=True)
    along = jnp.mean(scaled * normed, axis=-1, keepdims=True)
    return (scaled - mean - normed * along) * inverse_std


def to_parts(values, mp, block):
    own = values.shape[1] // mp
    return values.reshape(2, block, mp, own).transpose(2, 1, 0, 3).reshape(mp, block, 2 * own)


def from_parts(values):
    mp, block, wide = values.shape
    own = wide // 2
    return values.reshape(mp, block, 2, own).transpose(2, 1, 0, 3).reshape(2 * block, mp * own)


def per_device(
    tokens, cotangent, doc_lengths, in_weight, out_weight, up_weight, down_weight, gains, channel_weight,
    filter_in, filter_out, in_rows, in_cols, out_rows, out_cols, up_rows, up_cols, down_rows, down_cols,
    gain_moment, channel_moment, filter_in_moment, filter_out_moment,
):
    dp, mp = lax.axis_size("dp"), lax.axis_size("mp")
    m = lax.axis_index("mp")
    count, width = tokens.shape
    length = count * mp
    own = channel_weight.shape[1]
    rows = in_weight.shape[0]
    hidden = up_weight.shape[1]
    taps = (channel_weight.shape[0] - 1) // 3
    most = length // 2

    first_shard = jnp.concatenate([in_weight.reshape(rows, 3 * own), out_weight], axis=1)
    chunks = [v.astype(BF) for v in (first_shard, up_weight, down_weight)]
    lanes = 128
    gain_block = jnp.pad(gains.T.astype(BF), ((0, 14), (0, lanes - rows)))
    chan_block = jnp.pad(channel_weight, ((0, 16 - channel_weight.shape[0]), (0, 0)))
    edges = jnp.stack([tokens[count - EDGE :], tokens[:EDGE]])
    whole_first, whole_up, whole_down, gains_all, chan_all, edges_all = gather(chunks, gain_block, chan_block, edges)
    whole_first = whole_first.reshape(mp, width, width)
    whole_up = whole_up.reshape(mp, width, hidden)
    whole_down = whole_down.reshape(mp, width, hidden)
    w_in = whole_first[:, :, : 3 * own].reshape(mp, width, 3, own).transpose(1, 2, 0, 3).reshape(width, 3 * width)
    w_out = whole_first[:, :, 3 * own :].transpose(1, 0, 2).reshape(width, width)
    gain_rows = gains_all[:, 0:2, :rows].transpose(1, 0, 2).reshape(2, width).astype(F32)
    chan_rows = chan_all[:, : channel_weight.shape[0]].transpose(1, 0, 2).reshape(-1, width)
    conv_taps = chan_rows[:-1].reshape(taps, 3, width)
    skip_gain = chan_rows[-1]

    position = m * count - EDGE + jnp.arange(count + 2 * EDGE, dtype=jnp.int32)
    ends = jnp.cumsum(doc_lengths[0])
    doc = jnp.sum((position[:, None] >= ends[None, :]).astype(jnp.int32), axis=1)
    doc = jnp.where(position < 0, -1, doc)

    def alike(offset):
        return (doc[EDGE:] == doc[EDGE - offset : doc.shape[0] - offset])[:, None]

    extended = jnp.concatenate([edges_all[0], tokens, edges_all[1]]).astype(F32)
    n1, inv1 = norm_parts(extended)
    a = (n1 * gain_rows[0]).astype(BF)
    z = jnp.dot(a, w_in, preferred_element_type=F32)
    z_at = [[None] * 3 for _ in range(taps)]
    s = [None] * 3
    for j in range(3):
        stream = z[:, j * width : (j + 1) * width]
        total = None
        for k in range(taps):
            part = stream[EDGE - k : stream.shape[0] - k]
            if k:
                part = jnp.where(alike(k), part, 0.0)
            z_at[k][j] = part[:count]
            term = conv_taps[k, j] * part
            total = term if total is None else total + term
        s[j] = total
    w_own = s[2][:count] * s[1][:count]
    s0 = s[0][:count]

    table, step = features(length, filter_in.shape[0], most)
    phase = product(table, filter_in)
    hidden_filter = jnp.sin(phase)
    channel = (m * own + jnp.arange(own, dtype=jnp.int32)).astype(F32)
    rate = FAST_DECAY + (SLOW_DECAY - FAST_DECAY) * channel / (width - 1)
    decay = jnp.exp(-step[:, None] * rate[None, :])
    filters = product(hidden_filter, filter_out) * decay
    tables = tuple(jnp.asarray(t) for t in transform_tables(BLOCK))
    (w_parts,) = exchange([to_parts(w_own.astype(BF), mp, count // 2)], None, 3)
    y_parts, spectrum = conv_forward(w_parts, doc_lengths, filters, tables)
    (y_back,) = exchange([y_parts], None, 4)
    y = from_parts(y_back).astype(F32) + skip_gain * w_own

    o = (y * s0).astype(BF)
    x2 = tokens.astype(F32) + lax.dot_general(o, w_out, (((1,), (1,)), ((), ())), preferred_element_type=F32)
    n2, inv2 = norm_parts(x2)
    b = (n2 * gain_rows[1]).astype(BF)
    hpre = jnp.einsum("td,mdf->mtf", b, whole_up, preferred_element_type=F32)
    act, act_pull = jax.vjp(lambda v: jax.nn.gelu(v, approximate=True), hpre)
    act = act.astype(BF)
    activations = (x2 + jnp.einsum("mtf,mdf->td", act, whole_down, preferred_element_type=F32)).astype(BF)
    (g_hpre,) = act_pull(jnp.einsum("td,mdf->mtf", cotangent, whole_down, preferred_element_type=F32))
    g_hpre = g_hpre.astype(BF)
    up_part = jnp.einsum("td,mtf->mdf", b, g_hpre, preferred_element_type=F32).astype(BF)
    down_part = jnp.einsum("td,mtf->mdf", cotangent, act, preferred_element_type=F32).astype(BF)
    g_b = jnp.einsum("mtf,mdf->td", g_hpre, whole_up, preferred_element_type=F32)
    gain2_part = jnp.sum(g_b * n2, axis=0)
    g_x2 = cotangent.astype(F32) + norm_back(g_b, gain_rows[1], n2, inv2)
    g_mix = g_x2.astype(BF)
    g_o = jnp.dot(g_mix, w_out, preferred_element_type=F32)
    out_part = lax.dot_general(g_mix, o, (((0,), (0,)), ((), ())), preferred_element_type=F32)
    g_y = g_o * s0
    g_s0 = g_o * y
    skip_part = jnp.sum(g_y * w_own, axis=0)

    g_parts, g_s0_edge = exchange([to_parts(g_y.astype(BF), mp, count // 2)], g_s0[:EDGE].astype(BF), 5)
    gw_parts, gw_edges, g_filters = conv_backward(
        g_parts, w_parts, doc_lengths, spectrum, channel_weight[-1:], tables
    )
    gw_back, gw_edge = exchange([gw_parts, gw_edges], None, 6)
    gw_own = from_parts(gw_back).astype(F32) + skip_gain * g_y
    gw_next = gw_edge[:, :, :own].transpose(1, 0, 2).reshape(EDGE, width).astype(F32)
    g_w = jnp.concatenate([gw_own, gw_next])
    g_s = [jnp.concatenate([g_s0, g_s0_edge.astype(F32)]), g_w * s[2], g_w * s[1]]
    g_z, tap_parts = [], [[None] * 3 for _ in range(taps)]
    for j in range(3):
        total = None
        for k in range(taps):
            part = g_s[j][k : count + k]
            if k:
                part = jnp.where(alike(k)[k : count + k], part, 0.0)
            term = conv_taps[k, j] * part
            total = term if total is None else total + term
            tap_parts[k][j] = jnp.sum(g_s[j][:count] * z_at[k][j], axis=0)
        g_z.append(total.astype(BF))
    g_z = jnp.concatenate(g_z, axis=1)
    own_a = a[EDGE : EDGE + count]
    in_part = lax.dot_general(own_a, g_z, (((0,), (0,)), ((), ())), preferred_element_type=F32)
    g_a = lax.dot_general(g_z, w_in, (((1,), (1,)), ((), ())), preferred_element_type=F32)
    own_n1, own_inv1 = n1[EDGE : EDGE + count], inv1[EDGE : EDGE + count]
    gain1_part = jnp.sum(g_a * own_n1, axis=0)
    input_grad = (g_x2 + norm_back(g_a, gain_rows[0], own_n1, own_inv1)).astype(BF)

    g_raw = g_filters * decay
    fout_part = product(hidden_filter.T, g_raw)
    fin_part = product(table.T, product(g_raw, filter_out.T) * jnp.cos(phase))

    first_part = jnp.concatenate(
        [
            in_part.reshape(width, 3, mp, own).transpose(2, 0, 1, 3).reshape(mp, width, 3 * own),
            out_part.reshape(width, mp, own).transpose(1, 0, 2),
        ],
        axis=2,
    ).astype(BF)
    parts = [p.reshape(mp, dp, rows, p.shape[2]) for p in (first_part, up_part, down_part)]
    gain_part = jnp.stack([gain1_part, gain2_part]).reshape(2, dp, rows).transpose(1, 0, 2)
    gain_part = jnp.pad(gain_part, ((0, 0), (0, 0), (0, lanes - rows)))
    chan_part = jnp.stack([tap_parts[k][j] for k in range(taps) for j in range(3)] + [skip_part])
    chan_part = chan_part.reshape(-1, mp, own).transpose(1, 0, 2)
    g0, g1, g2, gain_sum, chan_sum, fin_sum, fout_sum = reduce(
        parts, [gain_part, chan_part, fin_part, fout_part], (True, True, True, False)
    )

    def padded(values, fill):
        return jnp.pad(values.T, ((0, 0), (0, lanes - rows)), constant_values=fill)

    first_cols = jnp.concatenate([in_cols.reshape(3 * own), out_cols])
    results = update(
        (g0, g1, g2),
        (first_shard, up_weight, down_weight),
        jnp.stack([in_rows, out_rows, up_rows, down_rows], axis=1),
        jnp.stack([first_cols, up_cols, down_cols]),
        (gain_sum, padded(gains, 0.0), padded(gain_moment, 1.0)),
        (chan_sum, channel_weight, channel_moment),
        (fin_sum, filter_in, filter_in_moment),
        (fout_sum, filter_out, filter_out_moment),
    )
    norm, c0, c1, c2, n0, n1_, n2_, rows_new, cols_new = results[:9]
    small = results[9:]
    gain_g, gain_n, gain_m = [v[:, :rows].T for v in small[0:3]]

    def parted(values):
        return values[:, : 3 * own].reshape(rows, 3, own), values[:, 3 * own :]

    in_grad, out_grad = parted(c0)
    in_new, out_new = parted(n0)
    return (
        activations, input_grad, norm.reshape(()),
        in_grad, out_grad, c1, c2, gain_g, small[3], small[6], small[9],
        in_new, out_new, n1_, n2_, gain_n, small[4], small[7], small[10],
        rows_new[:, 0], cols_new[0, : 3 * own].reshape(3, own),
        rows_new[:, 1], cols_new[0, 3 * own :],
        rows_new[:, 2], cols_new[1],
        rows_new[:, 3], cols_new[2],
        gain_m, small[5], small[8], small[11],
    )


def solution(mesh):
    tokens, by_rows, by_cols, both = P(("dp", "mp"), None), P("dp", None), P(None, "mp"), P("dp", "mp")
    cube, vec_dp, vec_mp = P("dp", None, "mp"), P("dp"), P("mp")
    moments = (vec_dp, by_cols, vec_dp, vec_mp, vec_dp, vec_mp, vec_dp, vec_mp)
    weights = (cube, both, both, both, by_rows, by_cols, P(), by_cols)
    small = (by_rows, by_cols, P(), by_cols)
    return jax.shard_map(
        per_device,
        mesh=mesh,
        in_specs=(tokens, tokens, by_rows) + weights + moments + small,
        out_specs=(tokens, tokens, P()) + weights + weights + moments + small,
        check_vma=False,
    )
```

```python
import functools
import math

import jax
import jax.numpy as jnp
import ml_dtypes
import numpy as np
from jax import lax
from jax.experimental import pallas as pl
from jax.experimental.pallas import tpu as pltpu
from jax.sharding import PartitionSpec as P

EPS_NORM = 1e-05
MOMENT_DECAY = 0.5
CLIP_NORM = 1.0
CLIP_STEP = 0.25
STEP_RATE = 2.0
FAST_DECAY = 15.35
SLOW_DECAY = 3.07
FULL_PRECISION = lax.Precision.HIGHEST
BF = jnp.bfloat16
F32 = jnp.float32
MESH = pl.DeviceIdType.MESH
BLOCK = 256
EDGE = 16
ROOM = 56 << 20
IN_VMEM = pl.BlockSpec(memory_space=pltpu.VMEM)
IN_HBM = pl.BlockSpec(memory_space=pl.ANY)
IN_SMEM = pl.BlockSpec(memory_space=pltpu.SMEM)


def struct(shape, dtype):
    return jax.ShapeDtypeStruct(tuple(shape), dtype)


def transform_tables(block):
    freq = 2 * np.arange(block)[:, None] + 1
    angle = np.pi * (freq * np.arange(block)[None, :] % (4 * block)) / (2 * block)
    table = np.concatenate([np.cos(angle), -np.sin(angle)], axis=0).astype(np.float32)
    high = table.astype(ml_dtypes.bfloat16)
    low = (table - high.astype(np.float32)).astype(ml_dtypes.bfloat16)
    return high, low, np.ascontiguousarray(high.T), np.ascontiguousarray(low.T)


def mm(left, right):
    return lax.dot_general(left, right, (((1,), (0,)), ((), ())), preferred_element_type=F32)


def split(values):
    high = values.astype(BF)
    return high, (values - high.astype(F32)).astype(BF)


def load_rows(ref, start, count, lead=()):
    odd = lax.rem(start, 8)
    tile = ref[lead + (pl.ds(lax.div(start, 8), count // 8 + 1),)]
    width = tile.shape[-1]
    tile = pltpu.roll(tile, lax.rem(8 - odd, 8), axis=1)
    first = lax.broadcasted_iota(jnp.int32, (count // 8, 8, width), 1) < 8 - odd
    return jnp.where(first, tile[:-1], tile[1:]).reshape(count, width)


def tiles(values):
    return values.reshape(values.shape[0] // 8, 8, values.shape[1])


def unpack(target, source):
    parts, block, width = source.shape
    half, count = width // 2, block // 8
    for part in range(parts):
        for side in range(2):
            values = source[part, :, side * half : (side + 1) * half].astype(F32)
            target[pl.ds((2 * part + side) * count, count)] = tiles(values)


def pair_rows(index, block, size):
    first = pl.multiple_of(index * size, size)
    return pl.ds(first, size), pl.ds(pl.multiple_of(block + first, size), size)


def signs(size, width, scale):
    odd = lax.broadcasted_iota(jnp.int32, (size, width), 0) % 2
    return jnp.where(odd == 0, scale, -scale).astype(F32)


def filter_spectrum(filter_ref, spectrum, raw, tables, block):
    count = raw.shape[0]
    high, low = tables[0][...], tables[1][...]
    for lag in range(count):
        top, rest = split(filter_ref[pl.ds(lag * block, block), :])
        raw[lag] = mm(high, top) + mm(high, rest) + mm(low, top)
    scale = 1.0 / block

    def body(index, carry):
        re_rows, im_rows = pair_rows(index, block, 8)
        sign = signs(8, raw.shape[2], scale)
        for lag in range(count):
            re, im = raw[lag, re_rows, :] * scale, raw[lag, im_rows, :] * scale
            if lag:
                re = re - sign * raw[lag - 1, im_rows, :]
                im = im + sign * raw[lag - 1, re_rows, :]
            spectrum[lag, re_rows, :] = re
            spectrum[lag, im_rows, :] = im
        return carry

    lax.fori_loop(0, block // 8, body, 0)


def slot_blocks(source, target, tables, start, length, block):
    high, low = tables[0][...], tables[1][...]
    for index in range(target.shape[0]):
        values = load_rows(source, start + index * block, block)
        inside = lax.broadcasted_iota(jnp.int32, values.shape, 0) + index * block < length
        values = jnp.where(inside, values, 0.0).astype(BF)
        target[index] = mm(high, values) + mm(low, values)


def inverse(top, rest, tables):
    high, low = tables[2][...], tables[3][...]
    return mm(high, top) + mm(high, rest) + mm(low, top)


def document_starts(len_ref, count):
    starts, at = [], jnp.int32(0)
    for slot in range(count):
        starts.append(at)
        at = at + len_ref[0, slot]
    return starts


def merge_slots(slots, starts, put, total, block, most):
    for index in range(total // block):
        first = index * block
        merged = None
        for slot, start in enumerate(starts):
            at = jnp.clip(first - start, -block, most) + block
            values = load_rows(slots, at, block, (slot,))
            if merged is None:
                merged = values
            else:
                inside = lax.broadcasted_iota(jnp.int32, values.shape, 0) + first >= start
                merged = jnp.where(inside, values, merged)
        put(index, merged)


def forward_products(spectrum, raw, top, rest, block):
    count = raw.shape[0]

    def body(index, carry):
        re_rows, im_rows = pair_rows(index, block, 16)
        hr = [spectrum[i, re_rows, :] for i in range(count)]
        hi = [spectrum[i, im_rows, :] for i in range(count)]
        xr = [raw[i, re_rows, :] for i in range(count)]
        xi = [raw[i, im_rows, :] for i in range(count)]
        for out in range(count):
            re = hr[0] * xr[out] - hi[0] * xi[out]
            im = hr[0] * xi[out] + hi[0] * xr[out]
            for lag in range(1, out + 1):
                re = re + (hr[lag] * xr[out - lag] - hi[lag] * xi[out - lag])
                im = im + (hr[lag] * xi[out - lag] + hi[lag] * xr[out - lag])
            top[out, re_rows, :], rest[out, re_rows, :] = split(re)
            top[out, im_rows, :], rest[out, im_rows, :] = split(im)
        return carry

    lax.fori_loop(0, block // 16, body, 0)


def backward_products(spectrum, grad, raw, total, top, rest, block, first_slot):
    count = raw.shape[0]

    def body(index, carry):
        re_rows, im_rows = pair_rows(index, block, 16)
        gr = [grad[i, re_rows, :] for i in range(count)]
        gi = [grad[i, im_rows, :] for i in range(count)]
        hr = [spectrum[i, re_rows, :] for i in range(count)]
        hi = [spectrum[i, im_rows, :] for i in range(count)]
        for out in range(count):
            re = hr[0] * gr[out] + hi[0] * gi[out]
            im = hr[0] * gi[out] - hi[0] * gr[out]
            for later in range(out + 1, count):
                lag = later - out
                re = re + (hr[lag] * gr[later] + hi[lag] * gi[later])
                im = im + (hr[lag] * gi[later] - hi[lag] * gr[later])
            top[out, re_rows, :], rest[out, re_rows, :] = split(re)
            top[out, im_rows, :], rest[out, im_rows, :] = split(im)
        xr = [raw[i, re_rows, :] for i in range(count)]
        xi = [raw[i, im_rows, :] for i in range(count)]
        for lag in range(count):
            re = im = None
            for at in range(count - lag):
                a = xr[at] * gr[at + lag] + xi[at] * gi[at + lag]
                b = xr[at] * gi[at + lag] - xi[at] * gr[at + lag]
                re = a if re is None else re + a
                im = b if im is None else im + b
            if not first_slot:
                re = re + total[lag, re_rows, :]
                im = im + total[lag, im_rows, :]
            total[lag, re_rows, :] = re
            total[lag, im_rows, :] = im
        return carry

    lax.fori_loop(0, block // 16, body, 0)


def filter_gradient(total, top, rest, tables, out_ref, block):
    count, width = total.shape[0], total.shape[2]
    scale = 1.0 / block

    def body(index, carry):
        re_rows, im_rows = pair_rows(index, block, 16)
        sign = signs(16, width, 1.0)
        for lag in range(count):
            re, im = total[lag, re_rows, :], total[lag, im_rows, :]
            if lag + 1 < count:
                re = re + sign * total[lag + 1, im_rows, :]
                im = im - sign * total[lag + 1, re_rows, :]
            top[lag, re_rows, :], rest[lag, re_rows, :] = split(re * scale)
            top[lag, im_rows, :], rest[lag, im_rows, :] = split(im * scale)
        return carry

    lax.fori_loop(0, block // 16, body, 0)
    for lag in range(count):
        out_ref[pl.ds(lag * block, block), :] = inverse(top[lag], rest[lag], tables)


def conv_forward_kernel(doc_count, len_ref, x_ref, filter_ref, t0, t1, t2, t3, y_ref, spectrum, full, raw, top, rest, slots):
    tables = (t0, t1, t2, t3)
    parts, block, width = x_ref.shape
    half = width // 2
    count = raw.shape[0]
    filter_spectrum(filter_ref, spectrum, raw, tables, block)
    unpack(full, x_ref)
    starts = document_starts(len_ref, doc_count)
    for slot in range(doc_count):
        slot_blocks(full, raw, tables, starts[slot], len_ref[0, slot], block)
        forward_products(spectrum, raw, top, rest, block)
        for out in range(count):
            slots[slot, pl.ds((1 + out) * block // 8, block // 8)] = tiles(inverse(top[out], rest[out], tables))

    def put(index, values):
        y_ref[index // 2, :, pl.ds((index % 2) * half, half)] = values.astype(y_ref.dtype)

    merge_slots(slots, starts, put, 2 * parts * block, block, count * block)


def conv_forward(x, lengths, filters, tables):
    parts, block, width = x.shape
    half, docs = width // 2, lengths.shape[1]
    count = filters.shape[0] // block
    wide = (count, 2 * block, half)
    return pl.pallas_call(
        functools.partial(conv_forward_kernel, docs),
        name="conv_forward",
        out_shape=(struct(x.shape, BF), struct(wide, F32)),
        in_specs=[IN_SMEM] + [IN_VMEM] * 6,
        out_specs=(IN_VMEM, IN_VMEM),
        scratch_shapes=[
            pltpu.VMEM(((2 * parts + count) * block // 8 + 1, 8, half), F32),
            pltpu.VMEM(wide, F32),
            pltpu.VMEM(wide, BF),
            pltpu.VMEM(wide, BF),
            pltpu.VMEM((docs, (count + 2) * block // 8 + 1, 8, half), F32),
        ],
        compiler_params=pltpu.CompilerParams(vmem_limit_bytes=ROOM),
    )(lengths, x, filters, *tables)


def conv_backward_kernel(doc_count, len_ref, g_ref, x_ref, spectrum, skip_ref, t0, t1, t2, t3, gw_ref, edge_ref, gf_ref, g_full, x_full, grad, raw, top, rest, total, slots):
    tables = (t0, t1, t2, t3)
    parts, block, width = x_ref.shape
    half = width // 2
    count = raw.shape[0]
    unpack(g_full, g_ref)
    unpack(x_full, x_ref)
    starts = document_starts(len_ref, doc_count)
    for slot in range(doc_count):
        slot_blocks(g_full, grad, tables, starts[slot], len_ref[0, slot], block)
        slot_blocks(x_full, raw, tables, starts[slot], len_ref[0, slot], block)
        backward_products(spectrum, grad, raw, total, top, rest, block, slot == 0)
        for out in range(count):
            slots[slot, pl.ds((1 + out) * block // 8, block // 8)] = tiles(inverse(top[out], rest[out], tables))
    edge_ref[...] = jnp.zeros(edge_ref.shape, edge_ref.dtype)

    def put(index, values):
        gw_ref[index // 2, :, pl.ds((index % 2) * half, half)] = values.astype(gw_ref.dtype)
        if index % 2 == 0 and index:
            own = g_full[pl.ds(index * block // 8, EDGE // 8)].reshape(EDGE, half) * skip_ref[...]
            edge_ref[index // 2 - 1, :, 0:half] = (values[0:EDGE] + own).astype(edge_ref.dtype)

    merge_slots(slots, starts, put, 2 * parts * block, block, count * block)
    filter_gradient(total, top, rest, tables, gf_ref, block)


def conv_backward(g, x, lengths, spectrum, skip_gain, tables):
    parts, block, width = x.shape
    half, docs, count = width // 2, lengths.shape[1], spectrum.shape[0]
    wide = (count, 2 * block, half)
    rows = pltpu.VMEM(((2 * parts + count) * block // 8 + 1, 8, half), F32)
    return pl.pallas_call(
        functools.partial(conv_backward_kernel, docs),
        name="conv_backward",
        out_shape=(
            struct(x.shape, BF),
            struct((parts, EDGE, -(-half // 128) * 128), BF),
            struct((count * block, half), F32),
        ),
        in_specs=[IN_SMEM] + [IN_VMEM] * 8,
        out_specs=(IN_VMEM,) * 3,
        scratch_shapes=[
            rows,
            rows,
            pltpu.VMEM(wide, F32),
            pltpu.VMEM(wide, F32),
            pltpu.VMEM(wide, BF),
            pltpu.VMEM(wide, BF),
            pltpu.VMEM(wide, F32),
            pltpu.VMEM((docs, (count + 2) * block // 8 + 1, 8, half), F32),
        ],
        compiler_params=pltpu.CompilerParams(vmem_limit_bytes=ROOM),
    )(lengths, g, x, spectrum, skip_gain, *tables)


def turned(value, bit):
    return value + bit - 2 * bit * ((value // bit) % 2)


def send(source, target, send_sem, recv_sem, device):
    copy = pltpu.make_async_remote_copy(
        src_ref=source,
        dst_ref=target,
        send_sem=send_sem,
        recv_sem=recv_sem,
        device_id=device,
        device_id_type=MESH,
    )
    copy.start()
    return copy


def greet(peers):
    barrier = pltpu.get_barrier_semaphore()
    for peer in peers:
        pl.semaphore_signal(barrier, inc=1, device_id=peer, device_id_type=MESH)
    pl.semaphore_wait(barrier, len(peers))


def ring(me, count):
    return [lax.rem(me + step, count) for step in range(1, count)]


def dma(*shape):
    return pltpu.SemaphoreType.DMA(shape)


def gather_kernel(chunk_count, *refs):
    chunks, refs = refs[:chunk_count], refs[chunk_count:]
    gains, channel, edges, refs = refs[0], refs[1], refs[2], refs[3:]
    whole, refs = refs[:chunk_count], refs[chunk_count:]
    gains_all, channel_all, edges_all, refs = refs[0], refs[1], refs[2], refs[3:]
    own_sem, z_send, z_recv, p_send, p_recv, s_send, s_recv = refs
    d, m = lax.axis_index("dp"), lax.axis_index("mp")
    dp, mp = lax.axis_size("dp"), lax.axis_size("mp")
    half = mp // 2
    dx, dy, dc = turned(d, 2), turned(d, 4), turned(d, 1)
    dxy = turned(dx, 4)
    greet([(e, m) for e in ring(d, dp)] + [(d, e) for e in ring(m, mp)])
    small = []
    for step, e in enumerate(ring(d, dp)):
        small.append(send(gains, gains_all.at[d], s_send.at[step], s_recv.at[step], (e, m)))
    for step, e in enumerate(ring(m, mp)):
        at = dp + step
        small.append(send(channel, channel_all.at[m], s_send.at[at], s_recv.at[at], (d, e)))
    gains_all[d] = gains[...]
    channel_all[m] = channel[...]
    at = dp + mp

    def edge(index, peer):
        return pltpu.make_async_remote_copy(
            src_ref=edges.at[index],
            dst_ref=edges_all.at[index],
            send_sem=s_send.at[at + index],
            recv_sem=s_recv.at[at + index],
            device_id=(d, peer),
            device_id_type=MESH,
        )

    up, down = lax.rem(m + 1, mp), lax.rem(m + mp - 1, mp)
    to_next, to_before = edge(0, up), edge(1, down)
    to_next.start()
    to_before.start()
    own, z = [], []
    for c in range(chunk_count):
        copy = pltpu.make_async_copy(chunks[c], whole[c].at[m, d], own_sem.at[c])
        copy.start()
        own.append(copy)
        z.append(
            [
                send(chunks[c], whole[c].at[m, d], z_send.at[c, step], z_recv.at[c, step], (d, e))
                for step, e in enumerate(ring(m, mp))
            ]
        )
    low, high = pl.ds(0, half), pl.ds(half, mp - half)
    first, second, last = [None] * chunk_count, [None] * chunk_count, [None] * chunk_count

    def push(c, slot, rows, owner, peer):
        block = whole[c].at[rows, owner]
        return send(block, block, p_send.at[c, slot], p_recv.at[c, slot], (peer, m))

    def stage_one(c):
        own[c].wait()
        for copy in z[c]:
            copy.wait_recv()
        first[c] = [push(c, 0, low, d, dx), push(c, 1, high, d, dy)]
        last[c] = [push(c, 2, pl.ds(0, mp), d, dc)]

    def stage_two(c):
        for copy in first[c]:
            copy.wait_recv()
        second[c] = [
            push(c, 3, low, d, dy),
            push(c, 4, high, d, dx),
            push(c, 5, low, dx, dy),
            push(c, 6, high, dy, dx),
        ]

    def stage_three(c):
        for copy in second[c]:
            copy.wait_recv()
        for slot, owner in enumerate((dx, dy, dxy)):
            last[c].append(push(c, 7 + slot, pl.ds(0, mp), owner, dc))

    for step in range(chunk_count + 3):
        if step < chunk_count:
            stage_one(step)
        if 0 <= step - 1 < chunk_count:
            stage_two(step - 1)
        if 0 <= step - 2 < chunk_count:
            stage_three(step - 2)
    for c in range(chunk_count):
        for copy in z[c] + first[c] + second[c]:
            copy.wait_send()
        for copy in last[c]:
            copy.wait()
    for copy in small:
        copy.wait()
    to_next.wait()
    to_before.wait()


def gather(chunks, gains, channel, edges):
    dp, mp = lax.axis_size("dp"), lax.axis_size("mp")
    count = len(chunks)
    outs = tuple(struct((mp, dp) + c.shape, c.dtype) for c in chunks)
    smalls = (
        struct((dp,) + gains.shape, gains.dtype),
        struct((mp,) + channel.shape, channel.dtype),
        struct(edges.shape, edges.dtype),
    )
    if dp != 8:
        down = [(i, (i + 1) % mp) for i in range(mp)]
        up = [(i, (i - 1) % mp) for i in range(mp)]
        spread = [lax.all_gather(lax.all_gather(c, "dp"), "mp") for c in chunks]
        return (
            *spread,
            lax.all_gather(gains, "dp"),
            lax.all_gather(channel, "mp"),
            jnp.stack([lax.ppermute(edges[0], "mp", down), lax.ppermute(edges[1], "mp", up)]),
        )
    return pl.pallas_call(
        functools.partial(gather_kernel, count),
        name="gather_weights",
        out_shape=outs + smalls,
        in_specs=[IN_VMEM] * (count + 3),
        out_specs=(IN_HBM,) * count + (IN_VMEM,) * 3,
        scratch_shapes=[
            dma(count),
            dma(count, mp - 1),
            dma(count, mp - 1),
            dma(count, 10),
            dma(count, 10),
            dma(dp + mp + 2),
            dma(dp + mp + 2),
        ],
        compiler_params=pltpu.CompilerParams(collective_id=0, has_side_effects=True, vmem_limit_bytes=ROOM),
    )(*chunks, gains, channel, edges)


def exchange_kernel(count, has_edge, *refs):
    sources, refs = refs[: count + has_edge], refs[count + has_edge :]
    targets, refs = refs[: count + has_edge], refs[count + has_edge :]
    send_sem, recv_sem, edge_send, edge_recv = refs
    d, m, mp = lax.axis_index("dp"), lax.axis_index("mp"), lax.axis_size("mp")
    greet([(d, e) for e in ring(m, mp)])
    copies = []
    for step, e in reversed(list(enumerate(ring(m, mp)))):
        for i in range(count):
            copies.append(
                send(sources[i].at[e], targets[i].at[m], send_sem.at[i, step], recv_sem.at[i, step], (d, e))
            )
    if has_edge:
        before = lax.rem(m + mp - 1, mp)
        copies.append(send(sources[count], targets[count], edge_send.at[0], edge_recv.at[0], (d, before)))
    for i in range(count):
        targets[i][m] = sources[i][m]
    for copy in copies:
        copy.wait()


def exchange(arrays, edge, collective_id):
    mp, count = lax.axis_size("mp"), len(arrays)
    inputs = list(arrays) + ([] if edge is None else [edge])
    return pl.pallas_call(
        functools.partial(exchange_kernel, count, int(edge is not None)),
        name="exchange_%d" % collective_id,
        out_shape=tuple(struct(a.shape, a.dtype) for a in inputs),
        in_specs=[IN_VMEM] * len(inputs),
        out_specs=(IN_VMEM,) * len(inputs),
        scratch_shapes=[dma(count, mp - 1), dma(count, mp - 1), dma(1), dma(1)],
        compiler_params=pltpu.CompilerParams(
            collective_id=collective_id, has_side_effects=True, vmem_limit_bytes=ROOM
        ),
    )(*inputs)


class Flow:
    def __init__(self, part, refs):
        self.part = part
        (self.own, self.from_core, self.from_y2, self.from_x2, self.from_x1, self.from_y1, self.from_z) = refs[:7]
        self.own_sem, self.p_send, self.p_recv, self.z_send, self.z_recv = refs[7:]
        self.d, self.m, self.mp = lax.axis_index("dp"), lax.axis_index("mp"), lax.axis_size("mp")
        self.half = self.mp // 2
        self.y, self.x, self.core = self.d // 4, (self.d // 2) % 2, self.d % 2
        self.pending = []

    def push(self, slot, source, target, bit):
        peer = (turned(self.d, bit), self.m)
        copy = send(source, target, self.p_send.at[slot], self.p_recv.at[slot], peer)
        self.pending.append(copy)
        return copy

    def start(self):
        self.copy = self.push(0, self.part.at[:, :, :, 1 - self.core], self.from_core, 1)
        self.local = pltpu.make_async_copy(self.part.at[:, :, :, self.core], self.own, self.own_sem.at[0])
        self.local.start()

    def core_stage(self):
        own, half, y, x = self.own, self.half, self.y, self.x
        self.local.wait()
        self.copy.wait_recv()

        def body(i, carry):
            at = (i // 4, (i // 2) % 2, i % 2)
            own[at] = own[at] + self.from_core[at]
            return carry

        lax.fori_loop(0, self.mp * 4, body, 0)
        low, high = pl.ds(0, half), pl.ds(half, self.mp - half)
        self.copies = [
            self.push(1, own.at[low, 1 - y], self.from_y2, 4),
            self.push(2, own.at[high, :, 1 - x], self.from_x2, 2),
        ]

    def second_stage(self):
        own, half, y, x = self.own, self.half, self.y, self.x
        for copy in self.copies:
            copy.wait_recv()

        def body(i, carry):
            a, b = i // 2, i % 2
            own[a, y, b] = own[a, y, b] + self.from_y2[a, b]
            own[half + a, b, x] = own[half + a, b, x] + self.from_x2[a, b]
            return carry

        lax.fori_loop(0, half * 2, body, 0)
        low, high = pl.ds(0, half), pl.ds(half, self.mp - half)
        self.copies = [
            self.push(3, own.at[low, y, 1 - x], self.from_x1, 2),
            self.push(4, own.at[high, 1 - y, x], self.from_y1, 4),
        ]

    def third_stage(self):
        own, half, y, x = self.own, self.half, self.y, self.x
        for copy in self.copies:
            copy.wait_recv()

        def body(a, carry):
            own[a, y, x] = own[a, y, x] + self.from_x1[a]
            own[half + a, y, x] = own[half + a, y, x] + self.from_y1[a]
            return carry

        lax.fori_loop(0, half, body, 0)

    def send_z(self):
        self.copies = [
            send(
                self.own.at[e, self.y, self.x], self.from_z.at[step], self.z_send.at[step], self.z_recv.at[step],
                (self.d, e),
            )
            for step, e in enumerate(ring(self.m, self.mp))
        ]
        self.pending.extend(self.copies)

    def finish(self, out):
        for copy in self.copies:
            copy.wait_recv()
        total = self.own[self.m, self.y, self.x].astype(F32)
        for step in range(self.mp - 1):
            total = total + self.from_z[step].astype(F32)
        out[...] = total

    def drain(self):
        for copy in self.pending:
            copy.wait_send()


FLOW_REFS = 12


def flow_scratch(mp, block):
    half = mp // 2
    leads = ((mp, 2, 2), (mp, 2, 2), (half, 2), (mp - half, 2), (half,), (mp - half,), (mp - 1,))
    return [pltpu.VMEM(lead + block, BF) for lead in leads] + [dma(1), dma(5), dma(5), dma(mp - 1), dma(mp - 1)]


class SmallSums:
    def __init__(self, small, outs, wide, refs):
        count = len(small)
        self.small, self.outs, self.wide = small, outs, wide
        self.running, self.from_dp, self.from_mp = [refs[i * count : (i + 1) * count] for i in range(3)]
        self.s_send, self.s_recv = refs[3 * count :]
        self.pending = []

    def start(self, stage):
        bit = (1, 2, 4)[stage]
        d, m = lax.axis_index("dp"), lax.axis_index("mp")
        if stage == 0:
            for i, ref in enumerate(self.small):
                self.running[i][0] = ref[...]
        self.copies = []
        for i in range(len(self.small)):
            at = i * 8 + stage
            self.copies.append(
                send(
                    self.running[i].at[stage], self.from_dp[i].at[stage], self.s_send.at[at], self.s_recv.at[at],
                    (turned(d, bit), m),
                )
            )
        self.pending.extend(self.copies)

    def end(self, stage):
        for i, copy in enumerate(self.copies):
            copy.wait_recv()
            self.running[i][stage + 1] = self.running[i][stage] + self.from_dp[i][stage]

    def start_mp(self):
        d, m, mp = lax.axis_index("dp"), lax.axis_index("mp"), lax.axis_size("mp")
        self.copies = []
        for i, wide in enumerate(self.wide):
            if wide:
                for step, e in enumerate(ring(m, mp)):
                    at = i * 8 + 3 + step
                    self.copies.append(
                        send(
                            self.running[i].at[3], self.from_mp[i].at[m], self.s_send.at[at], self.s_recv.at[at],
                            (d, e),
                        )
                    )
                self.from_mp[i][m] = self.running[i][3]
        self.pending.extend(self.copies)

    def end_mp(self):
        for copy in self.copies:
            copy.wait_recv()
        for i, wide in enumerate(self.wide):
            if wide:
                total = self.from_mp[i][0]
                for e in range(1, lax.axis_size("mp")):
                    total = total + self.from_mp[i][e]
                self.outs[i][...] = total
            else:
                self.outs[i][...] = self.running[i][3]

    def drain(self):
        for copy in self.pending:
            copy.wait_send()


def small_scratch(small, mp):
    scratch = []
    for lead in (4, 3, mp):
        scratch += [pltpu.VMEM((lead,) + s.shape, F32) for s in small]
    return scratch + [dma(8 * len(small)), dma(8 * len(small))]


def scatter_fallback(part):
    over_mp = lax.psum_scatter(part, "mp", scatter_dimension=0)
    return lax.psum_scatter(over_mp, "dp", scatter_dimension=0).astype(F32)


def cored(part):
    return part.reshape((part.shape[0], 2, 2, 2) + part.shape[2:])


class Blocks:
    def __init__(self, pairs, send_sem, recv_sem):
        self.pairs, self.send_sem, self.recv_sem = pairs, send_sem, recv_sem
        self.d, self.m, self.mp = lax.axis_index("dp"), lax.axis_index("mp"), lax.axis_size("mp")

    def start(self):
        self.copies = []
        for step, e in reversed(list(enumerate(ring(self.m, self.mp)))):
            for i, (source, target) in enumerate(self.pairs):
                sems = self.send_sem.at[i, step], self.recv_sem.at[i, step]
                self.copies.append(send(source.at[e], target.at[self.m], *sems, (self.d, e)))
        for source, target in self.pairs:
            target[self.m] = source[self.m]

    def arrive(self):
        for copy in self.copies:
            copy.wait_recv()

    def drain(self):
        for copy in self.copies:
            copy.wait_send()


def mixer_backward_kernel(
    doc_count, len_ref, g_parts, edge, x_ref, spectrum, skip_ref, t0, t1, t2, t3, part_a, part_b,
    gw_back, gw_edge_back, edge_back, gf_ref, total_a, partial_b,
    g_in, gw, gw_edge, g_full, x_full, grad, raw, top, rest, total, slots,
    b_send, b_recv, c_send, c_recv, e_sem, *flow_refs,
):
    tables = (t0, t1, t2, t3)
    parts, block, width = x_ref.shape
    half = width // 2
    count = raw.shape[0]
    d, m, mp = lax.axis_index("dp"), lax.axis_index("mp"), lax.axis_size("mp")
    a, b = Flow(part_a, flow_refs[:FLOW_REFS]), Flow(part_b, flow_refs[FLOW_REFS:])
    incoming = Blocks([(g_parts, g_in)], b_send, b_recv)
    outgoing = Blocks([(gw, gw_back), (gw_edge, gw_edge_back)], c_send, c_recv)
    greet([(turned(d, bit), m) for bit in (1, 2, 4)] + [(d, e) for e in ring(m, mp)])
    incoming.start()
    edge_copy = send(edge, edge_back, e_sem.at[0], e_sem.at[1], (d, lax.rem(m + mp - 1, mp)))
    a.start()
    b.start()
    unpack(x_full, x_ref)
    starts = document_starts(len_ref, doc_count)
    a.core_stage()
    incoming.arrive()
    unpack(g_full, g_in)
    for slot in range(doc_count):
        slot_blocks(g_full, grad, tables, starts[slot], len_ref[0, slot], block)
        slot_blocks(x_full, raw, tables, starts[slot], len_ref[0, slot], block)
        if slot == 0:
            a.second_stage()
            b.core_stage()
        backward_products(spectrum, grad, raw, total, top, rest, block, slot == 0)
        for out in range(count):
            slots[slot, pl.ds((1 + out) * block // 8, block // 8)] = tiles(inverse(top[out], rest[out], tables))
        if slot == 1:
            a.third_stage()
            a.send_z()
    gw_edge[...] = jnp.zeros(gw_edge.shape, gw_edge.dtype)

    def put(index, values):
        gw[index // 2, :, pl.ds((index % 2) * half, half)] = values.astype(gw.dtype)
        if index % 2 == 0 and index:
            own = g_full[pl.ds(index * block // 8, EDGE // 8)].reshape(EDGE, half) * skip_ref[...]
            gw_edge[index // 2 - 1, :, 0:half] = (values[0:EDGE] + own).astype(gw_edge.dtype)

    merge_slots(slots, starts, put, 2 * parts * block, block, count * block)
    outgoing.start()
    b.second_stage()
    filter_gradient(total, top, rest, tables, gf_ref, block)
    a.finish(total_a)
    b.third_stage()
    for e in range(parts):
        partial_b[e] = b.own[e, b.y, b.x]
    outgoing.arrive()
    edge_copy.wait()
    incoming.drain()
    outgoing.drain()
    a.drain()
    b.drain()


def mixer_backward(g_parts, edge, x, lengths, spectrum, skip_gain, tables, part_a, part_b):
    mp = lax.axis_size("mp")
    parts, block, width = x.shape
    half, docs, count = width // 2, lengths.shape[1], spectrum.shape[0]
    if lax.axis_size("dp") != 8:
        (g_in, edge_back) = exchange([g_parts], edge, 5)
        gw, gw_edge, gf = conv_backward(g_in, x, lengths, spectrum, skip_gain, tables)
        gw_back, gw_edge_back = exchange([gw, gw_edge], None, 6)
        over_dp = lax.psum_scatter(part_b, "dp", scatter_dimension=1)
        return gw_back, gw_edge_back, edge_back, gf, scatter_fallback(part_a), over_dp
    wide = (count, 2 * block, half)
    edge_shape = (parts, EDGE, -(-half // 128) * 128)
    own = part_a.shape[2:]
    rows = pltpu.VMEM(((2 * parts + count) * block // 8 + 1, 8, half), F32)
    return pl.pallas_call(
        functools.partial(mixer_backward_kernel, docs),
        name="mixer_backward",
        out_shape=(
            struct(x.shape, BF), struct(edge_shape, BF), struct(edge.shape, BF), struct((count * block, half), F32),
            struct(own, F32), struct((mp,) + own, BF),
        ),
        in_specs=[IN_SMEM] + [IN_VMEM] * 9 + [IN_HBM] * 2,
        out_specs=(IN_VMEM,) * 6,
        scratch_shapes=[
            pltpu.VMEM(x.shape, BF), pltpu.VMEM(x.shape, BF), pltpu.VMEM(edge_shape, BF), rows, rows,
            pltpu.VMEM(wide, F32), pltpu.VMEM(wide, F32), pltpu.VMEM(wide, BF), pltpu.VMEM(wide, BF),
            pltpu.VMEM(wide, F32), pltpu.VMEM((docs, (count + 2) * block // 8 + 1, 8, half), F32),
            dma(1, mp - 1), dma(1, mp - 1), dma(2, mp - 1), dma(2, mp - 1), dma(2),
            *flow_scratch(mp, own), *flow_scratch(mp, own),
        ],
        compiler_params=pltpu.CompilerParams(collective_id=5, has_side_effects=True, vmem_limit_bytes=ROOM),
    )(lengths, g_parts, edge, x, spectrum, skip_gain, *tables, cored(part_a), cored(part_b))


def spread_sum(block, slots, send_sem, recv_sem, axis, first):
    d, m = lax.axis_index("dp"), lax.axis_index("mp")
    count = lax.axis_size(axis)
    me = d if axis == "dp" else m
    copies = []
    for step, e in enumerate(ring(me, count)):
        peer = (e, m) if axis == "dp" else (d, e)
        copies.append(send(block, slots.at[me], send_sem.at[first + step], recv_sem.at[first + step], peer))
    slots[me] = block[...]
    for copy in copies:
        copy.wait()
    total = slots[0]
    for e in range(1, count):
        total = total + slots[e]
    return total


def total_of(values):
    return jnp.sum(jnp.sum(values, axis=1, keepdims=True), axis=0, keepdims=True)


def lanes_of(items):
    lane = lax.broadcasted_iota(jnp.int32, (1, 128), 1)
    row = jnp.zeros((1, 128), F32)
    for index, item in enumerate(items):
        row = row + jnp.where(lane == index, item, 0.0)
    return row


def update_body(
    g0, g1, g2, w0, w1, w2, rows, cols, gain_sum, gain, gain_mom, chan_sum, chan, chan_mom,
    fin_sum, fin, fin_mom, fout_sum, fout, fout_mom,
    norm_out, c0, c1, c2, n0, n1, n2, rows_out, cols_out, gain_g, gain_n, gain_m,
    chan_g, chan_n, chan_m, fin_g, fin_n, fin_m, fout_g, fout_n, fout_m,
    turn, mp_block, dp_block, mp_slots, dp_slots, last_block, mp_last, dp_last, send_sem, recv_sem,
):
    d, m = lax.axis_index("dp"), lax.axis_index("mp")
    dp, mp = lax.axis_size("dp"), lax.axis_size("mp")
    size, width = g0.shape
    in_width = 3 * (width // 4)
    is_in = lax.broadcasted_iota(jnp.int32, (size, width), 1) < in_width

    def four(v0, v1, v2, reduce_fn):
        return [
            reduce_fn(jnp.where(is_in, v0, 0.0)),
            reduce_fn(jnp.where(is_in, 0.0, v0)),
            reduce_fn(v1),
            reduce_fn(v2),
        ]

    def row_sum(v):
        return jnp.sum(v, axis=1, keepdims=True)

    def col_sum(v):
        return jnp.sum(v, axis=0, keepdims=True)

    s0, s1, s2 = g0[...] * g0[...], g1[...] * g1[...], g2[...] * g2[...]
    lane = lax.broadcasted_iota(jnp.int32, (size, 128), 1)
    row_parts = four(s0, s1, s2, row_sum)
    packed = jnp.zeros((size, 128), F32)
    for index, part in enumerate(row_parts):
        packed = packed + jnp.where(lane == index, part, 0.0)
    turn[...] = jnp.zeros(turn.shape, F32)
    dp_block[...] = jnp.zeros(dp_block.shape, F32)
    turn[pl.ds(0, size), :] = packed
    mp_block[pl.ds(0, 8), :] = jnp.transpose(turn[...])[0:8]
    old = rows[...]
    old_parts = [total_of(old[:, i : i + 1]) / mp for i in range(4)]
    weight_parts = four(w0[...] * w0[...], w1[...] * w1[...], w2[...] * w2[...], total_of)
    scalars = (
        [total_of(p) for p in row_parts]
        + old_parts
        + weight_parts
        + [
            total_of(gain[...] * gain[...]) / mp,
            total_of(chan[...] * chan[...]) / dp,
            total_of(fout[...] * fout[...]) / dp,
            total_of(fout_sum[...] * fout_sum[...]) / dp,
        ]
    )
    mp_block[pl.ds(8, 8), :] = jnp.broadcast_to(lanes_of(scalars), (8, 128))
    over_mp = spread_sum(mp_block, mp_slots, send_sem, recv_sem, "mp", 0)
    pieces = width // 128
    for index, values in enumerate((s0, s1, s2)):
        sums = col_sum(values)
        for piece in range(pieces):
            dp_block[pl.ds(index * pieces + piece, 1), :] = sums[:, piece * 128 : (piece + 1) * 128]
    dp_block[pl.ds(3 * pieces, 1), :] = over_mp[8:9]
    over_dp = spread_sum(dp_block, dp_slots, send_sem, recv_sem, "dp", mp)
    turn[pl.ds(0, 8), :] = over_mp[0:8]
    row_totals = jnp.transpose(turn[...])[0:size]
    shared = over_dp[3 * pieces : 3 * pieces + 1]

    def scalar(index):
        return shared[:, index : index + 1]

    gains_sq = total_of(jnp.sum(gain_sum[...] * gain_sum[...], axis=0))
    chan_sq = total_of(jnp.sum(chan_sum[...] * chan_sum[...], axis=0))
    fin_sq = total_of(fin_sum[...] * fin_sum[...])
    norm = jnp.sqrt(
        scalar(0) + scalar(1) + scalar(2) + scalar(3) + gains_sq + chan_sq + scalar(15) + fin_sq
    )
    norm_out[...] = norm
    clip = 1.0 / jnp.maximum(1.0, norm / CLIP_NORM)
    square = clip * clip
    fresh = 1.0 - MOMENT_DECAY
    all_rows = size * dp
    wide = [in_width * mp, (width - in_width) * mp, width * mp, width * mp]
    ratio = []
    lane4 = lax.broadcasted_iota(jnp.int32, (size, 4), 1)
    fresh_rows = jnp.zeros((size, 4), F32)
    for index in range(4):
        row_new = (
            MOMENT_DECAY * old[:, index : index + 1]
            + fresh * square * row_totals[:, index : index + 1] / wide[index]
        )
        mean = MOMENT_DECAY * scalar(4 + index) / all_rows + fresh * square * scalar(index) / (
            all_rows * wide[index]
        )
        ratio.append(row_new / mean)
        fresh_rows = fresh_rows + jnp.where(lane4 == index, row_new, 0.0)
    rows_out[...] = fresh_rows
    for index in range(3):
        for piece in range(pieces):
            at = pl.ds(piece * 128, 128)
            row = index * pieces + piece
            cols_out[pl.ds(index, 1), at] = (
                MOMENT_DECAY * cols[pl.ds(index, 1), at]
                + fresh * square * over_dp[row : row + 1] / all_rows
            )
    first_ratio = jnp.where(is_in, ratio[0], ratio[1])
    steps = []
    for grad, out, factor, index in ((g0, c0, first_ratio, 0), (g1, c1, ratio[2], 1), (g2, c2, ratio[3], 2)):
        clipped = grad[...] * clip
        out[...] = clipped
        steps.append(clipped * lax.rsqrt(factor * cols_out[pl.ds(index, 1), :]))
    u0, u1, u2 = steps

    def plain(clipped, moment, grad_out, moment_out):
        fresh_moment = MOMENT_DECAY * moment + fresh * clipped * clipped
        grad_out[...] = clipped
        moment_out[...] = fresh_moment
        return clipped * lax.rsqrt(fresh_moment)

    own_gain = gain_sum[0]
    for e in range(1, dp):
        own_gain = jnp.where(d == e, gain_sum[e], own_gain)
    own_chan = chan_sum[0]
    for e in range(1, mp):
        own_chan = jnp.where(m == e, chan_sum[e], own_chan)
    u_gain = plain(own_gain * clip, gain_mom[...], gain_g, gain_m)
    u_chan = plain(own_chan * clip, chan_mom[...], chan_g, chan_m)
    u_fin = plain(fin_sum[...] * clip, fin_mom[...], fin_g, fin_m)
    u_fout = plain(fout_sum[...] * clip, fout_mom[...], fout_g, fout_m)
    step_parts = four(u0 * u0, u1 * u1, u2 * u2, total_of) + [
        total_of(u_gain * u_gain) / mp,
        total_of(u_chan * u_chan) / dp,
        total_of(u_fout * u_fout) / dp,
    ]
    last_block[...] = jnp.broadcast_to(lanes_of(step_parts), (8, 128))
    half_way = spread_sum(last_block, mp_last, send_sem, recv_sem, "mp", mp + dp)
    mp_block[pl.ds(0, 8), :] = half_way
    step_sums = spread_sum(mp_block.at[pl.ds(0, 8)], dp_last, send_sem, recv_sem, "dp", 2 * mp + dp)[0:1]

    def factors(step_total, weight_total, entries):
        shrink = 1.0 / jnp.maximum(1.0, jnp.sqrt(step_total / entries) / CLIP_STEP)
        return STEP_RATE * jnp.sqrt(weight_total / entries) * shrink

    def step_sum(index):
        return step_sums[:, index : index + 1]

    rate = [factors(step_sum(i), scalar(8 + i), all_rows * wide[i]) for i in range(4)]
    n0[...] = w0[...] - jnp.where(is_in, rate[0], rate[1]) * u0
    n1[...] = w1[...] - rate[2] * u1
    n2[...] = w2[...] - rate[3] * u2
    gain_n[...] = gain[...] - factors(step_sum(4), scalar(12), 2 * all_rows) * u_gain
    chan_n[...] = chan[...] - factors(step_sum(5), scalar(13), chan.shape[0] * chan.shape[1] * mp) * u_chan
    fout_n[...] = fout[...] - factors(step_sum(6), scalar(14), fout.shape[0] * fout.shape[1] * mp) * u_fout
    fin_count = fin.shape[0] * fin.shape[1]
    fin_rate = factors(total_of(u_fin * u_fin), total_of(fin[...] * fin[...]), fin_count)
    fin_n[...] = fin[...] - fin_rate * u_fin


def greet_all():
    d, m = lax.axis_index("dp"), lax.axis_index("mp")
    greet([(e, m) for e in ring(d, lax.axis_size("dp"))] + [(d, e) for e in ring(m, lax.axis_size("mp"))])


def update_kernel(*refs):
    greet_all()
    update_body(*refs)


def finish_kernel(small_wide, part, total_up, partial_down, *refs):
    count = len(small_wide)
    small, refs = refs[:count], refs[count:]
    others, refs = refs[:13], refs[13:]
    outs, refs = refs[:21], refs[21:]
    g0, g2, refs = refs[0], refs[1], refs[2:]
    sums_out, refs = refs[:count], refs[count:]
    work, refs = refs[:10], refs[10:]
    from_z, z_send, z_recv, refs = refs[0], refs[1], refs[2], refs[3:]
    flow = Flow(part, refs[:FLOW_REFS])
    sums = SmallSums(small, sums_out, small_wide, refs[FLOW_REFS:])
    d, m, mp = lax.axis_index("dp"), lax.axis_index("mp"), lax.axis_size("mp")
    greet_all()
    flow.start()
    sums.start(0)
    down = [
        send(partial_down.at[e], from_z.at[step], z_send.at[step], z_recv.at[step], (d, e))
        for step, e in enumerate(ring(m, mp))
    ]
    flow.core_stage()
    sums.end(0)
    sums.start(1)
    flow.second_stage()
    sums.end(1)
    sums.start(2)
    flow.third_stage()
    flow.send_z()
    sums.end(2)
    sums.start_mp()
    for copy in down:
        copy.wait()
    total = partial_down[m].astype(F32)
    for step in range(mp - 1):
        total = total + from_z[step].astype(F32)
    g2[...] = total
    sums.end_mp()
    flow.finish(g0)
    flow.drain()
    sums.drain()
    w, rest = others[:5], others[5:]
    pairs = []
    for i in range(4):
        pairs += [sums_out[i], rest[2 * i], rest[2 * i + 1]]
    update_body(g0, total_up, g2, *w, *pairs, *outs, *work)


def update_scratch(dp, mp, width):
    pieces = 3 * width // 128 + 1
    tall = -(-pieces // 8) * 8
    sems = 2 * (dp + mp)
    return [
        pltpu.VMEM((128, 128), F32),
        pltpu.VMEM((16, 128), F32),
        pltpu.VMEM((tall, 128), F32),
        pltpu.VMEM((mp, 16, 128), F32),
        pltpu.VMEM((dp, tall, 128), F32),
        pltpu.VMEM((8, 128), F32),
        pltpu.VMEM((mp, 8, 128), F32),
        pltpu.VMEM((dp, 8, 128), F32),
        dma(sems),
        dma(sems),
    ]


def finish(part, total_up, partial_down, small, small_wide, weights, rows, cols, olds):
    dp, mp = lax.axis_size("dp"), lax.axis_size("mp")
    big = struct(weights[0].shape, F32)
    size, width = big.shape
    out_small = [struct(v[0].shape, F32) for v in olds for _ in range(3)]
    outs = (struct((1, 1), F32),) + (big,) * 6 + (struct(rows.shape, F32), struct(cols.shape, F32), *out_small)
    params = pltpu.CompilerParams(collective_id=2, has_side_effects=True, vmem_limit_bytes=ROOM)
    if dp != 8:
        sums = [lax.psum(s, ("dp", "mp") if wide else "dp") for s, wide in zip(small, small_wide)]
        inputs = [scatter_fallback(part), total_up, lax.psum_scatter(partial_down, "mp").astype(F32)]
        inputs += [*weights, rows, cols]
        for total, old in zip(sums, olds):
            inputs += [total, *old]
        return pl.pallas_call(
            update_kernel,
            name="clip_and_update",
            out_shape=outs,
            in_specs=[IN_VMEM] * len(inputs),
            out_specs=(IN_VMEM,) * len(outs),
            scratch_shapes=update_scratch(dp, mp, width),
            compiler_params=params,
        )(*inputs)
    inputs = [total_up, partial_down, *small, *weights, rows, cols]
    for old in olds:
        inputs += old
    return pl.pallas_call(
        functools.partial(finish_kernel, small_wide),
        name="sum_clip_update",
        out_shape=outs,
        in_specs=[IN_HBM] + [IN_VMEM] * len(inputs),
        out_specs=(IN_VMEM,) * len(outs),
        scratch_shapes=[
            pltpu.VMEM((size, width), F32),
            pltpu.VMEM((size, width), F32),
            *[pltpu.VMEM(s.shape, F32) for s in small],
            *update_scratch(dp, mp, width),
            pltpu.VMEM((mp - 1, size, width), BF),
            dma(mp - 1),
            dma(mp - 1),
            *flow_scratch(mp, (size, width)),
            *small_scratch(small, mp),
        ],
        compiler_params=params,
    )(cored(part), *inputs)


def dot_nt(left, right):
    return lax.dot_general(left, right, (((1,), (1,)), ((), ())), preferred_element_type=F32)


def dot_tn(left, right):
    return lax.dot_general(left, right, (((0,), (0,)), ((), ())), preferred_element_type=F32)


def gelu_parts(x):
    scale, cubic = math.sqrt(2.0 / math.pi), 0.044715
    square = x * x
    t = jnp.tanh(scale * x * (1.0 + cubic * square))
    half = 0.5 * (1.0 + t)
    slope = half + 0.5 * x * (1.0 - t * t) * (scale * (1.0 + 3.0 * cubic * square))
    return x * half, slope


def feed_kernel(
    y_ref, w_ref, s0_ref, tok, cot, w_out, gain, skip, up, down,
    act_out, up_part, down_part, out_part, g_parts, gy_out, gs0_out, gx2_out, sums,
    y, o, x2, n2, inv2, b, b_t, cot_t, mix, acc_out, acc_b,
):
    step, steps = pl.program_id(0), pl.num_programs(0)
    parts, block, wide = y_ref.shape
    own = wide // 2
    count = tok.shape[0]
    tile = 128

    @pl.when(step == 0)
    def _():
        for part in range(parts):
            for side in range(2):
                y[pl.ds(side * block, block), pl.ds(part * own, own)] = y_ref[
                    part, :, pl.ds(side * own, own)
                ].astype(F32)

        def body(index, carry):
            rows = pl.ds(pl.multiple_of(index * tile, tile), tile)
            values = y[rows, :] + skip[...] * w_ref[rows, :]
            y[rows, :] = values
            mixed = (values * s0_ref[rows, :]).astype(BF)
            o[rows, :] = mixed
            residual = tok[rows, :].astype(F32) + dot_nt(mixed, w_out[...])
            x2[rows, :] = residual
            normed, inverse_std = norm_parts(residual)
            n2[rows, :] = normed
            inv2[rows, :] = jnp.broadcast_to(inverse_std, (tile, 128))
            b[rows, :] = (normed * gain[...]).astype(BF)
            return carry

        lax.fori_loop(0, count // tile, body, 0)
        b_t[...] = b[...].T
        cot_t[...] = cot[...].T
        acc_out[...] = jnp.zeros(acc_out.shape, F32)
        acc_b[...] = jnp.zeros(acc_b.shape, F32)

    up_w, down_w = up[0], down[0]
    value, slope = gelu_parts(mm(b[...], up_w))
    act = value.astype(BF)
    g_hpre = (mm(cot[...], down_w) * slope).astype(BF)
    up_part[0] = mm(b_t[...], g_hpre).astype(BF)
    down_part[0] = mm(cot_t[...], act).astype(BF)
    acc_out[...] += dot_nt(act, down_w)
    acc_b[...] += dot_nt(g_hpre, up_w)

    @pl.when(step == steps - 1)
    def _():
        sums[...] = jnp.zeros(sums.shape, F32)

        def body(index, carry):
            rows = pl.ds(pl.multiple_of(index * tile, tile), tile)
            act_out[rows, :] = (x2[rows, :] + acc_out[rows, :]).astype(BF)
            g_b, normed = acc_b[rows, :], n2[rows, :]
            sums[0:1, :] += jnp.sum(g_b * normed, axis=0, keepdims=True)
            g_x2 = cot[rows, :].astype(F32) + norm_back(g_b, gain[...], normed, inv2[rows, 0:1])
            gx2_out[rows, :] = g_x2
            low = g_x2.astype(BF)
            mix[rows, :] = low
            g_o = mm(low, w_out[...])
            g_y = g_o * s0_ref[rows, :]
            gy_out[rows, :] = g_y
            gs0_out[rows, :] = g_o * y[rows, :]
            sums[1:2, :] += jnp.sum(g_y * w_ref[rows, :], axis=0, keepdims=True)
            return carry

        lax.fori_loop(0, count // tile, body, 0)
        for part in range(parts):
            for side in range(2):
                g_parts[part, :, pl.ds(side * own, own)] = gy_out[
                    pl.ds(side * block, block), pl.ds(part * own, own)
                ].astype(BF)
        grad = dot_tn(mix[...], o[...])
        for part in range(parts):
            out_part[part] = grad[:, part * own : (part + 1) * own].astype(BF)


def feed(y_parts, w_own, s0, tokens, cotangent, w_out, gain, skip, whole_up, whole_down):
    mp, width, hidden = whole_up.shape
    count = tokens.shape[0]
    own, cols = width // mp, 256
    each = hidden // cols
    once = pl.Buffered(1)

    def fixed(shape):
        return pl.BlockSpec(shape, lambda i: (0,) * len(shape), pipeline_mode=once)

    def moving():
        return pl.BlockSpec((1, width, cols), lambda i: (i // each, 0, i % each))

    full, half = (count, width), (mp, count // 2, 2 * own)
    outs = [
        (full, BF), (whole_up.shape, BF), (whole_up.shape, BF), ((mp, width, own), BF), (half, BF),
        (full, F32), (full, F32), (full, F32), ((8, width), F32),
    ]
    out_specs = [moving() if i in (1, 2) else fixed(s) for i, (s, _) in enumerate(outs)]
    inputs = (y_parts, w_own, s0, tokens, cotangent, w_out, gain, skip)
    return pl.pallas_call(
        feed_kernel,
        name="feed_forward",
        grid=(mp * each,),
        out_shape=tuple(struct(s, t) for s, t in outs),
        in_specs=[fixed(v.shape) for v in inputs] + [moving(), moving()],
        out_specs=tuple(out_specs),
        scratch_shapes=[
            pltpu.VMEM(full, F32), pltpu.VMEM(full, BF), pltpu.VMEM(full, F32), pltpu.VMEM(full, F32),
            pltpu.VMEM((count, 128), F32), pltpu.VMEM(full, BF), pltpu.VMEM((width, count), BF),
            pltpu.VMEM((width, count), BF), pltpu.VMEM(full, BF), pltpu.VMEM(full, F32), pltpu.VMEM(full, F32),
        ],
        compiler_params=pltpu.CompilerParams(vmem_limit_bytes=ROOM),
    )(*inputs, whole_up, whole_down)


def post_kernel(
    gw_ref, gw_edge, gy_ref, gs0_ref, gs0_edge, s1_ref, s2_ref, z_ref, a_ref, n1_ref, inv1_ref, gx2_ref,
    w_in, taps, skip, gain, doc_ref, out_part,
    first_part, input_grad, sums,
    gw, gs, gz,
):
    parts, block, wide = gw_ref.shape
    own = wide // 2
    count, width = gy_ref.shape
    offsets = (taps.shape[0]) // 3
    for part in range(parts):
        at = pl.ds(part * own, own)
        for side in range(2):
            gw[pl.ds(side * block, block), at] = gw_ref[part, :, pl.ds(side * own, own)].astype(F32)
        gw[pl.ds(count, EDGE), at] = gw_edge[part, :, 0:own].astype(F32)
    gw[pl.ds(0, count), :] += skip[...] * gy_ref[...]
    doc = doc_ref[...]
    same = [None] + [doc[EDGE:] == doc[EDGE - k : doc.shape[0] - k] for k in range(1, offsets)]
    sums[...] = jnp.zeros(sums.shape, F32)
    total = None
    for j in range(3):
        if j == 0:
            gs[pl.ds(0, count), :] = gs0_ref[...]
            gs[pl.ds(count, EDGE), :] = gs0_edge[...].astype(F32)
        else:
            gs[...] = gw[...] * (s2_ref if j == 1 else s1_ref)[...]
        z_cols = pl.ds(j * width, width)
        g_z = None
        for k in range(offsets):
            tap = taps[pl.ds(3 * k + j, 1), :]
            later = gs[pl.ds(k, count), :]
            before = z_ref[pl.ds(EDGE - k, count), z_cols]
            if k:
                later = jnp.where(same[k][k : count + k], later, 0.0)
                before = jnp.where(same[k][:count], before, 0.0)
            g_z = tap * later if g_z is None else g_z + tap * later
            sums[pl.ds(3 * k + j, 1), :] = jnp.sum(gs[pl.ds(0, count), :] * before, axis=0, keepdims=True)
        gz[...] = g_z.astype(BF)
        grad = dot_tn(a_ref[pl.ds(EDGE, count), :], gz[...])
        for part in range(parts):
            first_part[part, :, pl.ds(j * own, own)] = grad[:, part * own : (part + 1) * own].astype(BF)
        term = dot_nt(gz[...], w_in[:, z_cols])
        total = term if total is None else total + term
    for part in range(parts):
        first_part[part, :, pl.ds(3 * own, own)] = out_part[part]
    normed = n1_ref[pl.ds(EDGE, count), :]
    sums[pl.ds(3 * offsets, 1), :] = jnp.sum(total * normed, axis=0, keepdims=True)
    back = norm_back(total, gain[...], normed, inv1_ref[pl.ds(EDGE, count), 0:1])
    input_grad[...] = (gx2_ref[...] + back).astype(BF)


def post(gw_parts, gw_edge, g_y, g_s0, gs0_edge, s1, s2, z, a, n1, inv1, g_x2, w_in, taps, skip, gain, doc, out_part):
    mp, block, wide = gw_parts.shape
    count, width = g_y.shape
    inputs = (
        gw_parts, gw_edge, g_y, g_s0, gs0_edge, s1, s2, z, a, n1, inv1, g_x2, w_in, taps, skip, gain, doc, out_part
    )
    return pl.pallas_call(
        post_kernel,
        name="mixer_post",
        out_shape=(struct((mp, width, width), BF), struct((count, width), BF), struct((16, width), F32)),
        in_specs=[IN_VMEM] * len(inputs),
        out_specs=(IN_VMEM,) * 3,
        scratch_shapes=[
            pltpu.VMEM((count + EDGE, width), F32),
            pltpu.VMEM((count + EDGE, width), F32),
            pltpu.VMEM((count, width), BF),
        ],
        compiler_params=pltpu.CompilerParams(vmem_limit_bytes=ROOM),
    )(*inputs)


def features(length, feature_count, count):
    step = np.arange(count)
    band = np.arange(1, (feature_count - 1) // 2 + 1)
    phase = ((step[:, None] * band[None, :]) % length).astype(np.float32) * np.float32(2.0 * math.pi / length)
    position = (step / length).astype(np.float32)
    table = np.concatenate([position[:, None], np.cos(phase), np.sin(phase)], axis=1)
    return table.astype(np.float32), position


def product(left, right):
    return jnp.dot(left, right, precision=FULL_PRECISION, preferred_element_type=F32)


def norm_parts(values):
    centred = values - jnp.mean(values, axis=-1, keepdims=True)
    inverse_std = lax.rsqrt(jnp.mean(centred * centred, axis=-1, keepdims=True) + EPS_NORM)
    return centred * inverse_std, inverse_std


def norm_back(grad, gain, normed, inverse_std):
    scaled = grad * gain
    mean = jnp.mean(scaled, axis=-1, keepdims=True)
    along = jnp.mean(scaled * normed, axis=-1, keepdims=True)
    return (scaled - mean - normed * along) * inverse_std


def to_parts(values, mp, block):
    own = values.shape[1] // mp
    return values.reshape(2, block, mp, own).transpose(2, 1, 0, 3).reshape(mp, block, 2 * own)


def per_device(
    tokens, cotangent, doc_lengths, in_weight, out_weight, up_weight, down_weight, gains, channel_weight,
    filter_in, filter_out, in_rows, in_cols, out_rows, out_cols, up_rows, up_cols, down_rows, down_cols,
    gain_moment, channel_moment, filter_in_moment, filter_out_moment,
):
    dp, mp = lax.axis_size("dp"), lax.axis_size("mp")
    m = lax.axis_index("mp")
    count, width = tokens.shape
    length = count * mp
    own = channel_weight.shape[1]
    rows = in_weight.shape[0]
    hidden = up_weight.shape[1]
    taps = (channel_weight.shape[0] - 1) // 3
    most = length // 2

    first_shard = jnp.concatenate([in_weight.reshape(rows, 3 * own), out_weight], axis=1)
    chunks = [v.astype(BF) for v in (first_shard, up_weight, down_weight)]
    lanes = 128
    gain_block = jnp.pad(gains.T.astype(BF), ((0, 14), (0, lanes - rows)))
    chan_block = jnp.pad(channel_weight, ((0, 16 - channel_weight.shape[0]), (0, 0)))
    edges = jnp.stack([tokens[count - EDGE :], tokens[:EDGE]])
    whole_first, whole_up, whole_down, gains_all, chan_all, edges_all = gather(chunks, gain_block, chan_block, edges)
    whole_first = whole_first.reshape(mp, width, width)
    whole_up = whole_up.reshape(mp, width, hidden)
    whole_down = whole_down.reshape(mp, width, hidden)
    w_in = whole_first[:, :, : 3 * own].reshape(mp, width, 3, own).transpose(1, 2, 0, 3).reshape(width, 3 * width)
    w_out = whole_first[:, :, 3 * own :].transpose(1, 0, 2).reshape(width, width)
    gain_rows = gains_all[:, 0:2, :rows].transpose(1, 0, 2).reshape(2, width).astype(F32)
    chan_rows = chan_all[:, : channel_weight.shape[0]].transpose(1, 0, 2).reshape(-1, width)
    conv_taps = chan_rows[:-1].reshape(taps, 3, width)
    skip_gain = chan_rows[-1]

    position = m * count - EDGE + jnp.arange(count + 2 * EDGE, dtype=jnp.int32)
    ends = jnp.cumsum(doc_lengths[0])
    doc = jnp.sum((position[:, None] >= ends[None, :]).astype(jnp.int32), axis=1)
    doc = jnp.where(position < 0, -1, doc)

    def alike(offset):
        return (doc[EDGE:] == doc[EDGE - offset : doc.shape[0] - offset])[:, None]

    extended = jnp.concatenate([edges_all[0], tokens, edges_all[1]]).astype(F32)
    n1, inv1 = norm_parts(extended)
    a = (n1 * gain_rows[0]).astype(BF)
    z = jnp.dot(a, w_in, preferred_element_type=F32)
    s = [None] * 3
    for j in range(3):
        stream = z[:, j * width : (j + 1) * width]
        total = None
        for k in range(taps):
            part = stream[EDGE - k : stream.shape[0] - k]
            if k:
                part = jnp.where(alike(k), part, 0.0)
            term = conv_taps[k, j] * part
            total = term if total is None else total + term
        s[j] = total
    w_own = s[2][:count] * s[1][:count]
    s0 = s[0][:count]

    table, step = features(length, filter_in.shape[0], most)
    phase = product(table, filter_in)
    hidden_filter = jnp.sin(phase)
    channel = (m * own + jnp.arange(own, dtype=jnp.int32)).astype(F32)
    rate = FAST_DECAY + (SLOW_DECAY - FAST_DECAY) * channel / (width - 1)
    decay = jnp.exp(-step[:, None] * rate[None, :])
    filters = product(hidden_filter, filter_out) * decay
    tables = tuple(jnp.asarray(t) for t in transform_tables(BLOCK))
    (w_parts,) = exchange([to_parts(w_own.astype(BF), mp, count // 2)], None, 3)
    y_parts, spectrum = conv_forward(w_parts, doc_lengths, filters, tables)
    (y_back,) = exchange([y_parts], None, 4)

    activations, up_part, down_part, out_part, gy_parts, g_y, g_s0, g_x2, feed_sums = feed(
        y_back, w_own, s0, tokens, cotangent, w_out, gain_rows[1:2], skip_gain[None], whole_up, whole_down
    )

    up_part, down_part = [p.reshape(mp, dp, rows, hidden) for p in (up_part, down_part)]
    gw_back, gw_edge, g_s0_edge, g_filters, up_total, down_partial = mixer_backward(
        gy_parts, g_s0[:EDGE].astype(BF), w_parts, doc_lengths, spectrum, channel_weight[-1:], tables,
        up_part, down_part,
    )
    first_part, input_grad, post_sums = post(
        gw_back, gw_edge, g_y, g_s0, g_s0_edge, s[1], s[2], z, a, n1, inv1, g_x2, w_in, chan_rows[:-1],
        skip_gain[None], gain_rows[0:1], doc[:, None], out_part,
    )

    g_raw = g_filters * decay
    fout_part = product(hidden_filter.T, g_raw)
    fin_part = product(table.T, product(g_raw, filter_out.T) * jnp.cos(phase))

    gain_part = jnp.stack([post_sums[3 * taps], feed_sums[0]]).reshape(2, dp, rows).transpose(1, 0, 2)
    gain_part = jnp.pad(gain_part, ((0, 0), (0, 0), (0, lanes - rows)))
    chan_part = jnp.concatenate([post_sums[: 3 * taps], feed_sums[1:2]])
    chan_part = chan_part.reshape(-1, mp, own).transpose(1, 0, 2)

    def padded(values, fill):
        return jnp.pad(values.T, ((0, 0), (0, lanes - rows)), constant_values=fill)

    first_cols = jnp.concatenate([in_cols.reshape(3 * own), out_cols])
    results = finish(
        first_part.reshape(mp, dp, rows, width), up_total, down_partial,
        [gain_part, chan_part, fin_part, fout_part], (True, True, True, False),
        (first_shard, up_weight, down_weight),
        jnp.stack([in_rows, out_rows, up_rows, down_rows], axis=1),
        jnp.stack([first_cols, up_cols, down_cols]),
        [
            (padded(gains, 0.0), padded(gain_moment, 1.0)),
            (channel_weight, channel_moment),
            (filter_in, filter_in_moment),
            (filter_out, filter_out_moment),
        ],
    )
    norm, c0, c1, c2, n0, n1_, n2_, rows_new, cols_new = results[:9]
    small = results[9:]
    gain_g, gain_n, gain_m = [v[:, :rows].T for v in small[0:3]]

    def parted(values):
        return values[:, : 3 * own].reshape(rows, 3, own), values[:, 3 * own :]

    in_grad, out_grad = parted(c0)
    in_new, out_new = parted(n0)
    return (
        activations, input_grad, norm.reshape(()),
        in_grad, out_grad, c1, c2, gain_g, small[3], small[6], small[9],
        in_new, out_new, n1_, n2_, gain_n, small[4], small[7], small[10],
        rows_new[:, 0], cols_new[0, : 3 * own].reshape(3, own),
        rows_new[:, 1], cols_new[0, 3 * own :],
        rows_new[:, 2], cols_new[1],
        rows_new[:, 3], cols_new[2],
        gain_m, small[5], small[8], small[11],
    )


def solution(mesh):
    tokens, by_rows, by_cols, both = P(("dp", "mp"), None), P("dp", None), P(None, "mp"), P("dp", "mp")
    cube, vec_dp, vec_mp = P("dp", None, "mp"), P("dp"), P("mp")
    moments = (vec_dp, by_cols, vec_dp, vec_mp, vec_dp, vec_mp, vec_dp, vec_mp)
    weights = (cube, both, both, both, by_rows, by_cols, P(), by_cols)
    small = (by_rows, by_cols, P(), by_cols)
    return jax.shard_map(
        per_device,
        mesh=mesh,
        in_specs=(tokens, tokens, by_rows) + weights + moments + small,
        out_specs=(tokens, tokens, P()) + weights + weights + moments + small,
        check_vma=False,
    )
```

```python
import functools
import math

import jax
import jax.numpy as jnp
import ml_dtypes
import numpy as np
from jax import lax
from jax.experimental import pallas as pl
from jax.experimental.pallas import tpu as pltpu
from jax.sharding import PartitionSpec as P

EPS_NORM = 1e-05
MOMENT_DECAY = 0.5
CLIP_NORM = 1.0
CLIP_STEP = 0.25
STEP_RATE = 2.0
FAST_DECAY = 15.35
SLOW_DECAY = 3.07
FULL_PRECISION = lax.Precision.HIGHEST
BF = jnp.bfloat16
F32 = jnp.float32
MESH = pl.DeviceIdType.MESH
BLOCK = 256
EDGE = 16
ROOM = 56 << 20
IN_VMEM = pl.BlockSpec(memory_space=pltpu.VMEM)
IN_HBM = pl.BlockSpec(memory_space=pl.ANY)
IN_SMEM = pl.BlockSpec(memory_space=pltpu.SMEM)


def struct(shape, dtype):
    return jax.ShapeDtypeStruct(tuple(shape), dtype)


def transform_tables(block):
    freq = 2 * np.arange(block)[:, None] + 1
    angle = np.pi * (freq * np.arange(block)[None, :] % (4 * block)) / (2 * block)
    table = np.concatenate([np.cos(angle), -np.sin(angle)], axis=0).astype(np.float32)
    high = table.astype(ml_dtypes.bfloat16)
    low = (table - high.astype(np.float32)).astype(ml_dtypes.bfloat16)
    return high, low, np.ascontiguousarray(high.T), np.ascontiguousarray(low.T)


def mm(left, right):
    return lax.dot_general(left, right, (((1,), (0,)), ((), ())), preferred_element_type=F32)


def split(values):
    high = values.astype(BF)
    return high, (values - high.astype(F32)).astype(BF)


def load_rows(ref, start, count, lead=()):
    odd = lax.rem(start, 8)
    tile = ref[lead + (pl.ds(lax.div(start, 8), count // 8 + 1),)]
    width = tile.shape[-1]
    tile = pltpu.roll(tile, lax.rem(8 - odd, 8), axis=1)
    first = lax.broadcasted_iota(jnp.int32, (count // 8, 8, width), 1) < 8 - odd
    return jnp.where(first, tile[:-1], tile[1:]).reshape(count, width)


def tiles(values):
    return values.reshape(values.shape[0] // 8, 8, values.shape[1])


def unpack(target, source):
    parts, block, width = source.shape
    half, count = width // 2, block // 8
    for part in range(parts):
        for side in range(2):
            values = source[part, :, side * half : (side + 1) * half].astype(F32)
            target[pl.ds((2 * part + side) * count, count)] = tiles(values)


def pair_rows(index, block, size):
    first = pl.multiple_of(index * size, size)
    return pl.ds(first, size), pl.ds(pl.multiple_of(block + first, size), size)


def signs(size, width, scale):
    odd = lax.broadcasted_iota(jnp.int32, (size, width), 0) % 2
    return jnp.where(odd == 0, scale, -scale).astype(F32)


def filter_spectrum(filter_ref, spectrum, raw, tables, block):
    count = raw.shape[0]
    high, low = tables[0][...], tables[1][...]
    for lag in range(count):
        top, rest = split(filter_ref[pl.ds(lag * block, block), :])
        raw[lag] = mm(high, top) + mm(high, rest) + mm(low, top)
    scale = 1.0 / block

    def body(index, carry):
        re_rows, im_rows = pair_rows(index, block, 8)
        sign = signs(8, raw.shape[2], scale)
        for lag in range(count):
            re, im = raw[lag, re_rows, :] * scale, raw[lag, im_rows, :] * scale
            if lag:
                re = re - sign * raw[lag - 1, im_rows, :]
                im = im + sign * raw[lag - 1, re_rows, :]
            spectrum[lag, re_rows, :] = re
            spectrum[lag, im_rows, :] = im
        return carry

    lax.fori_loop(0, block // 8, body, 0)


def slot_blocks(source, target, tables, start, length, block):
    high, low = tables[0][...], tables[1][...]
    for index in range(target.shape[0]):
        values = load_rows(source, start + index * block, block)
        inside = lax.broadcasted_iota(jnp.int32, values.shape, 0) + index * block < length
        values = jnp.where(inside, values, 0.0).astype(BF)
        target[index] = mm(high, values) + mm(low, values)


def inverse(top, rest, tables):
    high, low = tables[2][...], tables[3][...]
    return mm(high, top) + mm(high, rest) + mm(low, top)


def document_starts(len_ref, count):
    starts, at = [], jnp.int32(0)
    for slot in range(count):
        starts.append(at)
        at = at + len_ref[0, slot]
    return starts


def merge_slots(slots, starts, put, total, block, most):
    for index in range(total // block):
        first = index * block
        merged = None
        for slot, start in enumerate(starts):
            at = jnp.clip(first - start, -block, most) + block
            values = load_rows(slots, at, block, (slot,))
            if merged is None:
                merged = values
            else:
                inside = lax.broadcasted_iota(jnp.int32, values.shape, 0) + first >= start
                merged = jnp.where(inside, values, merged)
        put(index, merged)


def forward_products(spectrum, raw, top, rest, block):
    count = raw.shape[0]

    def body(index, carry):
        re_rows, im_rows = pair_rows(index, block, 16)
        hr = [spectrum[i, re_rows, :] for i in range(count)]
        hi = [spectrum[i, im_rows, :] for i in range(count)]
        xr = [raw[i, re_rows, :] for i in range(count)]
        xi = [raw[i, im_rows, :] for i in range(count)]
        for out in range(count):
            re = hr[0] * xr[out] - hi[0] * xi[out]
            im = hr[0] * xi[out] + hi[0] * xr[out]
            for lag in range(1, out + 1):
                re = re + (hr[lag] * xr[out - lag] - hi[lag] * xi[out - lag])
                im = im + (hr[lag] * xi[out - lag] + hi[lag] * xr[out - lag])
            top[out, re_rows, :], rest[out, re_rows, :] = split(re)
            top[out, im_rows, :], rest[out, im_rows, :] = split(im)
        return carry

    lax.fori_loop(0, block // 16, body, 0)


def backward_products(spectrum, grad, raw, total, top, rest, block, first_slot):
    count = raw.shape[0]

    def body(index, carry):
        re_rows, im_rows = pair_rows(index, block, 16)
        gr = [grad[i, re_rows, :] for i in range(count)]
        gi = [grad[i, im_rows, :] for i in range(count)]
        hr = [spectrum[i, re_rows, :] for i in range(count)]
        hi = [spectrum[i, im_rows, :] for i in range(count)]
        for out in range(count):
            re = hr[0] * gr[out] + hi[0] * gi[out]
            im = hr[0] * gi[out] - hi[0] * gr[out]
            for later in range(out + 1, count):
                lag = later - out
                re = re + (hr[lag] * gr[later] + hi[lag] * gi[later])
                im = im + (hr[lag] * gi[later] - hi[lag] * gr[later])
            top[out, re_rows, :], rest[out, re_rows, :] = split(re)
            top[out, im_rows, :], rest[out, im_rows, :] = split(im)
        xr = [raw[i, re_rows, :] for i in range(count)]
        xi = [raw[i, im_rows, :] for i in range(count)]
        for lag in range(count):
            re = im = None
            for at in range(count - lag):
                a = xr[at] * gr[at + lag] + xi[at] * gi[at + lag]
                b = xr[at] * gi[at + lag] - xi[at] * gr[at + lag]
                re = a if re is None else re + a
                im = b if im is None else im + b
            if not first_slot:
                re = re + total[lag, re_rows, :]
                im = im + total[lag, im_rows, :]
            total[lag, re_rows, :] = re
            total[lag, im_rows, :] = im
        return carry

    lax.fori_loop(0, block // 16, body, 0)


def filter_gradient(total, top, rest, tables, out_ref, block):
    count, width = total.shape[0], total.shape[2]
    scale = 1.0 / block

    def body(index, carry):
        re_rows, im_rows = pair_rows(index, block, 16)
        sign = signs(16, width, 1.0)
        for lag in range(count):
            re, im = total[lag, re_rows, :], total[lag, im_rows, :]
            if lag + 1 < count:
                re = re + sign * total[lag + 1, im_rows, :]
                im = im - sign * total[lag + 1, re_rows, :]
            top[lag, re_rows, :], rest[lag, re_rows, :] = split(re * scale)
            top[lag, im_rows, :], rest[lag, im_rows, :] = split(im * scale)
        return carry

    lax.fori_loop(0, block // 16, body, 0)
    for lag in range(count):
        out_ref[pl.ds(lag * block, block), :] = inverse(top[lag], rest[lag], tables)


def conv_forward_kernel(doc_count, len_ref, x_ref, filter_ref, t0, t1, t2, t3, y_ref, spectrum, full, raw, top, rest, slots):
    tables = (t0, t1, t2, t3)
    parts, block, width = x_ref.shape
    half = width // 2
    count = raw.shape[0]
    filter_spectrum(filter_ref, spectrum, raw, tables, block)
    unpack(full, x_ref)
    starts = document_starts(len_ref, doc_count)
    for slot in range(doc_count):
        slot_blocks(full, raw, tables, starts[slot], len_ref[0, slot], block)
        forward_products(spectrum, raw, top, rest, block)
        for out in range(count):
            slots[slot, pl.ds((1 + out) * block // 8, block // 8)] = tiles(inverse(top[out], rest[out], tables))

    def put(index, values):
        y_ref[index // 2, :, pl.ds((index % 2) * half, half)] = values.astype(y_ref.dtype)

    merge_slots(slots, starts, put, 2 * parts * block, block, count * block)


def conv_forward(x, lengths, filters, tables):
    parts, block, width = x.shape
    half, docs = width // 2, lengths.shape[1]
    count = filters.shape[0] // block
    wide = (count, 2 * block, half)
    return pl.pallas_call(
        functools.partial(conv_forward_kernel, docs),
        name="conv_forward",
        out_shape=(struct(x.shape, BF), struct(wide, F32)),
        in_specs=[IN_SMEM] + [IN_VMEM] * 6,
        out_specs=(IN_VMEM, IN_VMEM),
        scratch_shapes=[
            pltpu.VMEM(((2 * parts + count) * block // 8 + 1, 8, half), F32),
            pltpu.VMEM(wide, F32),
            pltpu.VMEM(wide, BF),
            pltpu.VMEM(wide, BF),
            pltpu.VMEM((docs, (count + 2) * block // 8 + 1, 8, half), F32),
        ],
        compiler_params=pltpu.CompilerParams(vmem_limit_bytes=ROOM),
    )(lengths, x, filters, *tables)


def conv_backward_kernel(doc_count, len_ref, g_ref, x_ref, spectrum, skip_ref, t0, t1, t2, t3, gw_ref, edge_ref, gf_ref, g_full, x_full, grad, raw, top, rest, total, slots):
    tables = (t0, t1, t2, t3)
    parts, block, width = x_ref.shape
    half = width // 2
    count = raw.shape[0]
    unpack(g_full, g_ref)
    unpack(x_full, x_ref)
    starts = document_starts(len_ref, doc_count)
    for slot in range(doc_count):
        slot_blocks(g_full, grad, tables, starts[slot], len_ref[0, slot], block)
        slot_blocks(x_full, raw, tables, starts[slot], len_ref[0, slot], block)
        backward_products(spectrum, grad, raw, total, top, rest, block, slot == 0)
        for out in range(count):
            slots[slot, pl.ds((1 + out) * block // 8, block // 8)] = tiles(inverse(top[out], rest[out], tables))
    edge_ref[...] = jnp.zeros(edge_ref.shape, edge_ref.dtype)

    def put(index, values):
        gw_ref[index // 2, :, pl.ds((index % 2) * half, half)] = values.astype(gw_ref.dtype)
        if index % 2 == 0 and index:
            own = g_full[pl.ds(index * block // 8, EDGE // 8)].reshape(EDGE, half) * skip_ref[...]
            edge_ref[index // 2 - 1, :, 0:half] = (values[0:EDGE] + own).astype(edge_ref.dtype)

    merge_slots(slots, starts, put, 2 * parts * block, block, count * block)
    filter_gradient(total, top, rest, tables, gf_ref, block)


def conv_backward(g, x, lengths, spectrum, skip_gain, tables):
    parts, block, width = x.shape
    half, docs, count = width // 2, lengths.shape[1], spectrum.shape[0]
    wide = (count, 2 * block, half)
    rows = pltpu.VMEM(((2 * parts + count) * block // 8 + 1, 8, half), F32)
    return pl.pallas_call(
        functools.partial(conv_backward_kernel, docs),
        name="conv_backward",
        out_shape=(
            struct(x.shape, BF),
            struct((parts, EDGE, -(-half // 128) * 128), BF),
            struct((count * block, half), F32),
        ),
        in_specs=[IN_SMEM] + [IN_VMEM] * 8,
        out_specs=(IN_VMEM,) * 3,
        scratch_shapes=[
            rows,
            rows,
            pltpu.VMEM(wide, F32),
            pltpu.VMEM(wide, F32),
            pltpu.VMEM(wide, BF),
            pltpu.VMEM(wide, BF),
            pltpu.VMEM(wide, F32),
            pltpu.VMEM((docs, (count + 2) * block // 8 + 1, 8, half), F32),
        ],
        compiler_params=pltpu.CompilerParams(vmem_limit_bytes=ROOM),
    )(lengths, g, x, spectrum, skip_gain, *tables)


def turned(value, bit):
    return value + bit - 2 * bit * ((value // bit) % 2)


def send(source, target, send_sem, recv_sem, device):
    copy = pltpu.make_async_remote_copy(
        src_ref=source,
        dst_ref=target,
        send_sem=send_sem,
        recv_sem=recv_sem,
        device_id=device,
        device_id_type=MESH,
    )
    copy.start()
    return copy


def greet(peers):
    barrier = pltpu.get_barrier_semaphore()
    for peer in peers:
        pl.semaphore_signal(barrier, inc=1, device_id=peer, device_id_type=MESH)
    pl.semaphore_wait(barrier, len(peers))


def ring(me, count):
    return [lax.rem(me + step, count) for step in range(1, count)]


def dma(*shape):
    return pltpu.SemaphoreType.DMA(shape)


def gather_fallback(chunks, gains, channel, edges):
    mp = lax.axis_size("mp")
    down = [(i, (i + 1) % mp) for i in range(mp)]
    up = [(i, (i - 1) % mp) for i in range(mp)]
    spread = [lax.all_gather(lax.all_gather(c, "dp"), "mp") for c in chunks]
    return (
        *spread,
        lax.all_gather(gains, "dp"),
        lax.all_gather(channel, "mp"),
        jnp.stack([lax.ppermute(edges[0], "mp", down), lax.ppermute(edges[1], "mp", up)]),
    )


def exchange_kernel(count, has_edge, *refs):
    sources, refs = refs[: count + has_edge], refs[count + has_edge :]
    targets, refs = refs[: count + has_edge], refs[count + has_edge :]
    send_sem, recv_sem, edge_send, edge_recv = refs
    d, m, mp = lax.axis_index("dp"), lax.axis_index("mp"), lax.axis_size("mp")
    greet([(d, e) for e in ring(m, mp)])
    copies = []
    for step, e in reversed(list(enumerate(ring(m, mp)))):
        for i in range(count):
            copies.append(
                send(sources[i].at[e], targets[i].at[m], send_sem.at[i, step], recv_sem.at[i, step], (d, e))
            )
    if has_edge:
        before = lax.rem(m + mp - 1, mp)
        copies.append(send(sources[count], targets[count], edge_send.at[0], edge_recv.at[0], (d, before)))
    for i in range(count):
        targets[i][m] = sources[i][m]
    for copy in copies:
        copy.wait()


def exchange(arrays, edge, collective_id):
    mp, count = lax.axis_size("mp"), len(arrays)
    inputs = list(arrays) + ([] if edge is None else [edge])
    return pl.pallas_call(
        functools.partial(exchange_kernel, count, int(edge is not None)),
        name="exchange_%d" % collective_id,
        out_shape=tuple(struct(a.shape, a.dtype) for a in inputs),
        in_specs=[IN_VMEM] * len(inputs),
        out_specs=(IN_VMEM,) * len(inputs),
        scratch_shapes=[dma(count, mp - 1), dma(count, mp - 1), dma(1), dma(1)],
        compiler_params=pltpu.CompilerParams(
            collective_id=collective_id, has_side_effects=True, vmem_limit_bytes=ROOM
        ),
    )(*inputs)


class Flow:
    def __init__(self, part, refs):
        self.part = part
        (self.own, self.from_core, self.from_y2, self.from_x2, self.from_x1, self.from_y1, self.from_z) = refs[:7]
        self.own_sem, self.p_send, self.p_recv, self.z_send, self.z_recv = refs[7:]
        self.d, self.m, self.mp = lax.axis_index("dp"), lax.axis_index("mp"), lax.axis_size("mp")
        self.half = self.mp // 2
        self.y, self.x, self.core = self.d // 4, (self.d // 2) % 2, self.d % 2
        self.pending = []

    def push(self, slot, source, target, bit):
        peer = (turned(self.d, bit), self.m)
        copy = send(source, target, self.p_send.at[slot], self.p_recv.at[slot], peer)
        self.pending.append(copy)
        return copy

    def start(self):
        self.copy = self.push(0, self.part.at[:, :, :, 1 - self.core], self.from_core, 1)
        self.local = pltpu.make_async_copy(self.part.at[:, :, :, self.core], self.own, self.own_sem.at[0])
        self.local.start()

    def core_stage(self):
        own, half, y, x = self.own, self.half, self.y, self.x
        self.local.wait()
        self.copy.wait_recv()

        def body(i, carry):
            at = (i // 4, (i // 2) % 2, i % 2)
            own[at] = own[at] + self.from_core[at]
            return carry

        lax.fori_loop(0, self.mp * 4, body, 0)
        low, high = pl.ds(0, half), pl.ds(half, self.mp - half)
        self.copies = [
            self.push(1, own.at[low, 1 - y], self.from_y2, 4),
            self.push(2, own.at[high, :, 1 - x], self.from_x2, 2),
        ]

    def second_stage(self):
        own, half, y, x = self.own, self.half, self.y, self.x
        for copy in self.copies:
            copy.wait_recv()

        def body(i, carry):
            a, b = i // 2, i % 2
            own[a, y, b] = own[a, y, b] + self.from_y2[a, b]
            own[half + a, b, x] = own[half + a, b, x] + self.from_x2[a, b]
            return carry

        lax.fori_loop(0, half * 2, body, 0)
        low, high = pl.ds(0, half), pl.ds(half, self.mp - half)
        self.copies = [
            self.push(3, own.at[low, y, 1 - x], self.from_x1, 2),
            self.push(4, own.at[high, 1 - y, x], self.from_y1, 4),
        ]

    def third_stage(self):
        own, half, y, x = self.own, self.half, self.y, self.x
        for copy in self.copies:
            copy.wait_recv()

        def body(a, carry):
            own[a, y, x] = own[a, y, x] + self.from_x1[a]
            own[half + a, y, x] = own[half + a, y, x] + self.from_y1[a]
            return carry

        lax.fori_loop(0, half, body, 0)

    def send_z(self):
        self.copies = [
            send(
                self.own.at[e, self.y, self.x], self.from_z.at[step], self.z_send.at[step], self.z_recv.at[step],
                (self.d, e),
            )
            for step, e in enumerate(ring(self.m, self.mp))
        ]
        self.pending.extend(self.copies)

    def finish(self, out):
        for copy in self.copies:
            copy.wait_recv()
        total = self.own[self.m, self.y, self.x].astype(F32)
        for step in range(self.mp - 1):
            total = total + self.from_z[step].astype(F32)
        out[...] = total

    def drain(self):
        for copy in self.pending:
            copy.wait_send()


FLOW_REFS = 12


def flow_scratch(mp, block):
    half = mp // 2
    leads = ((mp, 2, 2), (mp, 2, 2), (half, 2), (mp - half, 2), (half,), (mp - half,), (mp - 1,))
    return [pltpu.VMEM(lead + block, BF) for lead in leads] + [dma(1), dma(5), dma(5), dma(mp - 1), dma(mp - 1)]


class SmallSums:
    def __init__(self, small, outs, wide, refs):
        count = len(small)
        self.small, self.outs, self.wide = small, outs, wide
        self.running, self.from_dp, self.from_mp = [refs[i * count : (i + 1) * count] for i in range(3)]
        self.s_send, self.s_recv = refs[3 * count :]
        self.pending = []

    def start(self, stage):
        bit = (1, 2, 4)[stage]
        d, m = lax.axis_index("dp"), lax.axis_index("mp")
        if stage == 0:
            for i, ref in enumerate(self.small):
                self.running[i][0] = ref[...]
        self.copies = []
        for i in range(len(self.small)):
            at = i * 8 + stage
            self.copies.append(
                send(
                    self.running[i].at[stage], self.from_dp[i].at[stage], self.s_send.at[at], self.s_recv.at[at],
                    (turned(d, bit), m),
                )
            )
        self.pending.extend(self.copies)

    def end(self, stage):
        for i, copy in enumerate(self.copies):
            copy.wait_recv()
            self.running[i][stage + 1] = self.running[i][stage] + self.from_dp[i][stage]

    def start_mp(self):
        d, m, mp = lax.axis_index("dp"), lax.axis_index("mp"), lax.axis_size("mp")
        self.copies = []
        for i, wide in enumerate(self.wide):
            if wide:
                for step, e in enumerate(ring(m, mp)):
                    at = i * 8 + 3 + step
                    self.copies.append(
                        send(
                            self.running[i].at[3], self.from_mp[i].at[m], self.s_send.at[at], self.s_recv.at[at],
                            (d, e),
                        )
                    )
                self.from_mp[i][m] = self.running[i][3]
        self.pending.extend(self.copies)

    def end_mp(self):
        for copy in self.copies:
            copy.wait_recv()
        for i, wide in enumerate(self.wide):
            if wide:
                total = self.from_mp[i][0]
                for e in range(1, lax.axis_size("mp")):
                    total = total + self.from_mp[i][e]
                self.outs[i][...] = total
            else:
                self.outs[i][...] = self.running[i][3]

    def drain(self):
        for copy in self.pending:
            copy.wait_send()


def small_scratch(small, mp):
    scratch = []
    for lead in (4, 3, mp):
        scratch += [pltpu.VMEM((lead,) + s.shape, F32) for s in small]
    return scratch + [dma(8 * len(small)), dma(8 * len(small))]


def scatter_fallback(part):
    over_mp = lax.psum_scatter(part, "mp", scatter_dimension=0)
    return lax.psum_scatter(over_mp, "dp", scatter_dimension=0).astype(F32)


def cored(part):
    return part.reshape((part.shape[0], 2, 2, 2) + part.shape[2:])


class Blocks:
    def __init__(self, pairs, send_sem, recv_sem):
        self.pairs, self.send_sem, self.recv_sem = pairs, send_sem, recv_sem
        self.d, self.m, self.mp = lax.axis_index("dp"), lax.axis_index("mp"), lax.axis_size("mp")

    def start(self):
        self.copies = []
        for step, e in reversed(list(enumerate(ring(self.m, self.mp)))):
            for i, (source, target) in enumerate(self.pairs):
                sems = self.send_sem.at[i, step], self.recv_sem.at[i, step]
                self.copies.append(send(source.at[e], target.at[self.m], *sems, (self.d, e)))
        for source, target in self.pairs:
            target[self.m] = source[self.m]

    def arrive(self):
        for copy in self.copies:
            copy.wait_recv()

    def drain(self):
        for copy in self.copies:
            copy.wait_send()


def mixer_backward_kernel(
    doc_count, len_ref, g_parts, edge, x_ref, spectrum, skip_ref, t0, t1, t2, t3, part_a, part_b,
    gw_back, gw_edge_back, edge_back, gf_ref, total_a, partial_b,
    g_in, gw, gw_edge, g_full, x_full, grad, raw, top, rest, total, slots,
    b_send, b_recv, c_send, c_recv, e_sem, *flow_refs,
):
    tables = (t0, t1, t2, t3)
    parts, block, width = x_ref.shape
    half = width // 2
    count = raw.shape[0]
    d, m, mp = lax.axis_index("dp"), lax.axis_index("mp"), lax.axis_size("mp")
    a, b = Flow(part_a, flow_refs[:FLOW_REFS]), Flow(part_b, flow_refs[FLOW_REFS:])
    incoming = Blocks([(g_parts, g_in)], b_send, b_recv)
    outgoing = Blocks([(gw, gw_back), (gw_edge, gw_edge_back)], c_send, c_recv)
    greet([(turned(d, bit), m) for bit in (1, 2, 4)] + [(d, e) for e in ring(m, mp)])
    incoming.start()
    edge_copy = send(edge, edge_back, e_sem.at[0], e_sem.at[1], (d, lax.rem(m + mp - 1, mp)))
    a.start()
    b.start()
    unpack(x_full, x_ref)
    starts = document_starts(len_ref, doc_count)
    a.core_stage()
    incoming.arrive()
    unpack(g_full, g_in)
    for slot in range(doc_count):
        slot_blocks(g_full, grad, tables, starts[slot], len_ref[0, slot], block)
        slot_blocks(x_full, raw, tables, starts[slot], len_ref[0, slot], block)
        if slot == 0:
            a.second_stage()
            b.core_stage()
        backward_products(spectrum, grad, raw, total, top, rest, block, slot == 0)
        for out in range(count):
            slots[slot, pl.ds((1 + out) * block // 8, block // 8)] = tiles(inverse(top[out], rest[out], tables))
        if slot == 1:
            a.third_stage()
            a.send_z()
    gw_edge[...] = jnp.zeros(gw_edge.shape, gw_edge.dtype)

    def put(index, values):
        gw[index // 2, :, pl.ds((index % 2) * half, half)] = values.astype(gw.dtype)
        if index % 2 == 0 and index:
            own = g_full[pl.ds(index * block // 8, EDGE // 8)].reshape(EDGE, half) * skip_ref[...]
            gw_edge[index // 2 - 1, :, 0:half] = (values[0:EDGE] + own).astype(gw_edge.dtype)

    merge_slots(slots, starts, put, 2 * parts * block, block, count * block)
    outgoing.start()
    b.second_stage()
    filter_gradient(total, top, rest, tables, gf_ref, block)
    a.finish(total_a)
    b.third_stage()
    for e in range(parts):
        partial_b[e] = b.own[e, b.y, b.x]
    outgoing.arrive()
    edge_copy.wait()
    incoming.drain()
    outgoing.drain()
    a.drain()
    b.drain()


def mixer_backward(g_parts, edge, x, lengths, spectrum, skip_gain, tables, part_a, part_b):
    mp = lax.axis_size("mp")
    parts, block, width = x.shape
    half, docs, count = width // 2, lengths.shape[1], spectrum.shape[0]
    if lax.axis_size("dp") != 8:
        (g_in, edge_back) = exchange([g_parts], edge, 5)
        gw, gw_edge, gf = conv_backward(g_in, x, lengths, spectrum, skip_gain, tables)
        gw_back, gw_edge_back = exchange([gw, gw_edge], None, 6)
        over_dp = lax.psum_scatter(part_b, "dp", scatter_dimension=1)
        return gw_back, gw_edge_back, edge_back, gf, scatter_fallback(part_a), over_dp
    wide = (count, 2 * block, half)
    edge_shape = (parts, EDGE, -(-half // 128) * 128)
    own = part_a.shape[2:]
    rows = pltpu.VMEM(((2 * parts + count) * block // 8 + 1, 8, half), F32)
    return pl.pallas_call(
        functools.partial(mixer_backward_kernel, docs),
        name="mixer_backward",
        out_shape=(
            struct(x.shape, BF), struct(edge_shape, BF), struct(edge.shape, BF), struct((count * block, half), F32),
            struct(own, F32), struct((mp,) + own, BF),
        ),
        in_specs=[IN_SMEM] + [IN_VMEM] * 9 + [IN_HBM] * 2,
        out_specs=(IN_VMEM,) * 6,
        scratch_shapes=[
            pltpu.VMEM(x.shape, BF), pltpu.VMEM(x.shape, BF), pltpu.VMEM(edge_shape, BF), rows, rows,
            pltpu.VMEM(wide, F32), pltpu.VMEM(wide, F32), pltpu.VMEM(wide, BF), pltpu.VMEM(wide, BF),
            pltpu.VMEM(wide, F32), pltpu.VMEM((docs, (count + 2) * block // 8 + 1, 8, half), F32),
            dma(1, mp - 1), dma(1, mp - 1), dma(2, mp - 1), dma(2, mp - 1), dma(2),
            *flow_scratch(mp, own), *flow_scratch(mp, own),
        ],
        compiler_params=pltpu.CompilerParams(collective_id=5, has_side_effects=True, vmem_limit_bytes=ROOM),
    )(lengths, g_parts, edge, x, spectrum, skip_gain, *tables, cored(part_a), cored(part_b))


def spread_sum(block, slots, send_sem, recv_sem, axis, first):
    d, m = lax.axis_index("dp"), lax.axis_index("mp")
    count = lax.axis_size(axis)
    me = d if axis == "dp" else m
    copies = []
    for step, e in enumerate(ring(me, count)):
        peer = (e, m) if axis == "dp" else (d, e)
        copies.append(send(block, slots.at[me], send_sem.at[first + step], recv_sem.at[first + step], peer))
    slots[me] = block[...]
    for copy in copies:
        copy.wait()
    total = slots[0]
    for e in range(1, count):
        total = total + slots[e]
    return total


def total_of(values):
    return jnp.sum(jnp.sum(values, axis=1, keepdims=True), axis=0, keepdims=True)


def lanes_of(items):
    lane = lax.broadcasted_iota(jnp.int32, (1, 128), 1)
    row = jnp.zeros((1, 128), F32)
    for index, item in enumerate(items):
        row = row + jnp.where(lane == index, item, 0.0)
    return row


def update_body(
    g0, g1, g2, w0, w1, w2, rows, cols, gain_sum, gain, gain_mom, chan_sum, chan, chan_mom,
    fin_sum, fin, fin_mom, fout_sum, fout, fout_mom,
    norm_out, c0, c1, c2, n0, n1, n2, rows_out, cols_out, gain_g, gain_n, gain_m,
    chan_g, chan_n, chan_m, fin_g, fin_n, fin_m, fout_g, fout_n, fout_m,
    turn, mp_block, dp_block, mp_slots, dp_slots, last_block, mp_last, dp_last, send_sem, recv_sem,
):
    d, m = lax.axis_index("dp"), lax.axis_index("mp")
    dp, mp = lax.axis_size("dp"), lax.axis_size("mp")
    size, width = g0.shape
    in_width = 3 * (width // 4)
    is_in = lax.broadcasted_iota(jnp.int32, (size, width), 1) < in_width

    def four(v0, v1, v2, reduce_fn):
        return [
            reduce_fn(jnp.where(is_in, v0, 0.0)),
            reduce_fn(jnp.where(is_in, 0.0, v0)),
            reduce_fn(v1),
            reduce_fn(v2),
        ]

    def row_sum(v):
        return jnp.sum(v, axis=1, keepdims=True)

    def col_sum(v):
        return jnp.sum(v, axis=0, keepdims=True)

    s0, s1, s2 = g0[...] * g0[...], g1[...] * g1[...], g2[...] * g2[...]
    lane = lax.broadcasted_iota(jnp.int32, (size, 128), 1)
    row_parts = four(s0, s1, s2, row_sum)
    packed = jnp.zeros((size, 128), F32)
    for index, part in enumerate(row_parts):
        packed = packed + jnp.where(lane == index, part, 0.0)
    turn[...] = jnp.zeros(turn.shape, F32)
    dp_block[...] = jnp.zeros(dp_block.shape, F32)
    turn[pl.ds(0, size), :] = packed
    mp_block[pl.ds(0, 8), :] = jnp.transpose(turn[...])[0:8]
    old = rows[...]
    old_parts = [total_of(old[:, i : i + 1]) / mp for i in range(4)]
    weight_parts = four(w0[...] * w0[...], w1[...] * w1[...], w2[...] * w2[...], total_of)
    scalars = (
        [total_of(p) for p in row_parts]
        + old_parts
        + weight_parts
        + [
            total_of(gain[...] * gain[...]) / mp,
            total_of(chan[...] * chan[...]) / dp,
            total_of(fout[...] * fout[...]) / dp,
            total_of(fout_sum[...] * fout_sum[...]) / dp,
        ]
    )
    mp_block[pl.ds(8, 8), :] = jnp.broadcast_to(lanes_of(scalars), (8, 128))
    over_mp = spread_sum(mp_block, mp_slots, send_sem, recv_sem, "mp", 0)
    pieces = width // 128
    for index, values in enumerate((s0, s1, s2)):
        sums = col_sum(values)
        for piece in range(pieces):
            dp_block[pl.ds(index * pieces + piece, 1), :] = sums[:, piece * 128 : (piece + 1) * 128]
    dp_block[pl.ds(3 * pieces, 1), :] = over_mp[8:9]
    over_dp = spread_sum(dp_block, dp_slots, send_sem, recv_sem, "dp", mp)
    turn[pl.ds(0, 8), :] = over_mp[0:8]
    row_totals = jnp.transpose(turn[...])[0:size]
    shared = over_dp[3 * pieces : 3 * pieces + 1]

    def scalar(index):
        return shared[:, index : index + 1]

    gains_sq = total_of(jnp.sum(gain_sum[...] * gain_sum[...], axis=0))
    chan_sq = total_of(jnp.sum(chan_sum[...] * chan_sum[...], axis=0))
    fin_sq = total_of(fin_sum[...] * fin_sum[...])
    norm = jnp.sqrt(
        scalar(0) + scalar(1) + scalar(2) + scalar(3) + gains_sq + chan_sq + scalar(15) + fin_sq
    )
    norm_out[...] = norm
    clip = 1.0 / jnp.maximum(1.0, norm / CLIP_NORM)
    square = clip * clip
    fresh = 1.0 - MOMENT_DECAY
    all_rows = size * dp
    wide = [in_width * mp, (width - in_width) * mp, width * mp, width * mp]
    ratio = []
    lane4 = lax.broadcasted_iota(jnp.int32, (size, 4), 1)
    fresh_rows = jnp.zeros((size, 4), F32)
    for index in range(4):
        row_new = (
            MOMENT_DECAY * old[:, index : index + 1]
            + fresh * square * row_totals[:, index : index + 1] / wide[index]
        )
        mean = MOMENT_DECAY * scalar(4 + index) / all_rows + fresh * square * scalar(index) / (
            all_rows * wide[index]
        )
        ratio.append(row_new / mean)
        fresh_rows = fresh_rows + jnp.where(lane4 == index, row_new, 0.0)
    rows_out[...] = fresh_rows
    for index in range(3):
        for piece in range(pieces):
            at = pl.ds(piece * 128, 128)
            row = index * pieces + piece
            cols_out[pl.ds(index, 1), at] = (
                MOMENT_DECAY * cols[pl.ds(index, 1), at]
                + fresh * square * over_dp[row : row + 1] / all_rows
            )
    first_ratio = jnp.where(is_in, ratio[0], ratio[1])
    steps = []
    for grad, out, factor, index in ((g0, c0, first_ratio, 0), (g1, c1, ratio[2], 1), (g2, c2, ratio[3], 2)):
        clipped = grad[...] * clip
        out[...] = clipped
        steps.append(clipped * lax.rsqrt(factor * cols_out[pl.ds(index, 1), :]))
    u0, u1, u2 = steps

    def plain(clipped, moment, grad_out, moment_out):
        fresh_moment = MOMENT_DECAY * moment + fresh * clipped * clipped
        grad_out[...] = clipped
        moment_out[...] = fresh_moment
        return clipped * lax.rsqrt(fresh_moment)

    own_gain = gain_sum[0]
    for e in range(1, dp):
        own_gain = jnp.where(d == e, gain_sum[e], own_gain)
    own_chan = chan_sum[0]
    for e in range(1, mp):
        own_chan = jnp.where(m == e, chan_sum[e], own_chan)
    u_gain = plain(own_gain * clip, gain_mom[...], gain_g, gain_m)
    u_chan = plain(own_chan * clip, chan_mom[...], chan_g, chan_m)
    u_fin = plain(fin_sum[...] * clip, fin_mom[...], fin_g, fin_m)
    u_fout = plain(fout_sum[...] * clip, fout_mom[...], fout_g, fout_m)
    step_parts = four(u0 * u0, u1 * u1, u2 * u2, total_of) + [
        total_of(u_gain * u_gain) / mp,
        total_of(u_chan * u_chan) / dp,
        total_of(u_fout * u_fout) / dp,
    ]
    last_block[...] = jnp.broadcast_to(lanes_of(step_parts), (8, 128))
    half_way = spread_sum(last_block, mp_last, send_sem, recv_sem, "mp", mp + dp)
    mp_block[pl.ds(0, 8), :] = half_way
    step_sums = spread_sum(mp_block.at[pl.ds(0, 8)], dp_last, send_sem, recv_sem, "dp", 2 * mp + dp)[0:1]

    def factors(step_total, weight_total, entries):
        shrink = 1.0 / jnp.maximum(1.0, jnp.sqrt(step_total / entries) / CLIP_STEP)
        return STEP_RATE * jnp.sqrt(weight_total / entries) * shrink

    def step_sum(index):
        return step_sums[:, index : index + 1]

    rate = [factors(step_sum(i), scalar(8 + i), all_rows * wide[i]) for i in range(4)]
    n0[...] = w0[...] - jnp.where(is_in, rate[0], rate[1]) * u0
    n1[...] = w1[...] - rate[2] * u1
    n2[...] = w2[...] - rate[3] * u2
    gain_n[...] = gain[...] - factors(step_sum(4), scalar(12), 2 * all_rows) * u_gain
    chan_n[...] = chan[...] - factors(step_sum(5), scalar(13), chan.shape[0] * chan.shape[1] * mp) * u_chan
    fout_n[...] = fout[...] - factors(step_sum(6), scalar(14), fout.shape[0] * fout.shape[1] * mp) * u_fout
    fin_count = fin.shape[0] * fin.shape[1]
    fin_rate = factors(total_of(u_fin * u_fin), total_of(fin[...] * fin[...]), fin_count)
    fin_n[...] = fin[...] - fin_rate * u_fin


def greet_all():
    d, m = lax.axis_index("dp"), lax.axis_index("mp")
    greet([(e, m) for e in ring(d, lax.axis_size("dp"))] + [(d, e) for e in ring(m, lax.axis_size("mp"))])


def update_kernel(*refs):
    greet_all()
    update_body(*refs)


def finish_kernel(small_wide, part, total_up, partial_down, *refs):
    count = len(small_wide)
    small, refs = refs[:count], refs[count:]
    others, refs = refs[:13], refs[13:]
    outs, refs = refs[:21], refs[21:]
    g0, g2, refs = refs[0], refs[1], refs[2:]
    sums_out, refs = refs[:count], refs[count:]
    work, refs = refs[:10], refs[10:]
    from_z, z_send, z_recv, refs = refs[0], refs[1], refs[2], refs[3:]
    flow = Flow(part, refs[:FLOW_REFS])
    sums = SmallSums(small, sums_out, small_wide, refs[FLOW_REFS:])
    d, m, mp = lax.axis_index("dp"), lax.axis_index("mp"), lax.axis_size("mp")
    greet_all()
    flow.start()
    sums.start(0)
    down = [
        send(partial_down.at[e], from_z.at[step], z_send.at[step], z_recv.at[step], (d, e))
        for step, e in enumerate(ring(m, mp))
    ]
    flow.core_stage()
    sums.end(0)
    sums.start(1)
    flow.second_stage()
    sums.end(1)
    sums.start(2)
    flow.third_stage()
    flow.send_z()
    sums.end(2)
    sums.start_mp()
    for copy in down:
        copy.wait()
    total = partial_down[m].astype(F32)
    for step in range(mp - 1):
        total = total + from_z[step].astype(F32)
    g2[...] = total
    sums.end_mp()
    flow.finish(g0)
    flow.drain()
    sums.drain()
    w, rest = others[:5], others[5:]
    pairs = []
    for i in range(4):
        pairs += [sums_out[i], rest[2 * i], rest[2 * i + 1]]
    update_body(g0, total_up, g2, *w, *pairs, *outs, *work)


def update_scratch(dp, mp, width):
    pieces = 3 * width // 128 + 1
    tall = -(-pieces // 8) * 8
    sems = 2 * (dp + mp)
    return [
        pltpu.VMEM((128, 128), F32),
        pltpu.VMEM((16, 128), F32),
        pltpu.VMEM((tall, 128), F32),
        pltpu.VMEM((mp, 16, 128), F32),
        pltpu.VMEM((dp, tall, 128), F32),
        pltpu.VMEM((8, 128), F32),
        pltpu.VMEM((mp, 8, 128), F32),
        pltpu.VMEM((dp, 8, 128), F32),
        dma(sems),
        dma(sems),
    ]


def finish(part, total_up, partial_down, small, small_wide, weights, rows, cols, olds):
    dp, mp = lax.axis_size("dp"), lax.axis_size("mp")
    big = struct(weights[0].shape, F32)
    size, width = big.shape
    out_small = [struct(v[0].shape, F32) for v in olds for _ in range(3)]
    outs = (struct((1, 1), F32),) + (big,) * 6 + (struct(rows.shape, F32), struct(cols.shape, F32), *out_small)
    params = pltpu.CompilerParams(collective_id=2, has_side_effects=True, vmem_limit_bytes=ROOM)
    if dp != 8:
        sums = [lax.psum(s, ("dp", "mp") if wide else "dp") for s, wide in zip(small, small_wide)]
        inputs = [scatter_fallback(part), total_up, lax.psum_scatter(partial_down, "mp").astype(F32)]
        inputs += [*weights, rows, cols]
        for total, old in zip(sums, olds):
            inputs += [total, *old]
        return pl.pallas_call(
            update_kernel,
            name="clip_and_update",
            out_shape=outs,
            in_specs=[IN_VMEM] * len(inputs),
            out_specs=(IN_VMEM,) * len(outs),
            scratch_shapes=update_scratch(dp, mp, width),
            compiler_params=params,
        )(*inputs)
    inputs = [total_up, partial_down, *small, *weights, rows, cols]
    for old in olds:
        inputs += old
    return pl.pallas_call(
        functools.partial(finish_kernel, small_wide),
        name="sum_clip_update",
        out_shape=outs,
        in_specs=[IN_HBM] + [IN_VMEM] * len(inputs),
        out_specs=(IN_VMEM,) * len(outs),
        scratch_shapes=[
            pltpu.VMEM((size, width), F32),
            pltpu.VMEM((size, width), F32),
            *[pltpu.VMEM(s.shape, F32) for s in small],
            *update_scratch(dp, mp, width),
            pltpu.VMEM((mp - 1, size, width), BF),
            dma(mp - 1),
            dma(mp - 1),
            *flow_scratch(mp, (size, width)),
            *small_scratch(small, mp),
        ],
        compiler_params=params,
    )(cored(part), *inputs)


class Spread:
    def __init__(self, own, whole, lanes, refs):
        self.whole, self.lanes = whole, lanes
        self.source = own.at[:, lanes]
        self.own_sem, self.z_send, self.z_recv, self.p_send, self.p_recv = refs
        self.d, self.m, self.mp = lax.axis_index("dp"), lax.axis_index("mp"), lax.axis_size("mp")
        d = self.d
        self.dx, self.dy, self.dc = turned(d, 2), turned(d, 4), turned(d, 1)
        half = self.mp // 2
        self.low, self.high, self.all = pl.ds(0, half), pl.ds(half, self.mp - half), pl.ds(0, self.mp)

    def start(self):
        target = self.whole.at[self.m, self.d, :, self.lanes]
        self.copy = pltpu.make_async_copy(self.source, target, self.own_sem.at[0])
        self.copy.start()
        self.z = [
            send(self.source, target, self.z_send.at[step], self.z_recv.at[step], (self.d, e))
            for step, e in enumerate(ring(self.m, self.mp))
        ]

    def push(self, slot, rows, owner, peer):
        block = self.whole.at[rows, owner, :, self.lanes]
        return send(block, block, self.p_send.at[slot], self.p_recv.at[slot], (peer, self.m))

    def stage_one(self):
        self.copy.wait()
        for copy in self.z:
            copy.wait_recv()
        d, dx, dy = self.d, self.dx, self.dy
        self.first = [self.push(0, self.low, d, dx), self.push(1, self.high, d, dy)]
        self.last = [self.push(2, self.all, d, self.dc)]

    def stage_two(self):
        for copy in self.first:
            copy.wait_recv()
        d, dx, dy = self.d, self.dx, self.dy
        self.second = [
            self.push(3, self.low, d, dy),
            self.push(4, self.high, d, dx),
            self.push(5, self.low, dx, dy),
            self.push(6, self.high, dy, dx),
        ]

    def stage_three(self):
        for copy in self.second:
            copy.wait_recv()
        for slot, owner in enumerate((self.dx, self.dy, turned(self.dx, 4))):
            self.last.append(self.push(7 + slot, self.all, owner, self.dc))

    def arrive(self):
        for copy in self.last:
            copy.wait_recv()

    def drain(self):
        for copy in self.z + self.first + self.second + self.last:
            copy.wait_send()


SPREAD_REFS = 5


def spread_scratch(mp):
    return [dma(1), dma(mp - 1), dma(mp - 1), dma(10), dma(10)]


def near_product(left, right):
    l_top, l_rest = split(left)
    r_top, r_rest = split(right)
    return mm(l_top, r_top) + mm(l_top, r_rest) + mm(l_rest, r_top)


def mixer_forward_kernel(
    doc_count, taps, len_ref, tok, chunk_first, chunk_up, chunk_down, gains, channel, edges, table, step_col, f_in, f_out,
    t0, t1, t2, t3,
    w_parts, y_back, spectrum, hidden, phase, decay, gain_rows, chan_rows,
    z_out, s0_out, s1_out, s2_out, w_out_own, a_out, n1_out, inv1_out, w_in_out, w_out_out, whole_up, whole_down,
    whole_first, gains_all, channel_all, edges_all, filters, w_send, y_parts, full, raw, top, rest, slots,
    ext, n1, inv1, a, z, s0, s1, s2, w_own, w_in, w_out, same,
    s_send, s_recv, save_sem, b_send, b_recv, c_send, c_recv, *spread_refs,
):
    tables = (t0, t1, t2, t3)
    d, m = lax.axis_index("dp"), lax.axis_index("mp")
    dp, mp = lax.axis_size("dp"), lax.axis_size("mp")
    count, width = tok.shape
    rows = chunk_first.shape[0]
    own = width // mp
    block = count // 2
    blocks = raw.shape[0]
    greet_all()

    small = []
    for step, e in enumerate(ring(d, dp)):
        small.append(send(gains, gains_all.at[d], s_send.at[step], s_recv.at[step], (e, m)))
    for step, e in enumerate(ring(m, mp)):
        at = dp + step
        small.append(send(channel, channel_all.at[m], s_send.at[at], s_recv.at[at], (d, e)))
    at = dp + mp
    for index, peer in ((0, lax.rem(m + 1, mp)), (1, lax.rem(m + mp - 1, mp))):
        sems = s_send.at[at + index], s_recv.at[at + index]
        small.append(send(edges.at[index], edges_all.at[index], *sems, (d, peer)))
    gains_all[d] = gains[...]
    channel_all[m] = channel[...]

    half = width // 2
    plan = [
        (chunk_first, whole_first, pl.ds(0, half)),
        (chunk_first, whole_first, pl.ds(half, width - half)),
        (chunk_up, whole_up, pl.ds(0, chunk_up.shape[1])),
        (chunk_down, whole_down, pl.ds(0, chunk_down.shape[1])),
    ]
    flows = [Spread(*p, spread_refs[i * SPREAD_REFS : (i + 1) * SPREAD_REFS]) for i, p in enumerate(plan)]
    left, right, up, down = flows
    for flow in flows:
        flow.start()

    phase[...] = near_product(table[...], f_in[...])
    hidden[...] = jnp.sin(phase[...])
    lane = (m * own + lax.broadcasted_iota(jnp.int32, (1, own), 1)).astype(F32)
    rate = FAST_DECAY + (SLOW_DECAY - FAST_DECAY) * lane / (width - 1)
    decay[...] = jnp.exp(-step_col[...] * rate)
    filters[...] = near_product(hidden[...], f_out[...]) * decay[...]
    filter_spectrum(filters, spectrum, raw, tables, block)

    position = lax.broadcasted_iota(jnp.int32, (ext.shape[0], 128), 0) + (m * count - EDGE)
    doc = jnp.zeros(position.shape, jnp.int32)
    end = jnp.int32(0)
    for slot in range(doc_count):
        end = end + len_ref[0, slot]
        doc = doc + (position >= end).astype(jnp.int32)
    doc = jnp.where(position < 0, -1, doc)
    tail = same.shape[1]
    for k in range(1, taps):
        same[k - 1] = jnp.where(doc[EDGE:] == doc[EDGE - k : EDGE - k + tail], 1.0, 0.0)

    left.stage_one()
    for copy in small:
        copy.wait()
    for e in range(dp):
        gain_rows[0:2, pl.ds(e * rows, rows)] = gains_all[e, 0:2, 0:rows].astype(F32)
    for e in range(mp):
        chan_rows[:, pl.ds(e * own, own)] = channel_all[e]
    ext[pl.ds(0, EDGE), :] = edges_all[0].astype(F32)
    ext[pl.ds(EDGE, count), :] = tok[...].astype(F32)
    ext[pl.ds(EDGE + count, EDGE), :] = edges_all[1].astype(F32)

    def norm_body(i, carry):
        at = pl.ds(pl.multiple_of(i * 32, 32), 32)
        normed, inverse_std = norm_parts(ext[at, :])
        n1[at, :] = normed
        inv1[at, :] = jnp.broadcast_to(inverse_std, (32, 128))
        a[at, :] = (normed * gain_rows[0:1, :]).astype(BF)
        return carry

    right.stage_one()
    lax.fori_loop(0, ext.shape[0] // 32, norm_body, 0)
    left.stage_two()
    right.stage_two()
    up.stage_one()
    left.stage_three()
    right.stage_three()

    def stream_weights(j):
        for e in range(mp):
            part = whole_first[e, :, :, pl.ds(j * own, own)].reshape(dp * rows, own)
            w_in[:, pl.ds(j * width + e * own, own)] = part

    def project(j):
        cols = pl.ds(j * width, width)
        z[:, cols] = mm(a[...], w_in[:, cols])

    left.arrive()
    stream_weights(0)
    stream_weights(1)
    project(0)
    project(1)
    right.arrive()
    stream_weights(2)
    project(2)
    up.stage_two()
    down.stage_one()

    def short_body(i, carry):
        first = pl.multiple_of(i * 48, 16)
        at = pl.ds(first, 48)
        streams = []
        for j in range(3):
            part = z[pl.ds(first + 8, 56), pl.ds(j * width, width)]
            total = chan_rows[j : j + 1, :] * part[8:56]
            for k in range(1, taps):
                keep = same[k - 1, at, 0:1] > 0.0
                total = total + chan_rows[3 * k + j : 3 * k + j + 1, :] * jnp.where(keep, part[8 - k : 56 - k], 0.0)
            streams.append(total)
        s0[at, :], s1[at, :], s2[at, :] = streams
        w_own[at, :] = streams[2] * streams[1]
        return carry

    lax.fori_loop(0, s0.shape[0] // 48, short_body, 0)
    for part in range(mp):
        for side in range(2):
            values = w_own[pl.ds(side * block, block), pl.ds(part * own, own)]
            w_send[part, :, pl.ds(side * own, own)] = values.astype(BF)
    going = Blocks([(w_send, w_parts)], b_send, b_recv)
    back = Blocks([(y_parts, y_back)], c_send, c_recv)
    going.start()
    saves = []

    def save(source, target):
        copy = pltpu.make_async_copy(source, target, save_sem.at[len(saves)])
        copy.start()
        saves.append(copy)

    own_rows = pl.ds(0, count)
    for source, target in (
        (z, z_out), (s0.at[own_rows], s0_out), (s1, s1_out), (s2, s2_out), (w_own.at[own_rows], w_out_own),
        (a, a_out), (n1, n1_out), (inv1, inv1_out), (w_in, w_in_out),
    ):
        save(source, target)
    for e in range(mp):
        part = whole_first[e, :, :, pl.ds(3 * own, own)].reshape(dp * rows, own)
        w_out[:, pl.ds(e * own, own)] = part
    save(w_out, w_out_out)
    going.arrive()
    down.stage_two()
    up.stage_three()
    unpack(full, w_parts)
    starts = document_starts(len_ref, doc_count)
    for slot in range(doc_count):
        slot_blocks(full, raw, tables, starts[slot], len_ref[0, slot], block)
        forward_products(spectrum, raw, top, rest, block)
        for out in range(blocks):
            slots[slot, pl.ds((1 + out) * block // 8, block // 8)] = tiles(inverse(top[out], rest[out], tables))

    def put(index, values):
        y_parts[index // 2, :, pl.ds((index % 2) * own, own)] = values.astype(BF)

    merge_slots(slots, starts, put, 2 * mp * block, block, blocks * block)
    back.start()
    down.stage_three()
    up.arrive()
    down.arrive()
    back.arrive()
    for copy in saves:
        copy.wait()
    going.drain()
    back.drain()
    for flow in flows:
        flow.drain()


def mixer_forward(lengths, tokens, chunks, gains, channel, edges, taps, table, step_col, f_in, f_out, tables):
    mp, dp = lax.axis_size("mp"), lax.axis_size("dp")
    count, width = tokens.shape
    own, block, docs = width // mp, count // 2, lengths.shape[1]
    lags = table.shape[0]
    blocks = lags // block
    wide = (blocks, 2 * block, own)
    whole = [(mp, dp) + c.shape for c in chunks]
    longer, later = (count + 2 * EDGE, width), (count + EDGE, width)
    parts = (mp, block, 2 * own)
    vmem_outs = [
        (parts, BF), (parts, BF), (wide, F32), ((lags, f_in.shape[1]), F32), ((lags, f_in.shape[1]), F32),
        ((lags, own), F32), ((8, width), F32), ((16, width), F32),
    ]
    hbm_outs = [
        ((longer[0], 3 * width), F32), ((count, width), F32), (later, F32), (later, F32), ((count, width), F32),
        (longer, BF), (longer, F32), ((longer[0], 128), F32), ((width, 3 * width), BF), ((width, width), BF),
        (whole[1], BF), (whole[2], BF),
    ]
    inputs = (lengths, tokens, *chunks, gains, channel, edges, table, step_col, f_in, f_out, *tables)
    return pl.pallas_call(
        functools.partial(mixer_forward_kernel, docs, taps),
        name="mixer_forward",
        out_shape=tuple(struct(*o) for o in vmem_outs + hbm_outs),
        in_specs=[IN_SMEM] + [IN_VMEM] * (len(inputs) - 1),
        out_specs=(IN_VMEM,) * len(vmem_outs) + (IN_HBM,) * len(hbm_outs),
        scratch_shapes=[
            pltpu.VMEM(whole[0], BF), pltpu.VMEM((dp,) + gains.shape, BF), pltpu.VMEM((mp,) + channel.shape, F32),
            pltpu.VMEM(edges.shape, BF), pltpu.VMEM((lags, own), F32), pltpu.VMEM(parts, BF), pltpu.VMEM(parts, BF),
            pltpu.VMEM(((2 * mp + blocks) * block // 8 + 1, 8, own), F32), pltpu.VMEM(wide, F32),
            pltpu.VMEM(wide, BF), pltpu.VMEM(wide, BF),
            pltpu.VMEM((docs, (blocks + 2) * block // 8 + 1, 8, own), F32),
            pltpu.VMEM(longer, F32), pltpu.VMEM(longer, F32), pltpu.VMEM((longer[0], 128), F32), pltpu.VMEM(longer, BF),
            pltpu.VMEM((longer[0], 3 * width), F32), pltpu.VMEM(later, F32), pltpu.VMEM(later, F32),
            pltpu.VMEM(later, F32), pltpu.VMEM(later, F32), pltpu.VMEM((width, 3 * width), BF),
            pltpu.VMEM((width, width), BF), pltpu.VMEM((taps - 1, later[0], 128), F32),
            dma(dp + mp + 2), dma(dp + mp + 2), dma(10), dma(1, mp - 1), dma(1, mp - 1), dma(1, mp - 1), dma(1, mp - 1),
            *(spread_scratch(mp) * 4),
        ],
        compiler_params=pltpu.CompilerParams(collective_id=0, has_side_effects=True, vmem_limit_bytes=ROOM),
    )(*inputs)


def dot_nt(left, right):
    return lax.dot_general(left, right, (((1,), (1,)), ((), ())), preferred_element_type=F32)


def dot_tn(left, right):
    return lax.dot_general(left, right, (((0,), (0,)), ((), ())), preferred_element_type=F32)


def gelu_parts(x):
    scale, cubic = math.sqrt(2.0 / math.pi), 0.044715
    square = x * x
    t = jnp.tanh(scale * x * (1.0 + cubic * square))
    half = 0.5 * (1.0 + t)
    slope = half + 0.5 * x * (1.0 - t * t) * (scale * (1.0 + 3.0 * cubic * square))
    return x * half, slope


def feed_kernel(
    y_ref, w_ref, s0_ref, tok, cot, w_out, gain, skip, up, down,
    act_out, up_part, down_part, out_part, g_parts, gy_out, gs0_out, gx2_out, sums,
    y, o, x2, n2, inv2, b, b_t, cot_t, mix, acc_out, acc_b,
):
    step, steps = pl.program_id(0), pl.num_programs(0)
    parts, block, wide = y_ref.shape
    own = wide // 2
    count = tok.shape[0]
    tile = 128

    @pl.when(step == 0)
    def _():
        for part in range(parts):
            for side in range(2):
                y[pl.ds(side * block, block), pl.ds(part * own, own)] = y_ref[
                    part, :, pl.ds(side * own, own)
                ].astype(F32)

        def body(index, carry):
            rows = pl.ds(pl.multiple_of(index * tile, tile), tile)
            values = y[rows, :] + skip[...] * w_ref[rows, :]
            y[rows, :] = values
            mixed = (values * s0_ref[rows, :]).astype(BF)
            o[rows, :] = mixed
            residual = tok[rows, :].astype(F32) + dot_nt(mixed, w_out[...])
            x2[rows, :] = residual
            normed, inverse_std = norm_parts(residual)
            n2[rows, :] = normed
            inv2[rows, :] = jnp.broadcast_to(inverse_std, (tile, 128))
            b[rows, :] = (normed * gain[...]).astype(BF)
            return carry

        lax.fori_loop(0, count // tile, body, 0)
        b_t[...] = b[...].T
        cot_t[...] = cot[...].T
        acc_out[...] = jnp.zeros(acc_out.shape, F32)
        acc_b[...] = jnp.zeros(acc_b.shape, F32)

    up_w, down_w = up[0], down[0]
    value, slope = gelu_parts(mm(b[...], up_w))
    act = value.astype(BF)
    g_hpre = (mm(cot[...], down_w) * slope).astype(BF)
    up_part[0] = mm(b_t[...], g_hpre).astype(BF)
    down_part[0] = mm(cot_t[...], act).astype(BF)
    acc_out[...] += dot_nt(act, down_w)
    acc_b[...] += dot_nt(g_hpre, up_w)

    @pl.when(step == steps - 1)
    def _():
        sums[...] = jnp.zeros(sums.shape, F32)

        def body(index, carry):
            rows = pl.ds(pl.multiple_of(index * tile, tile), tile)
            act_out[rows, :] = (x2[rows, :] + acc_out[rows, :]).astype(BF)
            g_b, normed = acc_b[rows, :], n2[rows, :]
            sums[0:1, :] += jnp.sum(g_b * normed, axis=0, keepdims=True)
            g_x2 = cot[rows, :].astype(F32) + norm_back(g_b, gain[...], normed, inv2[rows, 0:1])
            gx2_out[rows, :] = g_x2
            low = g_x2.astype(BF)
            mix[rows, :] = low
            g_o = mm(low, w_out[...])
            g_y = g_o * s0_ref[rows, :]
            gy_out[rows, :] = g_y
            gs0_out[rows, :] = g_o * y[rows, :]
            sums[1:2, :] += jnp.sum(g_y * w_ref[rows, :], axis=0, keepdims=True)
            return carry

        lax.fori_loop(0, count // tile, body, 0)
        for part in range(parts):
            for side in range(2):
                g_parts[part, :, pl.ds(side * own, own)] = gy_out[
                    pl.ds(side * block, block), pl.ds(part * own, own)
                ].astype(BF)
        grad = dot_tn(mix[...], o[...])
        for part in range(parts):
            out_part[part] = grad[:, part * own : (part + 1) * own].astype(BF)


def feed(y_parts, w_own, s0, tokens, cotangent, w_out, gain, skip, whole_up, whole_down):
    mp, width, hidden = whole_up.shape
    count = tokens.shape[0]
    own, cols = width // mp, 256
    each = hidden // cols
    once = pl.Buffered(1)

    def fixed(shape):
        return pl.BlockSpec(shape, lambda i: (0,) * len(shape), pipeline_mode=once)

    def moving():
        return pl.BlockSpec((1, width, cols), lambda i: (i // each, 0, i % each))

    full, half = (count, width), (mp, count // 2, 2 * own)
    outs = [
        (full, BF), (whole_up.shape, BF), (whole_up.shape, BF), ((mp, width, own), BF), (half, BF),
        (full, F32), (full, F32), (full, F32), ((8, width), F32),
    ]
    out_specs = [moving() if i in (1, 2) else fixed(s) for i, (s, _) in enumerate(outs)]
    inputs = (y_parts, w_own, s0, tokens, cotangent, w_out, gain, skip)
    return pl.pallas_call(
        feed_kernel,
        name="feed_forward",
        grid=(mp * each,),
        out_shape=tuple(struct(s, t) for s, t in outs),
        in_specs=[fixed(v.shape) for v in inputs] + [moving(), moving()],
        out_specs=tuple(out_specs),
        scratch_shapes=[
            pltpu.VMEM(full, F32), pltpu.VMEM(full, BF), pltpu.VMEM(full, F32), pltpu.VMEM(full, F32),
            pltpu.VMEM((count, 128), F32), pltpu.VMEM(full, BF), pltpu.VMEM((width, count), BF),
            pltpu.VMEM((width, count), BF), pltpu.VMEM(full, BF), pltpu.VMEM(full, F32), pltpu.VMEM(full, F32),
        ],
        compiler_params=pltpu.CompilerParams(vmem_limit_bytes=ROOM),
    )(*inputs, whole_up, whole_down)


def post_kernel(
    gw_ref, gw_edge, gy_ref, gs0_ref, gs0_edge, s1_ref, s2_ref, z_ref, a_ref, n1_ref, inv1_ref, gx2_ref,
    w_in, taps, skip, gain, doc_ref, out_part,
    first_part, input_grad, sums,
    gw, gs, gz,
):
    parts, block, wide = gw_ref.shape
    own = wide // 2
    count, width = gy_ref.shape
    offsets = (taps.shape[0]) // 3
    for part in range(parts):
        at = pl.ds(part * own, own)
        for side in range(2):
            gw[pl.ds(side * block, block), at] = gw_ref[part, :, pl.ds(side * own, own)].astype(F32)
        gw[pl.ds(count, EDGE), at] = gw_edge[part, :, 0:own].astype(F32)
    gw[pl.ds(0, count), :] += skip[...] * gy_ref[...]
    doc = doc_ref[...]
    same = [None] + [doc[EDGE:] == doc[EDGE - k : doc.shape[0] - k] for k in range(1, offsets)]
    sums[...] = jnp.zeros(sums.shape, F32)
    total = None
    for j in range(3):
        if j == 0:
            gs[pl.ds(0, count), :] = gs0_ref[...]
            gs[pl.ds(count, EDGE), :] = gs0_edge[...].astype(F32)
        else:
            gs[...] = gw[...] * (s2_ref if j == 1 else s1_ref)[...]
        z_cols = pl.ds(j * width, width)
        g_z = None
        for k in range(offsets):
            tap = taps[pl.ds(3 * k + j, 1), :]
            later = gs[pl.ds(k, count), :]
            before = z_ref[pl.ds(EDGE - k, count), z_cols]
            if k:
                later = jnp.where(same[k][k : count + k], later, 0.0)
                before = jnp.where(same[k][:count], before, 0.0)
            g_z = tap * later if g_z is None else g_z + tap * later
            sums[pl.ds(3 * k + j, 1), :] = jnp.sum(gs[pl.ds(0, count), :] * before, axis=0, keepdims=True)
        gz[...] = g_z.astype(BF)
        grad = dot_tn(a_ref[pl.ds(EDGE, count), :], gz[...])
        for part in range(parts):
            first_part[part, :, pl.ds(j * own, own)] = grad[:, part * own : (part + 1) * own].astype(BF)
        term = dot_nt(gz[...], w_in[:, z_cols])
        total = term if total is None else total + term
    for part in range(parts):
        first_part[part, :, pl.ds(3 * own, own)] = out_part[part]
    normed = n1_ref[pl.ds(EDGE, count), :]
    sums[pl.ds(3 * offsets, 1), :] = jnp.sum(total * normed, axis=0, keepdims=True)
    back = norm_back(total, gain[...], normed, inv1_ref[pl.ds(EDGE, count), 0:1])
    input_grad[...] = (gx2_ref[...] + back).astype(BF)


def post(gw_parts, gw_edge, g_y, g_s0, gs0_edge, s1, s2, z, a, n1, inv1, g_x2, w_in, taps, skip, gain, doc, out_part):
    mp, block, wide = gw_parts.shape
    count, width = g_y.shape
    inputs = (
        gw_parts, gw_edge, g_y, g_s0, gs0_edge, s1, s2, z, a, n1, inv1, g_x2, w_in, taps, skip, gain, doc, out_part
    )
    return pl.pallas_call(
        post_kernel,
        name="mixer_post",
        out_shape=(struct((mp, width, width), BF), struct((count, width), BF), struct((16, width), F32)),
        in_specs=[IN_VMEM] * len(inputs),
        out_specs=(IN_VMEM,) * 3,
        scratch_shapes=[
            pltpu.VMEM((count + EDGE, width), F32),
            pltpu.VMEM((count + EDGE, width), F32),
            pltpu.VMEM((count, width), BF),
        ],
        compiler_params=pltpu.CompilerParams(vmem_limit_bytes=ROOM),
    )(*inputs)


def features(length, feature_count, count):
    step = np.arange(count)
    band = np.arange(1, (feature_count - 1) // 2 + 1)
    phase = ((step[:, None] * band[None, :]) % length).astype(np.float32) * np.float32(2.0 * math.pi / length)
    position = (step / length).astype(np.float32)
    table = np.concatenate([position[:, None], np.cos(phase), np.sin(phase)], axis=1)
    return table.astype(np.float32), position


def product(left, right):
    return jnp.dot(left, right, precision=FULL_PRECISION, preferred_element_type=F32)


def norm_parts(values):
    centred = values - jnp.mean(values, axis=-1, keepdims=True)
    inverse_std = lax.rsqrt(jnp.mean(centred * centred, axis=-1, keepdims=True) + EPS_NORM)
    return centred * inverse_std, inverse_std


def norm_back(grad, gain, normed, inverse_std):
    scaled = grad * gain
    mean = jnp.mean(scaled, axis=-1, keepdims=True)
    along = jnp.mean(scaled * normed, axis=-1, keepdims=True)
    return (scaled - mean - normed * along) * inverse_std


def to_parts(values, mp, block):
    own = values.shape[1] // mp
    return values.reshape(2, block, mp, own).transpose(2, 1, 0, 3).reshape(mp, block, 2 * own)


def forward_fallback(lengths, tokens, chunks, gains, channel, edges, taps, table, step_col, f_in, f_out, tables):
    mp, m = lax.axis_size("mp"), lax.axis_index("mp")
    count, width = tokens.shape
    own, rows = width // mp, gains.shape[1]
    shard = chunks[0].shape[0]
    first, up, down, gains_all, channel_all, edges_all = gather_fallback(chunks, gains, channel, edges)
    first = first.reshape(mp, width, width)
    w_in = first[:, :, : 3 * own].reshape(mp, width, 3, own).transpose(1, 2, 0, 3).reshape(width, 3 * width)
    w_out = first[:, :, 3 * own :].transpose(1, 0, 2).reshape(width, width)
    gain_rows = gains_all[:, 0:8, :shard].transpose(1, 0, 2).reshape(8, width).astype(F32)
    chan_rows = channel_all.transpose(1, 0, 2).reshape(-1, width)
    position = m * count - EDGE + jnp.arange(count + 2 * EDGE, dtype=jnp.int32)
    doc = jnp.sum((position[:, None] >= jnp.cumsum(lengths[0])[None, :]).astype(jnp.int32), axis=1)
    doc = jnp.where(position < 0, -1, doc)
    n1, inv1 = norm_parts(jnp.concatenate([edges_all[0], tokens, edges_all[1]]).astype(F32))
    a = (n1 * gain_rows[0]).astype(BF)
    z = jnp.dot(a, w_in, preferred_element_type=F32)
    s = []
    for j in range(3):
        stream, total = z[:, j * width : (j + 1) * width], None
        for k in range(taps):
            part = stream[EDGE - k : stream.shape[0] - k]
            if k:
                part = jnp.where((doc[EDGE:] == doc[EDGE - k : doc.shape[0] - k])[:, None], part, 0.0)
            term = chan_rows[3 * k + j] * part
            total = term if total is None else total + term
        s.append(total)
    w_own = s[2][:count] * s[1][:count]
    phase = product(table, f_in)
    hidden = jnp.sin(phase)
    lane = (m * own + jnp.arange(own, dtype=jnp.int32)).astype(F32)
    decay = jnp.exp(-step_col * (FAST_DECAY + (SLOW_DECAY - FAST_DECAY) * lane / (width - 1)))
    (w_parts,) = exchange([to_parts(w_own.astype(BF), mp, count // 2)], None, 3)
    y_parts, spectrum = conv_forward(w_parts, lengths, product(hidden, f_out) * decay, tables)
    (y_back,) = exchange([y_parts], None, 4)
    return (
        w_parts, y_back, spectrum, hidden, phase, decay, gain_rows, chan_rows, z, s[0][:count], s[1], s[2], w_own,
        a, n1, jnp.broadcast_to(inv1, (inv1.shape[0], 128)), w_in, w_out, up, down,
    )


def per_device(
    tokens, cotangent, doc_lengths, in_weight, out_weight, up_weight, down_weight, gains, channel_weight,
    filter_in, filter_out, in_rows, in_cols, out_rows, out_cols, up_rows, up_cols, down_rows, down_cols,
    gain_moment, channel_moment, filter_in_moment, filter_out_moment,
):
    dp, mp = lax.axis_size("dp"), lax.axis_size("mp")
    m = lax.axis_index("mp")
    count, width = tokens.shape
    length = count * mp
    own = channel_weight.shape[1]
    rows = in_weight.shape[0]
    hidden = up_weight.shape[1]
    taps = (channel_weight.shape[0] - 1) // 3
    most = length // 2

    first_shard = jnp.concatenate([in_weight.reshape(rows, 3 * own), out_weight], axis=1)
    chunks = [v.astype(BF) for v in (first_shard, up_weight, down_weight)]
    lanes = 128
    gain_block = jnp.pad(gains.T.astype(BF), ((0, 14), (0, lanes - rows)))
    chan_block = jnp.pad(channel_weight, ((0, 16 - channel_weight.shape[0]), (0, 0)))
    edges = jnp.stack([tokens[count - EDGE :], tokens[:EDGE]])
    table, step = features(length, filter_in.shape[0], most)
    tables = tuple(jnp.asarray(t) for t in transform_tables(count // 2))
    run = mixer_forward if dp == 8 else forward_fallback
    (
        w_parts, y_back, spectrum, hidden_filter, phase, decay, gain_rows, chan_rows, z, s0, s1, s2, w_own,
        a, n1, inv1, w_in, w_out, whole_up, whole_down,
    ) = run(
        doc_lengths, tokens, chunks, gain_block, chan_block, edges, taps, table, step[:, None], filter_in, filter_out,
        tables,
    )
    skip_gain = chan_rows[3 * taps : 3 * taps + 1]
    whole_up = whole_up.reshape(mp, width, hidden)
    whole_down = whole_down.reshape(mp, width, hidden)

    position = m * count - EDGE + jnp.arange(count + 2 * EDGE, dtype=jnp.int32)
    doc = jnp.sum((position[:, None] >= jnp.cumsum(doc_lengths[0])[None, :]).astype(jnp.int32), axis=1)
    doc = jnp.where(position < 0, -1, doc)

    activations, up_part, down_part, out_part, gy_parts, g_y, g_s0, g_x2, feed_sums = feed(
        y_back, w_own, s0, tokens, cotangent, w_out, gain_rows[1:2], skip_gain, whole_up, whole_down
    )

    up_part, down_part = [p.reshape(mp, dp, rows, hidden) for p in (up_part, down_part)]
    gw_back, gw_edge, g_s0_edge, g_filters, up_total, down_partial = mixer_backward(
        gy_parts, g_s0[:EDGE].astype(BF), w_parts, doc_lengths, spectrum, channel_weight[-1:], tables,
        up_part, down_part,
    )
    first_part, input_grad, post_sums = post(
        gw_back, gw_edge, g_y, g_s0, g_s0_edge, s1, s2, z, a, n1, inv1, g_x2, w_in, chan_rows[: 3 * taps],
        skip_gain, gain_rows[0:1], doc[:, None], out_part,
    )

    g_raw = g_filters * decay
    fout_part = product(hidden_filter.T, g_raw)
    fin_part = product(table.T, product(g_raw, filter_out.T) * jnp.cos(phase))

    gain_part = jnp.stack([post_sums[3 * taps], feed_sums[0]]).reshape(2, dp, rows).transpose(1, 0, 2)
    gain_part = jnp.pad(gain_part, ((0, 0), (0, 0), (0, lanes - rows)))
    chan_part = jnp.concatenate([post_sums[: 3 * taps], feed_sums[1:2]])
    chan_part = chan_part.reshape(-1, mp, own).transpose(1, 0, 2)

    def padded(values, fill):
        return jnp.pad(values.T, ((0, 0), (0, lanes - rows)), constant_values=fill)

    first_cols = jnp.concatenate([in_cols.reshape(3 * own), out_cols])
    results = finish(
        first_part.reshape(mp, dp, rows, width), up_total, down_partial,
        [gain_part, chan_part, fin_part, fout_part], (True, True, True, False),
        (first_shard, up_weight, down_weight),
        jnp.stack([in_rows, out_rows, up_rows, down_rows], axis=1),
        jnp.stack([first_cols, up_cols, down_cols]),
        [
            (padded(gains, 0.0), padded(gain_moment, 1.0)),
            (channel_weight, channel_moment),
            (filter_in, filter_in_moment),
            (filter_out, filter_out_moment),
        ],
    )
    norm, c0, c1, c2, n0, n1_, n2_, rows_new, cols_new = results[:9]
    small = results[9:]
    gain_g, gain_n, gain_m = [v[:, :rows].T for v in small[0:3]]

    def parted(values):
        return values[:, : 3 * own].reshape(rows, 3, own), values[:, 3 * own :]

    in_grad, out_grad = parted(c0)
    in_new, out_new = parted(n0)
    return (
        activations, input_grad, norm.reshape(()),
        in_grad, out_grad, c1, c2, gain_g, small[3], small[6], small[9],
        in_new, out_new, n1_, n2_, gain_n, small[4], small[7], small[10],
        rows_new[:, 0], cols_new[0, : 3 * own].reshape(3, own),
        rows_new[:, 1], cols_new[0, 3 * own :],
        rows_new[:, 2], cols_new[1],
        rows_new[:, 3], cols_new[2],
        gain_m, small[5], small[8], small[11],
    )


def solution(mesh):
    tokens, by_rows, by_cols, both = P(("dp", "mp"), None), P("dp", None), P(None, "mp"), P("dp", "mp")
    cube, vec_dp, vec_mp = P("dp", None, "mp"), P("dp"), P("mp")
    moments = (vec_dp, by_cols, vec_dp, vec_mp, vec_dp, vec_mp, vec_dp, vec_mp)
    weights = (cube, both, both, both, by_rows, by_cols, P(), by_cols)
    small = (by_rows, by_cols, P(), by_cols)
    return jax.shard_map(
        per_device,
        mesh=mesh,
        in_specs=(tokens, tokens, by_rows) + weights + moments + small,
        out_specs=(tokens, tokens, P()) + weights + weights + moments + small,
        check_vma=False,
    )
```

```python
import functools
import math

import jax
import jax.numpy as jnp
import ml_dtypes
import numpy as np
from jax import lax
from jax.experimental import pallas as pl
from jax.experimental.pallas import tpu as pltpu
from jax.sharding import PartitionSpec as P

EPS_NORM = 1e-05
MOMENT_DECAY = 0.5
CLIP_NORM = 1.0
CLIP_STEP = 0.25
STEP_RATE = 2.0
FAST_DECAY = 15.35
SLOW_DECAY = 3.07
FULL_PRECISION = lax.Precision.HIGHEST
BF = jnp.bfloat16
F32 = jnp.float32
MESH = pl.DeviceIdType.MESH
BLOCK = 256
EDGE = 16
ROOM = 62 << 20
IN_VMEM = pl.BlockSpec(memory_space=pltpu.VMEM)
IN_HBM = pl.BlockSpec(memory_space=pl.ANY)
IN_SMEM = pl.BlockSpec(memory_space=pltpu.SMEM)


def struct(shape, dtype):
    return jax.ShapeDtypeStruct(tuple(shape), dtype)


def transform_tables(block):
    freq = 2 * np.arange(block)[:, None] + 1
    angle = np.pi * (freq * np.arange(block)[None, :] % (4 * block)) / (2 * block)
    table = np.concatenate([np.cos(angle), -np.sin(angle)], axis=0).astype(np.float32)
    high = table.astype(ml_dtypes.bfloat16)
    low = (table - high.astype(np.float32)).astype(ml_dtypes.bfloat16)
    return high, low, np.ascontiguousarray(high.T), np.ascontiguousarray(low.T)


def mm(left, right):
    return lax.dot_general(left, right, (((1,), (0,)), ((), ())), preferred_element_type=F32)


def split(values):
    high = values.astype(BF)
    return high, (values - high.astype(F32)).astype(BF)


def load_rows(ref, start, count, lead=()):
    odd = lax.rem(start, 8)
    tile = ref[lead + (pl.ds(lax.div(start, 8), count // 8 + 1),)]
    width = tile.shape[-1]
    tile = pltpu.roll(tile, lax.rem(8 - odd, 8), axis=1)
    first = lax.broadcasted_iota(jnp.int32, (count // 8, 8, width), 1) < 8 - odd
    return jnp.where(first, tile[:-1], tile[1:]).reshape(count, width)


def tiles(values):
    return values.reshape(values.shape[0] // 8, 8, values.shape[1])


def unpack(target, source):
    parts, block, width = source.shape
    half, count = width // 2, block // 8
    for part in range(parts):
        for side in range(2):
            values = source[part, :, side * half : (side + 1) * half].astype(F32)
            target[pl.ds((2 * part + side) * count, count)] = tiles(values)


def pair_rows(index, block, size):
    first = pl.multiple_of(index * size, size)
    return pl.ds(first, size), pl.ds(pl.multiple_of(block + first, size), size)


def signs(size, width, scale):
    odd = lax.broadcasted_iota(jnp.int32, (size, width), 0) % 2
    return jnp.where(odd == 0, scale, -scale).astype(F32)


def filter_spectrum(filter_ref, spectrum, raw, tables, block):
    count = raw.shape[0]
    high, low = tables[0][...], tables[1][...]
    for lag in range(count):
        top, rest = split(filter_ref[pl.ds(lag * block, block), :])
        raw[lag] = mm(high, top) + mm(high, rest) + mm(low, top)
    scale = 1.0 / block

    def body(index, carry):
        re_rows, im_rows = pair_rows(index, block, 8)
        sign = signs(8, raw.shape[2], scale)
        for lag in range(count):
            re, im = raw[lag, re_rows, :] * scale, raw[lag, im_rows, :] * scale
            if lag:
                re = re - sign * raw[lag - 1, im_rows, :]
                im = im + sign * raw[lag - 1, re_rows, :]
            spectrum[lag, re_rows, :] = re
            spectrum[lag, im_rows, :] = im
        return carry

    lax.fori_loop(0, block // 8, body, 0)


def slot_blocks(source, target, tables, start, length, block):
    high, low = tables[0][...], tables[1][...]
    for index in range(target.shape[0]):
        values = load_rows(source, start + index * block, block)
        inside = lax.broadcasted_iota(jnp.int32, values.shape, 0) + index * block < length
        values = jnp.where(inside, values, 0.0).astype(BF)
        target[index] = mm(high, values) + mm(low, values)


def inverse(top, rest, tables):
    high, low = tables[2][...], tables[3][...]
    return mm(high, top) + mm(high, rest) + mm(low, top)


def document_starts(len_ref, count):
    starts, at = [], jnp.int32(0)
    for slot in range(count):
        starts.append(at)
        at = at + len_ref[0, slot]
    return starts


def merge_slots(slots, starts, put, total, block, most):
    for index in range(total // block):
        first = index * block
        merged = None
        for slot, start in enumerate(starts):
            at = jnp.clip(first - start, -block, most) + block
            values = load_rows(slots, at, block, (slot,))
            if merged is None:
                merged = values
            else:
                inside = lax.broadcasted_iota(jnp.int32, values.shape, 0) + first >= start
                merged = jnp.where(inside, values, merged)
        put(index, merged)


def forward_products(spectrum, raw, top, rest, block):
    count = raw.shape[0]

    def body(index, carry):
        re_rows, im_rows = pair_rows(index, block, 16)
        hr = [spectrum[i, re_rows, :] for i in range(count)]
        hi = [spectrum[i, im_rows, :] for i in range(count)]
        xr = [raw[i, re_rows, :] for i in range(count)]
        xi = [raw[i, im_rows, :] for i in range(count)]
        for out in range(count):
            re = hr[0] * xr[out] - hi[0] * xi[out]
            im = hr[0] * xi[out] + hi[0] * xr[out]
            for lag in range(1, out + 1):
                re = re + (hr[lag] * xr[out - lag] - hi[lag] * xi[out - lag])
                im = im + (hr[lag] * xi[out - lag] + hi[lag] * xr[out - lag])
            top[out, re_rows, :], rest[out, re_rows, :] = split(re)
            top[out, im_rows, :], rest[out, im_rows, :] = split(im)
        return carry

    lax.fori_loop(0, block // 16, body, 0)


def backward_products(spectrum, grad, raw, total, top, rest, block, first_slot):
    count = raw.shape[0]

    def body(index, carry):
        re_rows, im_rows = pair_rows(index, block, 16)
        gr = [grad[i, re_rows, :] for i in range(count)]
        gi = [grad[i, im_rows, :] for i in range(count)]
        hr = [spectrum[i, re_rows, :] for i in range(count)]
        hi = [spectrum[i, im_rows, :] for i in range(count)]
        for out in range(count):
            re = hr[0] * gr[out] + hi[0] * gi[out]
            im = hr[0] * gi[out] - hi[0] * gr[out]
            for later in range(out + 1, count):
                lag = later - out
                re = re + (hr[lag] * gr[later] + hi[lag] * gi[later])
                im = im + (hr[lag] * gi[later] - hi[lag] * gr[later])
            top[out, re_rows, :], rest[out, re_rows, :] = split(re)
            top[out, im_rows, :], rest[out, im_rows, :] = split(im)
        xr = [raw[i, re_rows, :] for i in range(count)]
        xi = [raw[i, im_rows, :] for i in range(count)]
        for lag in range(count):
            re = im = None
            for at in range(count - lag):
                a = xr[at] * gr[at + lag] + xi[at] * gi[at + lag]
                b = xr[at] * gi[at + lag] - xi[at] * gr[at + lag]
                re = a if re is None else re + a
                im = b if im is None else im + b
            if not first_slot:
                re = re + total[lag, re_rows, :]
                im = im + total[lag, im_rows, :]
            total[lag, re_rows, :] = re
            total[lag, im_rows, :] = im
        return carry

    lax.fori_loop(0, block // 16, body, 0)


def filter_gradient(total, top, rest, tables, out_ref, block):
    count, width = total.shape[0], total.shape[2]
    scale = 1.0 / block

    def body(index, carry):
        re_rows, im_rows = pair_rows(index, block, 16)
        sign = signs(16, width, 1.0)
        for lag in range(count):
            re, im = total[lag, re_rows, :], total[lag, im_rows, :]
            if lag + 1 < count:
                re = re + sign * total[lag + 1, im_rows, :]
                im = im - sign * total[lag + 1, re_rows, :]
            top[lag, re_rows, :], rest[lag, re_rows, :] = split(re * scale)
            top[lag, im_rows, :], rest[lag, im_rows, :] = split(im * scale)
        return carry

    lax.fori_loop(0, block // 16, body, 0)
    for lag in range(count):
        out_ref[pl.ds(lag * block, block), :] = inverse(top[lag], rest[lag], tables)


def conv_forward_kernel(doc_count, len_ref, x_ref, filter_ref, t0, t1, t2, t3, y_ref, spectrum, full, raw, top, rest, slots):
    tables = (t0, t1, t2, t3)
    parts, block, width = x_ref.shape
    half = width // 2
    count = raw.shape[0]
    filter_spectrum(filter_ref, spectrum, raw, tables, block)
    unpack(full, x_ref)
    starts = document_starts(len_ref, doc_count)
    for slot in range(doc_count):
        slot_blocks(full, raw, tables, starts[slot], len_ref[0, slot], block)
        forward_products(spectrum, raw, top, rest, block)
        for out in range(count):
            slots[slot, pl.ds((1 + out) * block // 8, block // 8)] = tiles(inverse(top[out], rest[out], tables))

    def put(index, values):
        y_ref[index // 2, :, pl.ds((index % 2) * half, half)] = values.astype(y_ref.dtype)

    merge_slots(slots, starts, put, 2 * parts * block, block, count * block)


def conv_forward(x, lengths, filters, tables):
    parts, block, width = x.shape
    half, docs = width // 2, lengths.shape[1]
    count = filters.shape[0] // block
    wide = (count, 2 * block, half)
    return pl.pallas_call(
        functools.partial(conv_forward_kernel, docs),
        name="conv_forward",
        out_shape=(struct(x.shape, BF), struct(wide, F32)),
        in_specs=[IN_SMEM] + [IN_VMEM] * 6,
        out_specs=(IN_VMEM, IN_VMEM),
        scratch_shapes=[
            pltpu.VMEM(((2 * parts + count) * block // 8 + 1, 8, half), F32),
            pltpu.VMEM(wide, F32),
            pltpu.VMEM(wide, BF),
            pltpu.VMEM(wide, BF),
            pltpu.VMEM((docs, (count + 2) * block // 8 + 1, 8, half), F32),
        ],
        compiler_params=pltpu.CompilerParams(vmem_limit_bytes=ROOM),
    )(lengths, x, filters, *tables)


def conv_backward_kernel(doc_count, len_ref, g_ref, x_ref, spectrum, skip_ref, t0, t1, t2, t3, gw_ref, edge_ref, gf_ref, g_full, x_full, grad, raw, top, rest, total, slots):
    tables = (t0, t1, t2, t3)
    parts, block, width = x_ref.shape
    half = width // 2
    count = raw.shape[0]
    unpack(g_full, g_ref)
    unpack(x_full, x_ref)
    starts = document_starts(len_ref, doc_count)
    for slot in range(doc_count):
        slot_blocks(g_full, grad, tables, starts[slot], len_ref[0, slot], block)
        slot_blocks(x_full, raw, tables, starts[slot], len_ref[0, slot], block)
        backward_products(spectrum, grad, raw, total, top, rest, block, slot == 0)
        for out in range(count):
            slots[slot, pl.ds((1 + out) * block // 8, block // 8)] = tiles(inverse(top[out], rest[out], tables))
    edge_ref[...] = jnp.zeros(edge_ref.shape, edge_ref.dtype)

    def put(index, values):
        gw_ref[index // 2, :, pl.ds((index % 2) * half, half)] = values.astype(gw_ref.dtype)
        if index % 2 == 0 and index:
            own = g_full[pl.ds(index * block // 8, EDGE // 8)].reshape(EDGE, half) * skip_ref[...]
            edge_ref[index // 2 - 1, :, 0:half] = (values[0:EDGE] + own).astype(edge_ref.dtype)

    merge_slots(slots, starts, put, 2 * parts * block, block, count * block)
    filter_gradient(total, top, rest, tables, gf_ref, block)


def conv_backward(g, x, lengths, spectrum, skip_gain, tables):
    parts, block, width = x.shape
    half, docs, count = width // 2, lengths.shape[1], spectrum.shape[0]
    wide = (count, 2 * block, half)
    rows = pltpu.VMEM(((2 * parts + count) * block // 8 + 1, 8, half), F32)
    return pl.pallas_call(
        functools.partial(conv_backward_kernel, docs),
        name="conv_backward",
        out_shape=(
            struct(x.shape, BF),
            struct((parts, EDGE, -(-half // 128) * 128), BF),
            struct((count * block, half), F32),
        ),
        in_specs=[IN_SMEM] + [IN_VMEM] * 8,
        out_specs=(IN_VMEM,) * 3,
        scratch_shapes=[
            rows,
            rows,
            pltpu.VMEM(wide, F32),
            pltpu.VMEM(wide, F32),
            pltpu.VMEM(wide, BF),
            pltpu.VMEM(wide, BF),
            pltpu.VMEM(wide, F32),
            pltpu.VMEM((docs, (count + 2) * block // 8 + 1, 8, half), F32),
        ],
        compiler_params=pltpu.CompilerParams(vmem_limit_bytes=ROOM),
    )(lengths, g, x, spectrum, skip_gain, *tables)


def turned(value, bit):
    return value + bit - 2 * bit * ((value // bit) % 2)


def send(source, target, send_sem, recv_sem, device):
    copy = pltpu.make_async_remote_copy(
        src_ref=source,
        dst_ref=target,
        send_sem=send_sem,
        recv_sem=recv_sem,
        device_id=device,
        device_id_type=MESH,
    )
    copy.start()
    return copy


def greet(peers):
    barrier = pltpu.get_barrier_semaphore()
    for peer in peers:
        pl.semaphore_signal(barrier, inc=1, device_id=peer, device_id_type=MESH)
    pl.semaphore_wait(barrier, len(peers))


def ring(me, count):
    return [lax.rem(me + step, count) for step in range(1, count)]


def dma(*shape):
    return pltpu.SemaphoreType.DMA(shape)


def gather_fallback(chunks, gains, channel, edges):
    mp = lax.axis_size("mp")
    down = [(i, (i + 1) % mp) for i in range(mp)]
    up = [(i, (i - 1) % mp) for i in range(mp)]
    spread = [lax.all_gather(lax.all_gather(c, "dp"), "mp") for c in chunks]
    return (
        *spread,
        lax.all_gather(gains, "dp"),
        lax.all_gather(channel, "mp"),
        jnp.stack([lax.ppermute(edges[0], "mp", down), lax.ppermute(edges[1], "mp", up)]),
    )


def exchange_kernel(count, has_edge, *refs):
    sources, refs = refs[: count + has_edge], refs[count + has_edge :]
    targets, refs = refs[: count + has_edge], refs[count + has_edge :]
    send_sem, recv_sem, edge_send, edge_recv = refs
    d, m, mp = lax.axis_index("dp"), lax.axis_index("mp"), lax.axis_size("mp")
    greet([(d, e) for e in ring(m, mp)])
    copies = []
    for step, e in reversed(list(enumerate(ring(m, mp)))):
        for i in range(count):
            copies.append(
                send(sources[i].at[e], targets[i].at[m], send_sem.at[i, step], recv_sem.at[i, step], (d, e))
            )
    if has_edge:
        before = lax.rem(m + mp - 1, mp)
        copies.append(send(sources[count], targets[count], edge_send.at[0], edge_recv.at[0], (d, before)))
    for i in range(count):
        targets[i][m] = sources[i][m]
    for copy in copies:
        copy.wait()


def exchange(arrays, edge, collective_id):
    mp, count = lax.axis_size("mp"), len(arrays)
    inputs = list(arrays) + ([] if edge is None else [edge])
    return pl.pallas_call(
        functools.partial(exchange_kernel, count, int(edge is not None)),
        name="exchange_%d" % collective_id,
        out_shape=tuple(struct(a.shape, a.dtype) for a in inputs),
        in_specs=[IN_VMEM] * len(inputs),
        out_specs=(IN_VMEM,) * len(inputs),
        scratch_shapes=[dma(count, mp - 1), dma(count, mp - 1), dma(1), dma(1)],
        compiler_params=pltpu.CompilerParams(
            collective_id=collective_id, has_side_effects=True, vmem_limit_bytes=ROOM
        ),
    )(*inputs)


class Flow:
    def __init__(self, part, refs, lanes=slice(None)):
        self.part, self.lanes = part, lanes
        (self.own, self.from_core, self.from_y2, self.from_x2, self.from_x1, self.from_y1, self.from_z) = refs[:7]
        self.own_sem, self.p_send, self.p_recv, self.z_send, self.z_recv = refs[7:]
        self.d, self.m, self.mp = lax.axis_index("dp"), lax.axis_index("mp"), lax.axis_size("mp")
        self.half = self.mp // 2
        self.y, self.x, self.core = self.d // 4, (self.d // 2) % 2, self.d % 2
        self.pending = []

    def push(self, slot, source, target, bit):
        peer = (turned(self.d, bit), self.m)
        copy = send(source, target, self.p_send.at[slot], self.p_recv.at[slot], peer)
        self.pending.append(copy)
        return copy

    def start(self):
        self.copy = self.push(0, self.part.at[:, :, :, 1 - self.core, :, self.lanes], self.from_core, 1)
        self.local = pltpu.make_async_copy(self.part.at[:, :, :, self.core, :, self.lanes], self.own, self.own_sem.at[0])
        self.local.start()

    def core_stage(self):
        own, half, y, x = self.own, self.half, self.y, self.x
        self.local.wait()
        self.copy.wait_recv()

        def body(i, carry):
            at = (i // 4, (i // 2) % 2, i % 2)
            own[at] = own[at] + self.from_core[at]
            return carry

        lax.fori_loop(0, self.mp * 4, body, 0)
        low, high = pl.ds(0, half), pl.ds(half, self.mp - half)
        self.copies = [
            self.push(1, own.at[low, 1 - y], self.from_y2, 4),
            self.push(2, own.at[high, :, 1 - x], self.from_x2, 2),
        ]

    def second_stage(self):
        own, half, y, x = self.own, self.half, self.y, self.x
        for copy in self.copies:
            copy.wait_recv()

        def body(i, carry):
            a, b = i // 2, i % 2
            own[a, y, b] = own[a, y, b] + self.from_y2[a, b]
            own[half + a, b, x] = own[half + a, b, x] + self.from_x2[a, b]
            return carry

        lax.fori_loop(0, half * 2, body, 0)
        low, high = pl.ds(0, half), pl.ds(half, self.mp - half)
        self.copies = [
            self.push(3, own.at[low, y, 1 - x], self.from_x1, 2),
            self.push(4, own.at[high, 1 - y, x], self.from_y1, 4),
        ]

    def third_stage(self):
        own, half, y, x = self.own, self.half, self.y, self.x
        for copy in self.copies:
            copy.wait_recv()

        def body(a, carry):
            own[a, y, x] = own[a, y, x] + self.from_x1[a]
            own[half + a, y, x] = own[half + a, y, x] + self.from_y1[a]
            return carry

        lax.fori_loop(0, half, body, 0)

    def send_z(self):
        self.copies = [
            send(
                self.own.at[e, self.y, self.x], self.from_z.at[step], self.z_send.at[step], self.z_recv.at[step],
                (self.d, e),
            )
            for step, e in enumerate(ring(self.m, self.mp))
        ]
        self.pending.extend(self.copies)

    def finish(self, out):
        for copy in self.copies:
            copy.wait_recv()
        total = self.own[self.m, self.y, self.x].astype(F32)
        for step in range(self.mp - 1):
            total = total + self.from_z[step].astype(F32)
        out[:, self.lanes] = total

    def drain(self):
        for copy in self.pending:
            copy.wait_send()


FLOW_REFS = 12


def flow_scratch(mp, block, over_z=True):
    half = mp // 2
    leads = ((mp, 2, 2), (mp, 2, 2), (half, 2), (mp - half, 2), (half,), (mp - half,))
    last = (mp - 1,) + block if over_z else (1, 16, 128)
    return [pltpu.VMEM(lead + block, BF) for lead in leads] + [pltpu.VMEM(last, BF)] + [dma(1), dma(5), dma(5), dma(mp - 1), dma(mp - 1)]


class SmallSums:
    def __init__(self, small, outs, wide, refs):
        count = len(small)
        self.small, self.outs, self.wide = small, outs, wide
        self.running, self.from_dp, self.from_mp = [refs[i * count : (i + 1) * count] for i in range(3)]
        self.s_send, self.s_recv = refs[3 * count :]
        self.pending = []

    def start(self, stage):
        bit = (1, 2, 4)[stage]
        d, m = lax.axis_index("dp"), lax.axis_index("mp")
        if stage == 0:
            for i, ref in enumerate(self.small):
                self.running[i][0] = ref[...]
        self.copies = []
        for i in range(len(self.small)):
            at = i * 8 + stage
            self.copies.append(
                send(
                    self.running[i].at[stage], self.from_dp[i].at[stage], self.s_send.at[at], self.s_recv.at[at],
                    (turned(d, bit), m),
                )
            )
        self.pending.extend(self.copies)

    def end(self, stage):
        for i, copy in enumerate(self.copies):
            copy.wait_recv()
            self.running[i][stage + 1] = self.running[i][stage] + self.from_dp[i][stage]

    def start_mp(self):
        d, m, mp = lax.axis_index("dp"), lax.axis_index("mp"), lax.axis_size("mp")
        self.copies = []
        for i, wide in enumerate(self.wide):
            if wide:
                for step, e in enumerate(ring(m, mp)):
                    at = i * 8 + 3 + step
                    self.copies.append(
                        send(
                            self.running[i].at[3], self.from_mp[i].at[m], self.s_send.at[at], self.s_recv.at[at],
                            (d, e),
                        )
                    )
                self.from_mp[i][m] = self.running[i][3]
        self.pending.extend(self.copies)

    def end_mp(self):
        for copy in self.copies:
            copy.wait_recv()
        for i, wide in enumerate(self.wide):
            if wide:
                total = self.from_mp[i][0]
                for e in range(1, lax.axis_size("mp")):
                    total = total + self.from_mp[i][e]
                self.outs[i][...] = total
            else:
                self.outs[i][...] = self.running[i][3]

    def drain(self):
        for copy in self.pending:
            copy.wait_send()


def small_scratch(small, mp):
    scratch = []
    for lead in (4, 3, mp):
        scratch += [pltpu.VMEM((lead,) + s.shape, F32) for s in small]
    return scratch + [dma(8 * len(small)), dma(8 * len(small))]


def scatter_fallback(part):
    over_mp = lax.psum_scatter(part, "mp", scatter_dimension=0)
    return lax.psum_scatter(over_mp, "dp", scatter_dimension=0).astype(F32)


def cored(part):
    return part.reshape((part.shape[0], 2, 2, 2) + part.shape[2:])


class Blocks:
    def __init__(self, pairs, send_sem, recv_sem):
        self.pairs, self.send_sem, self.recv_sem = pairs, send_sem, recv_sem
        self.d, self.m, self.mp = lax.axis_index("dp"), lax.axis_index("mp"), lax.axis_size("mp")

    def start(self):
        self.copies = []
        for step, e in reversed(list(enumerate(ring(self.m, self.mp)))):
            for i, (source, target) in enumerate(self.pairs):
                sems = self.send_sem.at[i, step], self.recv_sem.at[i, step]
                self.copies.append(send(source.at[e], target.at[self.m], *sems, (self.d, e)))
        for source, target in self.pairs:
            target[self.m] = source[self.m]

    def arrive(self):
        for copy in self.copies:
            copy.wait_recv()

    def drain(self):
        for copy in self.copies:
            copy.wait_send()


def stream_zero(offsets, edge, gs, z, w, channel, marks, sums, feed_sums):
    count = gs.shape[0] - EDGE
    same = [None] + [marks[k - 1, :, 0:1] > 0.0 for k in range(1, offsets)]
    gs[pl.ds(count, EDGE), :] = edge[...].astype(F32)
    sums[...] = jnp.zeros(sums.shape, F32)
    g_z = short_backward(0, gs, z, channel, same, offsets, count, sums).astype(BF)
    sums[pl.ds(3 * offsets, 1), :] = feed_sums[1:2, :]
    sums[pl.ds(3 * offsets + 2, 1), :] = feed_sums[0:1, :]
    return g_z, dot_nt(g_z, w[...])


def mixer_backward_kernel(doc_count, offsets, len_ref, g_parts, edge, channel_own, feed_sums, part_a, part_b, *refs):
    late_refs, refs = refs[:17], refs[17:]
    gw_back, gw_edge_back, sums, ga0, fin_sum, fout_sum, total_a, partial_b, partial_c, refs = *refs[:9], refs[9:]
    held, refs = refs[:16], refs[16:]
    (
        late_sem, part_c, edge_back, gs, marks, fin_part, fout_part, gf_ref, g_in, gw, gw_edge, g_full, x_full, grad, raw,
        top, rest, total, slots, b_send, b_recv, c_send, c_recv, e_sem, *refs,
    ) = refs
    a_refs, b_refs, c_refs = [refs[i * FLOW_REFS : (i + 1) * FLOW_REFS] for i in range(3)]
    z, acts, w, channel, out_part, x_ref, t0, t1, t2, t3, spectrum, decay, hidden, f_out, phase, table = held
    tables = (t0, t1, t2, t3)
    parts, block, width = x_ref.shape
    half = width // 2
    count = raw.shape[0]
    own_count = ga0.shape[0]
    d, m, mp = lax.axis_index("dp"), lax.axis_index("mp"), lax.axis_size("mp")
    a, b, c = Flow(part_a, a_refs), Flow(part_b, b_refs), Flow(part_c, c_refs)
    smalls = SmallSums((fin_part, fout_part), (fin_sum, fout_sum), (True, False), refs[3 * FLOW_REFS :])
    incoming = Blocks([(g_parts, g_in)], b_send, b_recv)
    outgoing = Blocks([(gw, gw_back), (gw_edge, gw_edge_back)], c_send, c_recv)
    late = Late(late_refs, (gs.at[pl.ds(0, own_count)],) + tuple(held), late_sem)
    greet([(turned(d, bit), m) for bit in (1, 2, 4)] + [(d, e) for e in ring(m, mp)])
    edge_copy = send(edge, edge_back, e_sem.at[0], e_sem.at[1], (d, lax.rem(m + mp - 1, mp)))
    incoming.start()
    a.start()
    b.start()
    mark_same(marks, len_ref, doc_count, m * own_count - EDGE)
    starts = document_starts(len_ref, doc_count)
    a.core_stage()
    late.need(0, 1, 2, 3, 4, 5)
    edge_copy.wait_recv()
    g_z, back = stream_zero(offsets, edge_back, gs, z, w, channel, marks, sums, feed_sums)
    ga0[...] = back
    size = part_c.shape[4]
    for first in range(0, parts, 2):
        in_grad = dot_tn(acts[pl.ds(EDGE, own_count), :], g_z[:, first * half : (first + 2) * half])
        for part in range(first, first + 2):
            cols = slice((part - first) * half, (part - first + 1) * half)
            for owner in range(8):
                at = (part, owner // 4, owner // 2 % 2, owner % 2, slice(None))
                rows = slice(owner * size, (owner + 1) * size)
                part_c[at + (pl.ds(0, half),)] = in_grad[rows, cols].astype(BF)
                part_c[at + (pl.ds(half, half),)] = out_part[part, rows]
    c.start()
    late.need(*range(6, 17))
    unpack(x_full, x_ref)
    incoming.arrive()
    unpack(g_full, g_in)
    for slot in range(doc_count):
        slot_blocks(g_full, grad, tables, starts[slot], len_ref[0, slot], block)
        slot_blocks(x_full, raw, tables, starts[slot], len_ref[0, slot], block)
        if slot == 0:
            a.second_stage()
            b.core_stage()
        backward_products(spectrum, grad, raw, total, top, rest, block, slot == 0)
        for out in range(count):
            slots[slot, pl.ds((1 + out) * block // 8, block // 8)] = tiles(inverse(top[out], rest[out], tables))
        if slot == 1:
            a.third_stage()
            a.send_z()
            c.core_stage()
    gw_edge[...] = jnp.zeros(gw_edge.shape, gw_edge.dtype)

    def put(index, values):
        gw[index // 2, :, pl.ds((index % 2) * half, half)] = values.astype(gw.dtype)
        if index % 2 == 0 and index:
            skip = channel_own[channel_own.shape[0] - 1 :, :]
            own = g_full[pl.ds(index * block // 8, EDGE // 8)].reshape(EDGE, half) * skip
            gw_edge[index // 2 - 1, :, 0:half] = (values[0:EDGE] + own).astype(gw_edge.dtype)

    merge_slots(slots, starts, put, 2 * parts * block, block, count * block)
    outgoing.start()
    b.second_stage()
    filter_gradient(total, top, rest, tables, gf_ref, block)
    g_raw = gf_ref[...] * decay[...]
    fout_part[...] = near_product(hidden[...], g_raw, dot_tn)
    fin_part[...] = near_product(table[...], near_product(g_raw, f_out[...], dot_nt) * jnp.cos(phase[...]), dot_tn)
    smalls.start(0)
    c.second_stage()
    a.finish(total_a)
    smalls.end(0)
    smalls.start(1)
    b.third_stage()
    for e in range(parts):
        partial_b[e] = b.own[e, b.y, b.x]
    smalls.end(1)
    smalls.start(2)
    c.third_stage()
    for e in range(parts):
        partial_c[e] = c.own[e, c.y, c.x]
    smalls.end(2)
    smalls.start_mp()
    outgoing.arrive()
    smalls.end_mp()
    edge_copy.wait_send()
    incoming.drain()
    outgoing.drain()
    for flow in (a, b, c):
        flow.drain()
    smalls.drain()


def mixer_backward(
    lengths, offsets, g_parts, edge, channel_own, feed_sums, part_a, part_b, g_s0, z, a, w_in, channel, out_part, x,
    tables, spectrum, decay, hidden, f_out, phase, table,
):
    dp, mp = lax.axis_size("dp"), lax.axis_size("mp")
    parts, block, width = x.shape
    half, docs, count = width // 2, lengths.shape[1], spectrum.shape[0]
    size = part_a.shape[2]
    full = channel.shape[1]
    if dp != 8:
        (g_in, edge_back) = exchange([g_parts], edge, 5)
        gw, gw_edge, gf = conv_backward(g_in, x, lengths, spectrum, channel_own[-1:], tables)
        g_raw = gf * decay
        fin, fout = product(table.T, product(g_raw, f_out.T) * jnp.cos(phase)), product(hidden.T, g_raw)
        gw_back, gw_edge_back = exchange([gw, gw_edge], None, 6)
        count = g_s0.shape[0]
        gs = jnp.concatenate([g_s0, edge_back.astype(F32)])
        position = lax.axis_index("mp") * count - EDGE + jnp.arange(count + 2 * EDGE, dtype=jnp.int32)
        doc = jnp.sum((position[:, None] >= jnp.cumsum(lengths[0])[None, :]).astype(jnp.int32), axis=1)
        doc = jnp.where(position < 0, -1, doc)
        same = [None] + [(doc[EDGE:] == doc[EDGE - k : doc.shape[0] - k])[:, None] for k in range(1, offsets)]
        g_z, sums = None, jnp.zeros((16, full), F32)
        for k in range(offsets):
            later, before = gs[k : count + k], z[0, EDGE - k : EDGE - k + count]
            if k:
                later, before = jnp.where(same[k][k : count + k], later, 0.0), jnp.where(same[k][:count], before, 0.0)
            g_z = channel[3 * k] * later if g_z is None else g_z + channel[3 * k] * later
            sums = sums.at[3 * k].set(jnp.sum(gs[:count] * before, axis=0))
        sums = sums.at[3 * offsets].set(feed_sums[1]).at[3 * offsets + 2].set(feed_sums[0])
        g_z = g_z.astype(BF)
        grad = dot_tn(a[EDGE : EDGE + count], g_z).reshape(full, mp, half).transpose(1, 0, 2).astype(BF)
        part_c = jnp.concatenate([grad, out_part], axis=2).reshape(mp, dp, size, width)
        over_dp = [lax.psum_scatter(p, "dp", scatter_dimension=1) for p in (part_b, part_c)]
        return (
            gw_back, gw_edge_back, sums, dot_nt(g_z, w_in[0]), lax.psum(fin, ("dp", "mp")), lax.psum(fout, "dp"),
            scatter_fallback(part_a), *over_dp,
        )
    wide = (count, 2 * block, half)
    edge_shape = (parts, EDGE, -(-half // 128) * 128)
    own, own_c = part_a.shape[2:], (size, width)
    rows = pltpu.VMEM(((2 * parts + count) * block // 8 + 1, 8, half), F32)
    first = (g_parts, edge, channel_own, feed_sums)
    late = [
        (g_s0, None), (z, 0), (a, None), (w_in, 0), (channel, None), (out_part, None), (x, None),
        *[(t, None) for t in tables], (spectrum, None), (decay, None), (hidden, None), (f_out, None), (phase, None),
        (table, None),
    ]
    fin, fout = struct((table.shape[1], hidden.shape[1]), F32), struct((hidden.shape[1], half), F32)
    longer = (g_s0.shape[0] + EDGE, full)

    def kernel(*refs):
        start = 3 + len(first)
        chosen = [r if i is None else r.at[i] for r, (_, i) in zip(refs[start : start + len(late)], late)]
        mixer_backward_kernel(docs, offsets, *refs[:start], *chosen, *refs[start + len(late) :])

    return pl.pallas_call(
        kernel,
        name="mixer_backward",
        out_shape=(
            struct(x.shape, BF), struct(edge_shape, BF), struct((16, full), F32), struct(g_s0.shape, F32), fin, fout,
            struct(own, F32), struct((mp,) + own, BF), struct((mp,) + own_c, BF),
        ),
        in_specs=[IN_SMEM] + [IN_VMEM] * len(first) + [IN_HBM] * (2 + len(late)),
        out_specs=(IN_VMEM,) * 9,
        scratch_shapes=[
            *[pltpu.VMEM(v.shape if i is None else v.shape[1:], v.dtype) for v, i in late[1:]],
            dma(len(late)), pltpu.VMEM((mp, 2, 2, 2) + own_c, BF), pltpu.VMEM(edge.shape, BF), pltpu.VMEM(longer, F32),
            pltpu.VMEM((offsets - 1, longer[0], 128), F32), pltpu.VMEM(fin.shape, F32), pltpu.VMEM(fout.shape, F32),
            pltpu.VMEM((count * block, half), F32), pltpu.VMEM(x.shape, BF), pltpu.VMEM(x.shape, BF),
            pltpu.VMEM(edge_shape, BF), rows, rows,
            pltpu.VMEM(wide, F32), pltpu.VMEM(wide, F32), pltpu.VMEM(wide, BF), pltpu.VMEM(wide, BF),
            pltpu.VMEM(wide, F32), pltpu.VMEM((docs, (count + 2) * block // 8 + 1, 8, half), F32),
            dma(1, mp - 1), dma(1, mp - 1), dma(2, mp - 1), dma(2, mp - 1), dma(2),
            *flow_scratch(mp, own), *flow_scratch(mp, own, False), *flow_scratch(mp, own_c, False),
            *small_scratch((fin, fout), mp),
        ],
        compiler_params=pltpu.CompilerParams(collective_id=5, has_side_effects=True, vmem_limit_bytes=ROOM),
    )(lengths, *first, cored(part_a), cored(part_b), *[v for v, _ in late])


def spread_sum(block, slots, send_sem, recv_sem, axis, first):
    d, m = lax.axis_index("dp"), lax.axis_index("mp")
    count = lax.axis_size(axis)
    me = d if axis == "dp" else m
    copies = []
    for step, e in enumerate(ring(me, count)):
        peer = (e, m) if axis == "dp" else (d, e)
        copies.append(send(block, slots.at[me], send_sem.at[first + step], recv_sem.at[first + step], peer))
    slots[me] = block[...]
    for copy in copies:
        copy.wait()
    total = slots[0]
    for e in range(1, count):
        total = total + slots[e]
    return total


def total_of(values):
    return jnp.sum(jnp.sum(values, axis=1, keepdims=True), axis=0, keepdims=True)


def lanes_of(items):
    lane = lax.broadcasted_iota(jnp.int32, (1, 128), 1)
    row = jnp.zeros((1, 128), F32)
    for index, item in enumerate(items):
        row = row + jnp.where(lane == index, item, 0.0)
    return row


def update_body(
    taps, g0, g1, g2, w0, w1, w2, rows, cols, vec_sum, own_gain, gain, gain_mom, chan, chan_mom,
    fin_sum, fin, fin_mom, fout_sum, fout, fout_mom,
    norm_out, c0, c1, c2, n0, n1, n2, rows_out, cols_out, gain_g, gain_n, gain_m,
    chan_g, chan_n, chan_m, fin_g, fin_n, fin_m, fout_g, fout_n, fout_m,
    turn, mp_block, dp_block, mp_slots, dp_slots, last_block, mp_last, dp_last, send_sem, recv_sem,
):
    d, m = lax.axis_index("dp"), lax.axis_index("mp")
    dp, mp = lax.axis_size("dp"), lax.axis_size("mp")
    size, width = g0.shape
    in_width = 3 * (width // 4)
    is_in = lax.broadcasted_iota(jnp.int32, (size, width), 1) < in_width

    def four(v0, v1, v2, reduce_fn):
        return [
            reduce_fn(jnp.where(is_in, v0, 0.0)),
            reduce_fn(jnp.where(is_in, 0.0, v0)),
            reduce_fn(v1),
            reduce_fn(v2),
        ]

    def row_sum(v):
        return jnp.sum(v, axis=1, keepdims=True)

    def col_sum(v):
        return jnp.sum(v, axis=0, keepdims=True)

    s0, s1, s2 = g0[...] * g0[...], g1[...] * g1[...], g2[...] * g2[...]
    lane = lax.broadcasted_iota(jnp.int32, (size, 128), 1)
    row_parts = four(s0, s1, s2, row_sum)
    packed = jnp.zeros((size, 128), F32)
    for index, part in enumerate(row_parts):
        packed = packed + jnp.where(lane == index, part, 0.0)
    turn[...] = jnp.zeros(turn.shape, F32)
    dp_block[...] = jnp.zeros(dp_block.shape, F32)
    turn[pl.ds(0, size), :] = packed
    mp_block[pl.ds(0, 8), :] = jnp.transpose(turn[...])[0:8]
    old = rows[...]
    old_parts = [total_of(old[:, i : i + 1]) / mp for i in range(4)]
    weight_parts = four(w0[...] * w0[...], w1[...] * w1[...], w2[...] * w2[...], total_of)
    scalars = (
        [total_of(p) for p in row_parts]
        + old_parts
        + weight_parts
        + [
            total_of(gain[...] * gain[...]) / mp,
            total_of(chan[...] * chan[...]) / dp,
            total_of(fout[...] * fout[...]) / dp,
            total_of(fout_sum[...] * fout_sum[...]) / dp,
        ]
    )
    mp_block[pl.ds(8, 8), :] = jnp.broadcast_to(lanes_of(scalars), (8, 128))
    over_mp = spread_sum(mp_block, mp_slots, send_sem, recv_sem, "mp", 0)
    pieces = width // 128
    for index, values in enumerate((s0, s1, s2)):
        sums = col_sum(values)
        for piece in range(pieces):
            dp_block[pl.ds(index * pieces + piece, 1), :] = sums[:, piece * 128 : (piece + 1) * 128]
    dp_block[pl.ds(3 * pieces, 1), :] = over_mp[8:9]
    over_dp = spread_sum(dp_block, dp_slots, send_sem, recv_sem, "dp", mp)
    turn[pl.ds(0, 8), :] = over_mp[0:8]
    row_totals = jnp.transpose(turn[...])[0:size]
    shared = over_dp[3 * pieces : 3 * pieces + 1]

    def scalar(index):
        return shared[:, index : index + 1]

    last = 3 * taps + 1
    vec_sq = total_of(vec_sum[0 : last + 2, :] * vec_sum[0 : last + 2, :])
    fin_sq = total_of(fin_sum[...] * fin_sum[...])
    norm = jnp.sqrt(
        scalar(0) + scalar(1) + scalar(2) + scalar(3) + vec_sq + scalar(15) + fin_sq
    )
    norm_out[...] = norm
    clip = 1.0 / jnp.maximum(1.0, norm / CLIP_NORM)
    square = clip * clip
    fresh = 1.0 - MOMENT_DECAY
    all_rows = size * dp
    wide = [in_width * mp, (width - in_width) * mp, width * mp, width * mp]
    ratio = []
    fresh_rows = jnp.zeros((size, 128), F32)
    for index in range(4):
        row_new = (
            MOMENT_DECAY * old[:, index : index + 1]
            + fresh * square * row_totals[:, index : index + 1] / wide[index]
        )
        mean = MOMENT_DECAY * scalar(4 + index) / all_rows + fresh * square * scalar(index) / (
            all_rows * wide[index]
        )
        ratio.append(row_new / mean)
        fresh_rows = fresh_rows + jnp.where(lane == index, row_new, 0.0)
    turn[pl.ds(0, size), :] = fresh_rows
    rows_out[...] = jnp.transpose(turn[...])[0:8]
    for index in range(3):
        for piece in range(pieces):
            at = pl.ds(piece * 128, 128)
            row = index * pieces + piece
            cols_out[pl.ds(index, 1), at] = (
                MOMENT_DECAY * cols[pl.ds(index, 1), at]
                + fresh * square * over_dp[row : row + 1] / all_rows
            )
    first_ratio = jnp.where(is_in, ratio[0], ratio[1])
    steps = []
    for grad, out, factor, index in ((g0, c0, first_ratio, 0), (g1, c1, ratio[2], 1), (g2, c2, ratio[3], 2)):
        clipped = grad[...] * clip
        out[...] = clipped
        steps.append(clipped * lax.rsqrt(factor * cols_out[pl.ds(index, 1), :]))
    u0, u1, u2 = steps

    def plain(clipped, moment, grad_out, moment_out):
        fresh_moment = MOMENT_DECAY * moment + fresh * clipped * clipped
        grad_out[...] = clipped
        moment_out[...] = fresh_moment
        return clipped * lax.rsqrt(fresh_moment)

    picked = vec_sum[last : last + 2, 0:size]
    for e in range(1, dp):
        picked = jnp.where(d == e, vec_sum[last : last + 2, e * size : (e + 1) * size], picked)
    own_gain[...] = jnp.zeros(own_gain.shape, F32)
    own_gain[:, pl.ds(0, size)] = picked
    own = width // mp
    own_chan = vec_sum[0:last, 0:own]
    for e in range(1, mp):
        own_chan = jnp.where(m == e, vec_sum[0:last, e * own : (e + 1) * own], own_chan)
    u_gain = plain(own_gain[...] * clip, gain_mom[...], gain_g, gain_m)
    u_chan = plain(own_chan * clip, chan_mom[...], chan_g, chan_m)
    u_fin = plain(fin_sum[...] * clip, fin_mom[...], fin_g, fin_m)
    u_fout = plain(fout_sum[...] * clip, fout_mom[...], fout_g, fout_m)
    step_parts = four(u0 * u0, u1 * u1, u2 * u2, total_of) + [
        total_of(u_gain * u_gain) / mp,
        total_of(u_chan * u_chan) / dp,
        total_of(u_fout * u_fout) / dp,
    ]
    last_block[...] = jnp.broadcast_to(lanes_of(step_parts), (8, 128))
    half_way = spread_sum(last_block, mp_last, send_sem, recv_sem, "mp", mp + dp)
    mp_block[pl.ds(0, 8), :] = half_way
    step_sums = spread_sum(mp_block.at[pl.ds(0, 8)], dp_last, send_sem, recv_sem, "dp", 2 * mp + dp)[0:1]

    def factors(step_total, weight_total, entries):
        shrink = 1.0 / jnp.maximum(1.0, jnp.sqrt(step_total / entries) / CLIP_STEP)
        return STEP_RATE * jnp.sqrt(weight_total / entries) * shrink

    def step_sum(index):
        return step_sums[:, index : index + 1]

    rate = [factors(step_sum(i), scalar(8 + i), all_rows * wide[i]) for i in range(4)]
    n0[...] = w0[...] - jnp.where(is_in, rate[0], rate[1]) * u0
    n1[...] = w1[...] - rate[2] * u1
    n2[...] = w2[...] - rate[3] * u2
    gain_n[...] = gain[...] - factors(step_sum(4), scalar(12), 2 * all_rows) * u_gain
    chan_n[...] = chan[...] - factors(step_sum(5), scalar(13), chan.shape[0] * chan.shape[1] * mp) * u_chan
    fout_n[...] = fout[...] - factors(step_sum(6), scalar(14), fout.shape[0] * fout.shape[1] * mp) * u_fout
    fin_count = fin.shape[0] * fin.shape[1]
    fin_rate = factors(total_of(u_fin * u_fin), total_of(fin[...] * fin[...]), fin_count)
    fin_n[...] = fin[...] - fin_rate * u_fin


def greet_all():
    d, m = lax.axis_index("dp"), lax.axis_index("mp")
    greet([(e, m) for e in ring(d, lax.axis_size("dp"))] + [(d, e) for e in ring(m, lax.axis_size("mp"))])


def prepare(raw, ready, turn):
    in_w, out_w, in_rows, out_rows, up_rows, down_rows, in_cols, out_cols, up_cols, down_cols, gain_own, gain_mom_own = raw
    w0, rows, cols, gain, gain_mom = ready
    size, own = out_w.shape
    for j in range(3):
        w0[:, pl.ds(j * own, own)] = in_w[j]
        cols[0:1, pl.ds(j * own, own)] = in_cols[j : j + 1, :]
    w0[:, pl.ds(3 * own, own)] = out_w[...]
    cols[0:1, pl.ds(3 * own, own)] = out_cols[...].reshape(1, own)
    cols[1:2, :] = up_cols[...].reshape(1, -1)
    cols[2:3, :] = down_cols[...].reshape(1, -1)
    turn[...] = jnp.zeros(turn.shape, F32)
    for index, source in enumerate((in_rows, out_rows, up_rows, down_rows)):
        turn[pl.ds(index, 1), pl.ds(0, size)] = source[...].reshape(1, size)
    rows[...] = jnp.transpose(turn[...])[0:size]
    for source, target, fill in ((gain_own, gain, 0.0), (gain_mom_own, gain_mom, 1.0)):
        target[...] = jnp.full(target.shape, fill, F32)
        target[:, pl.ds(0, size)] = source[...]


def prepare_scratch(size, width):
    return [
        pltpu.VMEM((size, width), F32), pltpu.VMEM((size, 128), F32), pltpu.VMEM((8, width), F32),
        pltpu.VMEM((2, 128), F32), pltpu.VMEM((2, 128), F32),
    ]


OUTS = 21


def run_update(taps, grads, sums, w1, w2, ready, own_gain, old, outs, work):
    w0, rows, cols, gain, gain_mom = ready
    chan, chan_mom, fin, fin_mom, fout, fout_mom = old
    update_body(
        taps, *grads, w0, w1, w2, rows, cols, sums[0], own_gain, gain, gain_mom, chan, chan_mom,
        sums[1], fin, fin_mom, sums[2], fout, fout_mom, *outs, *work,
    )


def update_kernel(taps, *refs):
    grads, sums, refs = refs[:3], refs[3:6], refs[6:]
    raw, w1, w2, old, refs = refs[:12], refs[12], refs[13], refs[14:20], refs[20:]
    outs, ready, own_gain, work = refs[:OUTS], refs[OUTS : OUTS + 5], refs[OUTS + 5], refs[OUTS + 6 :]
    prepare(raw, ready, work[0])
    greet_all()
    run_update(taps, grads, sums, w1, w2, ready, own_gain, old, outs, work)


def place_first(g0, zero_and_out, one_and_two):
    own = g0.shape[1] // 4
    g0[:, pl.ds(0, own)] = zero_and_out[:, 0:own]
    g0[:, pl.ds(own, 2 * own)] = one_and_two
    g0[:, pl.ds(3 * own, own)] = zero_and_out[:, own : 2 * own]


def finish_kernel(taps, flow_count, part, total_up, partial_down, partial_c, vec, fin_sum, fout_sum, *refs):
    raw, w1, w2, old, refs = refs[:12], refs[12], refs[13], refs[14:20], refs[20:]
    outs, ready, own_gain, refs = refs[:OUTS], refs[OUTS : OUTS + 5], refs[OUTS + 5], refs[OUTS + 6 :]
    g0, g2, g_late, vec_sum, refs = refs[0], refs[1], refs[2], refs[3], refs[4:]
    work, refs = refs[:10], refs[10:]
    from_z, from_zc, z_send, z_recv, refs = refs[0], refs[1], refs[2], refs[3], refs[4:]
    d, m, mp = lax.axis_index("dp"), lax.axis_index("mp"), lax.axis_size("mp")
    lanes = g_late.shape[1] // flow_count
    flows = []
    for i in range(flow_count):
        flows.append(Flow(part, refs[i * FLOW_REFS : (i + 1) * FLOW_REFS], pl.ds(i * lanes, lanes)))
    sums = SmallSums((vec,), (vec_sum,), (True,), refs[flow_count * FLOW_REFS :])
    greet_all()
    for flow in flows:
        flow.start()
    sums.start(0)
    over_z = [
        send(source.at[e], target.at[step], z_send.at[i, step], z_recv.at[i, step], (d, e))
        for i, (source, target) in enumerate(((partial_down, from_z), (partial_c, from_zc)))
        for step, e in enumerate(ring(m, mp))
    ]
    prepare(raw, ready, work[0])
    for flow in flows:
        flow.core_stage()
    sums.end(0)
    sums.start(1)
    for flow in flows:
        flow.second_stage()
    sums.end(1)
    sums.start(2)
    for flow in flows:
        flow.third_stage()
        flow.send_z()
    sums.end(2)
    sums.start_mp()
    for copy in over_z:
        copy.wait()

    def z_total(partial, arrived):
        total = partial[m].astype(F32)
        for step in range(mp - 1):
            total = total + arrived[step].astype(F32)
        return total

    g2[...] = z_total(partial_down, from_z)
    zero_and_out = z_total(partial_c, from_zc)
    sums.end_mp()
    for flow in flows:
        flow.finish(g_late)
    place_first(g0, zero_and_out, g_late[...])
    for flow in flows:
        flow.drain()
    sums.drain()
    run_update(taps, (g0, total_up, g2), (vec_sum, fin_sum, fout_sum), w1, w2, ready, own_gain, old, outs, work)


def update_scratch(dp, mp, width):
    pieces = 3 * width // 128 + 1
    tall = -(-pieces // 8) * 8
    sems = 2 * (dp + mp)
    return [
        pltpu.VMEM((128, 128), F32),
        pltpu.VMEM((16, 128), F32),
        pltpu.VMEM((tall, 128), F32),
        pltpu.VMEM((mp, 16, 128), F32),
        pltpu.VMEM((dp, tall, 128), F32),
        pltpu.VMEM((8, 128), F32),
        pltpu.VMEM((mp, 8, 128), F32),
        pltpu.VMEM((dp, 8, 128), F32),
        dma(sems),
        dma(sems),
    ]


def hand_out_kernel(*refs):
    norm, c0, c1, c2, n0, n1, n2, rows, cols, gain_g, gain_n, gain_m, *small = refs[:OUTS]
    (
        norm_out, in_g, out_g, up_g, down_g, gain_g_out, in_n, out_n, up_n, down_n, gain_n_out, gain_m_out,
        in_r, out_r, up_r, down_r, in_c, out_c, up_c, down_c, *small_out,
    ) = refs[OUTS:]
    size, own = out_g.shape
    norm_out[...] = norm[...]
    for source, first, last in ((c0, in_g, out_g), (n0, in_n, out_n)):
        for j in range(3):
            first[j] = source[:, j * own : (j + 1) * own]
        last[...] = source[:, 3 * own : 4 * own]
    for source, target in ((c1, up_g), (c2, down_g), (n1, up_n), (n2, down_n)):
        target[...] = source[...]
    for source, target in ((gain_g, gain_g_out), (gain_n, gain_n_out), (gain_m, gain_m_out)):
        target[...] = source[:, 0:size]
    for index, target in enumerate((in_r, out_r, up_r, down_r)):
        target[...] = rows[index : index + 1, 0:size].reshape(size)
    for j in range(3):
        in_c[j : j + 1, :] = cols[0:1, j * own : (j + 1) * own]
    out_c[...] = cols[0:1, 3 * own : 4 * own].reshape(own)
    up_c[...] = cols[1:2, :].reshape(-1)
    down_c[...] = cols[2:3, :].reshape(-1)
    for source, target in zip(small, small_out):
        target[...] = source[...]


def hand_out(results, own):
    size, width = results[1].shape
    cube, part, full = (3, size, own), (size, own), (size, width)
    column, row, wide = (2, size), (size,), (width,)
    shapes = [(1, 1), cube, part, full, full, column, cube, part, full, full, column, column, row, row, row, row]
    shapes += [(3, own), (own,), wide, wide] + [v.shape for v in results[12:]]
    return pl.pallas_call(
        hand_out_kernel,
        name="hand_out",
        out_shape=tuple(struct(s, F32) for s in shapes),
        in_specs=[IN_VMEM] * len(results),
        out_specs=(IN_VMEM,) * len(shapes),
        compiler_params=pltpu.CompilerParams(vmem_limit_bytes=ROOM),
    )(*results)


FLOWS = 3


def finish(part, total_up, partial_down, partial_c, taps, vec, fin_sum, fout_sum, raw, w1, w2, old):
    dp, mp = lax.axis_size("dp"), lax.axis_size("mp")
    size, own = raw[1].shape
    width = w1.shape[1]
    big = struct((size, width), F32)
    flat = [(2, 128), old[0].shape, old[2].shape, old[4].shape]
    outs = [struct((1, 1), F32)] + [big] * 6 + [struct((8, 128), F32), struct((3, width), F32)]
    outs += [struct(s, F32) for s in flat for _ in range(3)]
    params = pltpu.CompilerParams(collective_id=2, has_side_effects=True, vmem_limit_bytes=ROOM)
    tail = [*raw, w1, w2, *old]
    own_gain = pltpu.VMEM((2, 128), F32)
    if dp != 8:
        over_mp = [lax.psum_scatter(p, "mp").astype(F32) for p in (partial_down, partial_c)]
        first = jnp.concatenate([over_mp[1][:, :own], scatter_fallback(part), over_mp[1][:, own:]], axis=1)
        inputs = [first, total_up, over_mp[0], lax.psum(vec, ("dp", "mp")), fin_sum, fout_sum, *tail]
        return pl.pallas_call(
            functools.partial(update_kernel, taps),
            name="clip_and_update",
            out_shape=tuple(outs),
            in_specs=[IN_VMEM] * len(inputs),
            out_specs=(IN_VMEM,) * len(outs),
            scratch_shapes=prepare_scratch(size, width) + [own_gain] + update_scratch(dp, mp, width),
            compiler_params=params,
        )(*inputs)
    inputs = [total_up, partial_down, partial_c, vec, fin_sum, fout_sum, *tail]
    late = part.shape[3]
    block = (size, late // FLOWS)
    flows = []
    for _ in range(FLOWS):
        flows += flow_scratch(mp, block)
    return pl.pallas_call(
        functools.partial(finish_kernel, taps, FLOWS),
        name="sum_clip_update",
        out_shape=tuple(outs),
        in_specs=[IN_HBM] + [IN_VMEM] * len(inputs),
        out_specs=(IN_VMEM,) * len(outs),
        scratch_shapes=[
            *prepare_scratch(size, width),
            own_gain,
            pltpu.VMEM((size, width), F32),
            pltpu.VMEM((size, width), F32),
            pltpu.VMEM((size, late), F32),
            pltpu.VMEM(vec.shape, F32),
            *update_scratch(dp, mp, width),
            pltpu.VMEM((mp - 1, size, width), BF),
            pltpu.VMEM((mp - 1,) + partial_c.shape[1:], BF),
            dma(2, mp - 1),
            dma(2, mp - 1),
            *flows,
            *small_scratch((vec,), mp),
        ],
        compiler_params=params,
    )(cored(part), *inputs)


class Spread:
    def __init__(self, own, whole, lanes, refs):
        self.whole, self.lanes = whole, lanes
        self.source = own.at[:, lanes]
        self.own_sem, self.z_send, self.z_recv, self.p_send, self.p_recv = refs
        self.d, self.m, self.mp = lax.axis_index("dp"), lax.axis_index("mp"), lax.axis_size("mp")
        d = self.d
        self.dx, self.dy, self.dc = turned(d, 2), turned(d, 4), turned(d, 1)
        half = self.mp // 2
        self.low, self.high, self.all = pl.ds(0, half), pl.ds(half, self.mp - half), pl.ds(0, self.mp)

    def start(self):
        target = self.whole.at[self.m, self.d, :, self.lanes]
        self.copy = pltpu.make_async_copy(self.source, target, self.own_sem.at[0])
        self.copy.start()
        self.z = [
            send(self.source, target, self.z_send.at[step], self.z_recv.at[step], (self.d, e))
            for step, e in enumerate(ring(self.m, self.mp))
        ]

    def push(self, slot, rows, owner, peer):
        block = self.whole.at[rows, owner, :, self.lanes]
        return send(block, block, self.p_send.at[slot], self.p_recv.at[slot], (peer, self.m))

    def stage_one(self):
        self.copy.wait()
        for copy in self.z:
            copy.wait_recv()
        d, dx, dy = self.d, self.dx, self.dy
        self.first = [self.push(0, self.low, d, dx), self.push(1, self.high, d, dy)]
        self.last = [self.push(2, self.all, d, self.dc)]

    def stage_two(self):
        for copy in self.first:
            copy.wait_recv()
        d, dx, dy = self.d, self.dx, self.dy
        self.second = [
            self.push(3, self.low, d, dy),
            self.push(4, self.high, d, dx),
            self.push(5, self.low, dx, dy),
            self.push(6, self.high, dy, dx),
        ]

    def stage_three(self):
        for copy in self.second:
            copy.wait_recv()
        for slot, owner in enumerate((self.dx, self.dy, turned(self.dx, 4))):
            self.last.append(self.push(7 + slot, self.all, owner, self.dc))

    def arrive(self):
        for copy in self.last:
            copy.wait_recv()

    def drain(self):
        for copy in self.z + self.first + self.second + self.last:
            copy.wait_send()


SPREAD_REFS = 5


def spread_scratch(mp):
    return [dma(1), dma(mp - 1), dma(mp - 1), dma(10), dma(10)]


def mark_same(same, len_ref, doc_count, first):
    tail = same.shape[1]
    position = lax.broadcasted_iota(jnp.int32, (tail + EDGE, 128), 0) + first
    doc = jnp.zeros(position.shape, jnp.int32)
    end = jnp.int32(0)
    for slot in range(doc_count):
        end = end + len_ref[0, slot]
        doc = doc + (position >= end).astype(jnp.int32)
    doc = jnp.where(position < 0, -1, doc)
    for k in range(1, same.shape[0] + 1):
        same[k - 1] = jnp.where(doc[EDGE:] == doc[EDGE - k : EDGE - k + tail], 1.0, 0.0)


def near_product(left, right, dot=mm):
    l_top, l_rest = split(left)
    r_top, r_rest = split(right)
    return dot(l_top, r_top) + dot(l_top, r_rest) + dot(l_rest, r_top)


def mixer_forward_kernel(
    doc_count, taps, len_ref, tok, in_w, out_w, up_w, down_w, gains_own, channel_own, table, step_col, f_in, f_out,
    t0, t1, t2, t3,
    w_parts, y_back, spectrum, hidden, phase, decay, gain_rows, chan_rows,
    z_out, s0_out, s1_out, s2_out, w_out_own, a_out, n1_out, inv1_out, w_in_out, w_out_out, whole_up, whole_down,
    chunk_first, chunk_up, chunk_down, gains, channel, turn, whole_first, gains_all, channel_all, edges_all, filters, w_send, y_parts, full, raw, top, rest, slots,
    ext, n1, inv1, a, z, s0, s1, s2, w_own, w_in, w_out, same,
    s_send, s_recv, save_sem, b_send, b_recv, c_send, c_recv, *spread_refs,
):
    tables = (t0, t1, t2, t3)
    d, m = lax.axis_index("dp"), lax.axis_index("mp")
    dp, mp = lax.axis_size("dp"), lax.axis_size("mp")
    count, width = tok.shape
    rows = chunk_first.shape[0]
    own = width // mp
    block = count // 2
    blocks = raw.shape[0]

    for j in range(3):
        chunk_first[:, pl.ds(j * own, own)] = in_w[j].astype(BF)
    chunk_first[:, pl.ds(3 * own, own)] = out_w[...].astype(BF)
    chunk_up[...] = up_w[...].astype(BF)
    chunk_down[...] = down_w[...].astype(BF)
    turn[...] = jnp.zeros(turn.shape, F32)
    turn[pl.ds(0, 2), pl.ds(0, rows)] = gains_own[...]
    gains[...] = turn[...].astype(BF)
    channel[...] = jnp.zeros(channel.shape, F32)
    channel[pl.ds(0, channel_own.shape[0]), :] = channel_own[...]
    greet_all()

    small = []
    for step, e in enumerate(ring(d, dp)):
        small.append(send(gains, gains_all.at[d], s_send.at[step], s_recv.at[step], (e, m)))
    for step, e in enumerate(ring(m, mp)):
        at = dp + step
        small.append(send(channel, channel_all.at[m], s_send.at[at], s_recv.at[at], (d, e)))
    at = dp + mp
    for index, first, peer in ((0, count - EDGE, lax.rem(m + 1, mp)), (1, 0, lax.rem(m + mp - 1, mp))):
        sems = s_send.at[at + index], s_recv.at[at + index]
        small.append(send(tok.at[pl.ds(first, EDGE)], edges_all.at[index], *sems, (d, peer)))
    gains_all[d] = gains[...]
    channel_all[m] = channel[...]

    half = width // 2
    plan = [
        (chunk_first, whole_first, pl.ds(0, half)),
        (chunk_first, whole_first, pl.ds(half, width - half)),
        (chunk_up, whole_up, pl.ds(0, chunk_up.shape[1])),
        (chunk_down, whole_down, pl.ds(0, chunk_down.shape[1])),
    ]
    flows = [Spread(*p, spread_refs[i * SPREAD_REFS : (i + 1) * SPREAD_REFS]) for i, p in enumerate(plan)]
    left, right, up, down = flows
    for flow in flows:
        flow.start()

    phase[...] = near_product(table[...], f_in[...])
    hidden[...] = jnp.sin(phase[...])
    lane = (m * own + lax.broadcasted_iota(jnp.int32, (1, own), 1)).astype(F32)
    rate = FAST_DECAY + (SLOW_DECAY - FAST_DECAY) * lane / (width - 1)
    decay[...] = jnp.exp(-step_col[...] * rate)
    filters[...] = near_product(hidden[...], f_out[...]) * decay[...]
    filter_spectrum(filters, spectrum, raw, tables, block)

    mark_same(same, len_ref, doc_count, m * count - EDGE)

    left.stage_one()
    for copy in small:
        copy.wait()
    for e in range(dp):
        gain_rows[0:2, pl.ds(e * rows, rows)] = gains_all[e, 0:2, 0:rows].astype(F32)
    for e in range(mp):
        chan_rows[:, pl.ds(e * own, own)] = channel_all[e]
    ext[pl.ds(0, EDGE), :] = edges_all[0].astype(F32)
    ext[pl.ds(EDGE, count), :] = tok[...].astype(F32)
    ext[pl.ds(EDGE + count, EDGE), :] = edges_all[1].astype(F32)

    def norm_body(i, carry):
        at = pl.ds(pl.multiple_of(i * 32, 32), 32)
        normed, inverse_std = norm_parts(ext[at, :])
        n1[at, :] = normed
        inv1[at, :] = jnp.broadcast_to(inverse_std, (32, 128))
        a[at, :] = (normed * gain_rows[0:1, :]).astype(BF)
        return carry

    right.stage_one()
    lax.fori_loop(0, ext.shape[0] // 32, norm_body, 0)
    left.stage_two()
    right.stage_two()
    up.stage_one()
    left.stage_three()
    right.stage_three()

    def stream_weights(j):
        for e in range(mp):
            part = whole_first[e, :, :, pl.ds(j * own, own)].reshape(dp * rows, own)
            w_in[:, pl.ds(j * width + e * own, own)] = part

    def project(j):
        cols = pl.ds(j * width, width)
        z[:, cols] = mm(a[...], w_in[:, cols])

    left.arrive()
    stream_weights(0)
    stream_weights(1)
    project(0)
    project(1)
    right.arrive()
    stream_weights(2)
    project(2)
    up.stage_two()
    down.stage_one()

    def short_body(i, carry):
        first = pl.multiple_of(i * 48, 16)
        at = pl.ds(first, 48)
        streams = []
        for j in range(3):
            part = z[pl.ds(first + 8, 56), pl.ds(j * width, width)]
            total = chan_rows[j : j + 1, :] * part[8:56]
            for k in range(1, taps):
                keep = same[k - 1, at, 0:1] > 0.0
                total = total + chan_rows[3 * k + j : 3 * k + j + 1, :] * jnp.where(keep, part[8 - k : 56 - k], 0.0)
            streams.append(total)
        s0[at, :], s1[at, :], s2[at, :] = streams
        w_own[at, :] = streams[2] * streams[1]
        return carry

    lax.fori_loop(0, s0.shape[0] // 48, short_body, 0)
    for part in range(mp):
        for side in range(2):
            values = w_own[pl.ds(side * block, block), pl.ds(part * own, own)]
            w_send[part, :, pl.ds(side * own, own)] = values.astype(BF)
    going = Blocks([(w_send, w_parts)], b_send, b_recv)
    back = Blocks([(y_parts, y_back)], c_send, c_recv)
    going.start()
    saves = []

    def save(source, target):
        copy = pltpu.make_async_copy(source, target, save_sem.at[len(saves)])
        copy.start()
        saves.append(copy)

    own_rows = pl.ds(0, count)
    for source, target in (
        *[(z.at[:, pl.ds(j * width, width)], z_out.at[j]) for j in range(3)], (s0.at[own_rows], s0_out), (s1, s1_out), (s2, s2_out), (w_own.at[own_rows], w_out_own),
        (a, a_out), (n1, n1_out), (inv1, inv1_out),
        *[(w_in.at[:, pl.ds(j * width, width)], w_in_out.at[j]) for j in range(3)],
    ):
        save(source, target)
    for e in range(mp):
        part = whole_first[e, :, :, pl.ds(3 * own, own)].reshape(dp * rows, own)
        w_out[:, pl.ds(e * own, own)] = part
    save(w_out, w_out_out)
    going.arrive()
    down.stage_two()
    up.stage_three()
    unpack(full, w_parts)
    starts = document_starts(len_ref, doc_count)
    for slot in range(doc_count):
        slot_blocks(full, raw, tables, starts[slot], len_ref[0, slot], block)
        forward_products(spectrum, raw, top, rest, block)
        for out in range(blocks):
            slots[slot, pl.ds((1 + out) * block // 8, block // 8)] = tiles(inverse(top[out], rest[out], tables))

    def put(index, values):
        y_parts[index // 2, :, pl.ds((index % 2) * own, own)] = values.astype(BF)

    merge_slots(slots, starts, put, 2 * mp * block, block, blocks * block)
    back.start()
    down.stage_three()
    up.arrive()
    down.arrive()
    back.arrive()
    for copy in saves:
        copy.wait()
    going.drain()
    back.drain()
    for flow in flows:
        flow.drain()


def mixer_forward(lengths, tokens, weights, gains, channel, taps, table, step_col, f_in, f_out, tables):
    mp, dp = lax.axis_size("mp"), lax.axis_size("dp")
    count, width = tokens.shape
    own, block, docs = width // mp, count // 2, lengths.shape[1]
    lags = table.shape[0]
    blocks = lags // block
    wide = (blocks, 2 * block, own)
    rows = weights[1].shape[0]
    shards = [(rows, 4 * own), weights[2].shape, weights[3].shape]
    whole = [(mp, dp) + s for s in shards]
    longer, later = (count + 2 * EDGE, width), (count + EDGE, width)
    parts = (mp, block, 2 * own)
    vmem_outs = [
        (parts, BF), (parts, BF), (wide, F32), ((lags, f_in.shape[1]), F32), ((lags, f_in.shape[1]), F32),
        ((lags, own), F32), ((8, width), F32), ((16, width), F32),
    ]
    hbm_outs = [
        ((3,) + longer, F32), ((count, width), F32), (later, F32), (later, F32), ((count, width), F32),
        (longer, BF), (longer, F32), ((longer[0], 128), F32), ((3, width, width), BF), ((width, width), BF),
        (whole[1], BF), (whole[2], BF),
    ]
    inputs = (lengths, tokens, *weights, gains, channel, table, step_col, f_in, f_out, *tables)
    return pl.pallas_call(
        functools.partial(mixer_forward_kernel, docs, taps),
        name="mixer_forward",
        out_shape=tuple(struct(*o) for o in vmem_outs + hbm_outs),
        in_specs=[IN_SMEM] + [IN_VMEM] * (len(inputs) - 1),
        out_specs=(IN_VMEM,) * len(vmem_outs) + (IN_HBM,) * len(hbm_outs),
        scratch_shapes=[
            *[pltpu.VMEM(s, BF) for s in shards], pltpu.VMEM((16, 128), BF), pltpu.VMEM((16, own), F32),
            pltpu.VMEM((16, 128), F32),
            pltpu.VMEM(whole[0], BF), pltpu.VMEM((dp, 16, 128), BF), pltpu.VMEM((mp, 16, own), F32),
            pltpu.VMEM((2, EDGE, width), BF), pltpu.VMEM((lags, own), F32), pltpu.VMEM(parts, BF), pltpu.VMEM(parts, BF),
            pltpu.VMEM(((2 * mp + blocks) * block // 8 + 1, 8, own), F32), pltpu.VMEM(wide, F32),
            pltpu.VMEM(wide, BF), pltpu.VMEM(wide, BF),
            pltpu.VMEM((docs, (blocks + 2) * block // 8 + 1, 8, own), F32),
            pltpu.VMEM(longer, F32), pltpu.VMEM(longer, F32), pltpu.VMEM((longer[0], 128), F32), pltpu.VMEM(longer, BF),
            pltpu.VMEM((longer[0], 3 * width), F32), pltpu.VMEM(later, F32), pltpu.VMEM(later, F32),
            pltpu.VMEM(later, F32), pltpu.VMEM(later, F32), pltpu.VMEM((width, 3 * width), BF),
            pltpu.VMEM((width, width), BF), pltpu.VMEM((taps - 1, later[0], 128), F32),
            dma(dp + mp + 2), dma(dp + mp + 2), dma(16), dma(1, mp - 1), dma(1, mp - 1), dma(1, mp - 1), dma(1, mp - 1),
            *(spread_scratch(mp) * 4),
        ],
        compiler_params=pltpu.CompilerParams(collective_id=0, has_side_effects=True, vmem_limit_bytes=ROOM),
    )(*inputs)


def dot_nt(left, right):
    return lax.dot_general(left, right, (((1,), (1,)), ((), ())), preferred_element_type=F32)


def dot_tn(left, right):
    return lax.dot_general(left, right, (((0,), (0,)), ((), ())), preferred_element_type=F32)


def gelu_parts(x):
    scale, cubic = math.sqrt(2.0 / math.pi), 0.044715
    square = x * x
    t = jnp.tanh(scale * x * (1.0 + cubic * square))
    half = 0.5 * (1.0 + t)
    slope = half + 0.5 * x * (1.0 - t * t) * (scale * (1.0 + 3.0 * cubic * square))
    return x * half, slope


def feed_kernel(
    skip_row, y_ref, w_ref, s0_ref, tok, cot, w_out, gains, channel, up, down,
    act_out, up_part, down_part, out_part, g_parts, gy_out, gs0_out, gx2_out, sums, edge_out,
    y, o, x2, n2, inv2, b, b_t, cot_t, mix, acc_out, acc_b,
):
    step, steps = pl.program_id(0), pl.num_programs(0)
    parts, block, wide = y_ref.shape
    own = wide // 2
    count = tok.shape[0]
    tile = 128
    gain, skip = gains.at[1:2], channel.at[skip_row : skip_row + 1]

    @pl.when(step == 0)
    def _():
        for part in range(parts):
            for side in range(2):
                y[pl.ds(side * block, block), pl.ds(part * own, own)] = y_ref[
                    part, :, pl.ds(side * own, own)
                ].astype(F32)

        def body(index, carry):
            rows = pl.ds(pl.multiple_of(index * tile, tile), tile)
            values = y[rows, :] + skip[...] * w_ref[rows, :]
            y[rows, :] = values
            mixed = (values * s0_ref[rows, :]).astype(BF)
            o[rows, :] = mixed
            residual = tok[rows, :].astype(F32) + dot_nt(mixed, w_out[...])
            x2[rows, :] = residual
            normed, inverse_std = norm_parts(residual)
            n2[rows, :] = normed
            inv2[rows, :] = jnp.broadcast_to(inverse_std, (tile, 128))
            b[rows, :] = (normed * gain[...]).astype(BF)
            return carry

        lax.fori_loop(0, count // tile, body, 0)
        b_t[...] = b[...].T
        cot_t[...] = cot[...].T
        acc_out[...] = jnp.zeros(acc_out.shape, F32)
        acc_b[...] = jnp.zeros(acc_b.shape, F32)

    up_w, down_w = up[0], down[0]
    value, slope = gelu_parts(mm(b[...], up_w))
    act = value.astype(BF)
    g_hpre = (mm(cot[...], down_w) * slope).astype(BF)
    up_part[0] = mm(b_t[...], g_hpre).astype(BF)
    down_part[0] = mm(cot_t[...], act).astype(BF)
    acc_out[...] += dot_nt(act, down_w)
    acc_b[...] += dot_nt(g_hpre, up_w)

    @pl.when(step == steps - 1)
    def _():
        sums[...] = jnp.zeros(sums.shape, F32)

        def body(index, carry):
            rows = pl.ds(pl.multiple_of(index * tile, tile), tile)
            act_out[rows, :] = (x2[rows, :] + acc_out[rows, :]).astype(BF)
            g_b, normed = acc_b[rows, :], n2[rows, :]
            sums[0:1, :] += jnp.sum(g_b * normed, axis=0, keepdims=True)
            g_x2 = cot[rows, :].astype(F32) + norm_back(g_b, gain[...], normed, inv2[rows, 0:1])
            gx2_out[rows, :] = g_x2
            low = g_x2.astype(BF)
            mix[rows, :] = low
            g_o = mm(low, w_out[...])
            g_y = g_o * s0_ref[rows, :]
            gy_out[rows, :] = g_y
            gs0_out[rows, :] = g_o * y[rows, :]
            sums[1:2, :] += jnp.sum(g_y * w_ref[rows, :], axis=0, keepdims=True)
            return carry

        lax.fori_loop(0, count // tile, body, 0)
        for part in range(parts):
            for side in range(2):
                g_parts[part, :, pl.ds(side * own, own)] = gy_out[
                    pl.ds(side * block, block), pl.ds(part * own, own)
                ].astype(BF)
        edge_out[...] = gs0_out[pl.ds(0, EDGE), :].astype(BF)
        grad = dot_tn(mix[...], o[...])
        for part in range(parts):
            out_part[part] = grad[:, part * own : (part + 1) * own].astype(BF)


def feed(y_parts, w_own, s0, tokens, cotangent, w_out, gains, channel, skip_row, whole_up, whole_down):
    mp, width, hidden = whole_up.shape
    count = tokens.shape[0]
    own, cols = width // mp, 256
    each = hidden // cols
    once = pl.Buffered(1)

    def fixed(shape):
        return pl.BlockSpec(shape, lambda i: (0,) * len(shape), pipeline_mode=once)

    def moving():
        return pl.BlockSpec((1, width, cols), lambda i: (i // each, 0, i % each))

    full, half = (count, width), (mp, count // 2, 2 * own)
    outs = [
        (full, BF), (whole_up.shape, BF), (whole_up.shape, BF), ((mp, width, own), BF), (half, BF),
        (full, F32), (full, F32), (full, F32), ((8, width), F32), ((EDGE, width), BF),
    ]
    out_specs = [moving() if i in (1, 2) else fixed(s) for i, (s, _) in enumerate(outs)]
    inputs = (y_parts, w_own, s0, tokens, cotangent, w_out, gains, channel)
    return pl.pallas_call(
        functools.partial(feed_kernel, skip_row),
        name="feed_forward",
        grid=(mp * each,),
        out_shape=tuple(struct(s, t) for s, t in outs),
        in_specs=[fixed(v.shape) for v in inputs] + [moving(), moving()],
        out_specs=tuple(out_specs),
        scratch_shapes=[
            pltpu.VMEM(full, F32), pltpu.VMEM(full, BF), pltpu.VMEM(full, F32), pltpu.VMEM(full, F32),
            pltpu.VMEM((count, 128), F32), pltpu.VMEM(full, BF), pltpu.VMEM((width, count), BF),
            pltpu.VMEM((width, count), BF), pltpu.VMEM(full, BF), pltpu.VMEM(full, F32), pltpu.VMEM(full, F32),
        ],
        compiler_params=pltpu.CompilerParams(vmem_limit_bytes=ROOM),
    )(*inputs, whole_up, whole_down)


class Late:
    def __init__(self, sources, targets, sem):
        self.copies = []
        for i, (source, target) in enumerate(zip(sources, targets)):
            copy = pltpu.make_async_copy(source, target, sem.at[i])
            copy.start()
            self.copies.append(copy)

    def need(self, *indices):
        for i in indices:
            self.copies[i].wait()


def short_backward(j, gs, z, channel, same, offsets, count, sums):
    tap_rows = [channel[3 * k + j : 3 * k + j + 1, :] for k in range(offsets)]
    g_z = None
    for k in range(offsets):
        later = gs[pl.ds(k, count), :]
        before = z[pl.ds(EDGE - k, count), :]
        if k:
            later = jnp.where(same[k][k : count + k], later, 0.0)
            before = jnp.where(same[k][:count], before, 0.0)
        g_z = tap_rows[k] * later if g_z is None else g_z + tap_rows[k] * later
        sums[pl.ds(3 * k + j, 1), :] = jnp.sum(gs[pl.ds(0, count), :] * before, axis=0, keepdims=True)
    return g_z


def post_kernel(
    doc_count, offsets, len_ref, gw_ref, gw_edge, channel, gains, sums_in, *refs,
):
    late_refs, refs = refs[:12], refs[12:]
    first_part, input_grad, sums, refs = refs[0], refs[1], refs[2], refs[3:]
    held, refs = refs[:12], refs[12:]
    late_sem, gw, gs, gz, marks = refs
    gy_ref, s2_ref, z1, a_ref, w1, s1_ref, z2, w2, ga0, n1_ref, inv1_ref, gx2_ref = held
    late = Late(late_refs, held, late_sem)
    parts, block, wide = gw_ref.shape
    own = wide // 2
    count, width = gy_ref.shape
    gain, skip = gains[0:1, :], channel[3 * offsets : 3 * offsets + 1, :]
    for part in range(parts):
        at = pl.ds(part * own, own)
        for side in range(2):
            gw[pl.ds(side * block, block), at] = gw_ref[part, :, pl.ds(side * own, own)].astype(F32)
        gw[pl.ds(count, EDGE), at] = gw_edge[part, :, 0:own].astype(F32)
    mark_same(marks, len_ref, doc_count, lax.axis_index("mp") * count - EDGE)
    same = [None] + [marks[k - 1, :, 0:1] > 0.0 for k in range(1, offsets)]
    sums[...] = sums_in[...]
    late.need(0)
    gw[pl.ds(0, count), :] += skip * gy_ref[...]
    total = None
    for j, other, z, w, order in ((1, s2_ref, z1, w1, (1, 2, 3, 4)), (2, s1_ref, z2, w2, (5, 6, 7))):
        late.need(*order)
        gs[...] = gw[...] * other[...]
        gz[...] = short_backward(j, gs, z, channel, same, offsets, count, sums).astype(BF)
        grad = dot_tn(a_ref[pl.ds(EDGE, count), :], gz[...])
        for part in range(parts):
            first_part[part, :, pl.ds((j - 1) * own, own)] = grad[:, part * own : (part + 1) * own].astype(BF)
        term = dot_nt(gz[...], w[...])
        total = term if total is None else total + term
    late.need(8, 9, 10, 11)
    total = total + ga0[...]
    normed = n1_ref[pl.ds(EDGE, count), :]
    sums[pl.ds(3 * offsets + 1, 1), :] = jnp.sum(total * normed, axis=0, keepdims=True)
    back = norm_back(total, gain, normed, inv1_ref[pl.ds(EDGE, count), 0:1])
    input_grad[...] = (gx2_ref[...] + back).astype(BF)


def post(lengths, offsets, gw_parts, gw_edge, channel, gains, sums_in, g_y, s1, s2, z, a, w_in, ga0, n1, inv1, g_x2):
    mp, block, wide = gw_parts.shape
    count, width = g_y.shape
    first = (gw_parts, gw_edge, channel, gains, sums_in)
    late = [
        (g_y, None), (s2, None), (z, 1), (a, None), (w_in, 1), (s1, None), (z, 2), (w_in, 2), (ga0, None), (n1, None),
        (inv1, None), (g_x2, None),
    ]

    def kernel(*refs):
        start = 1 + len(first)
        chosen = [r if i is None else r.at[i] for r, (_, i) in zip(refs[start : start + len(late)], late)]
        post_kernel(lengths.shape[1], offsets, *refs[:start], *chosen, *refs[start + len(late) :])

    return pl.pallas_call(
        kernel,
        name="mixer_post",
        out_shape=(struct((mp, width, wide), BF), struct((count, width), BF), struct((16, width), F32)),
        in_specs=[IN_SMEM] + [IN_VMEM] * len(first) + [IN_HBM] * len(late),
        out_specs=(IN_VMEM,) * 3,
        scratch_shapes=[
            *[pltpu.VMEM(v.shape if i is None else v.shape[1:], v.dtype) for v, i in late],
            dma(len(late)),
            pltpu.VMEM((count + EDGE, width), F32),
            pltpu.VMEM((count + EDGE, width), F32),
            pltpu.VMEM((count, width), BF),
            pltpu.VMEM((offsets - 1, count + EDGE, 128), F32),
        ],
        compiler_params=pltpu.CompilerParams(vmem_limit_bytes=ROOM),
    )(lengths, *first, *[v for v, _ in late])


def features(length, feature_count, count):
    step = np.arange(count)
    band = np.arange(1, (feature_count - 1) // 2 + 1)
    phase = ((step[:, None] * band[None, :]) % length).astype(np.float32) * np.float32(2.0 * math.pi / length)
    position = (step / length).astype(np.float32)
    table = np.concatenate([position[:, None], np.cos(phase), np.sin(phase)], axis=1)
    return table.astype(np.float32), position


def product(left, right):
    return jnp.dot(left, right, precision=FULL_PRECISION, preferred_element_type=F32)


def norm_parts(values):
    centred = values - jnp.mean(values, axis=-1, keepdims=True)
    inverse_std = lax.rsqrt(jnp.mean(centred * centred, axis=-1, keepdims=True) + EPS_NORM)
    return centred * inverse_std, inverse_std


def norm_back(grad, gain, normed, inverse_std):
    scaled = grad * gain
    mean = jnp.mean(scaled, axis=-1, keepdims=True)
    along = jnp.mean(scaled * normed, axis=-1, keepdims=True)
    return (scaled - mean - normed * along) * inverse_std


def to_parts(values, mp, block):
    own = values.shape[1] // mp
    return values.reshape(2, block, mp, own).transpose(2, 1, 0, 3).reshape(mp, block, 2 * own)


def forward_fallback(lengths, tokens, weights, gain_own, channel_own, taps, table, step_col, f_in, f_out, tables):
    mp, m = lax.axis_size("mp"), lax.axis_index("mp")
    count, width = tokens.shape
    own, shard = width // mp, weights[1].shape[0]
    first_shard = jnp.concatenate([*weights[0], weights[1]], axis=1)
    chunks = [v.astype(BF) for v in (first_shard, weights[2], weights[3])]
    gains = jnp.pad(gain_own.astype(BF), ((0, 14), (0, 128 - shard)))
    channel = jnp.pad(channel_own, ((0, 16 - channel_own.shape[0]), (0, 0)))
    edges = jnp.stack([tokens[count - EDGE :], tokens[:EDGE]])
    first, up, down, gains_all, channel_all, edges_all = gather_fallback(chunks, gains, channel, edges)
    first = first.reshape(mp, width, width)
    w_in = first[:, :, : 3 * own].reshape(mp, width, 3, own).transpose(1, 2, 0, 3).reshape(width, 3 * width)
    w_out = first[:, :, 3 * own :].transpose(1, 0, 2).reshape(width, width)
    gain_rows = gains_all[:, 0:8, :shard].transpose(1, 0, 2).reshape(8, width).astype(F32)
    chan_rows = channel_all.transpose(1, 0, 2).reshape(-1, width)
    position = m * count - EDGE + jnp.arange(count + 2 * EDGE, dtype=jnp.int32)
    doc = jnp.sum((position[:, None] >= jnp.cumsum(lengths[0])[None, :]).astype(jnp.int32), axis=1)
    doc = jnp.where(position < 0, -1, doc)
    n1, inv1 = norm_parts(jnp.concatenate([edges_all[0], tokens, edges_all[1]]).astype(F32))
    a = (n1 * gain_rows[0]).astype(BF)
    z = jnp.dot(a, w_in, preferred_element_type=F32)
    s = []
    for j in range(3):
        stream, total = z[:, j * width : (j + 1) * width], None
        for k in range(taps):
            part = stream[EDGE - k : stream.shape[0] - k]
            if k:
                part = jnp.where((doc[EDGE:] == doc[EDGE - k : doc.shape[0] - k])[:, None], part, 0.0)
            term = chan_rows[3 * k + j] * part
            total = term if total is None else total + term
        s.append(total)
    w_own = s[2][:count] * s[1][:count]
    phase = product(table, f_in)
    hidden = jnp.sin(phase)
    lane = (m * own + jnp.arange(own, dtype=jnp.int32)).astype(F32)
    decay = jnp.exp(-step_col * (FAST_DECAY + (SLOW_DECAY - FAST_DECAY) * lane / (width - 1)))
    (w_parts,) = exchange([to_parts(w_own.astype(BF), mp, count // 2)], None, 3)
    y_parts, spectrum = conv_forward(w_parts, lengths, product(hidden, f_out) * decay, tables)
    (y_back,) = exchange([y_parts], None, 4)
    return (
        w_parts, y_back, spectrum, hidden, phase, decay, gain_rows, chan_rows,
        z.reshape(-1, 3, width).transpose(1, 0, 2), s[0][:count], s[1], s[2], w_own, a, n1,
        jnp.broadcast_to(inv1, (inv1.shape[0], 128)), w_in.reshape(width, 3, width).transpose(1, 0, 2), w_out, up, down,
    )


def per_device(
    tokens, cotangent, doc_lengths, in_weight, out_weight, up_weight, down_weight, gains, channel_weight,
    filter_in, filter_out, in_rows, in_cols, out_rows, out_cols, up_rows, up_cols, down_rows, down_cols,
    gain_moment, channel_moment, filter_in_moment, filter_out_moment,
):
    dp, mp = lax.axis_size("dp"), lax.axis_size("mp")
    count, width = tokens.shape
    length = count * mp
    own = channel_weight.shape[1]
    rows = in_weight.shape[0]
    hidden = up_weight.shape[1]
    taps = (channel_weight.shape[0] - 1) // 3
    most = length // 2

    in_weight, gains, gain_moment = in_weight.transpose(1, 0, 2), gains.T, gain_moment.T

    table, step = features(length, filter_in.shape[0], most)
    tables = tuple(jnp.asarray(t) for t in transform_tables(count // 2))
    run = mixer_forward if dp == 8 else forward_fallback
    (
        w_parts, y_back, spectrum, hidden_filter, phase, decay, gain_rows, chan_rows, z, s0, s1, s2, w_own,
        a, n1, inv1, w_in, w_out, whole_up, whole_down,
    ) = run(
        doc_lengths, tokens, (in_weight, out_weight, up_weight, down_weight), gains, channel_weight, taps,
        table, step[:, None], filter_in, filter_out, tables,
    )
    whole_up = whole_up.reshape(mp, width, hidden)
    whole_down = whole_down.reshape(mp, width, hidden)

    activations, up_part, down_part, out_part, gy_parts, g_y, g_s0, g_x2, feed_sums, g_s0_own = feed(
        y_back, w_own, s0, tokens, cotangent, w_out, gain_rows, chan_rows, 3 * taps, whole_up, whole_down
    )

    up_part, down_part = [p.reshape(mp, dp, rows, hidden) for p in (up_part, down_part)]
    gw_back, gw_edge, sums, g_a0, fin_sum, fout_sum, up_total, down_partial, first_partial = mixer_backward(
        doc_lengths, taps, gy_parts, g_s0_own, channel_weight, feed_sums, up_part, down_part, g_s0, z, a, w_in,
        chan_rows, out_part, w_parts, tables, spectrum, decay, hidden_filter, filter_out, phase, table,
    )
    last_part, input_grad, vec = post(
        doc_lengths, taps, gw_back, gw_edge, chan_rows, gain_rows, sums, g_y, s1, s2, z, a, w_in, g_a0, n1, inv1, g_x2
    )

    results = finish(
        last_part.reshape(mp, dp, rows, 2 * own), up_total, down_partial, first_partial, taps, vec, fin_sum, fout_sum,
        (
            in_weight, out_weight, in_rows, out_rows, up_rows, down_rows,
            in_cols, out_cols, up_cols, down_cols, gains, gain_moment,
        ),
        up_weight, down_weight,
        (channel_weight, channel_moment, filter_in, filter_in_moment, filter_out, filter_out_moment),
    )
    (
        norm, in_g, out_g, up_g, down_g, gain_g, in_n, out_n, up_n, down_n, gain_n, gain_m,
        in_r, out_r, up_r, down_r, in_c, out_c, up_c, down_c,
        chan_g, chan_n, chan_m, fin_g, fin_n, fin_m, fout_g, fout_n, fout_m,
    ) = hand_out(results, own)
    return (
        activations, input_grad, norm.reshape(()),
        in_g.transpose(1, 0, 2), out_g, up_g, down_g, gain_g.T, chan_g, fin_g, fout_g,
        in_n.transpose(1, 0, 2), out_n, up_n, down_n, gain_n.T, chan_n, fin_n, fout_n,
        in_r, in_c, out_r, out_c, up_r, up_c, down_r, down_c, gain_m.T, chan_m, fin_m, fout_m,
    )


def solution(mesh):
    tokens, by_rows, by_cols, both = P(("dp", "mp"), None), P("dp", None), P(None, "mp"), P("dp", "mp")
    cube, vec_dp, vec_mp = P("dp", None, "mp"), P("dp"), P("mp")
    moments = (vec_dp, by_cols, vec_dp, vec_mp, vec_dp, vec_mp, vec_dp, vec_mp)
    weights = (cube, both, both, both, by_rows, by_cols, P(), by_cols)
    small = (by_rows, by_cols, P(), by_cols)
    return jax.shard_map(
        per_device,
        mesh=mesh,
        in_specs=(tokens, tokens, by_rows) + weights + moments + small,
        out_specs=(tokens, tokens, P()) + weights + weights + moments + small,
        check_vma=False,
    )
```

```python
import functools
import math

import jax
import jax.numpy as jnp
import ml_dtypes
import numpy as np
from jax import lax
from jax.experimental import pallas as pl
from jax.experimental.pallas import tpu as pltpu
from jax.sharding import PartitionSpec as P

EPS_NORM = 1e-05
MOMENT_DECAY = 0.5
CLIP_NORM = 1.0
CLIP_STEP = 0.25
STEP_RATE = 2.0
FAST_DECAY = 15.35
SLOW_DECAY = 3.07
FULL_PRECISION = lax.Precision.HIGHEST
BF = jnp.bfloat16
F32 = jnp.float32
MESH = pl.DeviceIdType.MESH
BLOCK = 256
EDGE = 16
HALVES = 2
FOLD = 4
ROOM = 62 << 20
IN_VMEM = pl.BlockSpec(memory_space=pltpu.VMEM)
IN_HBM = pl.BlockSpec(memory_space=pl.ANY)
IN_SMEM = pl.BlockSpec(memory_space=pltpu.SMEM)


def struct(shape, dtype):
    return jax.ShapeDtypeStruct(tuple(shape), dtype)


def transform_tables(block):
    freq = 2 * np.arange(block)[:, None] + 1
    angle = np.pi * (freq * np.arange(block)[None, :] % (4 * block)) / (2 * block)
    table = np.concatenate([np.cos(angle), -np.sin(angle)], axis=0).astype(np.float32)
    high = table.astype(ml_dtypes.bfloat16)
    low = (table - high.astype(np.float32)).astype(ml_dtypes.bfloat16)
    return high, low, np.ascontiguousarray(high.T), np.ascontiguousarray(low.T)


def mm(left, right):
    return lax.dot_general(left, right, (((1,), (0,)), ((), ())), preferred_element_type=F32)


def split(values):
    high = values.astype(BF)
    return high, (values - high.astype(F32)).astype(BF)


def load_rows(ref, start, count, lead=()):
    odd = lax.rem(start, 8)
    tile = ref[lead + (pl.ds(lax.div(start, 8), count // 8 + 1),)]
    width = tile.shape[-1]
    tile = pltpu.roll(tile, lax.rem(8 - odd, 8), axis=1)
    first = lax.broadcasted_iota(jnp.int32, (count // 8, 8, width), 1) < 8 - odd
    return jnp.where(first, tile[:-1], tile[1:]).reshape(count, width)


def tiles(values):
    return values.reshape(values.shape[0] // 8, 8, values.shape[1])


def unpack(target, source):
    parts, rows, width = source.shape
    channels = target.shape[2]
    fold, count = width // channels, rows // 8
    for part in range(parts):
        for piece in range(fold):
            values = source[part, :, piece * channels : (piece + 1) * channels].astype(F32)
            target[pl.ds((part * fold + piece) * count, count)] = tiles(values)


def pack_block(target, index, values):
    rows, channels = target.shape[1], values.shape[1]
    fold, pieces = target.shape[2] // channels, values.shape[0] // rows
    for i in range(pieces):
        part, piece = divmod(index * pieces + i, fold)
        target[part, :, pl.ds(piece * channels, channels)] = values[i * rows : (i + 1) * rows].astype(target.dtype)


def pair_rows(index, block, size):
    first = pl.multiple_of(index * size, size)
    return pl.ds(first, size), pl.ds(pl.multiple_of(block + first, size), size)


def signs(size, width, scale):
    odd = lax.broadcasted_iota(jnp.int32, (size, width), 0) % 2
    return jnp.where(odd == 0, scale, -scale).astype(F32)


def filter_spectrum(filter_ref, lanes, spectrum, raw, tables, block):
    count = raw.shape[0]
    high, low = tables[0][...], tables[1][...]
    for lag in range(count):
        top, rest = split(filter_ref[pl.ds(lag * block, block), lanes])
        raw[lag] = mm(high, top) + mm(high, rest) + mm(low, top)
    scale = 1.0 / block

    def body(index, carry):
        re_rows, im_rows = pair_rows(index, block, 8)
        sign = signs(8, raw.shape[2], scale)
        for lag in range(count):
            re, im = raw[lag, re_rows, :] * scale, raw[lag, im_rows, :] * scale
            if lag:
                re = re - sign * raw[lag - 1, im_rows, :]
                im = im + sign * raw[lag - 1, re_rows, :]
            spectrum[lag, re_rows, :] = re
            spectrum[lag, im_rows, :] = im
        return carry

    lax.fori_loop(0, block // 8, body, 0)


def slot_blocks(source, target, tables, start, length, block):
    high, low = tables[0][...], tables[1][...]
    for index in range(target.shape[0]):
        values = load_rows(source, start + index * block, block)
        inside = lax.broadcasted_iota(jnp.int32, values.shape, 0) + index * block < length
        values = jnp.where(inside, values, 0.0).astype(BF)
        target[index] = mm(high, values) + mm(low, values)


def inverse(top, rest, tables):
    high, low = tables[2][...], tables[3][...]
    return mm(high, top) + mm(high, rest) + mm(low, top)


def document_starts(len_ref, count):
    starts, at = [], jnp.int32(0)
    for slot in range(count):
        starts.append(at)
        at = at + len_ref[0, slot]
    return starts


def merge_slots(slots, starts, put, total, block, most):
    for index in range(total // block):
        first = index * block
        merged = None
        for slot, start in enumerate(starts):
            at = jnp.clip(first - start, -block, most) + block
            values = load_rows(slots, at, block, (slot,))
            if merged is None:
                merged = values
            else:
                inside = lax.broadcasted_iota(jnp.int32, values.shape, 0) + first >= start
                merged = jnp.where(inside, values, merged)
        put(index, merged)


def forward_products(spectrum, raw, top, rest, block):
    count = raw.shape[0]

    def body(index, carry):
        re_rows, im_rows = pair_rows(index, block, 16)
        hr = [spectrum[i, re_rows, :] for i in range(count)]
        hi = [spectrum[i, im_rows, :] for i in range(count)]
        xr = [raw[i, re_rows, :] for i in range(count)]
        xi = [raw[i, im_rows, :] for i in range(count)]
        for out in range(count):
            re = hr[0] * xr[out] - hi[0] * xi[out]
            im = hr[0] * xi[out] + hi[0] * xr[out]
            for lag in range(1, out + 1):
                re = re + (hr[lag] * xr[out - lag] - hi[lag] * xi[out - lag])
                im = im + (hr[lag] * xi[out - lag] + hi[lag] * xr[out - lag])
            top[out, re_rows, :], rest[out, re_rows, :] = split(re)
            top[out, im_rows, :], rest[out, im_rows, :] = split(im)
        return carry

    lax.fori_loop(0, block // 16, body, 0)


def backward_products(spectrum, grad, raw, total, top, rest, block, first_slot):
    count = raw.shape[0]

    def body(index, carry):
        re_rows, im_rows = pair_rows(index, block, 16)
        gr = [grad[i, re_rows, :] for i in range(count)]
        gi = [grad[i, im_rows, :] for i in range(count)]
        hr = [spectrum[i, re_rows, :] for i in range(count)]
        hi = [spectrum[i, im_rows, :] for i in range(count)]
        for out in range(count):
            re = hr[0] * gr[out] + hi[0] * gi[out]
            im = hr[0] * gi[out] - hi[0] * gr[out]
            for later in range(out + 1, count):
                lag = later - out
                re = re + (hr[lag] * gr[later] + hi[lag] * gi[later])
                im = im + (hr[lag] * gi[later] - hi[lag] * gr[later])
            top[out, re_rows, :], rest[out, re_rows, :] = split(re)
            top[out, im_rows, :], rest[out, im_rows, :] = split(im)
        xr = [raw[i, re_rows, :] for i in range(count)]
        xi = [raw[i, im_rows, :] for i in range(count)]
        for lag in range(count):
            re = im = None
            for at in range(count - lag):
                a = xr[at] * gr[at + lag] + xi[at] * gi[at + lag]
                b = xr[at] * gi[at + lag] - xi[at] * gr[at + lag]
                re = a if re is None else re + a
                im = b if im is None else im + b
            if not first_slot:
                re = re + total[lag, re_rows, :]
                im = im + total[lag, im_rows, :]
            total[lag, re_rows, :] = re
            total[lag, im_rows, :] = im
        return carry

    lax.fori_loop(0, block // 16, body, 0)


def filter_gradient(total, top, rest, tables, out_ref, lanes, block):
    count, width = total.shape[0], total.shape[2]
    scale = 1.0 / block

    def body(index, carry):
        re_rows, im_rows = pair_rows(index, block, 16)
        sign = signs(16, width, 1.0)
        for lag in range(count):
            re, im = total[lag, re_rows, :], total[lag, im_rows, :]
            if lag + 1 < count:
                re = re + sign * total[lag + 1, im_rows, :]
                im = im - sign * total[lag + 1, re_rows, :]
            top[lag, re_rows, :], rest[lag, re_rows, :] = split(re * scale)
            top[lag, im_rows, :], rest[lag, im_rows, :] = split(im * scale)
        return carry

    lax.fori_loop(0, block // 16, body, 0)
    for lag in range(count):
        out_ref[pl.ds(lag * block, block), lanes] = inverse(top[lag], rest[lag], tables)


def conv_forward_steps(doc_count, len_ref, x_ref, filters, tables, y_ref, spectrum, full, raw, top, rest, slots, between):
    block, blocks = spectrum.shape[1] // 2, spectrum.shape[0]
    unpack(full, x_ref)
    starts = document_starts(len_ref, doc_count)
    for slot in range(doc_count):
        slot_blocks(full, raw, tables, starts[slot], len_ref[0, slot], block)
        forward_products(spectrum, raw, top, rest, block)
        for out in range(blocks):
            slots[slot, pl.ds((1 + out) * block // 8, block // 8)] = tiles(inverse(top[out], rest[out], tables))
        between(slot)

    def put(index, values):
        pack_block(y_ref, index, values)

    tokens = x_ref.shape[0] * x_ref.shape[1] * x_ref.shape[2] // spectrum.shape[2]
    merge_slots(slots, starts, put, tokens, block, blocks * block)


def conv_backward_steps(
    doc_count, len_ref, g_ref, x_ref, spectrum, skip, tables, gw_ref, edge_ref, gf_ref, lanes,
    g_full, x_full, grad, raw, top, rest, total, slots, between,
):
    block, blocks, channels = spectrum.shape[1] // 2, spectrum.shape[0], spectrum.shape[2]
    unpack(g_full, g_ref)
    unpack(x_full, x_ref)
    starts = document_starts(len_ref, doc_count)
    for slot in range(doc_count):
        slot_blocks(g_full, grad, tables, starts[slot], len_ref[0, slot], block)
        slot_blocks(x_full, raw, tables, starts[slot], len_ref[0, slot], block)
        backward_products(spectrum, grad, raw, total, top, rest, block, slot == 0)
        for out in range(blocks):
            slots[slot, pl.ds((1 + out) * block // 8, block // 8)] = tiles(inverse(top[out], rest[out], tables))
        between(slot)
    edge_ref[...] = jnp.zeros(edge_ref.shape, edge_ref.dtype)
    parts = x_ref.shape[0]
    tokens = parts * x_ref.shape[1] * x_ref.shape[2] // channels
    each = tokens // parts // block

    def put(index, values):
        pack_block(gw_ref, index, values)
        if index % each == 0 and index:
            own = g_full[pl.ds(index * block // 8, EDGE // 8)].reshape(EDGE, channels) * skip
            edge_ref[index // each - 1, :, 0:channels] = (values[0:EDGE] + own).astype(edge_ref.dtype)

    merge_slots(slots, starts, put, tokens, block, blocks * block)
    between(doc_count)
    filter_gradient(total, top, rest, tables, gf_ref, lanes, block)


def conv_scratch(x_shape, blocks, block, channels, docs):
    tokens = math.prod(x_shape) // channels
    wide = (blocks, 2 * block, channels)
    full = pltpu.VMEM(((tokens + blocks * block) // 8 + 1, 8, channels), F32)
    slots = pltpu.VMEM((docs, (blocks + 2) * block // 8 + 1, 8, channels), F32)
    return full, pltpu.VMEM(wide, F32), pltpu.VMEM(wide, BF), slots


def conv_forward_kernel(doc_count, len_ref, x_ref, filter_ref, t0, t1, t2, t3, y_ref, spectrum, full, raw, top, rest, slots):
    tables = (t0, t1, t2, t3)
    filter_spectrum(filter_ref, slice(None), spectrum, raw, tables, spectrum.shape[1] // 2)
    conv_forward_steps(
        doc_count, len_ref, x_ref, filter_ref, tables, y_ref, spectrum, full, raw, top, rest, slots, lambda slot: None
    )


def conv_forward(x, lengths, filters, tables):
    docs, channels, block = lengths.shape[1], filters.shape[1], tables[0].shape[1]
    blocks = filters.shape[0] // block
    full, raw, low, slots = conv_scratch(x.shape, blocks, block, channels, docs)
    return pl.pallas_call(
        functools.partial(conv_forward_kernel, docs),
        name="conv_forward",
        out_shape=(struct(x.shape, BF), struct((blocks, 2 * block, channels), F32)),
        in_specs=[IN_SMEM] + [IN_VMEM] * 6,
        out_specs=(IN_VMEM, IN_VMEM),
        scratch_shapes=[full, raw, low, low, slots],
        compiler_params=pltpu.CompilerParams(vmem_limit_bytes=ROOM),
    )(lengths, x, filters, *tables)


def conv_backward_kernel(doc_count, len_ref, g_ref, x_ref, spectrum, skip_ref, t0, t1, t2, t3, gw_ref, edge_ref, gf_ref, *work):
    conv_backward_steps(
        doc_count, len_ref, g_ref, x_ref, spectrum, skip_ref[...], (t0, t1, t2, t3), gw_ref, edge_ref, gf_ref,
        slice(None), *work, lambda slot: None,
    )


def conv_backward(g, x, lengths, spectrum, skip_gain, tables):
    blocks, block, channels = spectrum.shape[0], spectrum.shape[1] // 2, spectrum.shape[2]
    docs = lengths.shape[1]
    full, raw, low, slots = conv_scratch(x.shape, blocks, block, channels, docs)
    return pl.pallas_call(
        functools.partial(conv_backward_kernel, docs),
        name="conv_backward",
        out_shape=(
            struct(x.shape, BF),
            struct((x.shape[0], EDGE, -(-channels // 128) * 128), BF),
            struct((blocks * block, channels), F32),
        ),
        in_specs=[IN_SMEM] + [IN_VMEM] * 8,
        out_specs=(IN_VMEM,) * 3,
        scratch_shapes=[full, full, raw, raw, low, low, raw, slots],
        compiler_params=pltpu.CompilerParams(vmem_limit_bytes=ROOM),
    )(lengths, g, x, spectrum, skip_gain, *tables)


def turned(value, bit):
    return value + bit - 2 * bit * ((value // bit) % 2)


def send(source, target, send_sem, recv_sem, device):
    copy = pltpu.make_async_remote_copy(
        src_ref=source,
        dst_ref=target,
        send_sem=send_sem,
        recv_sem=recv_sem,
        device_id=device,
        device_id_type=MESH,
    )
    copy.start()
    return copy


def greet(peers):
    barrier = pltpu.get_barrier_semaphore()
    for peer in peers:
        pl.semaphore_signal(barrier, inc=1, device_id=peer, device_id_type=MESH)
    pl.semaphore_wait(barrier, len(peers))


def ring(me, count):
    return [lax.rem(me + step, count) for step in range(1, count)]


def dma(*shape):
    return pltpu.SemaphoreType.DMA(shape)


def gather_fallback(chunks, gains, channel, edges):
    mp = lax.axis_size("mp")
    down = [(i, (i + 1) % mp) for i in range(mp)]
    up = [(i, (i - 1) % mp) for i in range(mp)]
    spread = [lax.all_gather(lax.all_gather(c, "dp"), "mp") for c in chunks]
    return (
        *spread,
        lax.all_gather(gains, "dp"),
        lax.all_gather(channel, "mp"),
        jnp.stack([lax.ppermute(edges[0], "mp", down), lax.ppermute(edges[1], "mp", up)]),
    )


def exchange_kernel(count, has_edge, *refs):
    sources, refs = refs[: count + has_edge], refs[count + has_edge :]
    targets, refs = refs[: count + has_edge], refs[count + has_edge :]
    send_sem, recv_sem, edge_send, edge_recv = refs
    d, m, mp = lax.axis_index("dp"), lax.axis_index("mp"), lax.axis_size("mp")
    greet([(d, e) for e in ring(m, mp)])
    copies = []
    for step, e in reversed(list(enumerate(ring(m, mp)))):
        for i in range(count):
            copies.append(
                send(sources[i].at[e], targets[i].at[m], send_sem.at[i, step], recv_sem.at[i, step], (d, e))
            )
    if has_edge:
        before = lax.rem(m + mp - 1, mp)
        copies.append(send(sources[count], targets[count], edge_send.at[0], edge_recv.at[0], (d, before)))
    for i in range(count):
        targets[i][m] = sources[i][m]
    for copy in copies:
        copy.wait()


def exchange(arrays, edge, collective_id):
    mp, count = lax.axis_size("mp"), len(arrays)
    inputs = list(arrays) + ([] if edge is None else [edge])
    return pl.pallas_call(
        functools.partial(exchange_kernel, count, int(edge is not None)),
        name="exchange_%d" % collective_id,
        out_shape=tuple(struct(a.shape, a.dtype) for a in inputs),
        in_specs=[IN_VMEM] * len(inputs),
        out_specs=(IN_VMEM,) * len(inputs),
        scratch_shapes=[dma(count, mp - 1), dma(count, mp - 1), dma(1), dma(1)],
        compiler_params=pltpu.CompilerParams(
            collective_id=collective_id, has_side_effects=True, vmem_limit_bytes=ROOM
        ),
    )(*inputs)


class Flow:
    def __init__(self, part, refs, lanes=slice(None)):
        self.part, self.lanes = part, lanes
        (self.own, self.from_core, self.from_y2, self.from_x2, self.from_x1, self.from_y1, self.from_z) = refs[:7]
        self.own_sem, self.p_send, self.p_recv, self.z_send, self.z_recv = refs[7:]
        self.d, self.m, self.mp = lax.axis_index("dp"), lax.axis_index("mp"), lax.axis_size("mp")
        self.half = self.mp // 2
        self.y, self.x, self.core = self.d // 4, (self.d // 2) % 2, self.d % 2
        self.pending = []

    def push(self, slot, source, target, bit):
        peer = (turned(self.d, bit), self.m)
        copy = send(source, target, self.p_send.at[slot], self.p_recv.at[slot], peer)
        self.pending.append(copy)
        return copy

    def start(self):
        self.copy = self.push(0, self.part.at[:, :, :, 1 - self.core, :, self.lanes], self.from_core, 1)
        self.local = pltpu.make_async_copy(self.part.at[:, :, :, self.core, :, self.lanes], self.own, self.own_sem.at[0])
        self.local.start()

    def core_stage(self):
        own, half, y, x = self.own, self.half, self.y, self.x
        self.local.wait()
        self.copy.wait_recv()

        def body(i, carry):
            at = (i // 4, (i // 2) % 2, i % 2)
            own[at] = own[at] + self.from_core[at]
            return carry

        lax.fori_loop(0, self.mp * 4, body, 0)
        low, high = pl.ds(0, half), pl.ds(half, self.mp - half)
        self.copies = [
            self.push(1, own.at[low, 1 - y], self.from_y2, 4),
            self.push(2, own.at[high, :, 1 - x], self.from_x2, 2),
        ]

    def second_stage(self):
        own, half, y, x = self.own, self.half, self.y, self.x
        for copy in self.copies:
            copy.wait_recv()

        def body(i, carry):
            a, b = i // 2, i % 2
            own[a, y, b] = own[a, y, b] + self.from_y2[a, b]
            own[half + a, b, x] = own[half + a, b, x] + self.from_x2[a, b]
            return carry

        lax.fori_loop(0, half * 2, body, 0)
        low, high = pl.ds(0, half), pl.ds(half, self.mp - half)
        self.copies = [
            self.push(3, own.at[low, y, 1 - x], self.from_x1, 2),
            self.push(4, own.at[high, 1 - y, x], self.from_y1, 4),
        ]

    def third_stage(self):
        own, half, y, x = self.own, self.half, self.y, self.x
        for copy in self.copies:
            copy.wait_recv()

        def body(a, carry):
            own[a, y, x] = own[a, y, x] + self.from_x1[a]
            own[half + a, y, x] = own[half + a, y, x] + self.from_y1[a]
            return carry

        lax.fori_loop(0, half, body, 0)

    def send_z(self):
        self.copies = [
            send(
                self.own.at[e, self.y, self.x], self.from_z.at[step], self.z_send.at[step], self.z_recv.at[step],
                (self.d, e),
            )
            for step, e in enumerate(ring(self.m, self.mp))
        ]
        self.pending.extend(self.copies)

    def finish(self, out):
        for copy in self.copies:
            copy.wait_recv()
        total = self.own[self.m, self.y, self.x].astype(F32)
        for step in range(self.mp - 1):
            total = total + self.from_z[step].astype(F32)
        out[:, self.lanes] = total

    def drain(self):
        for copy in self.pending:
            copy.wait_send()


FLOW_REFS = 12


def flow_scratch(mp, block, over_z=True):
    half = mp // 2
    leads = ((mp, 2, 2), (mp, 2, 2), (half, 2), (mp - half, 2), (half,), (mp - half,))
    last = (mp - 1,) + block if over_z else (1, 16, 128)
    return [pltpu.VMEM(lead + block, BF) for lead in leads] + [pltpu.VMEM(last, BF)] + [dma(1), dma(5), dma(5), dma(mp - 1), dma(mp - 1)]


class SmallSums:
    def __init__(self, small, outs, wide, refs):
        count = len(small)
        self.small, self.outs, self.wide = small, outs, wide
        self.running, self.from_dp, self.from_mp = [refs[i * count : (i + 1) * count] for i in range(3)]
        self.s_send, self.s_recv = refs[3 * count :]
        self.pending = []

    def start(self, stage):
        bit = (1, 2, 4)[stage]
        d, m = lax.axis_index("dp"), lax.axis_index("mp")
        if stage == 0:
            for i, ref in enumerate(self.small):
                self.running[i][0] = ref[...]
        self.copies = []
        for i in range(len(self.small)):
            at = i * 8 + stage
            self.copies.append(
                send(
                    self.running[i].at[stage], self.from_dp[i].at[stage], self.s_send.at[at], self.s_recv.at[at],
                    (turned(d, bit), m),
                )
            )
        self.pending.extend(self.copies)

    def end(self, stage):
        for i, copy in enumerate(self.copies):
            copy.wait_recv()
            self.running[i][stage + 1] = self.running[i][stage] + self.from_dp[i][stage]

    def start_mp(self):
        d, m, mp = lax.axis_index("dp"), lax.axis_index("mp"), lax.axis_size("mp")
        self.copies = []
        for i, wide in enumerate(self.wide):
            if wide:
                for step, e in enumerate(ring(m, mp)):
                    at = i * 8 + 3 + step
                    self.copies.append(
                        send(
                            self.running[i].at[3], self.from_mp[i].at[m], self.s_send.at[at], self.s_recv.at[at],
                            (d, e),
                        )
                    )
                self.from_mp[i][m] = self.running[i][3]
        self.pending.extend(self.copies)

    def end_mp(self):
        for copy in self.copies:
            copy.wait_recv()
        for i, wide in enumerate(self.wide):
            if wide:
                total = self.from_mp[i][0]
                for e in range(1, lax.axis_size("mp")):
                    total = total + self.from_mp[i][e]
                self.outs[i][...] = total
            else:
                self.outs[i][...] = self.running[i][3]

    def drain(self):
        for copy in self.pending:
            copy.wait_send()


def small_scratch(small, mp):
    scratch = []
    for lead in (4, 3, mp):
        scratch += [pltpu.VMEM((lead,) + s.shape, F32) for s in small]
    return scratch + [dma(8 * len(small)), dma(8 * len(small))]


def scatter_fallback(part):
    over_mp = lax.psum_scatter(part, "mp", scatter_dimension=0)
    return lax.psum_scatter(over_mp, "dp", scatter_dimension=0).astype(F32)


def cored(part):
    return part.reshape((part.shape[0], 2, 2, 2) + part.shape[2:])


class Blocks:
    def __init__(self, pairs, send_sem, recv_sem):
        self.pairs, self.send_sem, self.recv_sem = pairs, send_sem, recv_sem
        self.d, self.m, self.mp = lax.axis_index("dp"), lax.axis_index("mp"), lax.axis_size("mp")

    def start(self):
        self.copies = []
        for step, e in reversed(list(enumerate(ring(self.m, self.mp)))):
            for i, (source, target) in enumerate(self.pairs):
                sems = self.send_sem.at[i, step], self.recv_sem.at[i, step]
                self.copies.append(send(source.at[e], target.at[self.m], *sems, (self.d, e)))
        for source, target in self.pairs:
            target[self.m] = source[self.m]

    def arrive(self):
        for copy in self.copies:
            copy.wait_recv()

    def drain(self):
        for copy in self.copies:
            copy.wait_send()


def stream_zero(offsets, edge, gs, z, w, channel, marks, sums, feed_sums):
    count = gs.shape[0] - EDGE
    same = [None] + [marks[k - 1, :, 0:1] > 0.0 for k in range(1, offsets)]
    gs[pl.ds(count, EDGE), :] = edge[...].astype(F32)
    sums[...] = jnp.zeros(sums.shape, F32)
    g_z = short_backward(0, gs, z, channel, same, offsets, count, sums).astype(BF)
    sums[pl.ds(3 * offsets, 1), :] = feed_sums[1:2, :]
    sums[pl.ds(3 * offsets + 2, 1), :] = feed_sums[0:1, :]
    return g_z, dot_nt(g_z, w[...])


def mixer_backward_kernel(doc_count, offsets, len_ref, g_parts, edge, channel_own, feed_sums, part_a, part_b, *refs):
    late_refs, refs = refs[:17], refs[17:]
    gw_back, gw_edge_back, sums, ga0, fin_part, fout_part, partial_a, partial_b, partial_c, refs = *refs[:9], refs[9:]
    held, refs = refs[:16], refs[16:]
    (
        late_sem, part_c, edge_back, gs, marks, gf_ref, g_in, gw, gw_edge, g_full, x_full, grad, raw,
        top, rest, total, slots, b_send, b_recv, c_send, c_recv, e_sem, *refs,
    ) = refs
    a_refs, b_refs, c_refs = [refs[i * FLOW_REFS : (i + 1) * FLOW_REFS] for i in range(3)]
    z, acts, w, channel, out_part, x_ref, t0, t1, t2, t3, spectrum, decay, hidden, f_out, phase, table = held
    tables = (t0, t1, t2, t3)
    parts = x_ref.shape[1]
    near = raw.shape[2]
    half = near * HALVES
    own_count = ga0.shape[0]
    d, m, mp = lax.axis_index("dp"), lax.axis_index("mp"), lax.axis_size("mp")
    a, b, c = Flow(part_a, a_refs), Flow(part_b, b_refs), Flow(part_c, c_refs)
    incoming, outgoing = [], []
    for side in range(HALVES):
        incoming.append(Blocks([(g_parts.at[side], g_in.at[side])], b_send.at[side], b_recv.at[side]))
        pairs = [(gw.at[side], gw_back.at[side]), (gw_edge.at[side], gw_edge_back.at[side])]
        outgoing.append(Blocks(pairs, c_send.at[side], c_recv.at[side]))
    late = Late(late_refs, (gs.at[pl.ds(0, own_count)],) + tuple(held), late_sem)
    greet([(turned(d, bit), m) for bit in (1, 2, 4)] + [(d, e) for e in ring(m, mp)])
    edge_copy = send(edge, edge_back, e_sem.at[0], e_sem.at[1], (d, lax.rem(m + mp - 1, mp)))
    for copies in incoming:
        copies.start()
    a.start()
    b.start()
    mark_same(marks, len_ref, doc_count, m * own_count - EDGE)
    a.core_stage()
    late.need(0, 1, 2, 3, 4, 5)
    edge_copy.wait_recv()
    g_z, back = stream_zero(offsets, edge_back, gs, z, w, channel, marks, sums, feed_sums)
    ga0[...] = back
    size = part_c.shape[4]
    for first in range(0, parts, 2):
        in_grad = dot_tn(acts[pl.ds(EDGE, own_count), :], g_z[:, first * half : (first + 2) * half])
        for part in range(first, first + 2):
            cols = slice((part - first) * half, (part - first + 1) * half)
            for owner in range(8):
                at = (part, owner // 4, owner // 2 % 2, owner % 2, slice(None))
                rows = slice(owner * size, (owner + 1) * size)
                part_c[at + (pl.ds(0, half),)] = in_grad[rows, cols].astype(BF)
                part_c[at + (pl.ds(half, half),)] = out_part[part, rows]
    c.start()
    late.need(*range(6, 17))
    skip = channel_own[channel_own.shape[0] - 1 :, :]

    def first_side(step):
        if step == 0:
            a.second_stage()
            b.core_stage()
        if step == 2:
            a.third_stage()
            c.core_stage()

    def last_side(step):
        if step == 1:
            b.second_stage()

    for side in range(HALVES):
        incoming[side].arrive()
        between = (first_side, last_side)[side]
        lanes = pl.ds(side * near, near)

        def after(step, side=side, between=between):
            if step == doc_count:
                outgoing[side].start()
            between(step)

        conv_backward_steps(
            doc_count, len_ref, g_in.at[side], x_ref.at[side], spectrum.at[side], skip[:, side * near : (side + 1) * near],
            tables, gw.at[side], gw_edge.at[side], gf_ref, lanes, g_full, x_full, grad, raw, top, rest, total, slots, after,
        )
    g_raw = gf_ref[...] * decay[...]
    fout_part[...] = near_product(hidden[...], g_raw, dot_tn)
    fin_part[...] = near_product(table[...], near_product(g_raw, f_out[...], dot_nt) * jnp.cos(phase[...]), dot_tn)
    c.second_stage()
    for flow, partial in ((a, partial_a), (b, partial_b), (c, partial_c)):
        if flow is not a:
            flow.third_stage()
        for e in range(parts):
            partial[e] = flow.own[e, flow.y, flow.x]
    for copies in outgoing:
        copies.arrive()
    edge_copy.wait_send()
    for copies in incoming + outgoing:
        copies.drain()
    for flow in (a, b, c):
        flow.drain()


def mixer_backward(
    lengths, offsets, g_parts, edge, channel_own, feed_sums, part_a, part_b, g_s0, z, a, w_in, channel, out_part, x,
    tables, spectrum, decay, hidden, f_out, phase, table,
):
    dp, mp = lax.axis_size("dp"), lax.axis_size("mp")
    parts, docs = x.shape[1], lengths.shape[1]
    blocks, block, near = spectrum.shape[1], spectrum.shape[2] // 2, spectrum.shape[3]
    half, width = HALVES * near, 2 * HALVES * near
    size = part_a.shape[2]
    full = channel.shape[1]
    if dp != 8:
        g_in = exchange([*g_parts], edge, 5)
        edge_back = g_in[HALVES]
        halves = []
        for side in range(HALVES):
            skip = channel_own[-1:, side * near : (side + 1) * near]
            halves.append(conv_backward(g_in[side], x[side], lengths, spectrum[side], skip, tables))
        g_raw = jnp.concatenate([v[2] for v in halves], axis=1) * decay
        fin, fout = product(table.T, product(g_raw, f_out.T) * jnp.cos(phase)), product(hidden.T, g_raw)
        backs = exchange([v[i] for i in range(2) for v in halves], None, 6)
        gw_back, gw_edge_back = jnp.stack(backs[:HALVES]), jnp.stack(backs[HALVES:])
        count = g_s0.shape[0]
        gs = jnp.concatenate([g_s0, edge_back.astype(F32)])
        position = lax.axis_index("mp") * count - EDGE + jnp.arange(count + 2 * EDGE, dtype=jnp.int32)
        doc = jnp.sum((position[:, None] >= jnp.cumsum(lengths[0])[None, :]).astype(jnp.int32), axis=1)
        doc = jnp.where(position < 0, -1, doc)
        same = [None] + [(doc[EDGE:] == doc[EDGE - k : doc.shape[0] - k])[:, None] for k in range(1, offsets)]
        g_z, sums = None, jnp.zeros((16, full), F32)
        for k in range(offsets):
            later, before = gs[k : count + k], z[0, EDGE - k : EDGE - k + count]
            if k:
                later, before = jnp.where(same[k][k : count + k], later, 0.0), jnp.where(same[k][:count], before, 0.0)
            g_z = channel[3 * k] * later if g_z is None else g_z + channel[3 * k] * later
            sums = sums.at[3 * k].set(jnp.sum(gs[:count] * before, axis=0))
        sums = sums.at[3 * offsets].set(feed_sums[1]).at[3 * offsets + 2].set(feed_sums[0])
        g_z = g_z.astype(BF)
        grad = dot_tn(a[EDGE : EDGE + count], g_z).reshape(full, mp, half).transpose(1, 0, 2).astype(BF)
        part_c = jnp.concatenate([grad, out_part], axis=2).reshape(mp, dp, size, width)
        over_dp = [lax.psum_scatter(p, "dp", scatter_dimension=1) for p in (part_a, part_b, part_c)]
        return (
            gw_back, gw_edge_back, sums, dot_nt(g_z, w_in[0]), fin, fout, *over_dp,
        )
    edge_shape = (HALVES, parts, EDGE, -(-near // 128) * 128)
    own, own_c = part_a.shape[2:], (size, width)
    rows, raw, low, slots = conv_scratch(x.shape[1:], blocks, block, near, docs)
    first = (g_parts, edge, channel_own, feed_sums)
    late = [
        (g_s0, None), (z, 0), (a, None), (w_in, 0), (channel, None), (out_part, None), (x, None),
        *[(t, None) for t in tables], (spectrum, None), (decay, None), (hidden, None), (f_out, None), (phase, None),
        (table, None),
    ]
    fin, fout = struct((table.shape[1], hidden.shape[1]), F32), struct((hidden.shape[1], half), F32)
    longer = (g_s0.shape[0] + EDGE, full)

    def kernel(*refs):
        start = 3 + len(first)
        chosen = [r if i is None else r.at[i] for r, (_, i) in zip(refs[start : start + len(late)], late)]
        mixer_backward_kernel(docs, offsets, *refs[:start], *chosen, *refs[start + len(late) :])

    return pl.pallas_call(
        kernel,
        name="mixer_backward",
        out_shape=(
            struct(x.shape, BF), struct(edge_shape, BF), struct((16, full), F32), struct(g_s0.shape, F32), fin, fout,
            struct((mp,) + own, BF), struct((mp,) + own, BF), struct((mp,) + own_c, BF),
        ),
        in_specs=[IN_SMEM] + [IN_VMEM] * len(first) + [IN_HBM] * (2 + len(late)),
        out_specs=(IN_VMEM,) * 9,
        scratch_shapes=[
            *[pltpu.VMEM(v.shape if i is None else v.shape[1:], v.dtype) for v, i in late[1:]],
            dma(len(late)), pltpu.VMEM((mp, 2, 2, 2) + own_c, BF), pltpu.VMEM(edge.shape, BF), pltpu.VMEM(longer, F32),
            pltpu.VMEM((offsets - 1, longer[0], 128), F32),
            pltpu.VMEM((blocks * block, half), F32), pltpu.VMEM(x.shape, BF), pltpu.VMEM(x.shape, BF),
            pltpu.VMEM(edge_shape, BF), rows, rows, raw, raw, low, low, raw, slots,
            dma(HALVES, 1, mp - 1), dma(HALVES, 1, mp - 1), dma(HALVES, 2, mp - 1), dma(HALVES, 2, mp - 1), dma(2),
            *flow_scratch(mp, own, False), *flow_scratch(mp, own, False), *flow_scratch(mp, own_c, False),
        ],
        compiler_params=pltpu.CompilerParams(collective_id=5, has_side_effects=True, vmem_limit_bytes=ROOM),
    )(lengths, *first, cored(part_a), cored(part_b), *[v for v, _ in late])


def spread_sum(block, slots, send_sem, recv_sem, axis, first):
    d, m = lax.axis_index("dp"), lax.axis_index("mp")
    count = lax.axis_size(axis)
    me = d if axis == "dp" else m
    copies = []
    for step, e in enumerate(ring(me, count)):
        peer = (e, m) if axis == "dp" else (d, e)
        copies.append(send(block, slots.at[me], send_sem.at[first + step], recv_sem.at[first + step], peer))
    slots[me] = block[...]
    for copy in copies:
        copy.wait()
    total = slots[0]
    for e in range(1, count):
        total = total + slots[e]
    return total


def total_of(values):
    return jnp.sum(jnp.sum(values, axis=1, keepdims=True), axis=0, keepdims=True)


def lanes_of(items):
    lane = lax.broadcasted_iota(jnp.int32, (1, 128), 1)
    row = jnp.zeros((1, 128), F32)
    for index, item in enumerate(items):
        row = row + jnp.where(lane == index, item, 0.0)
    return row


def update_body(
    taps, g0, g1, g2, w0, w1, w2, rows, cols, vec_sum, own_gain, gain, gain_mom, chan, chan_mom,
    fin_sum, fin, fin_mom, fout_sum, fout, fout_mom,
    norm_out, c0, c1, c2, n0, n1, n2, rows_out, cols_out, gain_g, gain_n, gain_m,
    chan_g, chan_n, chan_m, fin_g, fin_n, fin_m, fout_g, fout_n, fout_m,
    turn, mp_block, dp_block, mp_slots, dp_slots, last_block, mp_last, dp_last, send_sem, recv_sem,
):
    d, m = lax.axis_index("dp"), lax.axis_index("mp")
    dp, mp = lax.axis_size("dp"), lax.axis_size("mp")
    size, width = g0.shape
    in_width = 3 * (width // 4)
    is_in = lax.broadcasted_iota(jnp.int32, (size, width), 1) < in_width

    def four(v0, v1, v2, reduce_fn):
        return [
            reduce_fn(jnp.where(is_in, v0, 0.0)),
            reduce_fn(jnp.where(is_in, 0.0, v0)),
            reduce_fn(v1),
            reduce_fn(v2),
        ]

    def row_sum(v):
        return jnp.sum(v, axis=1, keepdims=True)

    def col_sum(v):
        return jnp.sum(v, axis=0, keepdims=True)

    s0, s1, s2 = g0[...] * g0[...], g1[...] * g1[...], g2[...] * g2[...]
    lane = lax.broadcasted_iota(jnp.int32, (size, 128), 1)
    row_parts = four(s0, s1, s2, row_sum)
    packed = jnp.zeros((size, 128), F32)
    for index, part in enumerate(row_parts):
        packed = packed + jnp.where(lane == index, part, 0.0)
    turn[...] = jnp.zeros(turn.shape, F32)
    dp_block[...] = jnp.zeros(dp_block.shape, F32)
    turn[pl.ds(0, size), :] = packed
    mp_block[pl.ds(0, 8), :] = jnp.transpose(turn[...])[0:8]
    old = rows[...]
    old_parts = [total_of(old[:, i : i + 1]) / mp for i in range(4)]
    weight_parts = four(w0[...] * w0[...], w1[...] * w1[...], w2[...] * w2[...], total_of)
    scalars = (
        [total_of(p) for p in row_parts]
        + old_parts
        + weight_parts
        + [
            total_of(gain[...] * gain[...]) / mp,
            total_of(chan[...] * chan[...]) / dp,
            total_of(fout[...] * fout[...]) / dp,
            total_of(fout_sum[...] * fout_sum[...]) / dp,
        ]
    )
    mp_block[pl.ds(8, 8), :] = jnp.broadcast_to(lanes_of(scalars), (8, 128))
    over_mp = spread_sum(mp_block, mp_slots, send_sem, recv_sem, "mp", 0)
    pieces = width // 128
    for index, values in enumerate((s0, s1, s2)):
        sums = col_sum(values)
        for piece in range(pieces):
            dp_block[pl.ds(index * pieces + piece, 1), :] = sums[:, piece * 128 : (piece + 1) * 128]
    dp_block[pl.ds(3 * pieces, 1), :] = over_mp[8:9]
    over_dp = spread_sum(dp_block, dp_slots, send_sem, recv_sem, "dp", mp)
    turn[pl.ds(0, 8), :] = over_mp[0:8]
    row_totals = jnp.transpose(turn[...])[0:size]
    shared = over_dp[3 * pieces : 3 * pieces + 1]

    def scalar(index):
        return shared[:, index : index + 1]

    last = 3 * taps + 1
    vec_sq = total_of(vec_sum[0 : last + 2, :] * vec_sum[0 : last + 2, :])
    fin_sq = total_of(fin_sum[...] * fin_sum[...])
    norm = jnp.sqrt(
        scalar(0) + scalar(1) + scalar(2) + scalar(3) + vec_sq + scalar(15) + fin_sq
    )
    norm_out[...] = norm
    clip = 1.0 / jnp.maximum(1.0, norm / CLIP_NORM)
    square = clip * clip
    fresh = 1.0 - MOMENT_DECAY
    all_rows = size * dp
    wide = [in_width * mp, (width - in_width) * mp, width * mp, width * mp]
    ratio = []
    fresh_rows = jnp.zeros((size, 128), F32)
    for index in range(4):
        row_new = (
            MOMENT_DECAY * old[:, index : index + 1]
            + fresh * square * row_totals[:, index : index + 1] / wide[index]
        )
        mean = MOMENT_DECAY * scalar(4 + index) / all_rows + fresh * square * scalar(index) / (
            all_rows * wide[index]
        )
        ratio.append(row_new / mean)
        fresh_rows = fresh_rows + jnp.where(lane == index, row_new, 0.0)
    turn[pl.ds(0, size), :] = fresh_rows
    rows_out[...] = jnp.transpose(turn[...])[0:8]
    for index in range(3):
        for piece in range(pieces):
            at = pl.ds(piece * 128, 128)
            row = index * pieces + piece
            cols_out[pl.ds(index, 1), at] = (
                MOMENT_DECAY * cols[pl.ds(index, 1), at]
                + fresh * square * over_dp[row : row + 1] / all_rows
            )
    first_ratio = jnp.where(is_in, ratio[0], ratio[1])
    steps = []
    for grad, out, factor, index in ((g0, c0, first_ratio, 0), (g1, c1, ratio[2], 1), (g2, c2, ratio[3], 2)):
        clipped = grad[...] * clip
        out[...] = clipped
        steps.append(clipped * lax.rsqrt(factor * cols_out[pl.ds(index, 1), :]))
    u0, u1, u2 = steps

    def plain(clipped, moment, grad_out, moment_out):
        fresh_moment = MOMENT_DECAY * moment + fresh * clipped * clipped
        grad_out[...] = clipped
        moment_out[...] = fresh_moment
        return clipped * lax.rsqrt(fresh_moment)

    picked = vec_sum[last : last + 2, 0:size]
    for e in range(1, dp):
        picked = jnp.where(d == e, vec_sum[last : last + 2, e * size : (e + 1) * size], picked)
    own_gain[...] = jnp.zeros(own_gain.shape, F32)
    own_gain[:, pl.ds(0, size)] = picked
    own = width // mp
    own_chan = vec_sum[0:last, 0:own]
    for e in range(1, mp):
        own_chan = jnp.where(m == e, vec_sum[0:last, e * own : (e + 1) * own], own_chan)
    u_gain = plain(own_gain[...] * clip, gain_mom[...], gain_g, gain_m)
    u_chan = plain(own_chan * clip, chan_mom[...], chan_g, chan_m)
    u_fin = plain(fin_sum[...] * clip, fin_mom[...], fin_g, fin_m)
    u_fout = plain(fout_sum[...] * clip, fout_mom[...], fout_g, fout_m)
    step_parts = four(u0 * u0, u1 * u1, u2 * u2, total_of) + [
        total_of(u_gain * u_gain) / mp,
        total_of(u_chan * u_chan) / dp,
        total_of(u_fout * u_fout) / dp,
    ]
    last_block[...] = jnp.broadcast_to(lanes_of(step_parts), (8, 128))
    half_way = spread_sum(last_block, mp_last, send_sem, recv_sem, "mp", mp + dp)
    mp_block[pl.ds(0, 8), :] = half_way
    step_sums = spread_sum(mp_block.at[pl.ds(0, 8)], dp_last, send_sem, recv_sem, "dp", 2 * mp + dp)[0:1]

    def factors(step_total, weight_total, entries):
        shrink = 1.0 / jnp.maximum(1.0, jnp.sqrt(step_total / entries) / CLIP_STEP)
        return STEP_RATE * jnp.sqrt(weight_total / entries) * shrink

    def step_sum(index):
        return step_sums[:, index : index + 1]

    rate = [factors(step_sum(i), scalar(8 + i), all_rows * wide[i]) for i in range(4)]
    n0[...] = w0[...] - jnp.where(is_in, rate[0], rate[1]) * u0
    n1[...] = w1[...] - rate[2] * u1
    n2[...] = w2[...] - rate[3] * u2
    gain_n[...] = gain[...] - factors(step_sum(4), scalar(12), 2 * all_rows) * u_gain
    chan_n[...] = chan[...] - factors(step_sum(5), scalar(13), chan.shape[0] * chan.shape[1] * mp) * u_chan
    fout_n[...] = fout[...] - factors(step_sum(6), scalar(14), fout.shape[0] * fout.shape[1] * mp) * u_fout
    fin_count = fin.shape[0] * fin.shape[1]
    fin_rate = factors(total_of(u_fin * u_fin), total_of(fin[...] * fin[...]), fin_count)
    fin_n[...] = fin[...] - fin_rate * u_fin


def greet_all():
    d, m = lax.axis_index("dp"), lax.axis_index("mp")
    greet([(e, m) for e in ring(d, lax.axis_size("dp"))] + [(d, e) for e in ring(m, lax.axis_size("mp"))])


def prepare(raw, ready, turn):
    in_w, out_w, in_rows, out_rows, up_rows, down_rows, in_cols, out_cols, up_cols, down_cols, gain_own, gain_mom_own = raw
    w0, rows, cols, gain, gain_mom = ready
    size, own = out_w.shape
    for j in range(3):
        w0[:, pl.ds(j * own, own)] = in_w[j]
        cols[0:1, pl.ds(j * own, own)] = in_cols[j : j + 1, :]
    w0[:, pl.ds(3 * own, own)] = out_w[...]
    cols[0:1, pl.ds(3 * own, own)] = out_cols[...].reshape(1, own)
    cols[1:2, :] = up_cols[...].reshape(1, -1)
    cols[2:3, :] = down_cols[...].reshape(1, -1)
    turn[...] = jnp.zeros(turn.shape, F32)
    for index, source in enumerate((in_rows, out_rows, up_rows, down_rows)):
        turn[pl.ds(index, 1), pl.ds(0, size)] = source[...].reshape(1, size)
    rows[...] = jnp.transpose(turn[...])[0:size]
    for source, target, fill in ((gain_own, gain, 0.0), (gain_mom_own, gain_mom, 1.0)):
        target[...] = jnp.full(target.shape, fill, F32)
        target[:, pl.ds(0, size)] = source[...]


def prepare_scratch(size, width):
    return [
        pltpu.VMEM((size, width), F32), pltpu.VMEM((size, 128), F32), pltpu.VMEM((8, width), F32),
        pltpu.VMEM((2, 128), F32), pltpu.VMEM((2, 128), F32),
    ]


OUTS = 21


def run_update(taps, grads, sums, w1, w2, ready, own_gain, old, outs, work):
    w0, rows, cols, gain, gain_mom = ready
    chan, chan_mom, fin, fin_mom, fout, fout_mom = old
    update_body(
        taps, *grads, w0, w1, w2, rows, cols, sums[0], own_gain, gain, gain_mom, chan, chan_mom,
        sums[1], fin, fin_mom, sums[2], fout, fout_mom, *outs, *work,
    )


def update_kernel(taps, *refs):
    grads, sums, refs = refs[:3], refs[3:6], refs[6:]
    raw, w1, w2, old, refs = refs[:12], refs[12], refs[13], refs[14:20], refs[20:]
    outs, ready, own_gain, work = refs[:OUTS], refs[OUTS : OUTS + 5], refs[OUTS + 5], refs[OUTS + 6 :]
    prepare(raw, ready, work[0])
    greet_all()
    run_update(taps, grads, sums, w1, w2, ready, own_gain, old, outs, work)


def place_first(g0, zero_and_out, one_and_two):
    own = g0.shape[1] // 4
    g0[:, pl.ds(0, own)] = zero_and_out[:, 0:own]
    g0[:, pl.ds(own, 2 * own)] = one_and_two
    g0[:, pl.ds(3 * own, own)] = zero_and_out[:, own : 2 * own]


class OverMp:
    def __init__(self, partial, arrived, send_sem, recv_sem):
        self.partial, self.arrived = partial, arrived
        d, m, mp = lax.axis_index("dp"), lax.axis_index("mp"), lax.axis_size("mp")
        self.copies = [
            send(partial.at[e], arrived.at[step], send_sem.at[step], recv_sem.at[step], (d, e))
            for step, e in enumerate(ring(m, mp))
        ]

    def total(self):
        total = self.partial[lax.axis_index("mp")].astype(F32)
        for step, copy in enumerate(self.copies):
            copy.wait()
            total = total + self.arrived[step].astype(F32)
        return total


def end_kernel(doc_count, taps, len_ref, gw_ref, gw_edge, channel, gains, sums_in, *refs):
    late_refs, partials, fin_part, fout_part, refs = refs[:12], refs[12:15], refs[15], refs[16], refs[17:]
    raw, w1, w2, old, refs = refs[:12], refs[12], refs[13], refs[14:20], refs[20:]
    input_grad, outs, refs = refs[0], refs[1 : OUTS + 1], refs[OUTS + 1 :]
    held, late_sem, work, refs = refs[:12], refs[12], refs[13:17], refs[17:]
    ready, own_gain, refs = refs[:5], refs[5], refs[6:]
    g0, g1, g2, g_late, vec, vec_sum, fin_sum, fout_sum, part, refs = *refs[:9], refs[9:]
    update_work, refs = refs[:10], refs[10:]
    arrived, z_send, z_recv, refs = refs[:3], refs[3], refs[4], refs[5:]
    mp = lax.axis_size("mp")
    own = gw_ref.shape[3] // FOLD * HALVES
    size = g0.shape[0]
    lanes = g_late.shape[1] // FLOWS
    flows = []
    for i in range(FLOWS):
        flows.append(Flow(part, refs[i * FLOW_REFS : (i + 1) * FLOW_REFS], pl.ds(i * lanes, lanes)))
    refs = refs[FLOWS * FLOW_REFS :]
    early = SmallSums((fin_part, fout_part), (fin_sum, fout_sum), (True, False), refs[:8])
    final = SmallSums((vec,), (vec_sum,), (True,), refs[8:])
    late = Late(late_refs, held, late_sem)
    vec[...] = sums_in[...]
    greet_all()
    over_mp = [OverMp(partials[i], arrived[i], z_send.at[i], z_recv.at[i]) for i in range(3)]
    early.start(0)

    def stream_done(j, grad):
        for e in range(mp):
            for owner in range(8):
                at = (e, owner // 4, owner // 2 % 2, owner % 2, slice(None), pl.ds((j - 1) * own, own))
                part[at] = grad[owner * size : (owner + 1) * size, e * own : (e + 1) * own].astype(BF)
        if j == 1:
            flows[0].start()
            early.end(0)
            early.start(1)
        else:
            flows[1].start()
            flows[2].start()
            early.end(1)
            early.start(2)

    total = post_steps(
        doc_count, taps, len_ref, gw_ref, gw_edge, channel, gains, vec, held, late, work, stream_done
    )
    final.start(0)
    flows[0].core_stage()
    post_end(total, gains, held, input_grad)
    flows[1].core_stage()
    flows[2].core_stage()
    early.end(2)
    early.start_mp()
    final.end(0)
    final.start(1)
    prepare(raw, ready, update_work[0])
    for flow in flows:
        flow.second_stage()
    final.end(1)
    final.start(2)
    for flow in flows:
        flow.third_stage()
        flow.send_z()
    final.end(2)
    final.start_mp()
    g1[...] = over_mp[0].total()
    g2[...] = over_mp[1].total()
    zero_and_out = over_mp[2].total()
    early.end_mp()
    final.end_mp()
    for flow in flows:
        flow.finish(g_late)
    place_first(g0, zero_and_out, g_late[...])
    for flow in flows:
        flow.drain()
    early.drain()
    final.drain()
    run_update(taps, (g0, g1, g2), (vec_sum, fin_sum, fout_sum), w1, w2, ready, own_gain, old, outs, update_work)


def update_scratch(dp, mp, width):
    pieces = 3 * width // 128 + 1
    tall = -(-pieces // 8) * 8
    sems = 2 * (dp + mp)
    return [
        pltpu.VMEM((128, 128), F32),
        pltpu.VMEM((16, 128), F32),
        pltpu.VMEM((tall, 128), F32),
        pltpu.VMEM((mp, 16, 128), F32),
        pltpu.VMEM((dp, tall, 128), F32),
        pltpu.VMEM((8, 128), F32),
        pltpu.VMEM((mp, 8, 128), F32),
        pltpu.VMEM((dp, 8, 128), F32),
        dma(sems),
        dma(sems),
    ]


def hand_out_kernel(*refs):
    input_grad, norm, c0, c1, c2, n0, n1, n2, rows, cols, gain_g, gain_n, gain_m, *small = refs[: OUTS + 1]
    (
        input_grad_out, norm_out, in_g, out_g, up_g, down_g, gain_g_out, in_n, out_n, up_n, down_n, gain_n_out, gain_m_out,
        in_r, out_r, up_r, down_r, in_c, out_c, up_c, down_c, *small_out,
    ) = refs[OUTS + 1 :]
    size, own = out_g.shape
    input_grad_out[...] = input_grad[...]
    norm_out[...] = norm[...]
    for source, first, last in ((c0, in_g, out_g), (n0, in_n, out_n)):
        for j in range(3):
            first[j] = source[:, j * own : (j + 1) * own]
        last[...] = source[:, 3 * own : 4 * own]
    for source, target in ((c1, up_g), (c2, down_g), (n1, up_n), (n2, down_n)):
        target[...] = source[...]
    for source, target in ((gain_g, gain_g_out), (gain_n, gain_n_out), (gain_m, gain_m_out)):
        target[...] = source[:, 0:size]
    for index, target in enumerate((in_r, out_r, up_r, down_r)):
        target[...] = rows[index : index + 1, 0:size].reshape(size)
    for j in range(3):
        in_c[j : j + 1, :] = cols[0:1, j * own : (j + 1) * own]
    out_c[...] = cols[0:1, 3 * own : 4 * own].reshape(own)
    up_c[...] = cols[1:2, :].reshape(-1)
    down_c[...] = cols[2:3, :].reshape(-1)
    for source, target in zip(small, small_out):
        target[...] = source[...]


def hand_out(results, own):
    size, width = results[2].shape
    cube, part, full = (3, size, own), (size, own), (size, width)
    column, row, wide = (2, size), (size,), (width,)
    shapes = [(1, 1), cube, part, full, full, column, cube, part, full, full, column, column, row, row, row, row]
    shapes += [(3, own), (own,), wide, wide] + [v.shape for v in results[13:]]
    return pl.pallas_call(
        hand_out_kernel,
        name="hand_out",
        out_shape=(struct(results[0].shape, BF), *[struct(s, F32) for s in shapes]),
        in_specs=[IN_VMEM] * len(results),
        out_specs=(IN_VMEM,) * (1 + len(shapes)),
        compiler_params=pltpu.CompilerParams(vmem_limit_bytes=ROOM),
    )(*results)


FLOWS = 3


def finish(lengths, taps, first, late, partials, fin_part, fout_part, raw, w1, w2, old):
    dp, mp = lax.axis_size("dp"), lax.axis_size("mp")
    size, own = raw[1].shape
    width = w1.shape[1]
    count = late[0][0].shape[0]
    docs = lengths.shape[1]
    big = struct((size, width), F32)
    flat = [(2, 128), old[0].shape, old[2].shape, old[4].shape]
    outs = [struct((1, 1), F32)] + [big] * 6 + [struct((8, 128), F32), struct((3, width), F32)]
    outs += [struct(s, F32) for s in flat for _ in range(3)]
    params = pltpu.CompilerParams(collective_id=2, has_side_effects=True, vmem_limit_bytes=ROOM)
    tail = [*raw, w1, w2, *old]
    own_gain = pltpu.VMEM((2, 128), F32)
    if dp != 8:
        last_part, input_grad, vec = post(lengths, taps, *first, late)
        over_mp = [lax.psum_scatter(p, "mp").astype(F32) for p in partials]
        grad = scatter_fallback(last_part.reshape(mp, dp, size, 2 * own))
        grad = jnp.concatenate([over_mp[2][:, :own], grad, over_mp[2][:, own:]], axis=1)
        sums = [lax.psum(vec, ("dp", "mp")), lax.psum(fin_part, ("dp", "mp")), lax.psum(fout_part, "dp")]
        inputs = [grad, *over_mp[:2], *sums, *tail]
        results = pl.pallas_call(
            functools.partial(update_kernel, taps),
            name="clip_and_update",
            out_shape=tuple(outs),
            in_specs=[IN_VMEM] * len(inputs),
            out_specs=(IN_VMEM,) * len(outs),
            scratch_shapes=prepare_scratch(size, width) + [own_gain] + update_scratch(dp, mp, width),
            compiler_params=params,
        )(*inputs)
        return (input_grad, *results)
    flows = []
    for _ in range(FLOWS):
        flows += flow_scratch(mp, (size, 2 * own // FLOWS))
    vec = struct((16, width), F32)
    after = [*partials, fin_part, fout_part, *tail]

    def kernel(*refs):
        start = 1 + len(first)
        end = start + len(late)
        end_kernel(docs, taps, *refs[:start], *choose(refs[start:end], late), *refs[end:])

    return pl.pallas_call(
        kernel,
        name="sum_clip_update",
        out_shape=(struct((count, width), BF), *outs),
        in_specs=[IN_SMEM] + [IN_VMEM] * len(first) + [IN_HBM] * len(late) + [IN_VMEM] * len(after),
        out_specs=(IN_VMEM,) * (1 + len(outs)),
        scratch_shapes=[
            *post_scratch(late, taps, count, width),
            *prepare_scratch(size, width),
            own_gain,
            *[pltpu.VMEM((size, width), F32)] * 3,
            pltpu.VMEM((size, 2 * own), F32),
            *[pltpu.VMEM(v.shape, F32) for v in (vec, vec, fin_part, fout_part)],
            pltpu.VMEM((mp, 2, 2, 2, size, 2 * own), BF),
            *update_scratch(dp, mp, width),
            *[pltpu.VMEM((mp - 1,) + p.shape[1:], BF) for p in partials],
            dma(3, mp - 1),
            dma(3, mp - 1),
            *flows,
            *small_scratch((fin_part, fout_part), mp),
            *small_scratch((vec,), mp),
        ],
        compiler_params=params,
    )(lengths, *first, *[v for v, _ in late], *after)


class Spread:
    def __init__(self, own, whole, lanes, refs):
        self.whole, self.lanes = whole, lanes
        self.source = own.at[:, lanes]
        self.own_sem, self.z_send, self.z_recv, self.p_send, self.p_recv = refs
        self.d, self.m, self.mp = lax.axis_index("dp"), lax.axis_index("mp"), lax.axis_size("mp")
        d = self.d
        self.dx, self.dy, self.dc = turned(d, 2), turned(d, 4), turned(d, 1)
        half = self.mp // 2
        self.low, self.high, self.all = pl.ds(0, half), pl.ds(half, self.mp - half), pl.ds(0, self.mp)

    def start(self):
        target = self.whole.at[self.m, self.d, :, self.lanes]
        self.copy = pltpu.make_async_copy(self.source, target, self.own_sem.at[0])
        self.copy.start()
        self.z = [
            send(self.source, target, self.z_send.at[step], self.z_recv.at[step], (self.d, e))
            for step, e in enumerate(ring(self.m, self.mp))
        ]

    def push(self, slot, rows, owner, peer):
        block = self.whole.at[rows, owner, :, self.lanes]
        return send(block, block, self.p_send.at[slot], self.p_recv.at[slot], (peer, self.m))

    def stage_one(self):
        self.copy.wait()
        for copy in self.z:
            copy.wait_recv()
        d, dx, dy = self.d, self.dx, self.dy
        self.first = [self.push(0, self.low, d, dx), self.push(1, self.high, d, dy)]
        self.last = [self.push(2, self.all, d, self.dc)]

    def stage_two(self):
        for copy in self.first:
            copy.wait_recv()
        d, dx, dy = self.d, self.dx, self.dy
        self.second = [
            self.push(3, self.low, d, dy),
            self.push(4, self.high, d, dx),
            self.push(5, self.low, dx, dy),
            self.push(6, self.high, dy, dx),
        ]

    def stage_three(self):
        for copy in self.second:
            copy.wait_recv()
        for slot, owner in enumerate((self.dx, self.dy, turned(self.dx, 4))):
            self.last.append(self.push(7 + slot, self.all, owner, self.dc))

    def arrive(self):
        for copy in self.last:
            copy.wait_recv()

    def drain(self):
        for copy in self.z + self.first + self.second + self.last:
            copy.wait_send()


SPREAD_REFS = 5


def spread_scratch(mp):
    return [dma(1), dma(mp - 1), dma(mp - 1), dma(10), dma(10)]


def mark_same(same, len_ref, doc_count, first):
    tail = same.shape[1]
    position = lax.broadcasted_iota(jnp.int32, (tail + EDGE, 128), 0) + first
    doc = jnp.zeros(position.shape, jnp.int32)
    end = jnp.int32(0)
    for slot in range(doc_count):
        end = end + len_ref[0, slot]
        doc = doc + (position >= end).astype(jnp.int32)
    doc = jnp.where(position < 0, -1, doc)
    for k in range(1, same.shape[0] + 1):
        same[k - 1] = jnp.where(doc[EDGE:] == doc[EDGE - k : EDGE - k + tail], 1.0, 0.0)


def near_product(left, right, dot=mm):
    l_top, l_rest = split(left)
    r_top, r_rest = split(right)
    return dot(l_top, r_top) + dot(l_top, r_rest) + dot(l_rest, r_top)


def mixer_forward_kernel(
    doc_count, taps, len_ref, tok, in_w, out_w, up_w, down_w, gains_own, channel_own, table, step_col, f_in, f_out,
    t0, t1, t2, t3,
    w_parts, y_back, spectrum, hidden, phase, decay, gain_rows, chan_rows,
    z_out, s0_out, s1_out, s2_out, w_out_own, a_out, n1_out, inv1_out, w_in_out, w_out_out, whole_up, whole_down,
    chunk_first, chunk_up, chunk_down, gains, channel, turn, whole_first, gains_all, channel_all, edges_all, filters, w_send, y_parts, full, raw, top, rest, slots,
    ext, n1, inv1, a, z, s0, s1, s2, w_own, w_in, w_out, same,
    s_send, s_recv, save_sem, b_send, b_recv, c_send, c_recv, *spread_refs,
):
    tables = (t0, t1, t2, t3)
    d, m = lax.axis_index("dp"), lax.axis_index("mp")
    dp, mp = lax.axis_size("dp"), lax.axis_size("mp")
    count, width = tok.shape
    rows = chunk_first.shape[0]
    own = width // mp
    block = count // 2
    blocks = raw.shape[0]

    place = (2, 0, 1)
    for j in range(3):
        chunk_first[:, pl.ds(place[j] * own, own)] = in_w[j].astype(BF)
    chunk_first[:, pl.ds(3 * own, own)] = out_w[...].astype(BF)
    chunk_up[...] = up_w[...].astype(BF)
    chunk_down[...] = down_w[...].astype(BF)
    turn[...] = jnp.zeros(turn.shape, F32)
    turn[pl.ds(0, 2), pl.ds(0, rows)] = gains_own[...]
    gains[...] = turn[...].astype(BF)
    channel[...] = jnp.zeros(channel.shape, F32)
    channel[pl.ds(0, channel_own.shape[0]), :] = channel_own[...]
    greet_all()

    small = []
    for step, e in enumerate(ring(d, dp)):
        small.append(send(gains, gains_all.at[d], s_send.at[step], s_recv.at[step], (e, m)))
    for step, e in enumerate(ring(m, mp)):
        at = dp + step
        small.append(send(channel, channel_all.at[m], s_send.at[at], s_recv.at[at], (d, e)))
    at = dp + mp
    for index, first, peer in ((0, count - EDGE, lax.rem(m + 1, mp)), (1, 0, lax.rem(m + mp - 1, mp))):
        sems = s_send.at[at + index], s_recv.at[at + index]
        small.append(send(tok.at[pl.ds(first, EDGE)], edges_all.at[index], *sems, (d, peer)))
    gains_all[d] = gains[...]
    channel_all[m] = channel[...]

    half = width // 2
    plan = [
        (chunk_first, whole_first, pl.ds(0, half)),
        (chunk_first, whole_first, pl.ds(half, width - half)),
        (chunk_up, whole_up, pl.ds(0, chunk_up.shape[1])),
        (chunk_down, whole_down, pl.ds(0, chunk_down.shape[1])),
    ]
    flows = [Spread(*p, spread_refs[i * SPREAD_REFS : (i + 1) * SPREAD_REFS]) for i, p in enumerate(plan)]
    left, right, up, down = flows
    left.start()
    right.start()

    phase[...] = near_product(table[...], f_in[...])
    hidden[...] = jnp.sin(phase[...])
    lane = (m * own + lax.broadcasted_iota(jnp.int32, (1, own), 1)).astype(F32)
    rate = FAST_DECAY + (SLOW_DECAY - FAST_DECAY) * lane / (width - 1)
    decay[...] = jnp.exp(-step_col[...] * rate)
    filters[...] = near_product(hidden[...], f_out[...]) * decay[...]
    near = own // HALVES
    for side in range(HALVES):
        filter_spectrum(filters, pl.ds(side * near, near), spectrum.at[side], raw, tables, block)

    mark_same(same, len_ref, doc_count, m * count - EDGE)

    left.stage_one()
    for copy in small:
        copy.wait()
    for e in range(dp):
        gain_rows[0:2, pl.ds(e * rows, rows)] = gains_all[e, 0:2, 0:rows].astype(F32)
    for e in range(mp):
        chan_rows[:, pl.ds(e * own, own)] = channel_all[e]
    ext[pl.ds(0, EDGE), :] = edges_all[0].astype(F32)
    ext[pl.ds(EDGE, count), :] = tok[...].astype(F32)
    ext[pl.ds(EDGE + count, EDGE), :] = edges_all[1].astype(F32)

    def norm_body(i, carry):
        at = pl.ds(pl.multiple_of(i * 32, 32), 32)
        normed, inverse_std = norm_parts(ext[at, :])
        n1[at, :] = normed
        inv1[at, :] = jnp.broadcast_to(inverse_std, (32, 128))
        a[at, :] = (normed * gain_rows[0:1, :]).astype(BF)
        return carry

    def stream_weights(j):
        for e in range(mp):
            part = whole_first[e, :, :, pl.ds(place[j] * own, own)].reshape(dp * rows, own)
            w_in[:, pl.ds(j * width + e * own, own)] = part

    def project(j):
        cols = pl.ds(j * width, width)
        z[:, cols] = mm(a[...], w_in[:, cols])

    def short(first, size, j):
        part = z[pl.ds(first + 8, size + 8), pl.ds(j * width, width)]
        total = chan_rows[j : j + 1, :] * part[8 : size + 8]
        for k in range(1, taps):
            keep = same[k - 1, pl.ds(first, size), 0:1] > 0.0
            moved = jnp.where(keep, part[8 - k : size + 8 - k], 0.0)
            total = total + chan_rows[3 * k + j : 3 * k + j + 1, :] * moved
        return total

    def value_body(i, carry):
        first = pl.multiple_of(i * 48, 16)
        at = pl.ds(first, 48)
        one, two = short(first, 48, 1), short(first, 48, 2)
        s1[at, :], s2[at, :] = one, two
        w_own[at, :] = two * one
        return carry

    def gate_body(i, carry):
        first = pl.multiple_of(i * 48, 16)
        s0[pl.ds(first, 48), :] = short(first, 48, 0)
        return carry

    lax.fori_loop(0, ext.shape[0] // 32, norm_body, 0)
    left.stage_two()
    right.stage_one()
    up.start()
    left.stage_three()
    right.stage_two()
    left.arrive()
    for j in (1, 2):
        stream_weights(j)
        project(j)
    up.stage_one()
    down.start()
    lax.fori_loop(0, s0.shape[0] // 48, value_body, 0)
    piece = count // FOLD
    for side in range(HALVES):
        for part in range(mp):
            for i in range(FOLD):
                values = w_own[pl.ds(i * piece, piece), pl.ds(part * own + side * near, near)]
                w_send[side, part, :, pl.ds(i * near, near)] = values.astype(BF)
    going, back = [], []
    for side in range(HALVES):
        going.append(Blocks([(w_send.at[side], w_parts.at[side])], b_send.at[side], b_recv.at[side]))
        back.append(Blocks([(y_parts.at[side], y_back.at[side])], c_send.at[side], c_recv.at[side]))
        going[side].start()
    right.stage_three()
    up.stage_two()
    down.stage_one()
    right.arrive()
    stream_weights(0)
    project(0)
    lax.fori_loop(0, s0.shape[0] // 48, gate_body, 0)
    saves = []

    def save(source, target):
        copy = pltpu.make_async_copy(source, target, save_sem.at[len(saves)])
        copy.start()
        saves.append(copy)

    own_rows = pl.ds(0, count)
    for source, target in (
        *[(z.at[:, pl.ds(j * width, width)], z_out.at[j]) for j in range(3)], (s0.at[own_rows], s0_out), (s1, s1_out), (s2, s2_out), (w_own.at[own_rows], w_out_own),
        (a, a_out), (n1, n1_out), (inv1, inv1_out),
        *[(w_in.at[:, pl.ds(j * width, width)], w_in_out.at[j]) for j in range(3)],
    ):
        save(source, target)
    for e in range(mp):
        part = whole_first[e, :, :, pl.ds(3 * own, own)].reshape(dp * rows, own)
        w_out[:, pl.ds(e * own, own)] = part
    save(w_out, w_out_out)
    def between(slot):
        if slot == 0:
            down.stage_two()
            up.stage_three()

    for side in range(HALVES):
        going[side].arrive()
        conv_forward_steps(
            doc_count, len_ref, w_parts.at[side], filters, tables, y_parts.at[side], spectrum.at[side], full, raw, top, rest,
            slots, between if side == 0 else lambda slot: None,
        )
        back[side].start()
    down.stage_three()
    up.arrive()
    down.arrive()
    for side in range(HALVES):
        back[side].arrive()
    for copy in saves:
        copy.wait()
    for copies in going + back:
        copies.drain()
    for flow in flows:
        flow.drain()


def mixer_forward(lengths, tokens, weights, gains, channel, taps, table, step_col, f_in, f_out, tables):
    mp, dp = lax.axis_size("mp"), lax.axis_size("dp")
    count, width = tokens.shape
    own, block, docs = width // mp, count // 2, lengths.shape[1]
    lags = table.shape[0]
    blocks = lags // block
    near = own // HALVES
    rows = weights[1].shape[0]
    shards = [(rows, 4 * own), weights[2].shape, weights[3].shape]
    whole = [(mp, dp) + s for s in shards]
    longer, later = (count + 2 * EDGE, width), (count + EDGE, width)
    parts = (HALVES, mp, count // FOLD, FOLD * near)
    full, raw, low, slots = conv_scratch(parts[1:], blocks, block, near, docs)
    vmem_outs = [
        (parts, BF), (parts, BF), ((HALVES, blocks, 2 * block, near), F32), ((lags, f_in.shape[1]), F32), ((lags, f_in.shape[1]), F32),
        ((lags, own), F32), ((8, width), F32), ((16, width), F32),
    ]
    hbm_outs = [
        ((3,) + longer, F32), ((count, width), F32), (later, F32), (later, F32), ((count, width), F32),
        (longer, BF), (longer, F32), ((longer[0], 128), F32), ((3, width, width), BF), ((width, width), BF),
        (whole[1], BF), (whole[2], BF),
    ]
    inputs = (lengths, tokens, *weights, gains, channel, table, step_col, f_in, f_out, *tables)
    return pl.pallas_call(
        functools.partial(mixer_forward_kernel, docs, taps),
        name="mixer_forward",
        out_shape=tuple(struct(*o) for o in vmem_outs + hbm_outs),
        in_specs=[IN_SMEM] + [IN_VMEM] * (len(inputs) - 1),
        out_specs=(IN_VMEM,) * len(vmem_outs) + (IN_HBM,) * len(hbm_outs),
        scratch_shapes=[
            *[pltpu.VMEM(s, BF) for s in shards], pltpu.VMEM((16, 128), BF), pltpu.VMEM((16, own), F32),
            pltpu.VMEM((16, 128), F32),
            pltpu.VMEM(whole[0], BF), pltpu.VMEM((dp, 16, 128), BF), pltpu.VMEM((mp, 16, own), F32),
            pltpu.VMEM((2, EDGE, width), BF), pltpu.VMEM((lags, own), F32), pltpu.VMEM(parts, BF), pltpu.VMEM(parts, BF),
            full, raw, low, low, slots,
            pltpu.VMEM(longer, F32), pltpu.VMEM(longer, F32), pltpu.VMEM((longer[0], 128), F32), pltpu.VMEM(longer, BF),
            pltpu.VMEM((longer[0], 3 * width), F32), pltpu.VMEM(later, F32), pltpu.VMEM(later, F32),
            pltpu.VMEM(later, F32), pltpu.VMEM(later, F32), pltpu.VMEM((width, 3 * width), BF),
            pltpu.VMEM((width, width), BF), pltpu.VMEM((taps - 1, later[0], 128), F32),
            dma(dp + mp + 2), dma(dp + mp + 2), dma(16), *([dma(HALVES, 1, mp - 1)] * 4),
            *(spread_scratch(mp) * 4),
        ],
        compiler_params=pltpu.CompilerParams(collective_id=0, has_side_effects=True, vmem_limit_bytes=ROOM),
    )(*inputs)


def dot_nt(left, right):
    return lax.dot_general(left, right, (((1,), (1,)), ((), ())), preferred_element_type=F32)


def dot_tn(left, right):
    return lax.dot_general(left, right, (((0,), (0,)), ((), ())), preferred_element_type=F32)


def pieces(parts, count, width):
    near, rows = width // parts // HALVES, count // FOLD
    for side in range(HALVES):
        for part in range(parts):
            for i in range(FOLD):
                cols = pl.ds((part * HALVES + side) * near, near)
                yield pl.ds(i * rows, rows), cols, side, part, pl.ds(i * near, near)


def gelu_parts(x):
    scale, cubic = math.sqrt(2.0 / math.pi), 0.044715
    square = x * x
    t = jnp.tanh(scale * x * (1.0 + cubic * square))
    half = 0.5 * (1.0 + t)
    slope = half + 0.5 * x * (1.0 - t * t) * (scale * (1.0 + 3.0 * cubic * square))
    return x * half, slope


COLS = 768


def feed_kernel(
    skip_row, y_ref, w_ref, s0_ref, tok, cot, w_out, gains, channel, up, down,
    act_out, up_part, down_part, out_part, g_parts, gy_out, gs0_out, gx2_out, sums, edge_out,
    y, o, x2, n2, inv2, b, b_t, cot_t, mix, acc_out, acc_b,
):
    step, steps = pl.program_id(0), pl.num_programs(0)
    parts = y_ref.shape[1]
    count, width = tok.shape
    tile = 128
    gain, skip = gains.at[1:2], channel.at[skip_row : skip_row + 1]

    @pl.when(step == 0)
    def _():
        for rows, cols, side, part, lanes in pieces(parts, count, width):
            y[rows, cols] = y_ref[side, part, :, lanes].astype(F32)

        def body(index, carry):
            rows = pl.ds(pl.multiple_of(index * tile, tile), tile)
            values = y[rows, :] + skip[...] * w_ref[rows, :]
            y[rows, :] = values
            mixed = (values * s0_ref[rows, :]).astype(BF)
            o[rows, :] = mixed
            residual = tok[rows, :].astype(F32) + dot_nt(mixed, w_out[...])
            x2[rows, :] = residual
            normed, inverse_std = norm_parts(residual)
            n2[rows, :] = normed
            inv2[rows, :] = jnp.broadcast_to(inverse_std, (tile, 128))
            b[rows, :] = (normed * gain[...]).astype(BF)
            return carry

        lax.fori_loop(0, count // tile, body, 0)
        b_t[...] = b[...].T
        cot_t[...] = cot[...].T
        acc_out[...] = jnp.zeros(acc_out.shape, F32)
        acc_b[...] = jnp.zeros(acc_b.shape, F32)

    up_w, down_w = up[0], down[0]
    value, slope = gelu_parts(mm(b[...], up_w))
    act = value.astype(BF)
    g_hpre = (mm(cot[...], down_w) * slope).astype(BF)
    up_part[0] = mm(b_t[...], g_hpre).astype(BF)
    down_part[0] = mm(cot_t[...], act).astype(BF)
    acc_out[...] += dot_nt(act, down_w)
    acc_b[...] += dot_nt(g_hpre, up_w)

    @pl.when(step == steps - 1)
    def _():
        sums[...] = jnp.zeros(sums.shape, F32)

        def body(index, carry):
            rows = pl.ds(pl.multiple_of(index * tile, tile), tile)
            act_out[rows, :] = (x2[rows, :] + acc_out[rows, :]).astype(BF)
            g_b, normed = acc_b[rows, :], n2[rows, :]
            sums[0:1, :] += jnp.sum(g_b * normed, axis=0, keepdims=True)
            g_x2 = cot[rows, :].astype(F32) + norm_back(g_b, gain[...], normed, inv2[rows, 0:1])
            gx2_out[rows, :] = g_x2
            low = g_x2.astype(BF)
            mix[rows, :] = low
            g_o = mm(low, w_out[...])
            g_y = g_o * s0_ref[rows, :]
            gy_out[rows, :] = g_y
            gs0_out[rows, :] = g_o * y[rows, :]
            sums[1:2, :] += jnp.sum(g_y * w_ref[rows, :], axis=0, keepdims=True)
            return carry

        lax.fori_loop(0, count // tile, body, 0)
        for rows, cols, side, part, lanes in pieces(parts, count, width):
            g_parts[side, part, :, lanes] = gy_out[rows, cols].astype(BF)
        edge_out[...] = gs0_out[pl.ds(0, EDGE), :].astype(BF)
        grad = dot_tn(mix[...], o[...])
        own = width // parts
        for part in range(parts):
            out_part[part] = grad[:, part * own : (part + 1) * own].astype(BF)


def feed(y_parts, w_own, s0, tokens, cotangent, w_out, gains, channel, skip_row, whole_up, whole_down):
    mp, width, hidden = whole_up.shape
    count = tokens.shape[0]
    own, cols = width // mp, COLS
    each = hidden // cols
    once = pl.Buffered(1)

    def fixed(shape):
        return pl.BlockSpec(shape, lambda i: (0,) * len(shape), pipeline_mode=once)

    def moving():
        return pl.BlockSpec((1, width, cols), lambda i: (i // each, 0, i % each))

    full, half = (count, width), y_parts.shape
    outs = [
        (full, BF), (whole_up.shape, BF), (whole_up.shape, BF), ((mp, width, own), BF), (half, BF),
        (full, F32), (full, F32), (full, F32), ((8, width), F32), ((EDGE, width), BF),
    ]
    out_specs = [moving() if i in (1, 2) else fixed(s) for i, (s, _) in enumerate(outs)]
    inputs = (y_parts, w_own, s0, tokens, cotangent, w_out, gains, channel)
    return pl.pallas_call(
        functools.partial(feed_kernel, skip_row),
        name="feed_forward",
        grid=(mp * each,),
        out_shape=tuple(struct(s, t) for s, t in outs),
        in_specs=[fixed(v.shape) for v in inputs] + [moving(), moving()],
        out_specs=tuple(out_specs),
        scratch_shapes=[
            pltpu.VMEM(full, F32), pltpu.VMEM(full, BF), pltpu.VMEM(full, F32), pltpu.VMEM(full, F32),
            pltpu.VMEM((count, 128), F32), pltpu.VMEM(full, BF), pltpu.VMEM((width, count), BF),
            pltpu.VMEM((width, count), BF), pltpu.VMEM(full, BF), pltpu.VMEM(full, F32), pltpu.VMEM(full, F32),
        ],
        compiler_params=pltpu.CompilerParams(vmem_limit_bytes=ROOM),
    )(*inputs, whole_up, whole_down)


class Late:
    def __init__(self, sources, targets, sem):
        self.copies = []
        for i, (source, target) in enumerate(zip(sources, targets)):
            copy = pltpu.make_async_copy(source, target, sem.at[i])
            copy.start()
            self.copies.append(copy)

    def need(self, *indices):
        for i in indices:
            self.copies[i].wait()


def short_backward(j, gs, z, channel, same, offsets, count, sums):
    tap_rows = [channel[3 * k + j : 3 * k + j + 1, :] for k in range(offsets)]
    g_z = None
    for k in range(offsets):
        later = gs[pl.ds(k, count), :]
        before = z[pl.ds(EDGE - k, count), :]
        if k:
            later = jnp.where(same[k][k : count + k], later, 0.0)
            before = jnp.where(same[k][:count], before, 0.0)
        g_z = tap_rows[k] * later if g_z is None else g_z + tap_rows[k] * later
        sums[pl.ds(3 * k + j, 1), :] = jnp.sum(gs[pl.ds(0, count), :] * before, axis=0, keepdims=True)
    return g_z


def post_steps(doc_count, offsets, len_ref, gw_ref, gw_edge, channel, gains, sums, held, late, work, stream_done):
    gy_ref, s2_ref, z1, a_ref, w1, s1_ref, z2, w2, ga0, n1_ref, inv1_ref, gx2_ref = held
    gw, gs, gz, marks = work
    parts = gw_ref.shape[1]
    count, width = gy_ref.shape
    near = width // parts // HALVES
    skip = channel[3 * offsets : 3 * offsets + 1, :]
    for rows, cols, side, part, lanes in pieces(parts, count, width):
        gw[rows, cols] = gw_ref[side, part, :, lanes].astype(F32)
    for side in range(HALVES):
        for part in range(parts):
            at = pl.ds((part * HALVES + side) * near, near)
            gw[pl.ds(count, EDGE), at] = gw_edge[side, part, :, 0:near].astype(F32)
    mark_same(marks, len_ref, doc_count, lax.axis_index("mp") * count - EDGE)
    same = [None] + [marks[k - 1, :, 0:1] > 0.0 for k in range(1, offsets)]
    late.need(0)
    gw[pl.ds(0, count), :] += skip * gy_ref[...]
    total = None
    for j, other, z, w, order in ((1, s2_ref, z1, w1, (1, 2, 3, 4)), (2, s1_ref, z2, w2, (5, 6, 7))):
        late.need(*order)
        gs[...] = gw[...] * other[...]
        gz[...] = short_backward(j, gs, z, channel, same, offsets, count, sums).astype(BF)
        stream_done(j, dot_tn(a_ref[pl.ds(EDGE, count), :], gz[...]))
        term = dot_nt(gz[...], w[...])
        total = term if total is None else total + term
    late.need(8, 9, 10, 11)
    total = total + ga0[...]
    sums[pl.ds(3 * offsets + 1, 1), :] = jnp.sum(total * n1_ref[pl.ds(EDGE, count), :], axis=0, keepdims=True)
    return total


def post_end(total, gains, held, input_grad):
    n1_ref, inv1_ref, gx2_ref = held[9:]
    count = gx2_ref.shape[0]
    normed, inverse_std = n1_ref[pl.ds(EDGE, count), :], inv1_ref[pl.ds(EDGE, count), 0:1]
    input_grad[...] = (gx2_ref[...] + norm_back(total, gains[0:1, :], normed, inverse_std)).astype(BF)


def post_kernel(doc_count, offsets, len_ref, gw_ref, gw_edge, channel, gains, sums_in, *refs):
    late_refs, refs = refs[:12], refs[12:]
    last_part, input_grad, sums, refs = refs[0], refs[1], refs[2], refs[3:]
    held, late_sem, work = refs[:12], refs[12], refs[13:]
    late = Late(late_refs, held, late_sem)
    parts, own = gw_ref.shape[1], last_part.shape[2] // 2
    sums[...] = sums_in[...]

    def stream_done(j, grad):
        for part in range(parts):
            last_part[part, :, pl.ds((j - 1) * own, own)] = grad[:, part * own : (part + 1) * own].astype(BF)

    total = post_steps(
        doc_count, offsets, len_ref, gw_ref, gw_edge, channel, gains, sums, held, late, work, stream_done
    )
    post_end(total, gains, held, input_grad)


def post_late(g_y, s1, s2, z, a, w_in, ga0, n1, inv1, g_x2):
    return [
        (g_y, None), (s2, None), (z, 1), (a, None), (w_in, 1), (s1, None), (z, 2), (w_in, 2), (ga0, None), (n1, None),
        (inv1, None), (g_x2, None),
    ]


def post_scratch(late, offsets, count, width):
    return [
        *[pltpu.VMEM(v.shape if i is None else v.shape[1:], v.dtype) for v, i in late],
        dma(len(late)),
        pltpu.VMEM((count + EDGE, width), F32),
        pltpu.VMEM((count + EDGE, width), F32),
        pltpu.VMEM((count, width), BF),
        pltpu.VMEM((offsets - 1, count + EDGE, 128), F32),
    ]


def choose(refs, late):
    return [r if i is None else r.at[i] for r, (_, i) in zip(refs, late)]


def post(lengths, offsets, gw_parts, gw_edge, channel, gains, sums_in, late):
    mp = gw_parts.shape[1]
    count, width = late[0][0].shape
    first = (gw_parts, gw_edge, channel, gains, sums_in)

    def kernel(*refs):
        start = 1 + len(first)
        end = start + len(late)
        post_kernel(lengths.shape[1], offsets, *refs[:start], *choose(refs[start:end], late), *refs[end:])

    return pl.pallas_call(
        kernel,
        name="mixer_post",
        out_shape=(struct((mp, width, 2 * width // mp), BF), struct((count, width), BF), struct((16, width), F32)),
        in_specs=[IN_SMEM] + [IN_VMEM] * len(first) + [IN_HBM] * len(late),
        out_specs=(IN_VMEM,) * 3,
        scratch_shapes=post_scratch(late, offsets, count, width),
        compiler_params=pltpu.CompilerParams(vmem_limit_bytes=ROOM),
    )(lengths, *first, *[v for v, _ in late])


def features(length, feature_count, count):
    step = np.arange(count)
    band = np.arange(1, (feature_count - 1) // 2 + 1)
    phase = ((step[:, None] * band[None, :]) % length).astype(np.float32) * np.float32(2.0 * math.pi / length)
    position = (step / length).astype(np.float32)
    table = np.concatenate([position[:, None], np.cos(phase), np.sin(phase)], axis=1)
    return table.astype(np.float32), position


def product(left, right):
    return jnp.dot(left, right, precision=FULL_PRECISION, preferred_element_type=F32)


def norm_parts(values):
    centred = values - jnp.mean(values, axis=-1, keepdims=True)
    inverse_std = lax.rsqrt(jnp.mean(centred * centred, axis=-1, keepdims=True) + EPS_NORM)
    return centred * inverse_std, inverse_std


def norm_back(grad, gain, normed, inverse_std):
    scaled = grad * gain
    mean = jnp.mean(scaled, axis=-1, keepdims=True)
    along = jnp.mean(scaled * normed, axis=-1, keepdims=True)
    return (scaled - mean - normed * along) * inverse_std


def to_parts(values, mp):
    count, width = values.shape
    near = width // mp // HALVES
    cut = values.reshape(FOLD, count // FOLD, mp, HALVES, near).transpose(3, 2, 1, 0, 4)
    return cut.reshape(HALVES, mp, count // FOLD, FOLD * near)


def forward_fallback(lengths, tokens, weights, gain_own, channel_own, taps, table, step_col, f_in, f_out, tables):
    mp, m = lax.axis_size("mp"), lax.axis_index("mp")
    count, width = tokens.shape
    own, shard = width // mp, weights[1].shape[0]
    first_shard = jnp.concatenate([*weights[0], weights[1]], axis=1)
    chunks = [v.astype(BF) for v in (first_shard, weights[2], weights[3])]
    gains = jnp.pad(gain_own.astype(BF), ((0, 14), (0, 128 - shard)))
    channel = jnp.pad(channel_own, ((0, 16 - channel_own.shape[0]), (0, 0)))
    edges = jnp.stack([tokens[count - EDGE :], tokens[:EDGE]])
    first, up, down, gains_all, channel_all, edges_all = gather_fallback(chunks, gains, channel, edges)
    first = first.reshape(mp, width, width)
    w_in = first[:, :, : 3 * own].reshape(mp, width, 3, own).transpose(1, 2, 0, 3).reshape(width, 3 * width)
    w_out = first[:, :, 3 * own :].transpose(1, 0, 2).reshape(width, width)
    gain_rows = gains_all[:, 0:8, :shard].transpose(1, 0, 2).reshape(8, width).astype(F32)
    chan_rows = channel_all.transpose(1, 0, 2).reshape(-1, width)
    position = m * count - EDGE + jnp.arange(count + 2 * EDGE, dtype=jnp.int32)
    doc = jnp.sum((position[:, None] >= jnp.cumsum(lengths[0])[None, :]).astype(jnp.int32), axis=1)
    doc = jnp.where(position < 0, -1, doc)
    n1, inv1 = norm_parts(jnp.concatenate([edges_all[0], tokens, edges_all[1]]).astype(F32))
    a = (n1 * gain_rows[0]).astype(BF)
    z = jnp.dot(a, w_in, preferred_element_type=F32)
    s = []
    for j in range(3):
        stream, total = z[:, j * width : (j + 1) * width], None
        for k in range(taps):
            part = stream[EDGE - k : stream.shape[0] - k]
            if k:
                part = jnp.where((doc[EDGE:] == doc[EDGE - k : doc.shape[0] - k])[:, None], part, 0.0)
            term = chan_rows[3 * k + j] * part
            total = term if total is None else total + term
        s.append(total)
    w_own = s[2][:count] * s[1][:count]
    phase = product(table, f_in)
    hidden = jnp.sin(phase)
    lane = (m * own + jnp.arange(own, dtype=jnp.int32)).astype(F32)
    decay = jnp.exp(-step_col * (FAST_DECAY + (SLOW_DECAY - FAST_DECAY) * lane / (width - 1)))
    w_parts = exchange([*to_parts(w_own.astype(BF), mp)], None, 3)
    filters = jnp.split(product(hidden, f_out) * decay, HALVES, axis=1)
    halves = [conv_forward(w_parts[i], lengths, filters[i], tables) for i in range(HALVES)]
    y_back = jnp.stack(exchange([v[0] for v in halves], None, 4))
    w_parts, spectrum = jnp.stack(w_parts), jnp.stack([v[1] for v in halves])
    return (
        w_parts, y_back, spectrum, hidden, phase, decay, gain_rows, chan_rows,
        z.reshape(-1, 3, width).transpose(1, 0, 2), s[0][:count], s[1], s[2], w_own, a, n1,
        jnp.broadcast_to(inv1, (inv1.shape[0], 128)), w_in.reshape(width, 3, width).transpose(1, 0, 2), w_out, up, down,
    )


def per_device(
    tokens, cotangent, doc_lengths, in_weight, out_weight, up_weight, down_weight, gains, channel_weight,
    filter_in, filter_out, in_rows, in_cols, out_rows, out_cols, up_rows, up_cols, down_rows, down_cols,
    gain_moment, channel_moment, filter_in_moment, filter_out_moment,
):
    dp, mp = lax.axis_size("dp"), lax.axis_size("mp")
    count, width = tokens.shape
    length = count * mp
    own = channel_weight.shape[1]
    rows = in_weight.shape[0]
    hidden = up_weight.shape[1]
    taps = (channel_weight.shape[0] - 1) // 3
    most = length // 2

    in_weight, gains, gain_moment = in_weight.transpose(1, 0, 2), gains.T, gain_moment.T

    table, step = features(length, filter_in.shape[0], most)
    tables = tuple(jnp.asarray(t) for t in transform_tables(count // 2))
    run = mixer_forward if dp == 8 else forward_fallback
    (
        w_parts, y_back, spectrum, hidden_filter, phase, decay, gain_rows, chan_rows, z, s0, s1, s2, w_own,
        a, n1, inv1, w_in, w_out, whole_up, whole_down,
    ) = run(
        doc_lengths, tokens, (in_weight, out_weight, up_weight, down_weight), gains, channel_weight, taps,
        table, step[:, None], filter_in, filter_out, tables,
    )
    whole_up = whole_up.reshape(mp, width, hidden)
    whole_down = whole_down.reshape(mp, width, hidden)

    activations, up_part, down_part, out_part, gy_parts, g_y, g_s0, g_x2, feed_sums, g_s0_own = feed(
        y_back, w_own, s0, tokens, cotangent, w_out, gain_rows, chan_rows, 3 * taps, whole_up, whole_down
    )

    up_part, down_part = [p.reshape(mp, dp, rows, hidden) for p in (up_part, down_part)]
    gw_back, gw_edge, sums, g_a0, fin_part, fout_part, *partials = mixer_backward(
        doc_lengths, taps, gy_parts, g_s0_own, channel_weight, feed_sums, up_part, down_part, g_s0, z, a, w_in,
        chan_rows, out_part, w_parts, tables, spectrum, decay, hidden_filter, filter_out, phase, table,
    )

    results = finish(
        doc_lengths, taps, (gw_back, gw_edge, chan_rows, gain_rows, sums),
        post_late(g_y, s1, s2, z, a, w_in, g_a0, n1, inv1, g_x2), partials, fin_part, fout_part,
        (
            in_weight, out_weight, in_rows, out_rows, up_rows, down_rows,
            in_cols, out_cols, up_cols, down_cols, gains, gain_moment,
        ),
        up_weight, down_weight,
        (channel_weight, channel_moment, filter_in, filter_in_moment, filter_out, filter_out_moment),
    )
    (
        input_grad, norm, in_g, out_g, up_g, down_g, gain_g, in_n, out_n, up_n, down_n, gain_n, gain_m,
        in_r, out_r, up_r, down_r, in_c, out_c, up_c, down_c,
        chan_g, chan_n, chan_m, fin_g, fin_n, fin_m, fout_g, fout_n, fout_m,
    ) = hand_out(results, own)
    return (
        activations, input_grad, norm.reshape(()),
        in_g.transpose(1, 0, 2), out_g, up_g, down_g, gain_g.T, chan_g, fin_g, fout_g,
        in_n.transpose(1, 0, 2), out_n, up_n, down_n, gain_n.T, chan_n, fin_n, fout_n,
        in_r, in_c, out_r, out_c, up_r, up_c, down_r, down_c, gain_m.T, chan_m, fin_m, fout_m,
    )


def solution(mesh):
    tokens, by_rows, by_cols, both = P(("dp", "mp"), None), P("dp", None), P(None, "mp"), P("dp", "mp")
    cube, vec_dp, vec_mp = P("dp", None, "mp"), P("dp"), P("mp")
    moments = (vec_dp, by_cols, vec_dp, vec_mp, vec_dp, vec_mp, vec_dp, vec_mp)
    weights = (cube, both, both, both, by_rows, by_cols, P(), by_cols)
    small = (by_rows, by_cols, P(), by_cols)
    return jax.shard_map(
        per_device,
        mesh=mesh,
        in_specs=(tokens, tokens, by_rows) + weights + moments + small,
        out_specs=(tokens, tokens, P()) + weights + weights + moments + small,
        check_vma=False,
    )
```

```python
import functools
import math

import jax
import jax.numpy as jnp
import ml_dtypes
import numpy as np
from jax import lax
from jax.experimental import pallas as pl
from jax.experimental.pallas import tpu as pltpu
from jax.sharding import PartitionSpec as P

EPS_NORM = 1e-05
MOMENT_DECAY = 0.5
CLIP_NORM = 1.0
CLIP_STEP = 0.25
STEP_RATE = 2.0
FAST_DECAY = 15.35
SLOW_DECAY = 3.07
FULL_PRECISION = lax.Precision.HIGHEST
BF = jnp.bfloat16
F32 = jnp.float32
MESH = pl.DeviceIdType.MESH
BLOCK = 256
EDGE = 16
HALVES = 2
FOLD = 4
ROOM = 62 << 20
IN_VMEM = pl.BlockSpec(memory_space=pltpu.VMEM)
IN_HBM = pl.BlockSpec(memory_space=pl.ANY)
IN_SMEM = pl.BlockSpec(memory_space=pltpu.SMEM)


def struct(shape, dtype):
    return jax.ShapeDtypeStruct(tuple(shape), dtype)


def transform_tables(block):
    freq = 2 * np.arange(block)[:, None] + 1
    angle = np.pi * (freq * np.arange(block)[None, :] % (4 * block)) / (2 * block)
    table = np.concatenate([np.cos(angle), -np.sin(angle)], axis=0).astype(np.float32)
    high = table.astype(ml_dtypes.bfloat16)
    low = (table - high.astype(np.float32)).astype(ml_dtypes.bfloat16)
    return high, low, np.ascontiguousarray(high.T), np.ascontiguousarray(low.T)


def mm(left, right):
    return lax.dot_general(left, right, (((1,), (0,)), ((), ())), preferred_element_type=F32)


def split(values):
    high = values.astype(BF)
    return high, (values - high.astype(F32)).astype(BF)


def load_rows(ref, start, count, lead=()):
    odd = lax.rem(start, 8)
    tile = ref[lead + (pl.ds(lax.div(start, 8), count // 8 + 1),)]
    width = tile.shape[-1]
    tile = pltpu.roll(tile, lax.rem(8 - odd, 8), axis=1)
    first = lax.broadcasted_iota(jnp.int32, (count // 8, 8, width), 1) < 8 - odd
    return jnp.where(first, tile[:-1], tile[1:]).reshape(count, width)


def tiles(values):
    return values.reshape(values.shape[0] // 8, 8, values.shape[1])


def unpack(target, source, channels):
    parts, rows, width = source.shape
    fold, count = width // channels, rows // 8
    for part in range(parts):
        for piece in range(fold):
            values = source[part, :, piece * channels : (piece + 1) * channels].astype(F32)
            target[pl.ds((part * fold + piece) * count, count), :, 0:channels] = tiles(values)


def pack_block(target, index, values, channels):
    rows = target.shape[1]
    fold, pieces = target.shape[2] // channels, values.shape[0] // rows
    for i in range(pieces):
        part, piece = divmod(index * pieces + i, fold)
        source = values[i * rows : (i + 1) * rows, 0:channels]
        target[part, :, pl.ds(piece * channels, channels)] = source.astype(target.dtype)


def beside(values):
    return [jnp.concatenate(values[i : i + 2], axis=1) for i in range(0, len(values), 2)]


def apart(values, lanes):
    return [v[:, i : i + lanes] for v in values for i in range(0, v.shape[1], lanes)]


def pair_rows(index, block, size):
    first = pl.multiple_of(index * size, size)
    return pl.ds(first, size), pl.ds(pl.multiple_of(block + first, size), size)


def signs(size, width, scale):
    odd = lax.broadcasted_iota(jnp.int32, (size, width), 0) % 2
    return jnp.where(odd == 0, scale, -scale).astype(F32)


def filter_spectrum(filter_ref, spectrum, raw, tables, block):
    count, lanes = raw.shape[0], raw.shape[2]
    high, low = tables[0][...], tables[1][...]
    terms = [split(filter_ref[pl.ds(lag * block, block), :]) for lag in range(count)]
    tops, rests = beside([t[0] for t in terms]), beside([t[1] for t in terms])
    done = [mm(high, t) + mm(high, r) + mm(low, t) for t, r in zip(tops, rests)]
    for lag, values in enumerate(apart(done, lanes)):
        raw[lag] = values
    scale = 1.0 / block

    def body(index, carry):
        re_rows, im_rows = pair_rows(index, block, 8)
        sign = signs(8, raw.shape[2], scale)
        for lag in range(count):
            re, im = raw[lag, re_rows, :] * scale, raw[lag, im_rows, :] * scale
            if lag:
                re = re - sign * raw[lag - 1, im_rows, :]
                im = im + sign * raw[lag - 1, re_rows, :]
            spectrum[lag, re_rows, :] = re
            spectrum[lag, im_rows, :] = im
        return carry

    lax.fori_loop(0, block // 8, body, 0)


def slot_blocks(source, target, tables, start, length, block):
    high, low = tables[0][...], tables[1][...]
    blocks = []
    for index in range(target.shape[0]):
        values = load_rows(source, start + index * block, block)
        inside = lax.broadcasted_iota(jnp.int32, values.shape, 0) + index * block < length
        blocks.append(jnp.where(inside, values, 0.0).astype(BF))
    done = [mm(high, values) + mm(low, values) for values in beside(blocks)]
    for index, values in enumerate(apart(done, target.shape[2])):
        target[index] = values


def inverse(top, rest, tables):
    high, low = tables[2][...], tables[3][...]
    count, lanes = top.shape[0], top.shape[2]
    tops, rests = beside([top[i] for i in range(count)]), beside([rest[i] for i in range(count)])
    return apart([mm(high, t) + mm(high, r) + mm(low, t) for t, r in zip(tops, rests)], lanes)


def document_starts(len_ref, count):
    starts, at = [], jnp.int32(0)
    for slot in range(count):
        starts.append(at)
        at = at + len_ref[0, slot]
    return starts


def merge_slots(slots, starts, put, total, block, most):
    for index in range(total // block):
        first = index * block
        merged = None
        for slot, start in enumerate(starts):
            at = jnp.clip(first - start, -block, most) + block
            values = load_rows(slots, at, block, (slot,))
            if merged is None:
                merged = values
            else:
                inside = lax.broadcasted_iota(jnp.int32, values.shape, 0) + first >= start
                merged = jnp.where(inside, values, merged)
        put(index, merged)


def forward_products(spectrum, raw, top, rest, block):
    count = raw.shape[0]

    def body(index, carry):
        re_rows, im_rows = pair_rows(index, block, 16)
        hr = [spectrum[i, re_rows, :] for i in range(count)]
        hi = [spectrum[i, im_rows, :] for i in range(count)]
        xr = [raw[i, re_rows, :] for i in range(count)]
        xi = [raw[i, im_rows, :] for i in range(count)]
        for out in range(count):
            re = hr[0] * xr[out] - hi[0] * xi[out]
            im = hr[0] * xi[out] + hi[0] * xr[out]
            for lag in range(1, out + 1):
                re = re + (hr[lag] * xr[out - lag] - hi[lag] * xi[out - lag])
                im = im + (hr[lag] * xi[out - lag] + hi[lag] * xr[out - lag])
            top[out, re_rows, :], rest[out, re_rows, :] = split(re)
            top[out, im_rows, :], rest[out, im_rows, :] = split(im)
        return carry

    lax.fori_loop(0, block // 16, body, 0)


def backward_products(spectrum, grad, raw, total, top, rest, block, first_slot):
    count = raw.shape[0]

    def body(index, carry):
        re_rows, im_rows = pair_rows(index, block, 16)
        gr = [grad[i, re_rows, :] for i in range(count)]
        gi = [grad[i, im_rows, :] for i in range(count)]
        hr = [spectrum[i, re_rows, :] for i in range(count)]
        hi = [spectrum[i, im_rows, :] for i in range(count)]
        for out in range(count):
            re = hr[0] * gr[out] + hi[0] * gi[out]
            im = hr[0] * gi[out] - hi[0] * gr[out]
            for later in range(out + 1, count):
                lag = later - out
                re = re + (hr[lag] * gr[later] + hi[lag] * gi[later])
                im = im + (hr[lag] * gi[later] - hi[lag] * gr[later])
            top[out, re_rows, :], rest[out, re_rows, :] = split(re)
            top[out, im_rows, :], rest[out, im_rows, :] = split(im)
        xr = [raw[i, re_rows, :] for i in range(count)]
        xi = [raw[i, im_rows, :] for i in range(count)]
        for lag in range(count):
            re = im = None
            for at in range(count - lag):
                a = xr[at] * gr[at + lag] + xi[at] * gi[at + lag]
                b = xr[at] * gi[at + lag] - xi[at] * gr[at + lag]
                re = a if re is None else re + a
                im = b if im is None else im + b
            if not first_slot:
                re = re + total[lag, re_rows, :]
                im = im + total[lag, im_rows, :]
            total[lag, re_rows, :] = re
            total[lag, im_rows, :] = im
        return carry

    lax.fori_loop(0, block // 16, body, 0)


def filter_gradient(total, top, rest, tables, out_ref, lanes, channels, block):
    count, width = total.shape[0], total.shape[2]
    scale = 1.0 / block

    def body(index, carry):
        re_rows, im_rows = pair_rows(index, block, 16)
        sign = signs(16, width, 1.0)
        for lag in range(count):
            re, im = total[lag, re_rows, :], total[lag, im_rows, :]
            if lag + 1 < count:
                re = re + sign * total[lag + 1, im_rows, :]
                im = im - sign * total[lag + 1, re_rows, :]
            top[lag, re_rows, :], rest[lag, re_rows, :] = split(re * scale)
            top[lag, im_rows, :], rest[lag, im_rows, :] = split(im * scale)
        return carry

    lax.fori_loop(0, block // 16, body, 0)
    for lag, values in enumerate(inverse(top, rest, tables)):
        out_ref[pl.ds(lag * block, block), lanes] = values[:, 0:channels]


def conv_forward_steps(doc_count, len_ref, x_ref, tables, y_ref, spectrum, full, raw, top, rest, slots, between):
    block, blocks = spectrum.shape[1] // 2, spectrum.shape[0]
    channels = x_ref.shape[2] // FOLD
    unpack(full, x_ref, channels)
    starts = document_starts(len_ref, doc_count)
    for slot in range(doc_count):
        slot_blocks(full, raw, tables, starts[slot], len_ref[0, slot], block)
        forward_products(spectrum, raw, top, rest, block)
        for out, values in enumerate(inverse(top, rest, tables)):
            slots[slot, pl.ds((1 + out) * block // 8, block // 8)] = tiles(values)
        between(slot)

    def put(index, values):
        pack_block(y_ref, index, values, channels)

    tokens = math.prod(x_ref.shape) // channels
    merge_slots(slots, starts, put, tokens, block, blocks * block)


def conv_backward_steps(
    doc_count, len_ref, g_ref, x_ref, spectrum, skip, tables, gw_ref, edge_ref, gf_ref, lanes,
    g_full, x_full, grad, raw, top, rest, total, slots, between,
):
    block, blocks, channels = spectrum.shape[1] // 2, spectrum.shape[0], x_ref.shape[2] // FOLD
    unpack(g_full, g_ref, channels)
    unpack(x_full, x_ref, channels)
    starts = document_starts(len_ref, doc_count)
    for slot in range(doc_count):
        slot_blocks(g_full, grad, tables, starts[slot], len_ref[0, slot], block)
        slot_blocks(x_full, raw, tables, starts[slot], len_ref[0, slot], block)
        backward_products(spectrum, grad, raw, total, top, rest, block, slot == 0)
        for out, values in enumerate(inverse(top, rest, tables)):
            slots[slot, pl.ds((1 + out) * block // 8, block // 8)] = tiles(values)
        between(slot)
    edge_ref[...] = jnp.zeros(edge_ref.shape, edge_ref.dtype)
    parts = x_ref.shape[0]
    tokens = math.prod(x_ref.shape) // channels
    each = tokens // parts // block

    def put(index, values):
        pack_block(gw_ref, index, values, channels)
        if index % each == 0 and index:
            own = g_full[pl.ds(index * block // 8, EDGE // 8)].reshape(values[0:EDGE].shape)[:, 0:channels] * skip
            edge_ref[index // each - 1, :, 0:channels] = (values[0:EDGE, 0:channels] + own).astype(edge_ref.dtype)

    merge_slots(slots, starts, put, tokens, block, blocks * block)
    between(doc_count)
    filter_gradient(total, top, rest, tables, gf_ref, lanes, channels, block)


def lanes_for(channels):
    return -(-channels // 128) * 128


def conv_scratch(x_shape, blocks, block, docs):
    channels = x_shape[2] // FOLD
    tokens, lanes = math.prod(x_shape) // channels, lanes_for(channels)
    wide = (blocks, 2 * block, lanes)
    full = pltpu.VMEM(((tokens + blocks * block) // 8 + 1, 8, lanes), F32)
    slots = pltpu.VMEM((docs, (blocks + 2) * block // 8 + 1, 8, lanes), F32)
    return full, pltpu.VMEM(wide, F32), pltpu.VMEM(wide, BF), slots


def conv_forward_kernel(doc_count, len_ref, x_ref, filter_ref, t0, t1, t2, t3, y_ref, spectrum, full, raw, top, rest, slots):
    tables = (t0, t1, t2, t3)
    filter_spectrum(filter_ref, spectrum, raw, tables, spectrum.shape[1] // 2)
    conv_forward_steps(
        doc_count, len_ref, x_ref, tables, y_ref, spectrum, full, raw, top, rest, slots, lambda slot: None
    )


def conv_forward(x, lengths, filters, tables):
    docs, block = lengths.shape[1], tables[0].shape[1]
    blocks, channels = filters.shape[0] // block, filters.shape[1]
    filters = jnp.pad(filters, ((0, 0), (0, lanes_for(channels) - channels)))
    full, raw, low, slots = conv_scratch(x.shape, blocks, block, docs)
    return pl.pallas_call(
        functools.partial(conv_forward_kernel, docs),
        name="conv_forward",
        out_shape=(struct(x.shape, BF), struct((blocks, 2 * block, filters.shape[1]), F32)),
        in_specs=[IN_SMEM] + [IN_VMEM] * 6,
        out_specs=(IN_VMEM, IN_VMEM),
        scratch_shapes=[full, raw, low, low, slots],
        compiler_params=pltpu.CompilerParams(vmem_limit_bytes=ROOM),
    )(lengths, x, filters, *tables)


def conv_backward_kernel(doc_count, len_ref, g_ref, x_ref, spectrum, skip_ref, t0, t1, t2, t3, gw_ref, edge_ref, gf_ref, *work):
    conv_backward_steps(
        doc_count, len_ref, g_ref, x_ref, spectrum, skip_ref[...], (t0, t1, t2, t3), gw_ref, edge_ref, gf_ref,
        slice(None), *work, lambda slot: None,
    )


def conv_backward(g, x, lengths, spectrum, skip_gain, tables):
    blocks, block, channels = spectrum.shape[0], spectrum.shape[1] // 2, x.shape[2] // FOLD
    docs = lengths.shape[1]
    full, raw, low, slots = conv_scratch(x.shape, blocks, block, docs)
    return pl.pallas_call(
        functools.partial(conv_backward_kernel, docs),
        name="conv_backward",
        out_shape=(
            struct(x.shape, BF),
            struct((x.shape[0], EDGE, lanes_for(channels)), BF),
            struct((blocks * block, channels), F32),
        ),
        in_specs=[IN_SMEM] + [IN_VMEM] * 8,
        out_specs=(IN_VMEM,) * 3,
        scratch_shapes=[full, full, raw, raw, low, low, raw, slots],
        compiler_params=pltpu.CompilerParams(vmem_limit_bytes=ROOM),
    )(lengths, g, x, spectrum, skip_gain, *tables)


def turned(value, bit):
    return value + bit - 2 * bit * ((value // bit) % 2)


def send(source, target, send_sem, recv_sem, device):
    copy = pltpu.make_async_remote_copy(
        src_ref=source,
        dst_ref=target,
        send_sem=send_sem,
        recv_sem=recv_sem,
        device_id=device,
        device_id_type=MESH,
    )
    copy.start()
    return copy


def greet(peers):
    barrier = pltpu.get_barrier_semaphore()
    for peer in peers:
        pl.semaphore_signal(barrier, inc=1, device_id=peer, device_id_type=MESH)
    pl.semaphore_wait(barrier, len(peers))


def ring(me, count):
    return [lax.rem(me + step, count) for step in range(1, count)]


def dma(*shape):
    return pltpu.SemaphoreType.DMA(shape)


def gather_fallback(chunks, gains, channel, edges):
    mp = lax.axis_size("mp")
    down = [(i, (i + 1) % mp) for i in range(mp)]
    up = [(i, (i - 1) % mp) for i in range(mp)]
    spread = [lax.all_gather(lax.all_gather(c, "dp"), "mp") for c in chunks]
    return (
        *spread,
        lax.all_gather(gains, "dp"),
        lax.all_gather(channel, "mp"),
        jnp.stack([lax.ppermute(edges[0], "mp", down), lax.ppermute(edges[1], "mp", up)]),
    )


def exchange_kernel(count, has_edge, *refs):
    sources, refs = refs[: count + has_edge], refs[count + has_edge :]
    targets, refs = refs[: count + has_edge], refs[count + has_edge :]
    send_sem, recv_sem, edge_send, edge_recv = refs
    d, m, mp = lax.axis_index("dp"), lax.axis_index("mp"), lax.axis_size("mp")
    greet([(d, e) for e in ring(m, mp)])
    copies = []
    for step, e in reversed(list(enumerate(ring(m, mp)))):
        for i in range(count):
            copies.append(
                send(sources[i].at[e], targets[i].at[m], send_sem.at[i, step], recv_sem.at[i, step], (d, e))
            )
    if has_edge:
        before = lax.rem(m + mp - 1, mp)
        copies.append(send(sources[count], targets[count], edge_send.at[0], edge_recv.at[0], (d, before)))
    for i in range(count):
        targets[i][m] = sources[i][m]
    for copy in copies:
        copy.wait()


def exchange(arrays, edge, collective_id):
    mp, count = lax.axis_size("mp"), len(arrays)
    inputs = list(arrays) + ([] if edge is None else [edge])
    return pl.pallas_call(
        functools.partial(exchange_kernel, count, int(edge is not None)),
        name="exchange_%d" % collective_id,
        out_shape=tuple(struct(a.shape, a.dtype) for a in inputs),
        in_specs=[IN_VMEM] * len(inputs),
        out_specs=(IN_VMEM,) * len(inputs),
        scratch_shapes=[dma(count, mp - 1), dma(count, mp - 1), dma(1), dma(1)],
        compiler_params=pltpu.CompilerParams(
            collective_id=collective_id, has_side_effects=True, vmem_limit_bytes=ROOM
        ),
    )(*inputs)


class Flow:
    def __init__(self, part, refs, lanes=slice(None)):
        self.part, self.lanes = part, lanes
        (self.own, self.from_core, self.from_y2, self.from_x2, self.from_x1, self.from_y1, self.from_z) = refs[:7]
        self.own_sem, self.p_send, self.p_recv, self.z_send, self.z_recv = refs[7:]
        self.d, self.m, self.mp = lax.axis_index("dp"), lax.axis_index("mp"), lax.axis_size("mp")
        self.half = self.mp // 2
        self.y, self.x, self.core = self.d // 4, (self.d // 2) % 2, self.d % 2
        self.pending = []

    def push(self, slot, source, target, bit):
        peer = (turned(self.d, bit), self.m)
        copy = send(source, target, self.p_send.at[slot], self.p_recv.at[slot], peer)
        self.pending.append(copy)
        return copy

    def start(self):
        self.copy = self.push(0, self.part.at[:, :, :, 1 - self.core, :, self.lanes], self.from_core, 1)
        self.local = pltpu.make_async_copy(self.part.at[:, :, :, self.core, :, self.lanes], self.own, self.own_sem.at[0])
        self.local.start()

    def core_stage(self):
        own, half, y, x = self.own, self.half, self.y, self.x
        self.local.wait()
        self.copy.wait_recv()

        def body(i, carry):
            at = (i // 4, (i // 2) % 2, i % 2)
            own[at] = own[at] + self.from_core[at]
            return carry

        lax.fori_loop(0, self.mp * 4, body, 0)
        low, high = pl.ds(0, half), pl.ds(half, self.mp - half)
        self.copies = [
            self.push(1, own.at[low, 1 - y], self.from_y2, 4),
            self.push(2, own.at[high, :, 1 - x], self.from_x2, 2),
        ]

    def second_sum(self):
        own, half, y, x = self.own, self.half, self.y, self.x
        for copy in self.copies:
            copy.wait_recv()

        def body(i, carry):
            a, b = i // 2, i % 2
            own[a, y, b] = own[a, y, b] + self.from_y2[a, b]
            own[half + a, b, x] = own[half + a, b, x] + self.from_x2[a, b]
            return carry

        lax.fori_loop(0, half * 2, body, 0)

    def second_stage(self):
        own, half, y, x = self.own, self.half, self.y, self.x
        self.second_sum()
        low, high = pl.ds(0, half), pl.ds(half, self.mp - half)
        self.copies = [
            self.push(3, own.at[low, y, 1 - x], self.from_x1, 2),
            self.push(4, own.at[high, 1 - y, x], self.from_y1, 4),
        ]

    def third_stage(self):
        own, half, y, x = self.own, self.half, self.y, self.x
        for copy in self.copies:
            copy.wait_recv()

        def body(a, carry):
            own[a, y, x] = own[a, y, x] + self.from_x1[a]
            own[half + a, y, x] = own[half + a, y, x] + self.from_y1[a]
            return carry

        lax.fori_loop(0, half, body, 0)

    def send_z(self):
        self.copies = [
            send(
                self.own.at[e, self.y, self.x], self.from_z.at[step], self.z_send.at[step], self.z_recv.at[step],
                (self.d, e),
            )
            for step, e in enumerate(ring(self.m, self.mp))
        ]
        self.pending.extend(self.copies)

    def finish(self, out):
        for copy in self.copies:
            copy.wait_recv()
        total = self.own[self.m, self.y, self.x].astype(F32)
        for step in range(self.mp - 1):
            total = total + self.from_z[step].astype(F32)
        out[:, self.lanes] = total

    def drain(self):
        for copy in self.pending:
            copy.wait_send()


FLOW_REFS = 12


def flow_scratch(mp, block, over_z=True):
    half = mp // 2
    leads = ((mp, 2, 2), (mp, 2, 2), (half, 2), (mp - half, 2), (half,), (mp - half,))
    last = (mp - 1,) + block if over_z else (1, 16, 128)
    return [pltpu.VMEM(lead + block, BF) for lead in leads] + [pltpu.VMEM(last, BF)] + [dma(1), dma(5), dma(5), dma(mp - 1), dma(mp - 1)]


class SmallSums:
    def __init__(self, small, outs, wide, refs):
        count = len(small)
        self.small, self.outs, self.wide = small, outs, wide
        self.running, self.from_dp, self.from_mp = [refs[i * count : (i + 1) * count] for i in range(3)]
        self.s_send, self.s_recv = refs[3 * count :]
        self.pending = []

    def start(self, stage):
        bit = (1, 2, 4)[stage]
        d, m = lax.axis_index("dp"), lax.axis_index("mp")
        if stage == 0:
            for i, ref in enumerate(self.small):
                self.running[i][0] = ref[...]
        self.copies = []
        for i in range(len(self.small)):
            at = i * 8 + stage
            self.copies.append(
                send(
                    self.running[i].at[stage], self.from_dp[i].at[stage], self.s_send.at[at], self.s_recv.at[at],
                    (turned(d, bit), m),
                )
            )
        self.pending.extend(self.copies)

    def end(self, stage):
        for i, copy in enumerate(self.copies):
            copy.wait_recv()
            self.running[i][stage + 1] = self.running[i][stage] + self.from_dp[i][stage]

    def start_mp(self):
        d, m, mp = lax.axis_index("dp"), lax.axis_index("mp"), lax.axis_size("mp")
        self.copies = []
        for i, wide in enumerate(self.wide):
            if wide:
                for step, e in enumerate(ring(m, mp)):
                    at = i * 8 + 3 + step
                    self.copies.append(
                        send(
                            self.running[i].at[3], self.from_mp[i].at[m], self.s_send.at[at], self.s_recv.at[at],
                            (d, e),
                        )
                    )
                self.from_mp[i][m] = self.running[i][3]
        self.pending.extend(self.copies)

    def end_mp(self):
        for copy in self.copies:
            copy.wait_recv()
        for i, wide in enumerate(self.wide):
            if wide:
                total = self.from_mp[i][0]
                for e in range(1, lax.axis_size("mp")):
                    total = total + self.from_mp[i][e]
                self.outs[i][...] = total
            else:
                self.outs[i][...] = self.running[i][3]

    def drain(self):
        for copy in self.pending:
            copy.wait_send()


def small_scratch(small, mp):
    scratch = []
    for lead in (4, 3, mp):
        scratch += [pltpu.VMEM((lead,) + s.shape, F32) for s in small]
    return scratch + [dma(8 * len(small)), dma(8 * len(small))]


def scatter_fallback(part):
    over_mp = lax.psum_scatter(part, "mp", scatter_dimension=0)
    return lax.psum_scatter(over_mp, "dp", scatter_dimension=0).astype(F32)


def cored(part):
    return part.reshape((part.shape[0], 2, 2, 2) + part.shape[2:])


class Blocks:
    def __init__(self, pairs, send_sem, recv_sem):
        self.pairs, self.send_sem, self.recv_sem = pairs, send_sem, recv_sem
        self.d, self.m, self.mp = lax.axis_index("dp"), lax.axis_index("mp"), lax.axis_size("mp")

    def start(self):
        self.copies = []
        for step, e in reversed(list(enumerate(ring(self.m, self.mp)))):
            for i, (source, target) in enumerate(self.pairs):
                sems = self.send_sem.at[i, step], self.recv_sem.at[i, step]
                self.copies.append(send(source.at[e], target.at[self.m], *sems, (self.d, e)))
        for source, target in self.pairs:
            target[self.m] = source[self.m]

    def arrive(self):
        for copy in self.copies:
            copy.wait_recv()

    def drain(self):
        for copy in self.copies:
            copy.wait_send()


def stream_zero(offsets, edge, gs, z, w, channel, marks, sums, feed_sums):
    count = gs.shape[0] - EDGE
    same = [None] + [marks[k - 1, :, 0:1] > 0.0 for k in range(1, offsets)]
    gs[pl.ds(count, EDGE), :] = edge[...].astype(F32)
    sums[...] = jnp.zeros(sums.shape, F32)
    g_z = short_backward(0, gs, z, channel, same, offsets, count, sums).astype(BF)
    sums[pl.ds(3 * offsets, 1), :] = feed_sums[1:2, :]
    sums[pl.ds(3 * offsets + 2, 1), :] = feed_sums[0:1, :]
    return g_z, dot_nt(g_z, w[...])


def mixer_backward_kernel(doc_count, offsets, len_ref, g_parts, edge, channel_own, feed_sums, part_a, part_b, *refs):
    late_refs, refs = refs[:17], refs[17:]
    gw_back, gw_edge_back, sums, ga0, fin_part, fout_part, partial_a, b_low, b_high, part_c, refs = *refs[:10], refs[10:]
    held, refs = refs[:16], refs[16:]
    (
        late_sem, edge_back, gs, marks, gf_ref, g_in, gw, gw_edge, g_full, x_full, grad, raw,
        top, rest, total, slots, b_send, b_recv, c_send, c_recv, e_sem, *refs,
    ) = refs
    a_refs, b_refs = refs[:FLOW_REFS], refs[FLOW_REFS:]
    z, acts, w, channel, out_part, x_ref, t0, t1, t2, t3, spectrum, decay, hidden, f_out, phase, table = held
    tables = (t0, t1, t2, t3)
    parts = x_ref.shape[1]
    near = x_ref.shape[3] // FOLD
    half = near * HALVES
    own_count = ga0.shape[0]
    d, m, mp = lax.axis_index("dp"), lax.axis_index("mp"), lax.axis_size("mp")
    a, b = Flow(part_a, a_refs), Flow(part_b, b_refs)
    incoming, outgoing = [], []
    for side in range(HALVES):
        incoming.append(Blocks([(g_parts.at[side], g_in.at[side])], b_send.at[side], b_recv.at[side]))
        pairs = [(gw.at[side], gw_back.at[side]), (gw_edge.at[side], gw_edge_back.at[side])]
        outgoing.append(Blocks(pairs, c_send.at[side], c_recv.at[side]))
    late = Late(late_refs, (gs.at[pl.ds(0, own_count)],) + tuple(held), late_sem)
    greet([(turned(d, bit), m) for bit in (1, 2, 4)] + [(d, e) for e in ring(m, mp)])
    edge_copy = send(edge, edge_back, e_sem.at[0], e_sem.at[1], (d, lax.rem(m + mp - 1, mp)))
    for copies in incoming:
        copies.start()
    a.start()
    mark_same(marks, len_ref, doc_count, m * own_count - EDGE)
    a.core_stage()
    b.start()
    late.need(0, 1, 2, 3, 4, 5)
    edge_copy.wait_recv()
    g_z, back = stream_zero(offsets, edge_back, gs, z, w, channel, marks, sums, feed_sums)
    ga0[...] = back
    size = part_c.shape[4]
    for first in range(0, parts, 2):
        in_grad = dot_tn(acts[pl.ds(EDGE, own_count), :], g_z[:, first * half : (first + 2) * half])
        for part in range(first, first + 2):
            cols = slice((part - first) * half, (part - first + 1) * half)
            for owner in range(8):
                at = (part, owner // 4, owner // 2 % 2, owner % 2, slice(None))
                rows = slice(owner * size, (owner + 1) * size)
                part_c[at + (pl.ds(0, half),)] = in_grad[rows, cols].astype(BF)
                part_c[at + (pl.ds(half, half),)] = out_part[part, rows]
    late.need(*range(6, 17))
    skip = channel_own[channel_own.shape[0] - 1 :, :]

    def first_side(step):
        if step == 0:
            b.core_stage()
        if step == 2:
            a.second_stage()

    def last_side(step):
        if step == doc_count:
            a.third_stage()

    for side in range(HALVES):
        incoming[side].arrive()
        between = (first_side, last_side)[side]
        lanes = pl.ds(side * near, near)

        def after(step, side=side, between=between):
            if step == doc_count:
                outgoing[side].start()
            between(step)

        conv_backward_steps(
            doc_count, len_ref, g_in.at[side], x_ref.at[side], spectrum.at[side], skip[:, side * near : (side + 1) * near],
            tables, gw.at[side], gw_edge.at[side], gf_ref, lanes, g_full, x_full, grad, raw, top, rest, total, slots, after,
        )
    g_raw = gf_ref[...] * decay[...]
    fout_part[...] = near_product(hidden[...], g_raw, dot_tn)
    fin_part[...] = near_product(table[...], near_product(g_raw, f_out[...], dot_nt) * jnp.cos(phase[...]), dot_tn)
    for e in range(parts):
        partial_a[e] = a.own[e, a.y, a.x]
    b.second_sum()
    for e in range(parts // 2):
        for other in range(2):
            b_low[e, other] = b.own[e, b.y, other]
            b_high[e, other] = b.own[parts // 2 + e, other, b.x]
    for copies in outgoing:
        copies.arrive()
    edge_copy.wait_send()
    for copies in incoming + outgoing:
        copies.drain()
    for flow in (a, b):
        flow.drain()


def mixer_backward(
    lengths, offsets, g_parts, edge, channel_own, feed_sums, part_a, part_b, g_s0, z, a, w_in, channel, out_part, x,
    tables, spectrum, decay, hidden, f_out, phase, table,
):
    dp, mp = lax.axis_size("dp"), lax.axis_size("mp")
    parts, docs = x.shape[1], lengths.shape[1]
    blocks, block, near = spectrum.shape[1], spectrum.shape[2] // 2, x.shape[3] // FOLD
    half, width = HALVES * near, 2 * HALVES * near
    size = part_a.shape[2]
    full = channel.shape[1]
    if dp != 8:
        g_in = exchange([*g_parts], edge, 5)
        edge_back = g_in[HALVES]
        halves = []
        for side in range(HALVES):
            skip = channel_own[-1:, side * near : (side + 1) * near]
            halves.append(conv_backward(g_in[side], x[side], lengths, spectrum[side], skip, tables))
        g_raw = jnp.concatenate([v[2] for v in halves], axis=1) * decay
        fin, fout = product(table.T, product(g_raw, f_out.T) * jnp.cos(phase)), product(hidden.T, g_raw)
        backs = exchange([v[i] for i in range(2) for v in halves], None, 6)
        gw_back, gw_edge_back = jnp.stack(backs[:HALVES]), jnp.stack(backs[HALVES:])
        count = g_s0.shape[0]
        gs = jnp.concatenate([g_s0, edge_back.astype(F32)])
        position = lax.axis_index("mp") * count - EDGE + jnp.arange(count + 2 * EDGE, dtype=jnp.int32)
        doc = jnp.sum((position[:, None] >= jnp.cumsum(lengths[0])[None, :]).astype(jnp.int32), axis=1)
        doc = jnp.where(position < 0, -1, doc)
        same = [None] + [(doc[EDGE:] == doc[EDGE - k : doc.shape[0] - k])[:, None] for k in range(1, offsets)]
        g_z, sums = None, jnp.zeros((16, full), F32)
        for k in range(offsets):
            later, before = gs[k : count + k], z[0, EDGE - k : EDGE - k + count]
            if k:
                later, before = jnp.where(same[k][k : count + k], later, 0.0), jnp.where(same[k][:count], before, 0.0)
            g_z = channel[3 * k] * later if g_z is None else g_z + channel[3 * k] * later
            sums = sums.at[3 * k].set(jnp.sum(gs[:count] * before, axis=0))
        sums = sums.at[3 * offsets].set(feed_sums[1]).at[3 * offsets + 2].set(feed_sums[0])
        g_z = g_z.astype(BF)
        grad = dot_tn(a[EDGE : EDGE + count], g_z).reshape(full, mp, half).transpose(1, 0, 2).astype(BF)
        part_c = jnp.concatenate([grad, out_part], axis=2).reshape(mp, dp, size, width)
        over_dp = [lax.psum_scatter(p, "dp", scatter_dimension=1) for p in (part_a, part_b)]
        return (
            gw_back, gw_edge_back, sums, dot_nt(g_z, w_in[0]), fin, fout, *over_dp, None, part_c,
        )
    edge_shape = (HALVES, parts, EDGE, lanes_for(near))
    own, own_c = part_a.shape[2:], (size, width)
    rows, raw, low, slots = conv_scratch(x.shape[1:], blocks, block, docs)
    first = (g_parts, edge, channel_own, feed_sums)
    late = [
        (g_s0, None), (z, 0), (a, None), (w_in, 0), (channel, None), (out_part, None), (x, None),
        *[(t, None) for t in tables], (spectrum, None), (decay, None), (hidden, None), (f_out, None), (phase, None),
        (table, None),
    ]
    fin, fout = struct((table.shape[1], hidden.shape[1]), F32), struct((hidden.shape[1], half), F32)
    longer = (g_s0.shape[0] + EDGE, full)

    def kernel(*refs):
        start = 3 + len(first)
        chosen = [r if i is None else r.at[i] for r, (_, i) in zip(refs[start : start + len(late)], late)]
        mixer_backward_kernel(docs, offsets, *refs[:start], *chosen, *refs[start + len(late) :])

    return pl.pallas_call(
        kernel,
        name="mixer_backward",
        out_shape=(
            struct(x.shape, BF), struct(edge_shape, BF), struct((16, full), F32), struct(g_s0.shape, F32), fin, fout,
            struct((mp,) + own, BF), *[struct((mp // 2, 2) + own, BF)] * 2, struct((mp, 2, 2, 2) + own_c, BF),
        ),
        in_specs=[IN_SMEM] + [IN_VMEM] * len(first) + [IN_HBM] * (2 + len(late)),
        out_specs=(IN_VMEM,) * 10,
        scratch_shapes=[
            *[pltpu.VMEM(v.shape if i is None else v.shape[1:], v.dtype) for v, i in late[1:]],
            dma(len(late)), pltpu.VMEM(edge.shape, BF), pltpu.VMEM(longer, F32),
            pltpu.VMEM((offsets - 1, longer[0], 128), F32),
            pltpu.VMEM((blocks * block, half), F32), pltpu.VMEM(x.shape, BF), pltpu.VMEM(x.shape, BF),
            pltpu.VMEM(edge_shape, BF), rows, rows, raw, raw, low, low, raw, slots,
            dma(HALVES, 1, mp - 1), dma(HALVES, 1, mp - 1), dma(HALVES, 2, mp - 1), dma(HALVES, 2, mp - 1), dma(2),
            *flow_scratch(mp, own, False), *flow_scratch(mp, own, False),
        ],
        compiler_params=pltpu.CompilerParams(collective_id=5, has_side_effects=True, vmem_limit_bytes=ROOM),
    )(lengths, *first, cored(part_a), cored(part_b), *[v for v, _ in late])


def spread_sum(block, slots, send_sem, recv_sem, axis, first):
    d, m = lax.axis_index("dp"), lax.axis_index("mp")
    count = lax.axis_size(axis)
    me = d if axis == "dp" else m
    copies = []
    for step, e in enumerate(ring(me, count)):
        peer = (e, m) if axis == "dp" else (d, e)
        copies.append(send(block, slots.at[me], send_sem.at[first + step], recv_sem.at[first + step], peer))
    slots[me] = block[...]
    for copy in copies:
        copy.wait()
    total = slots[0]
    for e in range(1, count):
        total = total + slots[e]
    return total


def total_of(values):
    return jnp.sum(jnp.sum(values, axis=1, keepdims=True), axis=0, keepdims=True)


def lanes_of(items):
    lane = lax.broadcasted_iota(jnp.int32, (1, 128), 1)
    row = jnp.zeros((1, 128), F32)
    for index, item in enumerate(items):
        row = row + jnp.where(lane == index, item, 0.0)
    return row


def update_body(
    taps, g0, g1, g2, w0, w1, w2, rows, cols, vec_sum, own_gain, gain, gain_mom, chan, chan_mom,
    fin_sum, fin, fin_mom, fout_sum, fout, fout_mom,
    norm_out, c0, c1, c2, n0, n1, n2, rows_out, cols_out, gain_g, gain_n, gain_m,
    chan_g, chan_n, chan_m, fin_g, fin_n, fin_m, fout_g, fout_n, fout_m,
    turn, mp_block, dp_block, mp_slots, dp_slots, last_block, mp_last, dp_last, send_sem, recv_sem,
):
    d, m = lax.axis_index("dp"), lax.axis_index("mp")
    dp, mp = lax.axis_size("dp"), lax.axis_size("mp")
    size, width = g0.shape
    in_width = 3 * (width // 4)
    is_in = lax.broadcasted_iota(jnp.int32, (size, width), 1) < in_width

    def four(v0, v1, v2, reduce_fn):
        return [
            reduce_fn(jnp.where(is_in, v0, 0.0)),
            reduce_fn(jnp.where(is_in, 0.0, v0)),
            reduce_fn(v1),
            reduce_fn(v2),
        ]

    def row_sum(v):
        return jnp.sum(v, axis=1, keepdims=True)

    def col_sum(v):
        return jnp.sum(v, axis=0, keepdims=True)

    s0, s1, s2 = g0[...] * g0[...], g1[...] * g1[...], g2[...] * g2[...]
    lane = lax.broadcasted_iota(jnp.int32, (size, 128), 1)
    row_parts = four(s0, s1, s2, row_sum)
    packed = jnp.zeros((size, 128), F32)
    for index, part in enumerate(row_parts):
        packed = packed + jnp.where(lane == index, part, 0.0)
    turn[...] = jnp.zeros(turn.shape, F32)
    dp_block[...] = jnp.zeros(dp_block.shape, F32)
    turn[pl.ds(0, size), :] = packed
    mp_block[pl.ds(0, 8), :] = jnp.transpose(turn[...])[0:8]
    old = rows[...]
    old_parts = [total_of(old[:, i : i + 1]) / mp for i in range(4)]
    weight_parts = four(w0[...] * w0[...], w1[...] * w1[...], w2[...] * w2[...], total_of)
    scalars = (
        [total_of(p) for p in row_parts]
        + old_parts
        + weight_parts
        + [
            total_of(gain[...] * gain[...]) / mp,
            total_of(chan[...] * chan[...]) / dp,
            total_of(fout[...] * fout[...]) / dp,
            total_of(fout_sum[...] * fout_sum[...]) / dp,
        ]
    )
    mp_block[pl.ds(8, 8), :] = jnp.broadcast_to(lanes_of(scalars), (8, 128))
    over_mp = spread_sum(mp_block, mp_slots, send_sem, recv_sem, "mp", 0)
    pieces = width // 128
    for index, values in enumerate((s0, s1, s2)):
        sums = col_sum(values)
        for piece in range(pieces):
            dp_block[pl.ds(index * pieces + piece, 1), :] = sums[:, piece * 128 : (piece + 1) * 128]
    dp_block[pl.ds(3 * pieces, 1), :] = over_mp[8:9]
    over_dp = spread_sum(dp_block, dp_slots, send_sem, recv_sem, "dp", mp)
    turn[pl.ds(0, 8), :] = over_mp[0:8]
    row_totals = jnp.transpose(turn[...])[0:size]
    shared = over_dp[3 * pieces : 3 * pieces + 1]

    def scalar(index):
        return shared[:, index : index + 1]

    last = 3 * taps + 1
    vec_sq = total_of(vec_sum[0 : last + 2, :] * vec_sum[0 : last + 2, :])
    fin_sq = total_of(fin_sum[...] * fin_sum[...])
    norm = jnp.sqrt(
        scalar(0) + scalar(1) + scalar(2) + scalar(3) + vec_sq + scalar(15) + fin_sq
    )
    norm_out[...] = norm
    clip = 1.0 / jnp.maximum(1.0, norm / CLIP_NORM)
    square = clip * clip
    fresh = 1.0 - MOMENT_DECAY
    all_rows = size * dp
    wide = [in_width * mp, (width - in_width) * mp, width * mp, width * mp]
    ratio = []
    fresh_rows = jnp.zeros((size, 128), F32)
    for index in range(4):
        row_new = (
            MOMENT_DECAY * old[:, index : index + 1]
            + fresh * square * row_totals[:, index : index + 1] / wide[index]
        )
        mean = MOMENT_DECAY * scalar(4 + index) / all_rows + fresh * square * scalar(index) / (
            all_rows * wide[index]
        )
        ratio.append(row_new / mean)
        fresh_rows = fresh_rows + jnp.where(lane == index, row_new, 0.0)
    turn[pl.ds(0, size), :] = fresh_rows
    rows_out[...] = jnp.transpose(turn[...])[0:8]
    for index in range(3):
        for piece in range(pieces):
            at = pl.ds(piece * 128, 128)
            row = index * pieces + piece
            cols_out[pl.ds(index, 1), at] = (
                MOMENT_DECAY * cols[pl.ds(index, 1), at]
                + fresh * square * over_dp[row : row + 1] / all_rows
            )
    first_ratio = jnp.where(is_in, ratio[0], ratio[1])
    steps = []
    for grad, out, factor, index in ((g0, c0, first_ratio, 0), (g1, c1, ratio[2], 1), (g2, c2, ratio[3], 2)):
        clipped = grad[...] * clip
        out[...] = clipped
        steps.append(clipped * lax.rsqrt(factor * cols_out[pl.ds(index, 1), :]))
    u0, u1, u2 = steps

    def plain(clipped, moment, grad_out, moment_out):
        fresh_moment = MOMENT_DECAY * moment + fresh * clipped * clipped
        grad_out[...] = clipped
        moment_out[...] = fresh_moment
        return clipped * lax.rsqrt(fresh_moment)

    picked = vec_sum[last : last + 2, 0:size]
    for e in range(1, dp):
        picked = jnp.where(d == e, vec_sum[last : last + 2, e * size : (e + 1) * size], picked)
    own_gain[...] = jnp.zeros(own_gain.shape, F32)
    own_gain[:, pl.ds(0, size)] = picked
    own = width // mp
    own_chan = vec_sum[0:last, 0:own]
    for e in range(1, mp):
        own_chan = jnp.where(m == e, vec_sum[0:last, e * own : (e + 1) * own], own_chan)
    u_gain = plain(own_gain[...] * clip, gain_mom[...], gain_g, gain_m)
    u_chan = plain(own_chan * clip, chan_mom[...], chan_g, chan_m)
    u_fin = plain(fin_sum[...] * clip, fin_mom[...], fin_g, fin_m)
    u_fout = plain(fout_sum[...] * clip, fout_mom[...], fout_g, fout_m)
    step_parts = four(u0 * u0, u1 * u1, u2 * u2, total_of) + [
        total_of(u_gain * u_gain) / mp,
        total_of(u_chan * u_chan) / dp,
        total_of(u_fout * u_fout) / dp,
    ]
    last_block[...] = jnp.broadcast_to(lanes_of(step_parts), (8, 128))
    half_way = spread_sum(last_block, mp_last, send_sem, recv_sem, "mp", mp + dp)
    mp_block[pl.ds(0, 8), :] = half_way
    step_sums = spread_sum(mp_block.at[pl.ds(0, 8)], dp_last, send_sem, recv_sem, "dp", 2 * mp + dp)[0:1]

    def factors(step_total, weight_total, entries):
        shrink = 1.0 / jnp.maximum(1.0, jnp.sqrt(step_total / entries) / CLIP_STEP)
        return STEP_RATE * jnp.sqrt(weight_total / entries) * shrink

    def step_sum(index):
        return step_sums[:, index : index + 1]

    rate = [factors(step_sum(i), scalar(8 + i), all_rows * wide[i]) for i in range(4)]
    n0[...] = w0[...] - jnp.where(is_in, rate[0], rate[1]) * u0
    n1[...] = w1[...] - rate[2] * u1
    n2[...] = w2[...] - rate[3] * u2
    gain_n[...] = gain[...] - factors(step_sum(4), scalar(12), 2 * all_rows) * u_gain
    chan_n[...] = chan[...] - factors(step_sum(5), scalar(13), chan.shape[0] * chan.shape[1] * mp) * u_chan
    fout_n[...] = fout[...] - factors(step_sum(6), scalar(14), fout.shape[0] * fout.shape[1] * mp) * u_fout
    fin_count = fin.shape[0] * fin.shape[1]
    fin_rate = factors(total_of(u_fin * u_fin), total_of(fin[...] * fin[...]), fin_count)
    fin_n[...] = fin[...] - fin_rate * u_fin


def greet_all():
    d, m = lax.axis_index("dp"), lax.axis_index("mp")
    greet([(e, m) for e in ring(d, lax.axis_size("dp"))] + [(d, e) for e in ring(m, lax.axis_size("mp"))])


def prepare(raw, ready, turn):
    in_w, out_w, in_rows, out_rows, up_rows, down_rows, in_cols, out_cols, up_cols, down_cols, gain_own, gain_mom_own = raw
    w0, rows, cols, gain, gain_mom = ready
    size, own = out_w.shape
    for j in range(3):
        w0[:, pl.ds(j * own, own)] = in_w[j]
        cols[0:1, pl.ds(j * own, own)] = in_cols[j : j + 1, :]
    w0[:, pl.ds(3 * own, own)] = out_w[...]
    cols[0:1, pl.ds(3 * own, own)] = out_cols[...].reshape(1, own)
    cols[1:2, :] = up_cols[...].reshape(1, -1)
    cols[2:3, :] = down_cols[...].reshape(1, -1)
    turn[...] = jnp.zeros(turn.shape, F32)
    for index, source in enumerate((in_rows, out_rows, up_rows, down_rows)):
        turn[pl.ds(index, 1), pl.ds(0, size)] = source[...].reshape(1, size)
    rows[...] = jnp.transpose(turn[...])[0:size]
    for source, target, fill in ((gain_own, gain, 0.0), (gain_mom_own, gain_mom, 1.0)):
        target[...] = jnp.full(target.shape, fill, F32)
        target[:, pl.ds(0, size)] = source[...]


def prepare_scratch(size, width):
    return [
        pltpu.VMEM((size, width), F32), pltpu.VMEM((size, 128), F32), pltpu.VMEM((8, width), F32),
        pltpu.VMEM((2, 128), F32), pltpu.VMEM((2, 128), F32),
    ]


OUTS = 21


def run_update(taps, grads, sums, w1, w2, ready, own_gain, old, outs, work):
    w0, rows, cols, gain, gain_mom = ready
    chan, chan_mom, fin, fin_mom, fout, fout_mom = old
    update_body(
        taps, *grads, w0, w1, w2, rows, cols, sums[0], own_gain, gain, gain_mom, chan, chan_mom,
        sums[1], fin, fin_mom, sums[2], fout, fout_mom, *outs, *work,
    )


def update_kernel(taps, *refs):
    grads, sums, refs = refs[:3], refs[3:6], refs[6:]
    raw, w1, w2, old, refs = refs[:12], refs[12], refs[13], refs[14:20], refs[20:]
    outs, ready, own_gain, work = refs[:OUTS], refs[OUTS : OUTS + 5], refs[OUTS + 5], refs[OUTS + 6 :]
    prepare(raw, ready, work[0])
    greet_all()
    run_update(taps, grads, sums, w1, w2, ready, own_gain, old, outs, work)


def place_first(g0, zero_and_out, one_and_two):
    own = g0.shape[1] // 4
    g0[:, pl.ds(0, own)] = zero_and_out[:, 0:own]
    g0[:, pl.ds(own, 2 * own)] = one_and_two
    g0[:, pl.ds(3 * own, own)] = zero_and_out[:, own : 2 * own]


class LastOverDp:
    def __init__(self, low, high, from_low, from_high, send_sem, recv_sem):
        self.low, self.high, self.from_low, self.from_high = low, high, from_low, from_high
        d, m = lax.axis_index("dp"), lax.axis_index("mp")
        self.y, self.x = d // 4, (d // 2) % 2
        self.copies = [
            send(low.at[:, 1 - self.x], from_low, send_sem.at[0], recv_sem.at[0], (turned(d, 2), m)),
            send(high.at[:, 1 - self.y], from_high, send_sem.at[1], recv_sem.at[1], (turned(d, 4), m)),
        ]

    def finish(self, partial):
        for copy in self.copies:
            copy.wait()
        half = self.from_low.shape[0]
        for e in range(half):
            partial[e] = self.low[e, self.x] + self.from_low[e]
            partial[half + e] = self.high[e, self.y] + self.from_high[e]


class OverMp:
    def __init__(self, partial, arrived, passed, send_sem, recv_sem):
        self.partial, self.arrived, self.passed = partial, arrived, passed
        self.send_sem, self.recv_sem = send_sem, recv_sem
        self.d, self.m = lax.axis_index("dp"), lax.axis_index("mp")
        near = turned(self.m, 1)
        self.far = turned(self.m, 2)
        self.copies = [self.push(partial.at[e], slot, near) for slot, e in enumerate((near, turned(near, 2)))]

    def push(self, source, slot, peer):
        sems = self.send_sem.at[slot], self.recv_sem.at[slot]
        return send(source, self.arrived.at[slot], *sems, (self.d, peer))

    def step(self):
        for copy in self.copies:
            copy.wait()
        self.passed[...] = self.partial[self.far] + self.arrived[1]
        self.copies = [self.push(self.passed, 2, self.far)]

    def total(self):
        self.copies[0].wait()
        return self.partial[self.m].astype(F32) + self.arrived[0].astype(F32) + self.arrived[2].astype(F32)


def end_kernel(doc_count, taps, len_ref, gw_ref, gw_edge, channel, gains, sums_in, *refs):
    late_refs, partial_a, b_low, b_high, part_c, fin_part, fout_part, refs = refs[:12], *refs[12:18], refs[18:]
    raw, w1, w2, old, refs = refs[:12], refs[12], refs[13], refs[14:20], refs[20:]
    input_grad, outs, refs = refs[0], refs[1 : OUTS + 1], refs[OUTS + 1 :]
    held, late_sem, work, refs = refs[:12], refs[12], refs[13:17], refs[17:]
    ready, own_gain, refs = refs[:5], refs[5], refs[6:]
    g0, g1, g2, g_late, vec, vec_sum, fin_sum, fout_sum, part, refs = *refs[:9], refs[9:]
    update_work, refs = refs[:10], refs[10:]
    arrived, passed, z_send, z_recv, refs = refs[:2], refs[2:4], refs[4], refs[5], refs[6:]
    g_c, partial_b, from_low, from_high, l_send, l_recv, refs = *refs[:6], refs[6:]
    partials = (partial_a, partial_b)
    mp = lax.axis_size("mp")
    own = gw_ref.shape[3] // FOLD * HALVES
    size = g0.shape[0]
    lanes = g_late.shape[1] // FLOWS
    flows = []
    for i in range(FLOWS):
        flows.append(Flow(part, refs[i * FLOW_REFS : (i + 1) * FLOW_REFS], pl.ds(i * lanes, lanes)))
    refs = refs[FLOWS * FLOW_REFS :]
    flow_c, refs = Flow(part_c, refs[:FLOW_REFS]), refs[FLOW_REFS:]
    early = SmallSums((fin_part, fout_part), (fin_sum, fout_sum), (True, False), refs[:8])
    final = SmallSums((vec,), (vec_sum,), (True,), refs[8:])
    late = Late(late_refs, held, late_sem)
    vec[...] = sums_in[...]
    greet_all()
    last_b = LastOverDp(b_low, b_high, from_low, from_high, l_send, l_recv)
    flow_c.start()

    def start_mp(i):
        return OverMp(partials[i], arrived[i], passed[i], z_send.at[i], z_recv.at[i])

    over_mp = [start_mp(0)]
    early.start(0)

    def stream_done(j, grad):
        for e in range(mp):
            for owner in range(8):
                at = (e, owner // 4, owner // 2 % 2, owner % 2, slice(None), pl.ds((j - 1) * own, own))
                part[at] = grad[owner * size : (owner + 1) * size, e * own : (e + 1) * own].astype(BF)
        if j == 1:
            flows[0].start()
            flow_c.core_stage()
            early.end(0)
            early.start(1)
            over_mp[0].step()
            last_b.finish(partial_b)
            over_mp.append(start_mp(1))
        else:
            flows[1].start()
            flows[2].start()
            flow_c.second_stage()
            early.end(1)
            early.start(2)
            over_mp[1].step()

    total = post_steps(
        doc_count, taps, len_ref, gw_ref, gw_edge, channel, gains, vec, held, late, work, stream_done
    )
    final.start(0)
    flows[0].core_stage()
    post_end(total, gains, held, input_grad)
    flows[1].core_stage()
    flows[2].core_stage()
    flow_c.third_stage()
    flow_c.send_z()
    early.end(2)
    early.start_mp()
    final.end(0)
    final.start(1)
    prepare(raw, ready, update_work[0])
    for flow in flows:
        flow.second_stage()
    final.end(1)
    final.start(2)
    for flow in flows:
        flow.third_stage()
        flow.send_z()
    final.end(2)
    final.start_mp()
    g1[...] = over_mp[0].total()
    g2[...] = over_mp[1].total()
    flow_c.finish(g_c)
    early.end_mp()
    final.end_mp()
    for flow in flows:
        flow.finish(g_late)
    place_first(g0, g_c[...], g_late[...])
    for flow in (*flows, flow_c):
        flow.drain()
    early.drain()
    final.drain()
    run_update(taps, (g0, g1, g2), (vec_sum, fin_sum, fout_sum), w1, w2, ready, own_gain, old, outs, update_work)


def update_scratch(dp, mp, width):
    pieces = 3 * width // 128 + 1
    tall = -(-pieces // 8) * 8
    sems = 2 * (dp + mp)
    return [
        pltpu.VMEM((128, 128), F32),
        pltpu.VMEM((16, 128), F32),
        pltpu.VMEM((tall, 128), F32),
        pltpu.VMEM((mp, 16, 128), F32),
        pltpu.VMEM((dp, tall, 128), F32),
        pltpu.VMEM((8, 128), F32),
        pltpu.VMEM((mp, 8, 128), F32),
        pltpu.VMEM((dp, 8, 128), F32),
        dma(sems),
        dma(sems),
    ]


def hand_out_kernel(*refs):
    input_grad, norm, c0, c1, c2, n0, n1, n2, rows, cols, gain_g, gain_n, gain_m, *small = refs[: OUTS + 1]
    (
        input_grad_out, norm_out, in_g, out_g, up_g, down_g, gain_g_out, in_n, out_n, up_n, down_n, gain_n_out, gain_m_out,
        in_r, out_r, up_r, down_r, in_c, out_c, up_c, down_c, *small_out,
    ) = refs[OUTS + 1 :]
    size, own = out_g.shape
    input_grad_out[...] = input_grad[...]
    norm_out[...] = norm[...]
    for source, first, last in ((c0, in_g, out_g), (n0, in_n, out_n)):
        for j in range(3):
            first[j] = source[:, j * own : (j + 1) * own]
        last[...] = source[:, 3 * own : 4 * own]
    for source, target in ((c1, up_g), (c2, down_g), (n1, up_n), (n2, down_n)):
        target[...] = source[...]
    for source, target in ((gain_g, gain_g_out), (gain_n, gain_n_out), (gain_m, gain_m_out)):
        target[...] = source[:, 0:size]
    for index, target in enumerate((in_r, out_r, up_r, down_r)):
        target[...] = rows[index : index + 1, 0:size].reshape(size)
    for j in range(3):
        in_c[j : j + 1, :] = cols[0:1, j * own : (j + 1) * own]
    out_c[...] = cols[0:1, 3 * own : 4 * own].reshape(own)
    up_c[...] = cols[1:2, :].reshape(-1)
    down_c[...] = cols[2:3, :].reshape(-1)
    for source, target in zip(small, small_out):
        target[...] = source[...]


def hand_out(results, own):
    size, width = results[2].shape
    cube, part, full = (3, size, own), (size, own), (size, width)
    column, row, wide = (2, size), (size,), (width,)
    shapes = [(1, 1), cube, part, full, full, column, cube, part, full, full, column, column, row, row, row, row]
    shapes += [(3, own), (own,), wide, wide] + [v.shape for v in results[13:]]
    return pl.pallas_call(
        hand_out_kernel,
        name="hand_out",
        out_shape=(struct(results[0].shape, BF), *[struct(s, F32) for s in shapes]),
        in_specs=[IN_VMEM] * len(results),
        out_specs=(IN_VMEM,) * (1 + len(shapes)),
        compiler_params=pltpu.CompilerParams(vmem_limit_bytes=ROOM),
    )(*results)


FLOWS = 3


def finish(lengths, taps, first, late, partials, part_c, fin_part, fout_part, raw, w1, w2, old):
    dp, mp = lax.axis_size("dp"), lax.axis_size("mp")
    size, own = raw[1].shape
    width = w1.shape[1]
    count = late[0][0].shape[0]
    docs = lengths.shape[1]
    big = struct((size, width), F32)
    flat = [(2, 128), old[0].shape, old[2].shape, old[4].shape]
    outs = [struct((1, 1), F32)] + [big] * 6 + [struct((8, 128), F32), struct((3, width), F32)]
    outs += [struct(s, F32) for s in flat for _ in range(3)]
    params = pltpu.CompilerParams(collective_id=2, has_side_effects=True, vmem_limit_bytes=ROOM)
    tail = [*raw, w1, w2, *old]
    own_gain = pltpu.VMEM((2, 128), F32)
    if dp != 8:
        last_part, input_grad, vec = post(lengths, taps, *first, late)
        over_mp = [lax.psum_scatter(p, "mp").astype(F32) for p in partials[:2]]
        grad = scatter_fallback(last_part.reshape(mp, dp, size, 2 * own))
        first_grad = scatter_fallback(part_c)
        grad = jnp.concatenate([first_grad[:, :own], grad, first_grad[:, own:]], axis=1)
        sums = [lax.psum(vec, ("dp", "mp")), lax.psum(fin_part, ("dp", "mp")), lax.psum(fout_part, "dp")]
        inputs = [grad, *over_mp, *sums, *tail]
        results = pl.pallas_call(
            functools.partial(update_kernel, taps),
            name="clip_and_update",
            out_shape=tuple(outs),
            in_specs=[IN_VMEM] * len(inputs),
            out_specs=(IN_VMEM,) * len(outs),
            scratch_shapes=prepare_scratch(size, width) + [own_gain] + update_scratch(dp, mp, width),
            compiler_params=params,
        )(*inputs)
        return (input_grad, *results)
    flows = []
    for _ in range(FLOWS):
        flows += flow_scratch(mp, (size, 2 * own // FLOWS))
    vec = struct((16, width), F32)
    after = [fin_part, fout_part, *tail]

    def kernel(*refs):
        start = 1 + len(first)
        end = start + len(late)
        end_kernel(docs, taps, *refs[:start], *choose(refs[start:end], late), *refs[end:])

    return pl.pallas_call(
        kernel,
        name="sum_clip_update",
        out_shape=(struct((count, width), BF), *outs),
        in_specs=[IN_SMEM] + [IN_VMEM] * len(first) + [IN_HBM] * len(late) + [IN_VMEM] * 3 + [IN_HBM] + [IN_VMEM] * len(after),
        out_specs=(IN_VMEM,) * (1 + len(outs)),
        scratch_shapes=[
            *post_scratch(late, taps, count, width),
            *prepare_scratch(size, width),
            own_gain,
            *[pltpu.VMEM((size, width), F32)] * 3,
            pltpu.VMEM((size, 2 * own), F32),
            *[pltpu.VMEM(v.shape, F32) for v in (vec, vec, fin_part, fout_part)],
            pltpu.VMEM((mp, 2, 2, 2, size, 2 * own), BF),
            *update_scratch(dp, mp, width),
            *[pltpu.VMEM((mp - 1, size, width), BF)] * 2,
            *[pltpu.VMEM((size, width), BF)] * 2,
            dma(2, mp - 1),
            dma(2, mp - 1),
            pltpu.VMEM((size, 2 * own), F32),
            pltpu.VMEM((mp, size, width), BF),
            *[pltpu.VMEM((mp // 2, size, width), BF)] * 2,
            dma(2),
            dma(2),
            *flows,
            *flow_scratch(mp, (size, 2 * own)),
            *small_scratch((fin_part, fout_part), mp),
            *small_scratch((vec,), mp),
        ],
        compiler_params=params,
    )(lengths, *first, *[v for v, _ in late], *partials, part_c, *after)


class Spread:
    def __init__(self, own, whole, lanes, refs, direct):
        self.whole, self.lanes, self.direct = whole, lanes, direct
        self.source = own.at[:, lanes]
        self.own_sem, self.z_send, self.z_recv, self.p_send, self.p_recv = refs
        self.d, self.m, self.mp = lax.axis_index("dp"), lax.axis_index("mp"), lax.axis_size("mp")
        d = self.d
        self.dx, self.dy, self.dc = turned(d, 2), turned(d, 4), turned(d, 1)
        half = self.mp // 2
        self.low, self.high, self.all = pl.ds(0, half), pl.ds(half, self.mp - half), pl.ds(0, self.mp)

    def start(self):
        target = self.whole.at[self.m, self.d, :, self.lanes]
        self.copy = pltpu.make_async_copy(self.source, target, self.own_sem.at[0])
        self.copy.start()
        self.z = []
        if self.direct:
            for step, e in enumerate(ring(self.m, self.mp)):
                sems = self.z_send.at[step], self.z_recv.at[step]
                self.z.append(send(self.source, target, *sems, (self.d, e)))
        else:
            self.blocks, self.bit = [self.m], self.mp // 2
            self.send_blocks()

    def send_blocks(self):
        self.stepped = []
        for block in self.blocks:
            slot = len(self.z)
            target = self.whole.at[block, self.d, :, self.lanes]
            source = self.source if slot == 0 else target
            peer = (self.d, turned(self.m, self.bit))
            copy = send(source, target, self.z_send.at[slot], self.z_recv.at[slot], peer)
            self.stepped.append(copy)
            self.z.append(copy)

    def z_step(self):
        if self.bit == self.mp // 2:
            self.copy.wait()
        for copy in self.stepped:
            copy.wait_recv()
        self.blocks = self.blocks + [turned(block, self.bit) for block in self.blocks]
        self.bit //= 2
        self.send_blocks()

    def push(self, slot, rows, owner, peer):
        block = self.whole.at[rows, owner, :, self.lanes]
        return send(block, block, self.p_send.at[slot], self.p_recv.at[slot], (peer, self.m))

    def stage_one(self):
        if self.direct:
            self.copy.wait()
        for copy in self.z if self.direct else self.stepped:
            copy.wait_recv()
        d, dx, dy = self.d, self.dx, self.dy
        self.first = [self.push(0, self.low, d, dx), self.push(1, self.high, d, dy)]
        self.last = [self.push(2, self.all, d, self.dc)]

    def stage_two(self):
        for copy in self.first:
            copy.wait_recv()
        d, dx, dy = self.d, self.dx, self.dy
        self.second = [
            self.push(3, self.low, d, dy),
            self.push(4, self.high, d, dx),
            self.push(5, self.low, dx, dy),
            self.push(6, self.high, dy, dx),
        ]

    def stage_three(self):
        for copy in self.second:
            copy.wait_recv()
        for slot, owner in enumerate((self.dx, self.dy, turned(self.dx, 4))):
            self.last.append(self.push(7 + slot, self.all, owner, self.dc))

    def arrive(self):
        for copy in self.last:
            copy.wait_recv()

    def drain(self):
        for copy in self.z + self.first + self.second + self.last:
            copy.wait_send()


SPREAD_REFS = 5


def spread_scratch(mp):
    return [dma(1), dma(mp - 1), dma(mp - 1), dma(10), dma(10)]


def mark_same(same, len_ref, doc_count, first):
    tail = same.shape[1]
    position = lax.broadcasted_iota(jnp.int32, (tail + EDGE, 128), 0) + first
    doc = jnp.zeros(position.shape, jnp.int32)
    end = jnp.int32(0)
    for slot in range(doc_count):
        end = end + len_ref[0, slot]
        doc = doc + (position >= end).astype(jnp.int32)
    doc = jnp.where(position < 0, -1, doc)
    for k in range(1, same.shape[0] + 1):
        same[k - 1] = jnp.where(doc[EDGE:] == doc[EDGE - k : EDGE - k + tail], 1.0, 0.0)


def near_product(left, right, dot=mm):
    l_top, l_rest = split(left)
    r_top, r_rest = split(right)
    return dot(l_top, r_top) + dot(l_top, r_rest) + dot(l_rest, r_top)


def mixer_forward_kernel(
    doc_count, taps, len_ref, tok, in_w, out_w, up_w, down_w, gains_own, channel_own, table, step_col, f_in, f_out,
    t0, t1, t2, t3,
    w_parts, y_back, spectrum, hidden, phase, decay, gain_rows, chan_rows,
    z_out, s0_out, s1_out, s2_out, w_out_own, a_out, n1_out, inv1_out, w_in_out, w_out_out, whole_up, whole_down,
    chunk_first, chunk_up, chunk_down, gains, channel, turn, whole_first, gains_all, channel_all, edges_all, filters, w_send, y_parts, full, raw, top, rest, slots,
    ext, n1, inv1, a, z, s0, s1, s2, w_own, w_in, w_out, same,
    s_send, s_recv, save_sem, b_send, b_recv, c_send, c_recv, *spread_refs,
):
    tables = (t0, t1, t2, t3)
    d, m = lax.axis_index("dp"), lax.axis_index("mp")
    dp, mp = lax.axis_size("dp"), lax.axis_size("mp")
    count, width = tok.shape
    rows = chunk_first.shape[0]
    own = width // mp
    block = count // 2
    blocks = raw.shape[0]

    place = (2, 0, 1)
    for j in range(3):
        chunk_first[:, pl.ds(place[j] * own, own)] = in_w[j].astype(BF)
    chunk_first[:, pl.ds(3 * own, own)] = out_w[...].astype(BF)
    chunk_up[...] = up_w[...].astype(BF)
    chunk_down[...] = down_w[...].astype(BF)
    turn[...] = jnp.zeros(turn.shape, F32)
    turn[pl.ds(0, 2), pl.ds(0, rows)] = gains_own[...]
    gains[...] = turn[...].astype(BF)
    channel[...] = jnp.zeros(channel.shape, F32)
    channel[pl.ds(0, channel_own.shape[0]), :] = channel_own[...]
    greet_all()

    small = []
    for step, e in enumerate(ring(d, dp)):
        small.append(send(gains, gains_all.at[d], s_send.at[step], s_recv.at[step], (e, m)))
    for step, e in enumerate(ring(m, mp)):
        at = dp + step
        small.append(send(channel, channel_all.at[m], s_send.at[at], s_recv.at[at], (d, e)))
    at = dp + mp
    for index, first, peer in ((0, count - EDGE, lax.rem(m + 1, mp)), (1, 0, lax.rem(m + mp - 1, mp))):
        sems = s_send.at[at + index], s_recv.at[at + index]
        small.append(send(tok.at[pl.ds(first, EDGE)], edges_all.at[index], *sems, (d, peer)))
    gains_all[d] = gains[...]
    channel_all[m] = channel[...]

    half = width // 2
    plan = [
        (chunk_first, whole_first, pl.ds(0, half)),
        (chunk_first, whole_first, pl.ds(half, width - half)),
        (chunk_up, whole_up, pl.ds(0, chunk_up.shape[1])),
        (chunk_down, whole_down, pl.ds(0, chunk_down.shape[1])),
    ]
    flows = [
        Spread(*p, spread_refs[i * SPREAD_REFS : (i + 1) * SPREAD_REFS], direct=i == 0) for i, p in enumerate(plan)
    ]
    left, right, up, down = flows
    left.start()
    right.start()

    phase[...] = near_product(table[...], f_in[...])
    hidden[...] = jnp.sin(phase[...])
    lane = (m * own + lax.broadcasted_iota(jnp.int32, (1, own), 1)).astype(F32)
    rate = FAST_DECAY + (SLOW_DECAY - FAST_DECAY) * lane / (width - 1)
    decay[...] = jnp.exp(-step_col[...] * rate)
    near = own // HALVES
    values = near_product(hidden[...], f_out[...]) * decay[...]
    for side in range(HALVES):
        filters[side, :, 0:near] = values[:, side * near : (side + 1) * near]

    mark_same(same, len_ref, doc_count, m * count - EDGE)

    left.stage_one()
    for copy in small:
        copy.wait()
    for e in range(dp):
        gain_rows[0:2, pl.ds(e * rows, rows)] = gains_all[e, 0:2, 0:rows].astype(F32)
    for e in range(mp):
        chan_rows[:, pl.ds(e * own, own)] = channel_all[e]
    ext[pl.ds(0, EDGE), :] = edges_all[0].astype(F32)
    ext[pl.ds(EDGE, count), :] = tok[...].astype(F32)
    ext[pl.ds(EDGE + count, EDGE), :] = edges_all[1].astype(F32)

    def norm_body(i, carry):
        at = pl.ds(pl.multiple_of(i * 32, 32), 32)
        normed, inverse_std = norm_parts(ext[at, :])
        n1[at, :] = normed
        inv1[at, :] = jnp.broadcast_to(inverse_std, (32, 128))
        a[at, :] = (normed * gain_rows[0:1, :]).astype(BF)
        return carry

    def stream_weights(j):
        for e in range(mp):
            part = whole_first[e, :, :, pl.ds(place[j] * own, own)].reshape(dp * rows, own)
            w_in[:, pl.ds(j * width + e * own, own)] = part

    def project(j):
        cols = pl.ds(j * width, width)
        z[:, cols] = mm(a[...], w_in[:, cols])

    def short(first, size, j):
        part = z[pl.ds(first + 8, size + 8), pl.ds(j * width, width)]
        total = chan_rows[j : j + 1, :] * part[8 : size + 8]
        for k in range(1, taps):
            keep = same[k - 1, pl.ds(first, size), 0:1] > 0.0
            moved = jnp.where(keep, part[8 - k : size + 8 - k], 0.0)
            total = total + chan_rows[3 * k + j : 3 * k + j + 1, :] * moved
        return total

    def value_body(i, carry):
        first = pl.multiple_of(i * 48, 16)
        at = pl.ds(first, 48)
        one, two = short(first, 48, 1), short(first, 48, 2)
        s1[at, :], s2[at, :] = one, two
        w_own[at, :] = two * one
        return carry

    def gate_body(i, carry):
        first = pl.multiple_of(i * 48, 16)
        s0[pl.ds(first, 48), :] = short(first, 48, 0)
        return carry

    lax.fori_loop(0, ext.shape[0] // 32, norm_body, 0)
    right.z_step()
    up.start()
    left.stage_two()
    right.stage_one()
    up.z_step()
    for side in range(HALVES):
        filter_spectrum(filters.at[side], spectrum.at[side], raw, tables, block)
    down.start()
    left.stage_three()
    right.stage_two()
    left.arrive()
    for j in (1, 2):
        stream_weights(j)
        project(j)
    up.stage_one()
    down.z_step()
    lax.fori_loop(0, s0.shape[0] // 48, value_body, 0)
    piece = count // FOLD
    for side in range(HALVES):
        for part in range(mp):
            for i in range(FOLD):
                values = w_own[pl.ds(i * piece, piece), pl.ds(part * own + side * near, near)]
                w_send[side, part, :, pl.ds(i * near, near)] = values.astype(BF)
    going, back = [], []
    for side in range(HALVES):
        going.append(Blocks([(w_send.at[side], w_parts.at[side])], b_send.at[side], b_recv.at[side]))
        back.append(Blocks([(y_parts.at[side], y_back.at[side])], c_send.at[side], c_recv.at[side]))
        going[side].start()
    right.stage_three()
    up.stage_two()
    down.stage_one()
    right.arrive()
    stream_weights(0)
    project(0)
    lax.fori_loop(0, s0.shape[0] // 48, gate_body, 0)
    saves = []

    def save(source, target):
        copy = pltpu.make_async_copy(source, target, save_sem.at[len(saves)])
        copy.start()
        saves.append(copy)

    own_rows = pl.ds(0, count)
    for source, target in (
        *[(z.at[:, pl.ds(j * width, width)], z_out.at[j]) for j in range(3)], (s0.at[own_rows], s0_out), (s1, s1_out), (s2, s2_out), (w_own.at[own_rows], w_out_own),
        (a, a_out), (n1, n1_out), (inv1, inv1_out),
        *[(w_in.at[:, pl.ds(j * width, width)], w_in_out.at[j]) for j in range(3)],
    ):
        save(source, target)
    for e in range(mp):
        part = whole_first[e, :, :, pl.ds(3 * own, own)].reshape(dp * rows, own)
        w_out[:, pl.ds(e * own, own)] = part
    save(w_out, w_out_out)
    def between(slot):
        if slot == 0:
            down.stage_two()
            up.stage_three()

    for side in range(HALVES):
        going[side].arrive()
        conv_forward_steps(
            doc_count, len_ref, w_parts.at[side], tables, y_parts.at[side], spectrum.at[side], full, raw, top, rest,
            slots, between if side == 0 else lambda slot: None,
        )
        back[side].start()
    down.stage_three()
    up.arrive()
    down.arrive()
    for side in range(HALVES):
        back[side].arrive()
    for copy in saves:
        copy.wait()
    for copies in going + back:
        copies.drain()
    for flow in flows:
        flow.drain()


def mixer_forward(lengths, tokens, weights, gains, channel, taps, table, step_col, f_in, f_out, tables):
    mp, dp = lax.axis_size("mp"), lax.axis_size("dp")
    count, width = tokens.shape
    own, block, docs = width // mp, count // 2, lengths.shape[1]
    lags = table.shape[0]
    blocks = lags // block
    near = own // HALVES
    rows = weights[1].shape[0]
    shards = [(rows, 4 * own), weights[2].shape, weights[3].shape]
    whole = [(mp, dp) + s for s in shards]
    longer, later = (count + 2 * EDGE, width), (count + EDGE, width)
    parts = (HALVES, mp, count // FOLD, FOLD * near)
    full, raw, low, slots = conv_scratch(parts[1:], blocks, block, docs)
    vmem_outs = [
        (parts, BF), (parts, BF), ((HALVES, blocks, 2 * block, lanes_for(near)), F32), ((lags, f_in.shape[1]), F32), ((lags, f_in.shape[1]), F32),
        ((lags, own), F32), ((8, width), F32), ((16, width), F32),
    ]
    hbm_outs = [
        ((3,) + longer, F32), ((count, width), F32), (later, F32), (later, F32), ((count, width), F32),
        (longer, BF), (longer, F32), ((longer[0], 128), F32), ((3, width, width), BF), ((width, width), BF),
        (whole[1], BF), (whole[2], BF),
    ]
    inputs = (lengths, tokens, *weights, gains, channel, table, step_col, f_in, f_out, *tables)
    return pl.pallas_call(
        functools.partial(mixer_forward_kernel, docs, taps),
        name="mixer_forward",
        out_shape=tuple(struct(*o) for o in vmem_outs + hbm_outs),
        in_specs=[IN_SMEM] + [IN_VMEM] * (len(inputs) - 1),
        out_specs=(IN_VMEM,) * len(vmem_outs) + (IN_HBM,) * len(hbm_outs),
        scratch_shapes=[
            *[pltpu.VMEM(s, BF) for s in shards], pltpu.VMEM((16, 128), BF), pltpu.VMEM((16, own), F32),
            pltpu.VMEM((16, 128), F32),
            pltpu.VMEM(whole[0], BF), pltpu.VMEM((dp, 16, 128), BF), pltpu.VMEM((mp, 16, own), F32),
            pltpu.VMEM((2, EDGE, width), BF),
            pltpu.VMEM((HALVES, lags, lanes_for(near)), F32), pltpu.VMEM(parts, BF), pltpu.VMEM(parts, BF),
            full, raw, low, low, slots,
            pltpu.VMEM(longer, F32), pltpu.VMEM(longer, F32), pltpu.VMEM((longer[0], 128), F32), pltpu.VMEM(longer, BF),
            pltpu.VMEM((longer[0], 3 * width), F32), pltpu.VMEM(later, F32), pltpu.VMEM(later, F32),
            pltpu.VMEM(later, F32), pltpu.VMEM(later, F32), pltpu.VMEM((width, 3 * width), BF),
            pltpu.VMEM((width, width), BF), pltpu.VMEM((taps - 1, later[0], 128), F32),
            dma(dp + mp + 2), dma(dp + mp + 2), dma(16), *([dma(HALVES, 1, mp - 1)] * 4),
            *(spread_scratch(mp) * 4),
        ],
        compiler_params=pltpu.CompilerParams(collective_id=0, has_side_effects=True, vmem_limit_bytes=ROOM),
    )(*inputs)


def dot_nt(left, right):
    return lax.dot_general(left, right, (((1,), (1,)), ((), ())), preferred_element_type=F32)


def dot_tn(left, right):
    return lax.dot_general(left, right, (((0,), (0,)), ((), ())), preferred_element_type=F32)


def pieces(parts, count, width):
    near, rows = width // parts // HALVES, count // FOLD
    for side in range(HALVES):
        for part in range(parts):
            for i in range(FOLD):
                cols = pl.ds((part * HALVES + side) * near, near)
                yield pl.ds(i * rows, rows), cols, side, part, pl.ds(i * near, near)


def gelu_parts(x):
    scale, cubic = math.sqrt(2.0 / math.pi), 0.044715
    square = x * x
    t = jnp.tanh(x * (scale + (scale * cubic) * square))
    half = 0.5 + 0.5 * t
    value = x * half
    return value, half + value * (1.0 - t) * (scale + (3.0 * scale * cubic) * square)


COLS = 768


def feed_kernel(
    skip_row, y_ref, w_ref, s0_ref, tok, cot, w_out, gains, channel, up, down,
    act_out, up_part, down_part, out_part, g_parts, gy_out, gs0_out, gx2_out, sums, edge_out,
    y, o, x2, n2, inv2, b, b_t, cot_t, mix, acc_out, acc_b,
):
    step, steps = pl.program_id(0), pl.num_programs(0)
    parts = y_ref.shape[1]
    count, width = tok.shape
    tile = 128
    gain, skip = gains.at[1:2], channel.at[skip_row : skip_row + 1]

    @pl.when(step == 0)
    def _():
        for rows, cols, side, part, lanes in pieces(parts, count, width):
            y[rows, cols] = y_ref[side, part, :, lanes].astype(F32)

        def body(index, carry):
            rows = pl.ds(pl.multiple_of(index * tile, tile), tile)
            values = y[rows, :] + skip[...] * w_ref[rows, :]
            y[rows, :] = values
            mixed = (values * s0_ref[rows, :]).astype(BF)
            o[rows, :] = mixed
            residual = tok[rows, :].astype(F32) + dot_nt(mixed, w_out[...])
            x2[rows, :] = residual
            normed, inverse_std = norm_parts(residual)
            n2[rows, :] = normed
            inv2[rows, :] = jnp.broadcast_to(inverse_std, (tile, 128))
            b[rows, :] = (normed * gain[...]).astype(BF)
            return carry

        lax.fori_loop(0, count // tile, body, 0)
        b_t[...] = b[...].T
        cot_t[...] = cot[...].T
        acc_out[...] = jnp.zeros(acc_out.shape, F32)
        acc_b[...] = jnp.zeros(acc_b.shape, F32)

    up_w, down_w = up[0], down[0]
    value, slope = gelu_parts(mm(b[...], up_w))
    act = value.astype(BF)
    g_hpre = (mm(cot[...], down_w) * slope).astype(BF)
    up_part[0] = mm(b_t[...], g_hpre).astype(BF)
    down_part[0] = mm(cot_t[...], act).astype(BF)
    acc_out[...] += dot_nt(act, down_w)
    acc_b[...] += dot_nt(g_hpre, up_w)

    @pl.when(step == steps - 1)
    def _():
        sums[...] = jnp.zeros(sums.shape, F32)

        def body(index, carry):
            rows = pl.ds(pl.multiple_of(index * tile, tile), tile)
            act_out[rows, :] = (x2[rows, :] + acc_out[rows, :]).astype(BF)
            g_b, normed = acc_b[rows, :], n2[rows, :]
            sums[0:1, :] += jnp.sum(g_b * normed, axis=0, keepdims=True)
            g_x2 = cot[rows, :].astype(F32) + norm_back(g_b, gain[...], normed, inv2[rows, 0:1])
            gx2_out[rows, :] = g_x2
            low = g_x2.astype(BF)
            mix[rows, :] = low
            g_o = mm(low, w_out[...])
            g_y = g_o * s0_ref[rows, :]
            gy_out[rows, :] = g_y
            gs0_out[rows, :] = g_o * y[rows, :]
            sums[1:2, :] += jnp.sum(g_y * w_ref[rows, :], axis=0, keepdims=True)
            return carry

        lax.fori_loop(0, count // tile, body, 0)
        for rows, cols, side, part, lanes in pieces(parts, count, width):
            g_parts[side, part, :, lanes] = gy_out[rows, cols].astype(BF)
        edge_out[...] = gs0_out[pl.ds(0, EDGE), :].astype(BF)
        grad = dot_tn(mix[...], o[...])
        own = width // parts
        for part in range(parts):
            out_part[part] = grad[:, part * own : (part + 1) * own].astype(BF)


def feed(y_parts, w_own, s0, tokens, cotangent, w_out, gains, channel, skip_row, whole_up, whole_down):
    mp, width, hidden = whole_up.shape
    count = tokens.shape[0]
    own, cols = width // mp, COLS
    each = hidden // cols
    once = pl.Buffered(1)

    def fixed(shape):
        return pl.BlockSpec(shape, lambda i: (0,) * len(shape), pipeline_mode=once)

    def moving():
        return pl.BlockSpec((1, width, cols), lambda i: (i // each, 0, i % each))

    full, half = (count, width), y_parts.shape
    outs = [
        (full, BF), (whole_up.shape, BF), (whole_up.shape, BF), ((mp, width, own), BF), (half, BF),
        (full, F32), (full, F32), (full, F32), ((8, width), F32), ((EDGE, width), BF),
    ]
    out_specs = [moving() if i in (1, 2) else fixed(s) for i, (s, _) in enumerate(outs)]
    inputs = (y_parts, w_own, s0, tokens, cotangent, w_out, gains, channel)
    return pl.pallas_call(
        functools.partial(feed_kernel, skip_row),
        name="feed_forward",
        grid=(mp * each,),
        out_shape=tuple(struct(s, t) for s, t in outs),
        in_specs=[fixed(v.shape) for v in inputs] + [moving(), moving()],
        out_specs=tuple(out_specs),
        scratch_shapes=[
            pltpu.VMEM(full, F32), pltpu.VMEM(full, BF), pltpu.VMEM(full, F32), pltpu.VMEM(full, F32),
            pltpu.VMEM((count, 128), F32), pltpu.VMEM(full, BF), pltpu.VMEM((width, count), BF),
            pltpu.VMEM((width, count), BF), pltpu.VMEM(full, BF), pltpu.VMEM(full, F32), pltpu.VMEM(full, F32),
        ],
        compiler_params=pltpu.CompilerParams(vmem_limit_bytes=ROOM),
    )(*inputs, whole_up, whole_down)


class Late:
    def __init__(self, sources, targets, sem):
        self.copies = []
        for i, (source, target) in enumerate(zip(sources, targets)):
            copy = pltpu.make_async_copy(source, target, sem.at[i])
            copy.start()
            self.copies.append(copy)

    def need(self, *indices):
        for i in indices:
            self.copies[i].wait()


def short_backward(j, gs, z, channel, same, offsets, count, sums):
    tap_rows = [channel[3 * k + j : 3 * k + j + 1, :] for k in range(offsets)]
    g_z = None
    for k in range(offsets):
        later = gs[pl.ds(k, count), :]
        before = z[pl.ds(EDGE - k, count), :]
        if k:
            later = jnp.where(same[k][k : count + k], later, 0.0)
            before = jnp.where(same[k][:count], before, 0.0)
        g_z = tap_rows[k] * later if g_z is None else g_z + tap_rows[k] * later
        sums[pl.ds(3 * k + j, 1), :] = jnp.sum(gs[pl.ds(0, count), :] * before, axis=0, keepdims=True)
    return g_z


def post_steps(doc_count, offsets, len_ref, gw_ref, gw_edge, channel, gains, sums, held, late, work, stream_done):
    gy_ref, s2_ref, z1, a_ref, w1, s1_ref, z2, w2, ga0, n1_ref, inv1_ref, gx2_ref = held
    gw, gs, gz, marks = work
    parts = gw_ref.shape[1]
    count, width = gy_ref.shape
    near = width // parts // HALVES
    skip = channel[3 * offsets : 3 * offsets + 1, :]
    for rows, cols, side, part, lanes in pieces(parts, count, width):
        gw[rows, cols] = gw_ref[side, part, :, lanes].astype(F32)
    for side in range(HALVES):
        for part in range(parts):
            at = pl.ds((part * HALVES + side) * near, near)
            gw[pl.ds(count, EDGE), at] = gw_edge[side, part, :, 0:near].astype(F32)
    mark_same(marks, len_ref, doc_count, lax.axis_index("mp") * count - EDGE)
    same = [None] + [marks[k - 1, :, 0:1] > 0.0 for k in range(1, offsets)]
    late.need(0)
    gw[pl.ds(0, count), :] += skip * gy_ref[...]
    total = None
    for j, other, z, w, order in ((1, s2_ref, z1, w1, (1, 2, 3, 4)), (2, s1_ref, z2, w2, (5, 6, 7))):
        late.need(*order)
        gs[...] = gw[...] * other[...]
        gz[...] = short_backward(j, gs, z, channel, same, offsets, count, sums).astype(BF)
        stream_done(j, dot_tn(a_ref[pl.ds(EDGE, count), :], gz[...]))
        term = dot_nt(gz[...], w[...])
        total = term if total is None else total + term
    late.need(8, 9, 10, 11)
    total = total + ga0[...]
    sums[pl.ds(3 * offsets + 1, 1), :] = jnp.sum(total * n1_ref[pl.ds(EDGE, count), :], axis=0, keepdims=True)
    return total


def post_end(total, gains, held, input_grad):
    n1_ref, inv1_ref, gx2_ref = held[9:]
    count = gx2_ref.shape[0]
    normed, inverse_std = n1_ref[pl.ds(EDGE, count), :], inv1_ref[pl.ds(EDGE, count), 0:1]
    input_grad[...] = (gx2_ref[...] + norm_back(total, gains[0:1, :], normed, inverse_std)).astype(BF)


def post_kernel(doc_count, offsets, len_ref, gw_ref, gw_edge, channel, gains, sums_in, *refs):
    late_refs, refs = refs[:12], refs[12:]
    last_part, input_grad, sums, refs = refs[0], refs[1], refs[2], refs[3:]
    held, late_sem, work = refs[:12], refs[12], refs[13:]
    late = Late(late_refs, held, late_sem)
    parts, own = gw_ref.shape[1], last_part.shape[2] // 2
    sums[...] = sums_in[...]

    def stream_done(j, grad):
        for part in range(parts):
            last_part[part, :, pl.ds((j - 1) * own, own)] = grad[:, part * own : (part + 1) * own].astype(BF)

    total = post_steps(
        doc_count, offsets, len_ref, gw_ref, gw_edge, channel, gains, sums, held, late, work, stream_done
    )
    post_end(total, gains, held, input_grad)


def post_late(g_y, s1, s2, z, a, w_in, ga0, n1, inv1, g_x2):
    return [
        (g_y, None), (s2, None), (z, 1), (a, None), (w_in, 1), (s1, None), (z, 2), (w_in, 2), (ga0, None), (n1, None),
        (inv1, None), (g_x2, None),
    ]


def post_scratch(late, offsets, count, width):
    return [
        *[pltpu.VMEM(v.shape if i is None else v.shape[1:], v.dtype) for v, i in late],
        dma(len(late)),
        pltpu.VMEM((count + EDGE, width), F32),
        pltpu.VMEM((count + EDGE, width), F32),
        pltpu.VMEM((count, width), BF),
        pltpu.VMEM((offsets - 1, count + EDGE, 128), F32),
    ]


def choose(refs, late):
    return [r if i is None else r.at[i] for r, (_, i) in zip(refs, late)]


def post(lengths, offsets, gw_parts, gw_edge, channel, gains, sums_in, late):
    mp = gw_parts.shape[1]
    count, width = late[0][0].shape
    first = (gw_parts, gw_edge, channel, gains, sums_in)

    def kernel(*refs):
        start = 1 + len(first)
        end = start + len(late)
        post_kernel(lengths.shape[1], offsets, *refs[:start], *choose(refs[start:end], late), *refs[end:])

    return pl.pallas_call(
        kernel,
        name="mixer_post",
        out_shape=(struct((mp, width, 2 * width // mp), BF), struct((count, width), BF), struct((16, width), F32)),
        in_specs=[IN_SMEM] + [IN_VMEM] * len(first) + [IN_HBM] * len(late),
        out_specs=(IN_VMEM,) * 3,
        scratch_shapes=post_scratch(late, offsets, count, width),
        compiler_params=pltpu.CompilerParams(vmem_limit_bytes=ROOM),
    )(lengths, *first, *[v for v, _ in late])


def features(length, feature_count, count):
    step = np.arange(count)
    band = np.arange(1, (feature_count - 1) // 2 + 1)
    phase = ((step[:, None] * band[None, :]) % length).astype(np.float32) * np.float32(2.0 * math.pi / length)
    position = (step / length).astype(np.float32)
    table = np.concatenate([position[:, None], np.cos(phase), np.sin(phase)], axis=1)
    return table.astype(np.float32), position


def product(left, right):
    return jnp.dot(left, right, precision=FULL_PRECISION, preferred_element_type=F32)


def norm_parts(values):
    centred = values - jnp.mean(values, axis=-1, keepdims=True)
    inverse_std = lax.rsqrt(jnp.mean(centred * centred, axis=-1, keepdims=True) + EPS_NORM)
    return centred * inverse_std, inverse_std


def norm_back(grad, gain, normed, inverse_std):
    scaled = grad * gain
    mean = jnp.mean(scaled, axis=-1, keepdims=True)
    along = jnp.mean(scaled * normed, axis=-1, keepdims=True)
    return (scaled - mean - normed * along) * inverse_std


def to_parts(values, mp):
    count, width = values.shape
    near = width // mp // HALVES
    cut = values.reshape(FOLD, count // FOLD, mp, HALVES, near).transpose(3, 2, 1, 0, 4)
    return cut.reshape(HALVES, mp, count // FOLD, FOLD * near)


def forward_fallback(lengths, tokens, weights, gain_own, channel_own, taps, table, step_col, f_in, f_out, tables):
    mp, m = lax.axis_size("mp"), lax.axis_index("mp")
    count, width = tokens.shape
    own, shard = width // mp, weights[1].shape[0]
    first_shard = jnp.concatenate([*weights[0], weights[1]], axis=1)
    chunks = [v.astype(BF) for v in (first_shard, weights[2], weights[3])]
    gains = jnp.pad(gain_own.astype(BF), ((0, 14), (0, 128 - shard)))
    channel = jnp.pad(channel_own, ((0, 16 - channel_own.shape[0]), (0, 0)))
    edges = jnp.stack([tokens[count - EDGE :], tokens[:EDGE]])
    first, up, down, gains_all, channel_all, edges_all = gather_fallback(chunks, gains, channel, edges)
    first = first.reshape(mp, width, width)
    w_in = first[:, :, : 3 * own].reshape(mp, width, 3, own).transpose(1, 2, 0, 3).reshape(width, 3 * width)
    w_out = first[:, :, 3 * own :].transpose(1, 0, 2).reshape(width, width)
    gain_rows = gains_all[:, 0:8, :shard].transpose(1, 0, 2).reshape(8, width).astype(F32)
    chan_rows = channel_all.transpose(1, 0, 2).reshape(-1, width)
    position = m * count - EDGE + jnp.arange(count + 2 * EDGE, dtype=jnp.int32)
    doc = jnp.sum((position[:, None] >= jnp.cumsum(lengths[0])[None, :]).astype(jnp.int32), axis=1)
    doc = jnp.where(position < 0, -1, doc)
    n1, inv1 = norm_parts(jnp.concatenate([edges_all[0], tokens, edges_all[1]]).astype(F32))
    a = (n1 * gain_rows[0]).astype(BF)
    z = jnp.dot(a, w_in, preferred_element_type=F32)
    s = []
    for j in range(3):
        stream, total = z[:, j * width : (j + 1) * width], None
        for k in range(taps):
            part = stream[EDGE - k : stream.shape[0] - k]
            if k:
                part = jnp.where((doc[EDGE:] == doc[EDGE - k : doc.shape[0] - k])[:, None], part, 0.0)
            term = chan_rows[3 * k + j] * part
            total = term if total is None else total + term
        s.append(total)
    w_own = s[2][:count] * s[1][:count]
    phase = product(table, f_in)
    hidden = jnp.sin(phase)
    lane = (m * own + jnp.arange(own, dtype=jnp.int32)).astype(F32)
    decay = jnp.exp(-step_col * (FAST_DECAY + (SLOW_DECAY - FAST_DECAY) * lane / (width - 1)))
    w_parts = exchange([*to_parts(w_own.astype(BF), mp)], None, 3)
    filters = jnp.split(product(hidden, f_out) * decay, HALVES, axis=1)
    halves = [conv_forward(w_parts[i], lengths, filters[i], tables) for i in range(HALVES)]
    y_back = jnp.stack(exchange([v[0] for v in halves], None, 4))
    w_parts, spectrum = jnp.stack(w_parts), jnp.stack([v[1] for v in halves])
    return (
        w_parts, y_back, spectrum, hidden, phase, decay, gain_rows, chan_rows,
        z.reshape(-1, 3, width).transpose(1, 0, 2), s[0][:count], s[1], s[2], w_own, a, n1,
        jnp.broadcast_to(inv1, (inv1.shape[0], 128)), w_in.reshape(width, 3, width).transpose(1, 0, 2), w_out, up, down,
    )


def per_device(
    tokens, cotangent, doc_lengths, in_weight, out_weight, up_weight, down_weight, gains, channel_weight,
    filter_in, filter_out, in_rows, in_cols, out_rows, out_cols, up_rows, up_cols, down_rows, down_cols,
    gain_moment, channel_moment, filter_in_moment, filter_out_moment,
):
    dp, mp = lax.axis_size("dp"), lax.axis_size("mp")
    count, width = tokens.shape
    length = count * mp
    own = channel_weight.shape[1]
    rows = in_weight.shape[0]
    hidden = up_weight.shape[1]
    taps = (channel_weight.shape[0] - 1) // 3
    most = length // 2

    in_weight, gains, gain_moment = in_weight.transpose(1, 0, 2), gains.T, gain_moment.T

    table, step = features(length, filter_in.shape[0], most)
    tables = tuple(jnp.asarray(t) for t in transform_tables(count // 2))
    run = mixer_forward if dp == 8 else forward_fallback
    (
        w_parts, y_back, spectrum, hidden_filter, phase, decay, gain_rows, chan_rows, z, s0, s1, s2, w_own,
        a, n1, inv1, w_in, w_out, whole_up, whole_down,
    ) = run(
        doc_lengths, tokens, (in_weight, out_weight, up_weight, down_weight), gains, channel_weight, taps,
        table, step[:, None], filter_in, filter_out, tables,
    )
    whole_up = whole_up.reshape(mp, width, hidden)
    whole_down = whole_down.reshape(mp, width, hidden)

    activations, up_part, down_part, out_part, gy_parts, g_y, g_s0, g_x2, feed_sums, g_s0_own = feed(
        y_back, w_own, s0, tokens, cotangent, w_out, gain_rows, chan_rows, 3 * taps, whole_up, whole_down
    )

    up_part, down_part = [p.reshape(mp, dp, rows, hidden) for p in (up_part, down_part)]
    gw_back, gw_edge, sums, g_a0, fin_part, fout_part, *partials, first_part = mixer_backward(
        doc_lengths, taps, gy_parts, g_s0_own, channel_weight, feed_sums, up_part, down_part, g_s0, z, a, w_in,
        chan_rows, out_part, w_parts, tables, spectrum, decay, hidden_filter, filter_out, phase, table,
    )

    results = finish(
        doc_lengths, taps, (gw_back, gw_edge, chan_rows, gain_rows, sums),
        post_late(g_y, s1, s2, z, a, w_in, g_a0, n1, inv1, g_x2), partials, first_part, fin_part, fout_part,
        (
            in_weight, out_weight, in_rows, out_rows, up_rows, down_rows,
            in_cols, out_cols, up_cols, down_cols, gains, gain_moment,
        ),
        up_weight, down_weight,
        (channel_weight, channel_moment, filter_in, filter_in_moment, filter_out, filter_out_moment),
    )
    (
        input_grad, norm, in_g, out_g, up_g, down_g, gain_g, in_n, out_n, up_n, down_n, gain_n, gain_m,
        in_r, out_r, up_r, down_r, in_c, out_c, up_c, down_c,
        chan_g, chan_n, chan_m, fin_g, fin_n, fin_m, fout_g, fout_n, fout_m,
    ) = hand_out(results, own)
    return (
        activations, input_grad, norm.reshape(()),
        in_g.transpose(1, 0, 2), out_g, up_g, down_g, gain_g.T, chan_g, fin_g, fout_g,
        in_n.transpose(1, 0, 2), out_n, up_n, down_n, gain_n.T, chan_n, fin_n, fout_n,
        in_r, in_c, out_r, out_c, up_r, up_c, down_r, down_c, gain_m.T, chan_m, fin_m, fout_m,
    )


def solution(mesh):
    tokens, by_rows, by_cols, both = P(("dp", "mp"), None), P("dp", None), P(None, "mp"), P("dp", "mp")
    cube, vec_dp, vec_mp = P("dp", None, "mp"), P("dp"), P("mp")
    moments = (vec_dp, by_cols, vec_dp, vec_mp, vec_dp, vec_mp, vec_dp, vec_mp)
    weights = (cube, both, both, both, by_rows, by_cols, P(), by_cols)
    small = (by_rows, by_cols, P(), by_cols)
    return jax.shard_map(
        per_device,
        mesh=mesh,
        in_specs=(tokens, tokens, by_rows) + weights + moments + small,
        out_specs=(tokens, tokens, P()) + weights + weights + moments + small,
        check_vma=False,
    )
```

```python
import functools
import math

import jax
import jax.numpy as jnp
import ml_dtypes
import numpy as np
from jax import lax
from jax.experimental import pallas as pl
from jax.experimental.pallas import tpu as pltpu
from jax.sharding import PartitionSpec as P

EPS_NORM = 1e-05
MOMENT_DECAY = 0.5
CLIP_NORM = 1.0
CLIP_STEP = 0.25
STEP_RATE = 2.0
FAST_DECAY = 15.35
SLOW_DECAY = 3.07
FULL_PRECISION = lax.Precision.HIGHEST
BF = jnp.bfloat16
F32 = jnp.float32
MESH = pl.DeviceIdType.MESH
BLOCK = 256
EDGE = 16
HALVES = 2
FOLD = 4
ROOM = 62 << 20
IN_VMEM = pl.BlockSpec(memory_space=pltpu.VMEM)
IN_HBM = pl.BlockSpec(memory_space=pl.ANY)
IN_SMEM = pl.BlockSpec(memory_space=pltpu.SMEM)


def struct(shape, dtype):
    return jax.ShapeDtypeStruct(tuple(shape), dtype)


def transform_tables(block):
    freq = 2 * np.arange(block)[:, None] + 1
    angle = np.pi * (freq * np.arange(block)[None, :] % (4 * block)) / (2 * block)
    table = np.concatenate([np.cos(angle), -np.sin(angle)], axis=0).astype(np.float32)
    high = table.astype(ml_dtypes.bfloat16)
    low = (table - high.astype(np.float32)).astype(ml_dtypes.bfloat16)
    return high, low, np.ascontiguousarray(high.T), np.ascontiguousarray(low.T)


def mm(left, right):
    return lax.dot_general(left, right, (((1,), (0,)), ((), ())), preferred_element_type=F32)


def split(values):
    high = values.astype(BF)
    return high, (values - high.astype(F32)).astype(BF)


def load_rows(ref, start, count, lead=()):
    odd = lax.rem(start, 8)
    tile = ref[lead + (pl.ds(lax.div(start, 8), count // 8 + 1),)]
    width = tile.shape[-1]
    tile = pltpu.roll(tile, lax.rem(8 - odd, 8), axis=1)
    first = lax.broadcasted_iota(jnp.int32, (count // 8, 8, width), 1) < 8 - odd
    return jnp.where(first, tile[:-1], tile[1:]).reshape(count, width)


def tiles(values):
    return values.reshape(values.shape[0] // 8, 8, values.shape[1])


def unpack(target, source, channels):
    parts, rows, width = source.shape
    fold, count = width // channels, rows // 8
    for part in range(parts):
        for piece in range(fold):
            values = source[part, :, piece * channels : (piece + 1) * channels].astype(F32)
            target[pl.ds((part * fold + piece) * count, count), :, 0:channels] = tiles(values)


def pack_block(target, index, values, channels):
    rows = target.shape[1]
    fold, pieces = target.shape[2] // channels, values.shape[0] // rows
    for i in range(pieces):
        part, piece = divmod(index * pieces + i, fold)
        source = values[i * rows : (i + 1) * rows, 0:channels]
        target[part, :, pl.ds(piece * channels, channels)] = source.astype(target.dtype)


def beside(values):
    return [jnp.concatenate(values[i : i + 2], axis=1) for i in range(0, len(values), 2)]


def apart(values, lanes):
    return [v[:, i : i + lanes] for v in values for i in range(0, v.shape[1], lanes)]


def pair_rows(index, block, size):
    first = pl.multiple_of(index * size, size)
    return pl.ds(first, size), pl.ds(pl.multiple_of(block + first, size), size)


def signs(size, width, scale):
    odd = lax.broadcasted_iota(jnp.int32, (size, width), 0) % 2
    return jnp.where(odd == 0, scale, -scale).astype(F32)


def filter_spectrum(filter_ref, spectrum, raw, tables, block):
    count, lanes = raw.shape[0], raw.shape[2]
    high, low = tables[0][...], tables[1][...]
    terms = [split(filter_ref[pl.ds(lag * block, block), :]) for lag in range(count)]
    tops, rests = beside([t[0] for t in terms]), beside([t[1] for t in terms])
    done = [mm(high, t) + mm(high, r) + mm(low, t) for t, r in zip(tops, rests)]
    for lag, values in enumerate(apart(done, lanes)):
        raw[lag] = values
    scale = 1.0 / block

    def body(index, carry):
        re_rows, im_rows = pair_rows(index, block, 8)
        sign = signs(8, raw.shape[2], scale)
        for lag in range(count):
            re, im = raw[lag, re_rows, :] * scale, raw[lag, im_rows, :] * scale
            if lag:
                re = re - sign * raw[lag - 1, im_rows, :]
                im = im + sign * raw[lag - 1, re_rows, :]
            spectrum[lag, re_rows, :] = re
            spectrum[lag, im_rows, :] = im
        return carry

    lax.fori_loop(0, block // 8, body, 0)


def slot_blocks(source, target, tables, start, length, block):
    high, low = tables[0][...], tables[1][...]
    blocks = []
    for index in range(target.shape[0]):
        values = load_rows(source, start + index * block, block)
        inside = lax.broadcasted_iota(jnp.int32, values.shape, 0) + index * block < length
        blocks.append(jnp.where(inside, values, 0.0).astype(BF))
    done = [mm(high, values) + mm(low, values) for values in beside(blocks)]
    for index, values in enumerate(apart(done, target.shape[2])):
        target[index] = values


def inverse(top, rest, tables):
    high, low = tables[2][...], tables[3][...]
    count, lanes = top.shape[0], top.shape[2]
    tops, rests = beside([top[i] for i in range(count)]), beside([rest[i] for i in range(count)])
    return apart([mm(high, t) + mm(high, r) + mm(low, t) for t, r in zip(tops, rests)], lanes)


def document_starts(len_ref, count):
    starts, at = [], jnp.int32(0)
    for slot in range(count):
        starts.append(at)
        at = at + len_ref[0, slot]
    return starts


def merge_slots(slots, starts, put, total, block, most):
    for index in range(total // block):
        first = index * block
        merged = None
        for slot, start in enumerate(starts):
            at = jnp.clip(first - start, -block, most) + block
            values = load_rows(slots, at, block, (slot,))
            if merged is None:
                merged = values
            else:
                inside = lax.broadcasted_iota(jnp.int32, values.shape, 0) + first >= start
                merged = jnp.where(inside, values, merged)
        put(index, merged)


def forward_products(spectrum, raw, top, rest, block):
    count = raw.shape[0]

    def body(index, carry):
        re_rows, im_rows = pair_rows(index, block, 16)
        hr = [spectrum[i, re_rows, :] for i in range(count)]
        hi = [spectrum[i, im_rows, :] for i in range(count)]
        xr = [raw[i, re_rows, :] for i in range(count)]
        xi = [raw[i, im_rows, :] for i in range(count)]
        for out in range(count):
            re = hr[0] * xr[out] - hi[0] * xi[out]
            im = hr[0] * xi[out] + hi[0] * xr[out]
            for lag in range(1, out + 1):
                re = re + (hr[lag] * xr[out - lag] - hi[lag] * xi[out - lag])
                im = im + (hr[lag] * xi[out - lag] + hi[lag] * xr[out - lag])
            top[out, re_rows, :], rest[out, re_rows, :] = split(re)
            top[out, im_rows, :], rest[out, im_rows, :] = split(im)
        return carry

    lax.fori_loop(0, block // 16, body, 0)


def backward_products(spectrum, grad, raw, total, top, rest, block, first_slot):
    count = raw.shape[0]

    def body(index, carry):
        re_rows, im_rows = pair_rows(index, block, 16)
        gr = [grad[i, re_rows, :] for i in range(count)]
        gi = [grad[i, im_rows, :] for i in range(count)]
        hr = [spectrum[i, re_rows, :] for i in range(count)]
        hi = [spectrum[i, im_rows, :] for i in range(count)]
        for out in range(count):
            re = hr[0] * gr[out] + hi[0] * gi[out]
            im = hr[0] * gi[out] - hi[0] * gr[out]
            for later in range(out + 1, count):
                lag = later - out
                re = re + (hr[lag] * gr[later] + hi[lag] * gi[later])
                im = im + (hr[lag] * gi[later] - hi[lag] * gr[later])
            top[out, re_rows, :], rest[out, re_rows, :] = split(re)
            top[out, im_rows, :], rest[out, im_rows, :] = split(im)
        xr = [raw[i, re_rows, :] for i in range(count)]
        xi = [raw[i, im_rows, :] for i in range(count)]
        for lag in range(count):
            re = im = None
            for at in range(count - lag):
                a = xr[at] * gr[at + lag] + xi[at] * gi[at + lag]
                b = xr[at] * gi[at + lag] - xi[at] * gr[at + lag]
                re = a if re is None else re + a
                im = b if im is None else im + b
            if not first_slot:
                re = re + total[lag, re_rows, :]
                im = im + total[lag, im_rows, :]
            total[lag, re_rows, :] = re
            total[lag, im_rows, :] = im
        return carry

    lax.fori_loop(0, block // 16, body, 0)


def filter_gradient(total, top, rest, tables, out_ref, lanes, channels, block):
    count, width = total.shape[0], total.shape[2]
    scale = 1.0 / block

    def body(index, carry):
        re_rows, im_rows = pair_rows(index, block, 16)
        sign = signs(16, width, 1.0)
        for lag in range(count):
            re, im = total[lag, re_rows, :], total[lag, im_rows, :]
            if lag + 1 < count:
                re = re + sign * total[lag + 1, im_rows, :]
                im = im - sign * total[lag + 1, re_rows, :]
            top[lag, re_rows, :], rest[lag, re_rows, :] = split(re * scale)
            top[lag, im_rows, :], rest[lag, im_rows, :] = split(im * scale)
        return carry

    lax.fori_loop(0, block // 16, body, 0)
    for lag, values in enumerate(inverse(top, rest, tables)):
        out_ref[pl.ds(lag * block, block), lanes] = values[:, 0:channels]


def conv_forward_steps(doc_count, len_ref, x_ref, tables, y_ref, spectrum, full, raw, top, rest, slots, between):
    block, blocks = spectrum.shape[1] // 2, spectrum.shape[0]
    channels = x_ref.shape[2] // FOLD
    unpack(full, x_ref, channels)
    starts = document_starts(len_ref, doc_count)
    for slot in range(doc_count):
        slot_blocks(full, raw, tables, starts[slot], len_ref[0, slot], block)
        forward_products(spectrum, raw, top, rest, block)
        for out, values in enumerate(inverse(top, rest, tables)):
            slots[slot, pl.ds((1 + out) * block // 8, block // 8)] = tiles(values)
        between(slot)

    def put(index, values):
        pack_block(y_ref, index, values, channels)

    tokens = math.prod(x_ref.shape) // channels
    merge_slots(slots, starts, put, tokens, block, blocks * block)


def conv_backward_steps(
    doc_count, len_ref, g_ref, x_ref, spectrum, skip, tables, gw_ref, edge_ref, gf_ref, lanes,
    g_full, x_full, grad, raw, top, rest, total, slots, between,
):
    block, blocks, channels = spectrum.shape[1] // 2, spectrum.shape[0], x_ref.shape[2] // FOLD
    unpack(g_full, g_ref, channels)
    unpack(x_full, x_ref, channels)
    starts = document_starts(len_ref, doc_count)
    for slot in range(doc_count):
        slot_blocks(g_full, grad, tables, starts[slot], len_ref[0, slot], block)
        slot_blocks(x_full, raw, tables, starts[slot], len_ref[0, slot], block)
        backward_products(spectrum, grad, raw, total, top, rest, block, slot == 0)
        for out, values in enumerate(inverse(top, rest, tables)):
            slots[slot, pl.ds((1 + out) * block // 8, block // 8)] = tiles(values)
        between(slot)
    edge_ref[...] = jnp.zeros(edge_ref.shape, edge_ref.dtype)
    parts = x_ref.shape[0]
    tokens = math.prod(x_ref.shape) // channels
    each = tokens // parts // block

    def put(index, values):
        pack_block(gw_ref, index, values, channels)
        if index % each == 0 and index:
            own = g_full[pl.ds(index * block // 8, EDGE // 8)].reshape(values[0:EDGE].shape)[:, 0:channels] * skip
            edge_ref[index // each - 1, :, 0:channels] = (values[0:EDGE, 0:channels] + own).astype(edge_ref.dtype)

    merge_slots(slots, starts, put, tokens, block, blocks * block)
    between(doc_count)
    filter_gradient(total, top, rest, tables, gf_ref, lanes, channels, block)


def lanes_for(channels):
    return -(-channels // 128) * 128


def conv_scratch(x_shape, blocks, block, docs):
    channels = x_shape[2] // FOLD
    tokens, lanes = math.prod(x_shape) // channels, lanes_for(channels)
    wide = (blocks, 2 * block, lanes)
    full = pltpu.VMEM(((tokens + blocks * block) // 8 + 1, 8, lanes), F32)
    slots = pltpu.VMEM((docs, (blocks + 2) * block // 8 + 1, 8, lanes), F32)
    return full, pltpu.VMEM(wide, F32), pltpu.VMEM(wide, BF), slots


def conv_forward_kernel(doc_count, len_ref, x_ref, filter_ref, t0, t1, t2, t3, y_ref, spectrum, full, raw, top, rest, slots):
    tables = (t0, t1, t2, t3)
    filter_spectrum(filter_ref, spectrum, raw, tables, spectrum.shape[1] // 2)
    conv_forward_steps(
        doc_count, len_ref, x_ref, tables, y_ref, spectrum, full, raw, top, rest, slots, lambda slot: None
    )


def conv_forward(x, lengths, filters, tables):
    docs, block = lengths.shape[1], tables[0].shape[1]
    blocks, channels = filters.shape[0] // block, filters.shape[1]
    filters = jnp.pad(filters, ((0, 0), (0, lanes_for(channels) - channels)))
    full, raw, low, slots = conv_scratch(x.shape, blocks, block, docs)
    return pl.pallas_call(
        functools.partial(conv_forward_kernel, docs),
        name="conv_forward",
        out_shape=(struct(x.shape, BF), struct((blocks, 2 * block, filters.shape[1]), F32)),
        in_specs=[IN_SMEM] + [IN_VMEM] * 6,
        out_specs=(IN_VMEM, IN_VMEM),
        scratch_shapes=[full, raw, low, low, slots],
        compiler_params=pltpu.CompilerParams(vmem_limit_bytes=ROOM),
    )(lengths, x, filters, *tables)


def conv_backward_kernel(doc_count, len_ref, g_ref, x_ref, spectrum, skip_ref, t0, t1, t2, t3, gw_ref, edge_ref, gf_ref, *work):
    conv_backward_steps(
        doc_count, len_ref, g_ref, x_ref, spectrum, skip_ref[...], (t0, t1, t2, t3), gw_ref, edge_ref, gf_ref,
        slice(None), *work, lambda slot: None,
    )


def conv_backward(g, x, lengths, spectrum, skip_gain, tables):
    blocks, block, channels = spectrum.shape[0], spectrum.shape[1] // 2, x.shape[2] // FOLD
    docs = lengths.shape[1]
    full, raw, low, slots = conv_scratch(x.shape, blocks, block, docs)
    return pl.pallas_call(
        functools.partial(conv_backward_kernel, docs),
        name="conv_backward",
        out_shape=(
            struct(x.shape, BF),
            struct((x.shape[0], EDGE, lanes_for(channels)), BF),
            struct((blocks * block, channels), F32),
        ),
        in_specs=[IN_SMEM] + [IN_VMEM] * 8,
        out_specs=(IN_VMEM,) * 3,
        scratch_shapes=[full, full, raw, raw, low, low, raw, slots],
        compiler_params=pltpu.CompilerParams(vmem_limit_bytes=ROOM),
    )(lengths, g, x, spectrum, skip_gain, *tables)


def turned(value, bit):
    return value + bit - 2 * bit * ((value // bit) % 2)


def send(source, target, send_sem, recv_sem, device):
    copy = pltpu.make_async_remote_copy(
        src_ref=source,
        dst_ref=target,
        send_sem=send_sem,
        recv_sem=recv_sem,
        device_id=device,
        device_id_type=MESH,
    )
    copy.start()
    return copy


def greet(peers):
    barrier = pltpu.get_barrier_semaphore()
    for peer in peers:
        pl.semaphore_signal(barrier, inc=1, device_id=peer, device_id_type=MESH)
    pl.semaphore_wait(barrier, len(peers))


def ring(me, count):
    return [lax.rem(me + step, count) for step in range(1, count)]


def dma(*shape):
    return pltpu.SemaphoreType.DMA(shape)


def gather_fallback(chunks, gains, channel, edges):
    mp = lax.axis_size("mp")
    down = [(i, (i + 1) % mp) for i in range(mp)]
    up = [(i, (i - 1) % mp) for i in range(mp)]
    spread = [lax.all_gather(lax.all_gather(c, "dp"), "mp") for c in chunks]
    return (
        *spread,
        lax.all_gather(gains, "dp"),
        lax.all_gather(channel, "mp"),
        jnp.stack([lax.ppermute(edges[0], "mp", down), lax.ppermute(edges[1], "mp", up)]),
    )


def exchange_kernel(count, has_edge, *refs):
    sources, refs = refs[: count + has_edge], refs[count + has_edge :]
    targets, refs = refs[: count + has_edge], refs[count + has_edge :]
    send_sem, recv_sem, edge_send, edge_recv = refs
    d, m, mp = lax.axis_index("dp"), lax.axis_index("mp"), lax.axis_size("mp")
    greet([(d, e) for e in ring(m, mp)])
    copies = []
    for step, e in reversed(list(enumerate(ring(m, mp)))):
        for i in range(count):
            copies.append(
                send(sources[i].at[e], targets[i].at[m], send_sem.at[i, step], recv_sem.at[i, step], (d, e))
            )
    if has_edge:
        before = lax.rem(m + mp - 1, mp)
        copies.append(send(sources[count], targets[count], edge_send.at[0], edge_recv.at[0], (d, before)))
    for i in range(count):
        targets[i][m] = sources[i][m]
    for copy in copies:
        copy.wait()


def exchange(arrays, edge, collective_id):
    mp, count = lax.axis_size("mp"), len(arrays)
    inputs = list(arrays) + ([] if edge is None else [edge])
    return pl.pallas_call(
        functools.partial(exchange_kernel, count, int(edge is not None)),
        name="exchange_%d" % collective_id,
        out_shape=tuple(struct(a.shape, a.dtype) for a in inputs),
        in_specs=[IN_VMEM] * len(inputs),
        out_specs=(IN_VMEM,) * len(inputs),
        scratch_shapes=[dma(count, mp - 1), dma(count, mp - 1), dma(1), dma(1)],
        compiler_params=pltpu.CompilerParams(
            collective_id=collective_id, has_side_effects=True, vmem_limit_bytes=ROOM
        ),
    )(*inputs)


class Flow:
    def __init__(self, part, refs, lanes=slice(None)):
        self.part, self.lanes = part, lanes
        (self.own, self.from_core, self.from_y2, self.from_x2, self.from_x1, self.from_y1, self.from_z) = refs[:7]
        self.own_sem, self.p_send, self.p_recv, self.z_send, self.z_recv = refs[7:]
        self.d, self.m, self.mp = lax.axis_index("dp"), lax.axis_index("mp"), lax.axis_size("mp")
        self.half = self.mp // 2
        self.y, self.x, self.core = self.d // 4, (self.d // 2) % 2, self.d % 2
        self.pending = []

    def push(self, slot, source, target, bit):
        peer = (turned(self.d, bit), self.m)
        copy = send(source, target, self.p_send.at[slot], self.p_recv.at[slot], peer)
        self.pending.append(copy)
        return copy

    def start(self):
        self.copy = self.push(0, self.part.at[:, :, :, 1 - self.core, :, self.lanes], self.from_core, 1)
        self.local = pltpu.make_async_copy(self.part.at[:, :, :, self.core, :, self.lanes], self.own, self.own_sem.at[0])
        self.local.start()

    def core_stage(self):
        own, half, y, x = self.own, self.half, self.y, self.x
        self.local.wait()
        self.copy.wait_recv()

        def body(i, carry):
            at = (i // 4, (i // 2) % 2, i % 2)
            own[at] = own[at] + self.from_core[at]
            return carry

        lax.fori_loop(0, self.mp * 4, body, 0)
        low, high = pl.ds(0, half), pl.ds(half, self.mp - half)
        self.copies = [
            self.push(1, own.at[low, 1 - y], self.from_y2, 4),
            self.push(2, own.at[high, :, 1 - x], self.from_x2, 2),
        ]

    def second_sum(self):
        own, half, y, x = self.own, self.half, self.y, self.x
        for copy in self.copies:
            copy.wait_recv()

        def body(i, carry):
            a, b = i // 2, i % 2
            own[a, y, b] = own[a, y, b] + self.from_y2[a, b]
            own[half + a, b, x] = own[half + a, b, x] + self.from_x2[a, b]
            return carry

        lax.fori_loop(0, half * 2, body, 0)

    def second_stage(self):
        own, half, y, x = self.own, self.half, self.y, self.x
        self.second_sum()
        low, high = pl.ds(0, half), pl.ds(half, self.mp - half)
        self.copies = [
            self.push(3, own.at[low, y, 1 - x], self.from_x1, 2),
            self.push(4, own.at[high, 1 - y, x], self.from_y1, 4),
        ]

    def third_stage(self):
        own, half, y, x = self.own, self.half, self.y, self.x
        for copy in self.copies:
            copy.wait_recv()

        def body(a, carry):
            own[a, y, x] = own[a, y, x] + self.from_x1[a]
            own[half + a, y, x] = own[half + a, y, x] + self.from_y1[a]
            return carry

        lax.fori_loop(0, half, body, 0)

    def send_z(self):
        self.copies = [
            send(
                self.own.at[e, self.y, self.x], self.from_z.at[step], self.z_send.at[step], self.z_recv.at[step],
                (self.d, e),
            )
            for step, e in enumerate(ring(self.m, self.mp))
        ]
        self.pending.extend(self.copies)

    def finish(self, out):
        for copy in self.copies:
            copy.wait_recv()
        total = self.own[self.m, self.y, self.x].astype(F32)
        for step in range(self.mp - 1):
            total = total + self.from_z[step].astype(F32)
        out[:, self.lanes] = total

    def drain(self):
        for copy in self.pending:
            copy.wait_send()


FLOW_REFS = 12


def flow_scratch(mp, block, over_z=True):
    half = mp // 2
    leads = ((mp, 2, 2), (mp, 2, 2), (half, 2), (mp - half, 2), (half,), (mp - half,))
    last = (mp - 1,) + block if over_z else (1, 16, 128)
    return [pltpu.VMEM(lead + block, BF) for lead in leads] + [pltpu.VMEM(last, BF)] + [dma(1), dma(5), dma(5), dma(mp - 1), dma(mp - 1)]


class SmallSums:
    def __init__(self, small, outs, wide, refs):
        count = len(small)
        self.small, self.outs, self.wide = small, outs, wide
        self.running, self.from_dp, self.from_mp = [refs[i * count : (i + 1) * count] for i in range(3)]
        self.s_send, self.s_recv = refs[3 * count :]
        self.pending = []

    def start(self, stage):
        bit = (1, 2, 4)[stage]
        d, m = lax.axis_index("dp"), lax.axis_index("mp")
        if stage == 0:
            for i, ref in enumerate(self.small):
                self.running[i][0] = ref[...]
        self.copies = []
        for i in range(len(self.small)):
            at = i * 8 + stage
            self.copies.append(
                send(
                    self.running[i].at[stage], self.from_dp[i].at[stage], self.s_send.at[at], self.s_recv.at[at],
                    (turned(d, bit), m),
                )
            )
        self.pending.extend(self.copies)

    def end(self, stage):
        for i, copy in enumerate(self.copies):
            copy.wait_recv()
            self.running[i][stage + 1] = self.running[i][stage] + self.from_dp[i][stage]

    def start_mp(self):
        d, m, mp = lax.axis_index("dp"), lax.axis_index("mp"), lax.axis_size("mp")
        self.copies = []
        for i, wide in enumerate(self.wide):
            if wide:
                for step, e in enumerate(ring(m, mp)):
                    at = i * 8 + 3 + step
                    self.copies.append(
                        send(
                            self.running[i].at[3], self.from_mp[i].at[m], self.s_send.at[at], self.s_recv.at[at],
                            (d, e),
                        )
                    )
                self.from_mp[i][m] = self.running[i][3]
        self.pending.extend(self.copies)

    def end_mp(self):
        for copy in self.copies:
            copy.wait_recv()
        for i, wide in enumerate(self.wide):
            if wide:
                total = self.from_mp[i][0]
                for e in range(1, lax.axis_size("mp")):
                    total = total + self.from_mp[i][e]
                self.outs[i][...] = total
            else:
                self.outs[i][...] = self.running[i][3]

    def drain(self):
        for copy in self.pending:
            copy.wait_send()


def small_scratch(small, mp):
    scratch = []
    for lead in (4, 3, mp):
        scratch += [pltpu.VMEM((lead,) + s.shape, F32) for s in small]
    return scratch + [dma(8 * len(small)), dma(8 * len(small))]


def scatter_fallback(part):
    over_mp = lax.psum_scatter(part, "mp", scatter_dimension=0)
    return lax.psum_scatter(over_mp, "dp", scatter_dimension=0).astype(F32)


def cored(part):
    return part.reshape((part.shape[0], 2, 2, 2) + part.shape[2:])


class Blocks:
    def __init__(self, pairs, send_sem, recv_sem):
        self.pairs, self.send_sem, self.recv_sem = pairs, send_sem, recv_sem
        self.d, self.m, self.mp = lax.axis_index("dp"), lax.axis_index("mp"), lax.axis_size("mp")

    def start(self):
        self.copies = []
        for step, e in reversed(list(enumerate(ring(self.m, self.mp)))):
            for i, (source, target) in enumerate(self.pairs):
                sems = self.send_sem.at[i, step], self.recv_sem.at[i, step]
                self.copies.append(send(source.at[e], target.at[self.m], *sems, (self.d, e)))
        for source, target in self.pairs:
            target[self.m] = source[self.m]

    def arrive(self):
        for copy in self.copies:
            copy.wait_recv()

    def drain(self):
        for copy in self.copies:
            copy.wait_send()


def stream_zero(offsets, edge, gs, z, w, channel, marks, sums, feed_sums):
    count = gs.shape[0] - EDGE
    same = [None] + [marks[k - 1, :, 0:1] > 0.0 for k in range(1, offsets)]
    gs[pl.ds(count, EDGE), :] = edge[...].astype(F32)
    sums[...] = jnp.zeros(sums.shape, F32)
    g_z = short_backward(0, gs, z, channel, same, offsets, count, sums).astype(BF)
    sums[pl.ds(3 * offsets, 1), :] = feed_sums[1:2, :]
    sums[pl.ds(3 * offsets + 2, 1), :] = feed_sums[0:1, :]
    return g_z, dot_nt(g_z, w[...])


def mixer_backward_kernel(doc_count, offsets, len_ref, g_parts, edge, channel_own, feed_sums, part_a, part_b, *refs):
    late_refs, refs = refs[:17], refs[17:]
    gw_back, gw_edge_back, sums, ga0, fin_part, fout_part, partial_a, b_low, b_high, part_c, refs = *refs[:10], refs[10:]
    held, refs = refs[:16], refs[16:]
    (
        late_sem, edge_back, gs, marks, gf_ref, g_in, gw, gw_edge, g_full, x_full, grad, raw,
        top, rest, total, slots, b_send, b_recv, c_send, c_recv, e_sem, *refs,
    ) = refs
    a_refs, b_refs = refs[:FLOW_REFS], refs[FLOW_REFS:]
    z, acts, w, channel, out_part, x_ref, t0, t1, t2, t3, spectrum, decay, hidden, f_out, phase, table = held
    tables = (t0, t1, t2, t3)
    parts = x_ref.shape[1]
    near = x_ref.shape[3] // FOLD
    half = near * HALVES
    own_count = ga0.shape[0]
    d, m, mp = lax.axis_index("dp"), lax.axis_index("mp"), lax.axis_size("mp")
    a, b = Flow(part_a, a_refs), Flow(part_b, b_refs)
    incoming, outgoing = [], []
    for side in range(HALVES):
        incoming.append(Blocks([(g_parts.at[side], g_in.at[side])], b_send.at[side], b_recv.at[side]))
        pairs = [(gw.at[side], gw_back.at[side]), (gw_edge.at[side], gw_edge_back.at[side])]
        outgoing.append(Blocks(pairs, c_send.at[side], c_recv.at[side]))
    late = Late(late_refs, (gs.at[pl.ds(0, own_count)],) + tuple(held), late_sem)
    greet([(turned(d, bit), m) for bit in (1, 2, 4)] + [(d, e) for e in ring(m, mp)])
    edge_copy = send(edge, edge_back, e_sem.at[0], e_sem.at[1], (d, lax.rem(m + mp - 1, mp)))
    for copies in incoming:
        copies.start()
    a.start()
    mark_same(marks, len_ref, doc_count, m * own_count - EDGE)
    a.core_stage()
    b.start()
    late.need(0, 1, 2, 3, 4, 5)
    edge_copy.wait_recv()
    g_z, back = stream_zero(offsets, edge_back, gs, z, w, channel, marks, sums, feed_sums)
    ga0[...] = back
    size = part_c.shape[4]
    for first in range(0, parts, 2):
        in_grad = dot_tn(acts[pl.ds(EDGE, own_count), :], g_z[:, first * half : (first + 2) * half])
        for part in range(first, first + 2):
            cols = slice((part - first) * half, (part - first + 1) * half)
            for owner in range(8):
                at = (part, owner // 4, owner // 2 % 2, owner % 2, slice(None))
                rows = slice(owner * size, (owner + 1) * size)
                part_c[at + (pl.ds(0, half),)] = in_grad[rows, cols].astype(BF)
                part_c[at + (pl.ds(half, half),)] = out_part[part, rows]
    late.need(*range(6, 17))
    skip = channel_own[channel_own.shape[0] - 1 :, :]

    def first_side(step):
        if step == 0:
            b.core_stage()
        if step == 2:
            a.second_stage()

    def last_side(step):
        if step == doc_count:
            a.third_stage()

    for side in range(HALVES):
        incoming[side].arrive()
        between = (first_side, last_side)[side]
        lanes = pl.ds(side * near, near)

        def after(step, side=side, between=between):
            if step == doc_count:
                outgoing[side].start()
            between(step)

        conv_backward_steps(
            doc_count, len_ref, g_in.at[side], x_ref.at[side], spectrum.at[side], skip[:, side * near : (side + 1) * near],
            tables, gw.at[side], gw_edge.at[side], gf_ref, lanes, g_full, x_full, grad, raw, top, rest, total, slots, after,
        )
    g_raw = gf_ref[...] * decay[...]
    fout_part[...] = near_product(hidden[...], g_raw, dot_tn)
    fin_part[...] = near_product(table[...], near_product(g_raw, f_out[...], dot_nt) * jnp.cos(phase[...]), dot_tn)
    for e in range(parts):
        partial_a[e] = a.own[e, a.y, a.x]
    b.second_sum()
    for e in range(parts // 2):
        for other in range(2):
            b_low[e, other] = b.own[e, b.y, other]
            b_high[e, other] = b.own[parts // 2 + e, other, b.x]
    for copies in outgoing:
        copies.arrive()
    edge_copy.wait_send()
    for copies in incoming + outgoing:
        copies.drain()
    for flow in (a, b):
        flow.drain()


def mixer_backward(
    lengths, offsets, g_parts, edge, channel_own, feed_sums, part_a, part_b, g_s0, z, a, w_in, channel, out_part, x,
    tables, spectrum, decay, hidden, f_out, phase, table,
):
    dp, mp = lax.axis_size("dp"), lax.axis_size("mp")
    parts, docs = x.shape[1], lengths.shape[1]
    blocks, block, near = spectrum.shape[1], spectrum.shape[2] // 2, x.shape[3] // FOLD
    half, width = HALVES * near, 2 * HALVES * near
    size = part_a.shape[2]
    full = channel.shape[1]
    if dp != 8:
        g_in = exchange([*g_parts], edge, 5)
        edge_back = g_in[HALVES]
        halves = []
        for side in range(HALVES):
            skip = channel_own[-1:, side * near : (side + 1) * near]
            halves.append(conv_backward(g_in[side], x[side], lengths, spectrum[side], skip, tables))
        g_raw = jnp.concatenate([v[2] for v in halves], axis=1) * decay
        fin, fout = product(table.T, product(g_raw, f_out.T) * jnp.cos(phase)), product(hidden.T, g_raw)
        backs = exchange([v[i] for i in range(2) for v in halves], None, 6)
        gw_back, gw_edge_back = jnp.stack(backs[:HALVES]), jnp.stack(backs[HALVES:])
        count = g_s0.shape[0]
        gs = jnp.concatenate([g_s0, edge_back.astype(F32)])
        position = lax.axis_index("mp") * count - EDGE + jnp.arange(count + 2 * EDGE, dtype=jnp.int32)
        doc = jnp.sum((position[:, None] >= jnp.cumsum(lengths[0])[None, :]).astype(jnp.int32), axis=1)
        doc = jnp.where(position < 0, -1, doc)
        same = [None] + [(doc[EDGE:] == doc[EDGE - k : doc.shape[0] - k])[:, None] for k in range(1, offsets)]
        g_z, sums = None, jnp.zeros((16, full), F32)
        for k in range(offsets):
            later, before = gs[k : count + k], z[0, EDGE - k : EDGE - k + count]
            if k:
                later, before = jnp.where(same[k][k : count + k], later, 0.0), jnp.where(same[k][:count], before, 0.0)
            g_z = channel[3 * k] * later if g_z is None else g_z + channel[3 * k] * later
            sums = sums.at[3 * k].set(jnp.sum(gs[:count] * before, axis=0))
        sums = sums.at[3 * offsets].set(feed_sums[1]).at[3 * offsets + 2].set(feed_sums[0])
        g_z = g_z.astype(BF)
        grad = dot_tn(a[EDGE : EDGE + count], g_z).reshape(full, mp, half).transpose(1, 0, 2).astype(BF)
        part_c = jnp.concatenate([grad, out_part], axis=2).reshape(mp, dp, size, width)
        over_dp = [lax.psum_scatter(p, "dp", scatter_dimension=1) for p in (part_a, part_b)]
        return (
            gw_back, gw_edge_back, sums, dot_nt(g_z, w_in[0]), fin, fout, *over_dp, None, part_c,
        )
    edge_shape = (HALVES, parts, EDGE, lanes_for(near))
    own, own_c = part_a.shape[2:], (size, width)
    rows, raw, low, slots = conv_scratch(x.shape[1:], blocks, block, docs)
    first = (g_parts, edge, channel_own, feed_sums)
    late = [
        (g_s0, None), (z, 0), (a, None), (w_in, 0), (channel, None), (out_part, None), (x, None),
        *[(t, None) for t in tables], (spectrum, None), (decay, None), (hidden, None), (f_out, None), (phase, None),
        (table, None),
    ]
    fin, fout = struct((table.shape[1], hidden.shape[1]), F32), struct((hidden.shape[1], half), F32)
    longer = (g_s0.shape[0] + EDGE, full)

    def kernel(*refs):
        start = 3 + len(first)
        chosen = [r if i is None else r.at[i] for r, (_, i) in zip(refs[start : start + len(late)], late)]
        mixer_backward_kernel(docs, offsets, *refs[:start], *chosen, *refs[start + len(late) :])

    return pl.pallas_call(
        kernel,
        name="mixer_backward",
        out_shape=(
            struct(x.shape, BF), struct(edge_shape, BF), struct((16, full), F32), struct(g_s0.shape, F32), fin, fout,
            struct((mp,) + own, BF), *[struct((mp // 2, 2) + own, BF)] * 2, struct((mp, 2, 2, 2) + own_c, BF),
        ),
        in_specs=[IN_SMEM] + [IN_VMEM] * len(first) + [IN_HBM] * (2 + len(late)),
        out_specs=(IN_VMEM,) * 10,
        scratch_shapes=[
            *[pltpu.VMEM(v.shape if i is None else v.shape[1:], v.dtype) for v, i in late[1:]],
            dma(len(late)), pltpu.VMEM(edge.shape, BF), pltpu.VMEM(longer, F32),
            pltpu.VMEM((offsets - 1, longer[0], 128), F32),
            pltpu.VMEM((blocks * block, half), F32), pltpu.VMEM(x.shape, BF), pltpu.VMEM(x.shape, BF),
            pltpu.VMEM(edge_shape, BF), rows, rows, raw, raw, low, low, raw, slots,
            dma(HALVES, 1, mp - 1), dma(HALVES, 1, mp - 1), dma(HALVES, 2, mp - 1), dma(HALVES, 2, mp - 1), dma(2),
            *flow_scratch(mp, own, False), *flow_scratch(mp, own, False),
        ],
        compiler_params=pltpu.CompilerParams(collective_id=5, has_side_effects=True, vmem_limit_bytes=ROOM),
    )(lengths, *first, cored(part_a), cored(part_b), *[v for v, _ in late])


def spread_sum(block, slots, send_sem, recv_sem, axis, first):
    d, m = lax.axis_index("dp"), lax.axis_index("mp")
    count = lax.axis_size(axis)
    me = d if axis == "dp" else m
    copies = []
    for step, e in enumerate(ring(me, count)):
        peer = (e, m) if axis == "dp" else (d, e)
        copies.append(send(block, slots.at[me], send_sem.at[first + step], recv_sem.at[first + step], peer))
    slots[me] = block[...]
    for copy in copies:
        copy.wait()
    total = slots[0]
    for e in range(1, count):
        total = total + slots[e]
    return total


def total_of(values):
    return jnp.sum(jnp.sum(values, axis=1, keepdims=True), axis=0, keepdims=True)


def lanes_of(items):
    lane = lax.broadcasted_iota(jnp.int32, (1, 128), 1)
    row = jnp.zeros((1, 128), F32)
    for index, item in enumerate(items):
        row = row + jnp.where(lane == index, item, 0.0)
    return row


def update_body(
    taps, g0, g1, g2, w0, w1, w2, rows, cols, vec_sum, own_gain, gain, gain_mom, chan, chan_mom,
    fin_sum, fin, fin_mom, fout_sum, fout, fout_mom,
    norm_out, c0, c1, c2, n0, n1, n2, rows_out, cols_out, gain_g, gain_n, gain_m,
    chan_g, chan_n, chan_m, fin_g, fin_n, fin_m, fout_g, fout_n, fout_m,
    turn, mp_block, dp_block, mp_slots, dp_slots, last_block, mp_last, dp_last, send_sem, recv_sem,
):
    d, m = lax.axis_index("dp"), lax.axis_index("mp")
    dp, mp = lax.axis_size("dp"), lax.axis_size("mp")
    size, width = g0.shape
    in_width = 3 * (width // 4)
    is_in = lax.broadcasted_iota(jnp.int32, (size, width), 1) < in_width

    def four(v0, v1, v2, reduce_fn):
        return [
            reduce_fn(jnp.where(is_in, v0, 0.0)),
            reduce_fn(jnp.where(is_in, 0.0, v0)),
            reduce_fn(v1),
            reduce_fn(v2),
        ]

    def row_sum(v):
        return jnp.sum(v, axis=1, keepdims=True)

    def col_sum(v):
        return jnp.sum(v, axis=0, keepdims=True)

    s0, s1, s2 = g0[...] * g0[...], g1[...] * g1[...], g2[...] * g2[...]
    lane = lax.broadcasted_iota(jnp.int32, (size, 128), 1)
    row_parts = four(s0, s1, s2, row_sum)
    packed = jnp.zeros((size, 128), F32)
    for index, part in enumerate(row_parts):
        packed = packed + jnp.where(lane == index, part, 0.0)
    turn[...] = jnp.zeros(turn.shape, F32)
    dp_block[...] = jnp.zeros(dp_block.shape, F32)
    turn[pl.ds(0, size), :] = packed
    mp_block[pl.ds(0, 8), :] = jnp.transpose(turn[...])[0:8]
    old = rows[...]
    old_parts = [total_of(old[:, i : i + 1]) / mp for i in range(4)]
    weight_parts = four(w0[...] * w0[...], w1[...] * w1[...], w2[...] * w2[...], total_of)
    scalars = (
        [total_of(p) for p in row_parts]
        + old_parts
        + weight_parts
        + [
            total_of(gain[...] * gain[...]) / mp,
            total_of(chan[...] * chan[...]) / dp,
            total_of(fout[...] * fout[...]) / dp,
            total_of(fout_sum[...] * fout_sum[...]) / dp,
        ]
    )
    mp_block[pl.ds(8, 8), :] = jnp.broadcast_to(lanes_of(scalars), (8, 128))
    over_mp = spread_sum(mp_block, mp_slots, send_sem, recv_sem, "mp", 0)
    pieces = width // 128
    for index, values in enumerate((s0, s1, s2)):
        sums = col_sum(values)
        for piece in range(pieces):
            dp_block[pl.ds(index * pieces + piece, 1), :] = sums[:, piece * 128 : (piece + 1) * 128]
    dp_block[pl.ds(3 * pieces, 1), :] = over_mp[8:9]
    over_dp = spread_sum(dp_block, dp_slots, send_sem, recv_sem, "dp", mp)
    turn[pl.ds(0, 8), :] = over_mp[0:8]
    row_totals = jnp.transpose(turn[...])[0:size]
    shared = over_dp[3 * pieces : 3 * pieces + 1]

    def scalar(index):
        return shared[:, index : index + 1]

    last = 3 * taps + 1
    vec_sq = total_of(vec_sum[0 : last + 2, :] * vec_sum[0 : last + 2, :])
    fin_sq = total_of(fin_sum[...] * fin_sum[...])
    norm = jnp.sqrt(
        scalar(0) + scalar(1) + scalar(2) + scalar(3) + vec_sq + scalar(15) + fin_sq
    )
    norm_out[...] = norm
    clip = 1.0 / jnp.maximum(1.0, norm / CLIP_NORM)
    square = clip * clip
    fresh = 1.0 - MOMENT_DECAY
    all_rows = size * dp
    wide = [in_width * mp, (width - in_width) * mp, width * mp, width * mp]
    ratio = []
    fresh_rows = jnp.zeros((size, 128), F32)
    for index in range(4):
        row_new = (
            MOMENT_DECAY * old[:, index : index + 1]
            + fresh * square * row_totals[:, index : index + 1] / wide[index]
        )
        mean = MOMENT_DECAY * scalar(4 + index) / all_rows + fresh * square * scalar(index) / (
            all_rows * wide[index]
        )
        ratio.append(row_new / mean)
        fresh_rows = fresh_rows + jnp.where(lane == index, row_new, 0.0)
    turn[pl.ds(0, size), :] = fresh_rows
    rows_out[...] = jnp.transpose(turn[...])[0:8]
    for index in range(3):
        for piece in range(pieces):
            at = pl.ds(piece * 128, 128)
            row = index * pieces + piece
            cols_out[pl.ds(index, 1), at] = (
                MOMENT_DECAY * cols[pl.ds(index, 1), at]
                + fresh * square * over_dp[row : row + 1] / all_rows
            )
    first_ratio = jnp.where(is_in, ratio[0], ratio[1])
    steps = []
    for grad, out, factor, index in ((g0, c0, first_ratio, 0), (g1, c1, ratio[2], 1), (g2, c2, ratio[3], 2)):
        clipped = grad[...] * clip
        out[...] = clipped
        steps.append(clipped * lax.rsqrt(factor * cols_out[pl.ds(index, 1), :]))
    u0, u1, u2 = steps

    def plain(clipped, moment, grad_out, moment_out):
        fresh_moment = MOMENT_DECAY * moment + fresh * clipped * clipped
        grad_out[...] = clipped
        moment_out[...] = fresh_moment
        return clipped * lax.rsqrt(fresh_moment)

    picked = vec_sum[last : last + 2, 0:size]
    for e in range(1, dp):
        picked = jnp.where(d == e, vec_sum[last : last + 2, e * size : (e + 1) * size], picked)
    own_gain[...] = jnp.zeros(own_gain.shape, F32)
    own_gain[:, pl.ds(0, size)] = picked
    own = width // mp
    own_chan = vec_sum[0:last, 0:own]
    for e in range(1, mp):
        own_chan = jnp.where(m == e, vec_sum[0:last, e * own : (e + 1) * own], own_chan)
    u_gain = plain(own_gain[...] * clip, gain_mom[...], gain_g, gain_m)
    u_chan = plain(own_chan * clip, chan_mom[...], chan_g, chan_m)
    u_fin = plain(fin_sum[...] * clip, fin_mom[...], fin_g, fin_m)
    u_fout = plain(fout_sum[...] * clip, fout_mom[...], fout_g, fout_m)
    step_parts = four(u0 * u0, u1 * u1, u2 * u2, total_of) + [
        total_of(u_gain * u_gain) / mp,
        total_of(u_chan * u_chan) / dp,
        total_of(u_fout * u_fout) / dp,
    ]
    last_block[...] = jnp.broadcast_to(lanes_of(step_parts), (8, 128))
    half_way = spread_sum(last_block, mp_last, send_sem, recv_sem, "mp", mp + dp)
    mp_block[pl.ds(0, 8), :] = half_way
    step_sums = spread_sum(mp_block.at[pl.ds(0, 8)], dp_last, send_sem, recv_sem, "dp", 2 * mp + dp)[0:1]

    def factors(step_total, weight_total, entries):
        shrink = 1.0 / jnp.maximum(1.0, jnp.sqrt(step_total / entries) / CLIP_STEP)
        return STEP_RATE * jnp.sqrt(weight_total / entries) * shrink

    def step_sum(index):
        return step_sums[:, index : index + 1]

    rate = [factors(step_sum(i), scalar(8 + i), all_rows * wide[i]) for i in range(4)]
    n0[...] = w0[...] - jnp.where(is_in, rate[0], rate[1]) * u0
    n1[...] = w1[...] - rate[2] * u1
    n2[...] = w2[...] - rate[3] * u2
    gain_n[...] = gain[...] - factors(step_sum(4), scalar(12), 2 * all_rows) * u_gain
    chan_n[...] = chan[...] - factors(step_sum(5), scalar(13), chan.shape[0] * chan.shape[1] * mp) * u_chan
    fout_n[...] = fout[...] - factors(step_sum(6), scalar(14), fout.shape[0] * fout.shape[1] * mp) * u_fout
    fin_count = fin.shape[0] * fin.shape[1]
    fin_rate = factors(total_of(u_fin * u_fin), total_of(fin[...] * fin[...]), fin_count)
    fin_n[...] = fin[...] - fin_rate * u_fin


def greet_all():
    d, m = lax.axis_index("dp"), lax.axis_index("mp")
    greet([(e, m) for e in ring(d, lax.axis_size("dp"))] + [(d, e) for e in ring(m, lax.axis_size("mp"))])


def prepare(raw, ready, turn):
    in_w, out_w, in_rows, out_rows, up_rows, down_rows, in_cols, out_cols, up_cols, down_cols, gain_own, gain_mom_own = raw
    w0, rows, cols, gain, gain_mom = ready
    size, own = out_w.shape
    for j in range(3):
        w0[:, pl.ds(j * own, own)] = in_w[j]
        cols[0:1, pl.ds(j * own, own)] = in_cols[j : j + 1, :]
    w0[:, pl.ds(3 * own, own)] = out_w[...]
    cols[0:1, pl.ds(3 * own, own)] = out_cols[...].reshape(1, own)
    cols[1:2, :] = up_cols[...].reshape(1, -1)
    cols[2:3, :] = down_cols[...].reshape(1, -1)
    turn[...] = jnp.zeros(turn.shape, F32)
    for index, source in enumerate((in_rows, out_rows, up_rows, down_rows)):
        turn[pl.ds(index, 1), pl.ds(0, size)] = source[...].reshape(1, size)
    rows[...] = jnp.transpose(turn[...])[0:size]
    for source, target, fill in ((gain_own, gain, 0.0), (gain_mom_own, gain_mom, 1.0)):
        target[...] = jnp.full(target.shape, fill, F32)
        target[:, pl.ds(0, size)] = source[...]


def prepare_scratch(size, width):
    return [
        pltpu.VMEM((size, width), F32), pltpu.VMEM((size, 128), F32), pltpu.VMEM((8, width), F32),
        pltpu.VMEM((2, 128), F32), pltpu.VMEM((2, 128), F32),
    ]


OUTS = 21


def run_update(taps, grads, sums, w1, w2, ready, own_gain, old, outs, work):
    w0, rows, cols, gain, gain_mom = ready
    chan, chan_mom, fin, fin_mom, fout, fout_mom = old
    update_body(
        taps, *grads, w0, w1, w2, rows, cols, sums[0], own_gain, gain, gain_mom, chan, chan_mom,
        sums[1], fin, fin_mom, sums[2], fout, fout_mom, *outs, *work,
    )


def update_kernel(taps, *refs):
    grads, sums, refs = refs[:3], refs[3:6], refs[6:]
    raw, w1, w2, old, refs = refs[:12], refs[12], refs[13], refs[14:20], refs[20:]
    outs, ready, own_gain, work = refs[:OUTS], refs[OUTS : OUTS + 5], refs[OUTS + 5], refs[OUTS + 6 :]
    prepare(raw, ready, work[0])
    greet_all()
    run_update(taps, grads, sums, w1, w2, ready, own_gain, old, outs, work)


def place_first(g0, zero_and_out, one_and_two):
    own = g0.shape[1] // 4
    g0[:, pl.ds(0, own)] = zero_and_out[:, 0:own]
    g0[:, pl.ds(own, 2 * own)] = one_and_two
    g0[:, pl.ds(3 * own, own)] = zero_and_out[:, own : 2 * own]


class LastOverDp:
    def __init__(self, low, high, from_low, from_high, send_sem, recv_sem):
        self.low, self.high, self.from_low, self.from_high = low, high, from_low, from_high
        d, m = lax.axis_index("dp"), lax.axis_index("mp")
        self.y, self.x = d // 4, (d // 2) % 2
        self.copies = [
            send(low.at[:, 1 - self.x], from_low, send_sem.at[0], recv_sem.at[0], (turned(d, 2), m)),
            send(high.at[:, 1 - self.y], from_high, send_sem.at[1], recv_sem.at[1], (turned(d, 4), m)),
        ]

    def finish(self, partial):
        for copy in self.copies:
            copy.wait()
        half = self.from_low.shape[0]
        for e in range(half):
            partial[e] = self.low[e, self.x] + self.from_low[e]
            partial[half + e] = self.high[e, self.y] + self.from_high[e]


class OverMp:
    def __init__(self, partial, arrived, passed, send_sem, recv_sem):
        self.partial, self.arrived, self.passed = partial, arrived, passed
        self.send_sem, self.recv_sem = send_sem, recv_sem
        self.d, self.m = lax.axis_index("dp"), lax.axis_index("mp")
        near = turned(self.m, 1)
        self.far = turned(self.m, 2)
        self.copies = [self.push(partial.at[e], slot, near) for slot, e in enumerate((near, turned(near, 2)))]

    def push(self, source, slot, peer):
        sems = self.send_sem.at[slot], self.recv_sem.at[slot]
        return send(source, self.arrived.at[slot], *sems, (self.d, peer))

    def step(self):
        for copy in self.copies:
            copy.wait()
        self.passed[...] = self.partial[self.far] + self.arrived[1]
        self.copies = [self.push(self.passed, 2, self.far)]

    def total(self):
        self.copies[0].wait()
        return self.partial[self.m].astype(F32) + self.arrived[0].astype(F32) + self.arrived[2].astype(F32)


def end_kernel(doc_count, taps, len_ref, gw_ref, gw_edge, channel, gains, sums_in, *refs):
    late_refs, partial_a, b_low, b_high, part_c, fin_part, fout_part, refs = refs[:12], *refs[12:18], refs[18:]
    raw, w1, w2, old, refs = refs[:12], refs[12], refs[13], refs[14:20], refs[20:]
    input_grad, outs, refs = refs[0], refs[1 : OUTS + 1], refs[OUTS + 1 :]
    held, late_sem, work, refs = refs[:12], refs[12], refs[13:17], refs[17:]
    ready, own_gain, refs = refs[:5], refs[5], refs[6:]
    g0, g1, g2, g_late, vec, vec_sum, fin_sum, fout_sum, part, refs = *refs[:9], refs[9:]
    update_work, refs = refs[:10], refs[10:]
    arrived, passed, z_send, z_recv, refs = refs[:2], refs[2:4], refs[4], refs[5], refs[6:]
    g_c, partial_b, from_low, from_high, l_send, l_recv, refs = *refs[:6], refs[6:]
    partials = (partial_a, partial_b)
    mp = lax.axis_size("mp")
    own = gw_ref.shape[3] // FOLD * HALVES
    size = g0.shape[0]
    lanes = g_late.shape[1] // FLOWS
    flows = []
    for i in range(FLOWS):
        flows.append(Flow(part, refs[i * FLOW_REFS : (i + 1) * FLOW_REFS], pl.ds(i * lanes, lanes)))
    refs = refs[FLOWS * FLOW_REFS :]
    flow_c, refs = Flow(part_c, refs[:FLOW_REFS]), refs[FLOW_REFS:]
    early = SmallSums((fin_part, fout_part), (fin_sum, fout_sum), (True, False), refs[:8])
    final = SmallSums((vec,), (vec_sum,), (True,), refs[8:])
    late = Late(late_refs, held, late_sem)
    vec[...] = sums_in[...]
    greet_all()
    last_b = LastOverDp(b_low, b_high, from_low, from_high, l_send, l_recv)
    flow_c.start()

    def start_mp(i):
        return OverMp(partials[i], arrived[i], passed[i], z_send.at[i], z_recv.at[i])

    over_mp = [start_mp(0)]
    early.start(0)

    def stream_done(j, grad):
        for e in range(mp):
            for owner in range(8):
                at = (e, owner // 4, owner // 2 % 2, owner % 2, slice(None), pl.ds((j - 1) * own, own))
                part[at] = grad[owner * size : (owner + 1) * size, e * own : (e + 1) * own].astype(BF)
        if j == 1:
            flows[0].start()
            flow_c.core_stage()
            early.end(0)
            early.start(1)
            over_mp[0].step()
            last_b.finish(partial_b)
            over_mp.append(start_mp(1))
        else:
            flows[1].start()
            flows[2].start()
            flow_c.second_stage()
            early.end(1)
            early.start(2)
            over_mp[1].step()

    total = post_steps(
        doc_count, taps, len_ref, gw_ref, gw_edge, channel, gains, vec, held, late, work, stream_done
    )
    final.start(0)
    flows[0].core_stage()
    flow_c.third_stage()
    flow_c.send_z()
    final.end(0)
    final.start(1)
    flows[1].core_stage()
    flows[2].core_stage()
    early.end(2)
    early.start_mp()
    post_end(total, gains, held, input_grad)
    final.end(1)
    final.start(2)
    for flow in flows:
        flow.second_stage()
    final.end(2)
    final.start_mp()
    prepare(raw, ready, update_work[0])
    for flow in flows:
        flow.third_stage()
        flow.send_z()
    g1[...] = over_mp[0].total()
    g2[...] = over_mp[1].total()
    flow_c.finish(g_c)
    early.end_mp()
    final.end_mp()
    for flow in flows:
        flow.finish(g_late)
    place_first(g0, g_c[...], g_late[...])
    for flow in (*flows, flow_c):
        flow.drain()
    early.drain()
    final.drain()
    run_update(taps, (g0, g1, g2), (vec_sum, fin_sum, fout_sum), w1, w2, ready, own_gain, old, outs, update_work)


def update_scratch(dp, mp, width):
    pieces = 3 * width // 128 + 1
    tall = -(-pieces // 8) * 8
    sems = 2 * (dp + mp)
    return [
        pltpu.VMEM((128, 128), F32),
        pltpu.VMEM((16, 128), F32),
        pltpu.VMEM((tall, 128), F32),
        pltpu.VMEM((mp, 16, 128), F32),
        pltpu.VMEM((dp, tall, 128), F32),
        pltpu.VMEM((8, 128), F32),
        pltpu.VMEM((mp, 8, 128), F32),
        pltpu.VMEM((dp, 8, 128), F32),
        dma(sems),
        dma(sems),
    ]


def hand_out_kernel(*refs):
    input_grad, norm, c0, c1, c2, n0, n1, n2, rows, cols, gain_g, gain_n, gain_m, *small = refs[: OUTS + 1]
    (
        input_grad_out, norm_out, in_g, out_g, up_g, down_g, gain_g_out, in_n, out_n, up_n, down_n, gain_n_out, gain_m_out,
        in_r, out_r, up_r, down_r, in_c, out_c, up_c, down_c, *small_out,
    ) = refs[OUTS + 1 :]
    size, own = out_g.shape
    input_grad_out[...] = input_grad[...]
    norm_out[...] = norm[...]
    for source, first, last in ((c0, in_g, out_g), (n0, in_n, out_n)):
        for j in range(3):
            first[j] = source[:, j * own : (j + 1) * own]
        last[...] = source[:, 3 * own : 4 * own]
    for source, target in ((c1, up_g), (c2, down_g), (n1, up_n), (n2, down_n)):
        target[...] = source[...]
    for source, target in ((gain_g, gain_g_out), (gain_n, gain_n_out), (gain_m, gain_m_out)):
        target[...] = source[:, 0:size]
    for index, target in enumerate((in_r, out_r, up_r, down_r)):
        target[...] = rows[index : index + 1, 0:size].reshape(size)
    for j in range(3):
        in_c[j : j + 1, :] = cols[0:1, j * own : (j + 1) * own]
    out_c[...] = cols[0:1, 3 * own : 4 * own].reshape(own)
    up_c[...] = cols[1:2, :].reshape(-1)
    down_c[...] = cols[2:3, :].reshape(-1)
    for source, target in zip(small, small_out):
        target[...] = source[...]


def hand_out(results, own):
    size, width = results[2].shape
    cube, part, full = (3, size, own), (size, own), (size, width)
    column, row, wide = (2, size), (size,), (width,)
    shapes = [(1, 1), cube, part, full, full, column, cube, part, full, full, column, column, row, row, row, row]
    shapes += [(3, own), (own,), wide, wide] + [v.shape for v in results[13:]]
    return pl.pallas_call(
        hand_out_kernel,
        name="hand_out",
        out_shape=(struct(results[0].shape, BF), *[struct(s, F32) for s in shapes]),
        in_specs=[IN_VMEM] * len(results),
        out_specs=(IN_VMEM,) * (1 + len(shapes)),
        compiler_params=pltpu.CompilerParams(vmem_limit_bytes=ROOM),
    )(*results)


FLOWS = 3


def finish(lengths, taps, first, late, partials, part_c, fin_part, fout_part, raw, w1, w2, old):
    dp, mp = lax.axis_size("dp"), lax.axis_size("mp")
    size, own = raw[1].shape
    width = w1.shape[1]
    count = late[0][0].shape[0]
    docs = lengths.shape[1]
    big = struct((size, width), F32)
    flat = [(2, 128), old[0].shape, old[2].shape, old[4].shape]
    outs = [struct((1, 1), F32)] + [big] * 6 + [struct((8, 128), F32), struct((3, width), F32)]
    outs += [struct(s, F32) for s in flat for _ in range(3)]
    params = pltpu.CompilerParams(collective_id=2, has_side_effects=True, vmem_limit_bytes=ROOM)
    tail = [*raw, w1, w2, *old]
    own_gain = pltpu.VMEM((2, 128), F32)
    if dp != 8:
        last_part, input_grad, vec = post(lengths, taps, *first, late)
        over_mp = [lax.psum_scatter(p, "mp").astype(F32) for p in partials[:2]]
        grad = scatter_fallback(last_part.reshape(mp, dp, size, 2 * own))
        first_grad = scatter_fallback(part_c)
        grad = jnp.concatenate([first_grad[:, :own], grad, first_grad[:, own:]], axis=1)
        sums = [lax.psum(vec, ("dp", "mp")), lax.psum(fin_part, ("dp", "mp")), lax.psum(fout_part, "dp")]
        inputs = [grad, *over_mp, *sums, *tail]
        results = pl.pallas_call(
            functools.partial(update_kernel, taps),
            name="clip_and_update",
            out_shape=tuple(outs),
            in_specs=[IN_VMEM] * len(inputs),
            out_specs=(IN_VMEM,) * len(outs),
            scratch_shapes=prepare_scratch(size, width) + [own_gain] + update_scratch(dp, mp, width),
            compiler_params=params,
        )(*inputs)
        return (input_grad, *results)
    flows = []
    for _ in range(FLOWS):
        flows += flow_scratch(mp, (size, 2 * own // FLOWS))
    vec = struct((16, width), F32)
    after = [fin_part, fout_part, *tail]

    def kernel(*refs):
        start = 1 + len(first)
        end = start + len(late)
        end_kernel(docs, taps, *refs[:start], *choose(refs[start:end], late), *refs[end:])

    return pl.pallas_call(
        kernel,
        name="sum_clip_update",
        out_shape=(struct((count, width), BF), *outs),
        in_specs=[IN_SMEM] + [IN_VMEM] * len(first) + [IN_HBM] * len(late) + [IN_VMEM] * 3 + [IN_HBM] + [IN_VMEM] * len(after),
        out_specs=(IN_VMEM,) * (1 + len(outs)),
        scratch_shapes=[
            *post_scratch(late, taps, count, width),
            *prepare_scratch(size, width),
            own_gain,
            *[pltpu.VMEM((size, width), F32)] * 3,
            pltpu.VMEM((size, 2 * own), F32),
            *[pltpu.VMEM(v.shape, F32) for v in (vec, vec, fin_part, fout_part)],
            pltpu.VMEM((mp, 2, 2, 2, size, 2 * own), BF),
            *update_scratch(dp, mp, width),
            *[pltpu.VMEM((mp - 1, size, width), BF)] * 2,
            *[pltpu.VMEM((size, width), BF)] * 2,
            dma(2, mp - 1),
            dma(2, mp - 1),
            pltpu.VMEM((size, 2 * own), F32),
            pltpu.VMEM((mp, size, width), BF),
            *[pltpu.VMEM((mp // 2, size, width), BF)] * 2,
            dma(2),
            dma(2),
            *flows,
            *flow_scratch(mp, (size, 2 * own)),
            *small_scratch((fin_part, fout_part), mp),
            *small_scratch((vec,), mp),
        ],
        compiler_params=params,
    )(lengths, *first, *[v for v, _ in late], *partials, part_c, *after)


class Spread:
    def __init__(self, own, whole, lanes, refs, direct):
        self.whole, self.lanes, self.direct = whole, lanes, direct
        self.source = own.at[:, lanes]
        self.own_sem, self.z_send, self.z_recv, self.p_send, self.p_recv = refs
        self.d, self.m, self.mp = lax.axis_index("dp"), lax.axis_index("mp"), lax.axis_size("mp")
        d = self.d
        self.dx, self.dy, self.dc = turned(d, 2), turned(d, 4), turned(d, 1)
        half = self.mp // 2
        self.low, self.high, self.all = pl.ds(0, half), pl.ds(half, self.mp - half), pl.ds(0, self.mp)

    def start(self):
        target = self.whole.at[self.m, self.d, :, self.lanes]
        self.copy = pltpu.make_async_copy(self.source, target, self.own_sem.at[0])
        self.copy.start()
        self.z = []
        if self.direct:
            for step, e in enumerate(ring(self.m, self.mp)):
                sems = self.z_send.at[step], self.z_recv.at[step]
                self.z.append(send(self.source, target, *sems, (self.d, e)))
        else:
            self.blocks, self.bit = [self.m], self.mp // 2
            self.send_blocks()

    def send_blocks(self):
        self.stepped = []
        for block in self.blocks:
            slot = len(self.z)
            target = self.whole.at[block, self.d, :, self.lanes]
            source = self.source if slot == 0 else target
            peer = (self.d, turned(self.m, self.bit))
            copy = send(source, target, self.z_send.at[slot], self.z_recv.at[slot], peer)
            self.stepped.append(copy)
            self.z.append(copy)

    def z_step(self):
        if self.bit == self.mp // 2:
            self.copy.wait()
        for copy in self.stepped:
            copy.wait_recv()
        self.blocks = self.blocks + [turned(block, self.bit) for block in self.blocks]
        self.bit //= 2
        self.send_blocks()

    def push(self, slot, rows, owner, peer):
        block = self.whole.at[rows, owner, :, self.lanes]
        return send(block, block, self.p_send.at[slot], self.p_recv.at[slot], (peer, self.m))

    def stage_one(self):
        if self.direct:
            self.copy.wait()
        for copy in self.z if self.direct else self.stepped:
            copy.wait_recv()
        d, dx, dy = self.d, self.dx, self.dy
        self.first = [self.push(0, self.low, d, dx), self.push(1, self.high, d, dy)]
        self.last = [self.push(2, self.all, d, self.dc)]

    def stage_two(self):
        for copy in self.first:
            copy.wait_recv()
        d, dx, dy = self.d, self.dx, self.dy
        self.second = [
            self.push(3, self.low, d, dy),
            self.push(4, self.high, d, dx),
            self.push(5, self.low, dx, dy),
            self.push(6, self.high, dy, dx),
        ]

    def stage_three(self):
        for copy in self.second:
            copy.wait_recv()
        for slot, owner in enumerate((self.dx, self.dy, turned(self.dx, 4))):
            self.last.append(self.push(7 + slot, self.all, owner, self.dc))

    def arrive(self):
        for copy in self.last:
            copy.wait_recv()

    def drain(self):
        for copy in self.z + self.first + self.second + self.last:
            copy.wait_send()


SPREAD_REFS = 5


def spread_scratch(mp):
    return [dma(1), dma(mp - 1), dma(mp - 1), dma(10), dma(10)]


def mark_same(same, len_ref, doc_count, first):
    tail = same.shape[1]
    position = lax.broadcasted_iota(jnp.int32, (tail + EDGE, 128), 0) + first
    doc = jnp.zeros(position.shape, jnp.int32)
    end = jnp.int32(0)
    for slot in range(doc_count):
        end = end + len_ref[0, slot]
        doc = doc + (position >= end).astype(jnp.int32)
    doc = jnp.where(position < 0, -1, doc)
    for k in range(1, same.shape[0] + 1):
        same[k - 1] = jnp.where(doc[EDGE:] == doc[EDGE - k : EDGE - k + tail], 1.0, 0.0)


def near_product(left, right, dot=mm):
    l_top, l_rest = split(left)
    r_top, r_rest = split(right)
    return dot(l_top, r_top) + dot(l_top, r_rest) + dot(l_rest, r_top)


def mixer_forward_kernel(
    doc_count, taps, len_ref, tok, in_w, out_w, up_w, down_w, gains_own, channel_own, table, step_col, f_in, f_out,
    t0, t1, t2, t3,
    w_parts, y_back, spectrum, hidden, phase, decay, gain_rows, chan_rows,
    z_out, s0_out, s1_out, s2_out, w_out_own, a_out, n1_out, inv1_out, w_in_out, w_out_out, whole_up, whole_down,
    chunk_first, chunk_up, chunk_down, gains, channel, turn, whole_first, gains_all, channel_all, edges_all, filters, w_send, y_parts, full, raw, top, rest, slots,
    ext, n1, inv1, a, z, s0, s1, s2, w_own, w_in, w_out, same,
    s_send, s_recv, save_sem, b_send, b_recv, c_send, c_recv, *spread_refs,
):
    tables = (t0, t1, t2, t3)
    d, m = lax.axis_index("dp"), lax.axis_index("mp")
    dp, mp = lax.axis_size("dp"), lax.axis_size("mp")
    count, width = tok.shape
    rows = chunk_first.shape[0]
    own = width // mp
    block = count // 2
    blocks = raw.shape[0]

    place = (2, 0, 1)
    for j in range(3):
        chunk_first[:, pl.ds(place[j] * own, own)] = in_w[j].astype(BF)
    chunk_first[:, pl.ds(3 * own, own)] = out_w[...].astype(BF)
    chunk_up[...] = up_w[...].astype(BF)
    chunk_down[...] = down_w[...].astype(BF)
    turn[...] = jnp.zeros(turn.shape, F32)
    turn[pl.ds(0, 2), pl.ds(0, rows)] = gains_own[...]
    gains[...] = turn[...].astype(BF)
    channel[...] = jnp.zeros(channel.shape, F32)
    channel[pl.ds(0, channel_own.shape[0]), :] = channel_own[...]
    greet_all()

    small = []
    for step, e in enumerate(ring(d, dp)):
        small.append(send(gains, gains_all.at[d], s_send.at[step], s_recv.at[step], (e, m)))
    for step, e in enumerate(ring(m, mp)):
        at = dp + step
        small.append(send(channel, channel_all.at[m], s_send.at[at], s_recv.at[at], (d, e)))
    at = dp + mp
    for index, first, peer in ((0, count - EDGE, lax.rem(m + 1, mp)), (1, 0, lax.rem(m + mp - 1, mp))):
        sems = s_send.at[at + index], s_recv.at[at + index]
        small.append(send(tok.at[pl.ds(first, EDGE)], edges_all.at[index], *sems, (d, peer)))
    gains_all[d] = gains[...]
    channel_all[m] = channel[...]

    half = width // 2
    plan = [
        (chunk_first, whole_first, pl.ds(0, half)),
        (chunk_first, whole_first, pl.ds(half, width - half)),
        (chunk_up, whole_up, pl.ds(0, chunk_up.shape[1])),
        (chunk_down, whole_down, pl.ds(0, chunk_down.shape[1])),
    ]
    flows = [
        Spread(*p, spread_refs[i * SPREAD_REFS : (i + 1) * SPREAD_REFS], direct=i == 0) for i, p in enumerate(plan)
    ]
    left, right, up, down = flows
    left.start()
    right.start()

    phase[...] = near_product(table[...], f_in[...])
    hidden[...] = jnp.sin(phase[...])
    lane = (m * own + lax.broadcasted_iota(jnp.int32, (1, own), 1)).astype(F32)
    rate = FAST_DECAY + (SLOW_DECAY - FAST_DECAY) * lane / (width - 1)
    decay[...] = jnp.exp(-step_col[...] * rate)
    near = own // HALVES
    values = near_product(hidden[...], f_out[...]) * decay[...]
    for side in range(HALVES):
        filters[side, :, 0:near] = values[:, side * near : (side + 1) * near]

    mark_same(same, len_ref, doc_count, m * count - EDGE)

    left.stage_one()
    right.z_step()
    up.start()
    down.start()
    for copy in small:
        copy.wait()
    for e in range(dp):
        gain_rows[0:2, pl.ds(e * rows, rows)] = gains_all[e, 0:2, 0:rows].astype(F32)
    for e in range(mp):
        chan_rows[:, pl.ds(e * own, own)] = channel_all[e]
    ext[pl.ds(0, EDGE), :] = edges_all[0].astype(F32)
    ext[pl.ds(EDGE, count), :] = tok[...].astype(F32)
    ext[pl.ds(EDGE + count, EDGE), :] = edges_all[1].astype(F32)

    def norm_body(i, carry):
        at = pl.ds(pl.multiple_of(i * 32, 32), 32)
        normed, inverse_std = norm_parts(ext[at, :])
        n1[at, :] = normed
        inv1[at, :] = jnp.broadcast_to(inverse_std, (32, 128))
        a[at, :] = (normed * gain_rows[0:1, :]).astype(BF)
        return carry

    def stream_weights(j):
        for e in range(mp):
            part = whole_first[e, :, :, pl.ds(place[j] * own, own)].reshape(dp * rows, own)
            w_in[:, pl.ds(j * width + e * own, own)] = part

    def project(j):
        cols = pl.ds(j * width, width)
        z[:, cols] = mm(a[...], w_in[:, cols])

    def short(first, size, j):
        part = z[pl.ds(first + 8, size + 8), pl.ds(j * width, width)]
        total = chan_rows[j : j + 1, :] * part[8 : size + 8]
        for k in range(1, taps):
            keep = same[k - 1, pl.ds(first, size), 0:1] > 0.0
            moved = jnp.where(keep, part[8 - k : size + 8 - k], 0.0)
            total = total + chan_rows[3 * k + j : 3 * k + j + 1, :] * moved
        return total

    def value_body(i, carry):
        first = pl.multiple_of(i * 48, 16)
        at = pl.ds(first, 48)
        one, two = short(first, 48, 1), short(first, 48, 2)
        s1[at, :], s2[at, :] = one, two
        w_own[at, :] = two * one
        return carry

    def gate_body(i, carry):
        first = pl.multiple_of(i * 48, 16)
        s0[pl.ds(first, 48), :] = short(first, 48, 0)
        return carry

    lax.fori_loop(0, ext.shape[0] // 32, norm_body, 0)
    left.stage_two()
    right.stage_one()
    up.z_step()
    for side in range(HALVES):
        filter_spectrum(filters.at[side], spectrum.at[side], raw, tables, block)
    left.stage_three()
    right.stage_two()
    down.z_step()
    left.arrive()
    for j in (1, 2):
        stream_weights(j)
        project(j)
    up.stage_one()
    lax.fori_loop(0, s0.shape[0] // 48, value_body, 0)
    piece = count // FOLD
    for side in range(HALVES):
        for part in range(mp):
            for i in range(FOLD):
                values = w_own[pl.ds(i * piece, piece), pl.ds(part * own + side * near, near)]
                w_send[side, part, :, pl.ds(i * near, near)] = values.astype(BF)
    going, back = [], []
    for side in range(HALVES):
        going.append(Blocks([(w_send.at[side], w_parts.at[side])], b_send.at[side], b_recv.at[side]))
        back.append(Blocks([(y_parts.at[side], y_back.at[side])], c_send.at[side], c_recv.at[side]))
        going[side].start()
    right.stage_three()
    down.stage_one()
    right.arrive()
    stream_weights(0)
    project(0)
    lax.fori_loop(0, s0.shape[0] // 48, gate_body, 0)
    saves = []

    def save(source, target):
        copy = pltpu.make_async_copy(source, target, save_sem.at[len(saves)])
        copy.start()
        saves.append(copy)

    own_rows = pl.ds(0, count)
    for source, target in (
        *[(z.at[:, pl.ds(j * width, width)], z_out.at[j]) for j in range(3)], (s0.at[own_rows], s0_out), (s1, s1_out), (s2, s2_out), (w_own.at[own_rows], w_out_own),
        (a, a_out), (n1, n1_out), (inv1, inv1_out),
        *[(w_in.at[:, pl.ds(j * width, width)], w_in_out.at[j]) for j in range(3)],
    ):
        save(source, target)
    for e in range(mp):
        part = whole_first[e, :, :, pl.ds(3 * own, own)].reshape(dp * rows, own)
        w_out[:, pl.ds(e * own, own)] = part
    save(w_out, w_out_out)
    def between(slot):
        if slot == 2:
            down.stage_two()

    up.stage_two()
    for side in range(HALVES):
        going[side].arrive()
        conv_forward_steps(
            doc_count, len_ref, w_parts.at[side], tables, y_parts.at[side], spectrum.at[side], full, raw, top, rest,
            slots, between if side == 0 else lambda slot: None,
        )
        back[side].start()
    up.stage_three()
    down.stage_three()
    up.arrive()
    down.arrive()
    for side in range(HALVES):
        back[side].arrive()
    for copy in saves:
        copy.wait()
    for copies in going + back:
        copies.drain()
    for flow in flows:
        flow.drain()


def mixer_forward(lengths, tokens, weights, gains, channel, taps, table, step_col, f_in, f_out, tables):
    mp, dp = lax.axis_size("mp"), lax.axis_size("dp")
    count, width = tokens.shape
    own, block, docs = width // mp, count // 2, lengths.shape[1]
    lags = table.shape[0]
    blocks = lags // block
    near = own // HALVES
    rows = weights[1].shape[0]
    shards = [(rows, 4 * own), weights[2].shape, weights[3].shape]
    whole = [(mp, dp) + s for s in shards]
    longer, later = (count + 2 * EDGE, width), (count + EDGE, width)
    parts = (HALVES, mp, count // FOLD, FOLD * near)
    full, raw, low, slots = conv_scratch(parts[1:], blocks, block, docs)
    vmem_outs = [
        (parts, BF), (parts, BF), ((HALVES, blocks, 2 * block, lanes_for(near)), F32), ((lags, f_in.shape[1]), F32), ((lags, f_in.shape[1]), F32),
        ((lags, own), F32), ((8, width), F32), ((16, width), F32),
    ]
    hbm_outs = [
        ((3,) + longer, F32), ((count, width), F32), (later, F32), (later, F32), ((count, width), F32),
        (longer, BF), (longer, F32), ((longer[0], 128), F32), ((3, width, width), BF), ((width, width), BF),
        (whole[1], BF), (whole[2], BF),
    ]
    inputs = (lengths, tokens, *weights, gains, channel, table, step_col, f_in, f_out, *tables)
    return pl.pallas_call(
        functools.partial(mixer_forward_kernel, docs, taps),
        name="mixer_forward",
        out_shape=tuple(struct(*o) for o in vmem_outs + hbm_outs),
        in_specs=[IN_SMEM] + [IN_VMEM] * (len(inputs) - 1),
        out_specs=(IN_VMEM,) * len(vmem_outs) + (IN_HBM,) * len(hbm_outs),
        scratch_shapes=[
            *[pltpu.VMEM(s, BF) for s in shards], pltpu.VMEM((16, 128), BF), pltpu.VMEM((16, own), F32),
            pltpu.VMEM((16, 128), F32),
            pltpu.VMEM(whole[0], BF), pltpu.VMEM((dp, 16, 128), BF), pltpu.VMEM((mp, 16, own), F32),
            pltpu.VMEM((2, EDGE, width), BF),
            pltpu.VMEM((HALVES, lags, lanes_for(near)), F32), pltpu.VMEM(parts, BF), pltpu.VMEM(parts, BF),
            full, raw, low, low, slots,
            pltpu.VMEM(longer, F32), pltpu.VMEM(longer, F32), pltpu.VMEM((longer[0], 128), F32), pltpu.VMEM(longer, BF),
            pltpu.VMEM((longer[0], 3 * width), F32), pltpu.VMEM(later, F32), pltpu.VMEM(later, F32),
            pltpu.VMEM(later, F32), pltpu.VMEM(later, F32), pltpu.VMEM((width, 3 * width), BF),
            pltpu.VMEM((width, width), BF), pltpu.VMEM((taps - 1, later[0], 128), F32),
            dma(dp + mp + 2), dma(dp + mp + 2), dma(16), *([dma(HALVES, 1, mp - 1)] * 4),
            *(spread_scratch(mp) * 4),
        ],
        compiler_params=pltpu.CompilerParams(collective_id=0, has_side_effects=True, vmem_limit_bytes=ROOM),
    )(*inputs)


def dot_nt(left, right):
    return lax.dot_general(left, right, (((1,), (1,)), ((), ())), preferred_element_type=F32)


def dot_tn(left, right):
    return lax.dot_general(left, right, (((0,), (0,)), ((), ())), preferred_element_type=F32)


def pieces(parts, count, width):
    near, rows = width // parts // HALVES, count // FOLD
    for side in range(HALVES):
        for part in range(parts):
            for i in range(FOLD):
                cols = pl.ds((part * HALVES + side) * near, near)
                yield pl.ds(i * rows, rows), cols, side, part, pl.ds(i * near, near)


def gelu_parts(x):
    scale, cubic = math.sqrt(2.0 / math.pi), 0.044715
    square = x * x
    t = jnp.tanh(x * (scale + (scale * cubic) * square))
    half = 0.5 + 0.5 * t
    value = x * half
    return value, half + value * (1.0 - t) * (scale + (3.0 * scale * cubic) * square)


COLS = 768


def feed_kernel(
    skip_row, y_ref, w_ref, s0_ref, tok, cot, w_out, gains, channel, up, down,
    act_out, up_part, down_part, out_part, g_parts, gy_out, gs0_out, gx2_out, sums, edge_out,
    y, o, x2, n2, inv2, b, b_t, cot_t, mix, acc_out, acc_b,
):
    step, steps = pl.program_id(0), pl.num_programs(0)
    parts = y_ref.shape[1]
    count, width = tok.shape
    tile = 128
    gain, skip = gains.at[1:2], channel.at[skip_row : skip_row + 1]

    @pl.when(step == 0)
    def _():
        for rows, cols, side, part, lanes in pieces(parts, count, width):
            y[rows, cols] = y_ref[side, part, :, lanes].astype(F32)

        def body(index, carry):
            rows = pl.ds(pl.multiple_of(index * tile, tile), tile)
            values = y[rows, :] + skip[...] * w_ref[rows, :]
            y[rows, :] = values
            mixed = (values * s0_ref[rows, :]).astype(BF)
            o[rows, :] = mixed
            residual = tok[rows, :].astype(F32) + dot_nt(mixed, w_out[...])
            x2[rows, :] = residual
            normed, inverse_std = norm_parts(residual)
            n2[rows, :] = normed
            inv2[rows, :] = jnp.broadcast_to(inverse_std, (tile, 128))
            b[rows, :] = (normed * gain[...]).astype(BF)
            return carry

        lax.fori_loop(0, count // tile, body, 0)
        b_t[...] = b[...].T
        cot_t[...] = cot[...].T
        acc_out[...] = jnp.zeros(acc_out.shape, F32)
        acc_b[...] = jnp.zeros(acc_b.shape, F32)

    up_w, down_w = up[0], down[0]
    value, slope = gelu_parts(mm(b[...], up_w))
    act = value.astype(BF)
    g_hpre = (mm(cot[...], down_w) * slope).astype(BF)
    up_part[0] = mm(b_t[...], g_hpre).astype(BF)
    down_part[0] = mm(cot_t[...], act).astype(BF)
    acc_out[...] += dot_nt(act, down_w)
    acc_b[...] += dot_nt(g_hpre, up_w)

    @pl.when(step == steps - 1)
    def _():
        sums[...] = jnp.zeros(sums.shape, F32)

        def body(index, carry):
            rows = pl.ds(pl.multiple_of(index * tile, tile), tile)
            act_out[rows, :] = (x2[rows, :] + acc_out[rows, :]).astype(BF)
            g_b, normed = acc_b[rows, :], n2[rows, :]
            sums[0:1, :] += jnp.sum(g_b * normed, axis=0, keepdims=True)
            g_x2 = cot[rows, :].astype(F32) + norm_back(g_b, gain[...], normed, inv2[rows, 0:1])
            gx2_out[rows, :] = g_x2
            low = g_x2.astype(BF)
            mix[rows, :] = low
            g_o = mm(low, w_out[...])
            g_y = g_o * s0_ref[rows, :]
            gy_out[rows, :] = g_y
            gs0_out[rows, :] = g_o * y[rows, :]
            sums[1:2, :] += jnp.sum(g_y * w_ref[rows, :], axis=0, keepdims=True)
            return carry

        lax.fori_loop(0, count // tile, body, 0)
        for rows, cols, side, part, lanes in pieces(parts, count, width):
            g_parts[side, part, :, lanes] = gy_out[rows, cols].astype(BF)
        edge_out[...] = gs0_out[pl.ds(0, EDGE), :].astype(BF)
        grad = dot_tn(mix[...], o[...])
        own = width // parts
        for part in range(parts):
            out_part[part] = grad[:, part * own : (part + 1) * own].astype(BF)


def feed(y_parts, w_own, s0, tokens, cotangent, w_out, gains, channel, skip_row, whole_up, whole_down):
    mp, width, hidden = whole_up.shape
    count = tokens.shape[0]
    own, cols = width // mp, COLS
    each = hidden // cols
    once = pl.Buffered(1)

    def fixed(shape):
        return pl.BlockSpec(shape, lambda i: (0,) * len(shape), pipeline_mode=once)

    def moving():
        return pl.BlockSpec((1, width, cols), lambda i: (i // each, 0, i % each))

    full, half = (count, width), y_parts.shape
    outs = [
        (full, BF), (whole_up.shape, BF), (whole_up.shape, BF), ((mp, width, own), BF), (half, BF),
        (full, F32), (full, F32), (full, F32), ((8, width), F32), ((EDGE, width), BF),
    ]
    out_specs = [moving() if i in (1, 2) else fixed(s) for i, (s, _) in enumerate(outs)]
    inputs = (y_parts, w_own, s0, tokens, cotangent, w_out, gains, channel)
    return pl.pallas_call(
        functools.partial(feed_kernel, skip_row),
        name="feed_forward",
        grid=(mp * each,),
        out_shape=tuple(struct(s, t) for s, t in outs),
        in_specs=[fixed(v.shape) for v in inputs] + [moving(), moving()],
        out_specs=tuple(out_specs),
        scratch_shapes=[
            pltpu.VMEM(full, F32), pltpu.VMEM(full, BF), pltpu.VMEM(full, F32), pltpu.VMEM(full, F32),
            pltpu.VMEM((count, 128), F32), pltpu.VMEM(full, BF), pltpu.VMEM((width, count), BF),
            pltpu.VMEM((width, count), BF), pltpu.VMEM(full, BF), pltpu.VMEM(full, F32), pltpu.VMEM(full, F32),
        ],
        compiler_params=pltpu.CompilerParams(vmem_limit_bytes=ROOM),
    )(*inputs, whole_up, whole_down)


class Late:
    def __init__(self, sources, targets, sem):
        self.copies = []
        for i, (source, target) in enumerate(zip(sources, targets)):
            copy = pltpu.make_async_copy(source, target, sem.at[i])
            copy.start()
            self.copies.append(copy)

    def need(self, *indices):
        for i in indices:
            self.copies[i].wait()


def short_backward(j, gs, z, channel, same, offsets, count, sums):
    tap_rows = [channel[3 * k + j : 3 * k + j + 1, :] for k in range(offsets)]
    g_z = None
    for k in range(offsets):
        later = gs[pl.ds(k, count), :]
        before = z[pl.ds(EDGE - k, count), :]
        if k:
            later = jnp.where(same[k][k : count + k], later, 0.0)
            before = jnp.where(same[k][:count], before, 0.0)
        g_z = tap_rows[k] * later if g_z is None else g_z + tap_rows[k] * later
        sums[pl.ds(3 * k + j, 1), :] = jnp.sum(gs[pl.ds(0, count), :] * before, axis=0, keepdims=True)
    return g_z


def post_steps(doc_count, offsets, len_ref, gw_ref, gw_edge, channel, gains, sums, held, late, work, stream_done):
    gy_ref, s2_ref, z1, a_ref, w1, s1_ref, z2, w2, ga0, n1_ref, inv1_ref, gx2_ref = held
    gw, gs, gz, marks = work
    parts = gw_ref.shape[1]
    count, width = gy_ref.shape
    near = width // parts // HALVES
    skip = channel[3 * offsets : 3 * offsets + 1, :]
    for rows, cols, side, part, lanes in pieces(parts, count, width):
        gw[rows, cols] = gw_ref[side, part, :, lanes].astype(F32)
    for side in range(HALVES):
        for part in range(parts):
            at = pl.ds((part * HALVES + side) * near, near)
            gw[pl.ds(count, EDGE), at] = gw_edge[side, part, :, 0:near].astype(F32)
    mark_same(marks, len_ref, doc_count, lax.axis_index("mp") * count - EDGE)
    same = [None] + [marks[k - 1, :, 0:1] > 0.0 for k in range(1, offsets)]
    late.need(0)
    gw[pl.ds(0, count), :] += skip * gy_ref[...]
    total = None
    for j, other, z, w, order in ((1, s2_ref, z1, w1, (1, 2, 3, 4)), (2, s1_ref, z2, w2, (5, 6, 7))):
        late.need(*order)
        gs[...] = gw[...] * other[...]
        gz[...] = short_backward(j, gs, z, channel, same, offsets, count, sums).astype(BF)
        stream_done(j, dot_tn(a_ref[pl.ds(EDGE, count), :], gz[...]))
        term = dot_nt(gz[...], w[...])
        total = term if total is None else total + term
    late.need(8, 9, 10, 11)
    total = total + ga0[...]
    sums[pl.ds(3 * offsets + 1, 1), :] = jnp.sum(total * n1_ref[pl.ds(EDGE, count), :], axis=0, keepdims=True)
    return total


def post_end(total, gains, held, input_grad):
    n1_ref, inv1_ref, gx2_ref = held[9:]
    count = gx2_ref.shape[0]
    normed, inverse_std = n1_ref[pl.ds(EDGE, count), :], inv1_ref[pl.ds(EDGE, count), 0:1]
    input_grad[...] = (gx2_ref[...] + norm_back(total, gains[0:1, :], normed, inverse_std)).astype(BF)


def post_kernel(doc_count, offsets, len_ref, gw_ref, gw_edge, channel, gains, sums_in, *refs):
    late_refs, refs = refs[:12], refs[12:]
    last_part, input_grad, sums, refs = refs[0], refs[1], refs[2], refs[3:]
    held, late_sem, work = refs[:12], refs[12], refs[13:]
    late = Late(late_refs, held, late_sem)
    parts, own = gw_ref.shape[1], last_part.shape[2] // 2
    sums[...] = sums_in[...]

    def stream_done(j, grad):
        for part in range(parts):
            last_part[part, :, pl.ds((j - 1) * own, own)] = grad[:, part * own : (part + 1) * own].astype(BF)

    total = post_steps(
        doc_count, offsets, len_ref, gw_ref, gw_edge, channel, gains, sums, held, late, work, stream_done
    )
    post_end(total, gains, held, input_grad)


def post_late(g_y, s1, s2, z, a, w_in, ga0, n1, inv1, g_x2):
    return [
        (g_y, None), (s2, None), (z, 1), (a, None), (w_in, 1), (s1, None), (z, 2), (w_in, 2), (ga0, None), (n1, None),
        (inv1, None), (g_x2, None),
    ]


def post_scratch(late, offsets, count, width):
    return [
        *[pltpu.VMEM(v.shape if i is None else v.shape[1:], v.dtype) for v, i in late],
        dma(len(late)),
        pltpu.VMEM((count + EDGE, width), F32),
        pltpu.VMEM((count + EDGE, width), F32),
        pltpu.VMEM((count, width), BF),
        pltpu.VMEM((offsets - 1, count + EDGE, 128), F32),
    ]


def choose(refs, late):
    return [r if i is None else r.at[i] for r, (_, i) in zip(refs, late)]


def post(lengths, offsets, gw_parts, gw_edge, channel, gains, sums_in, late):
    mp = gw_parts.shape[1]
    count, width = late[0][0].shape
    first = (gw_parts, gw_edge, channel, gains, sums_in)

    def kernel(*refs):
        start = 1 + len(first)
        end = start + len(late)
        post_kernel(lengths.shape[1], offsets, *refs[:start], *choose(refs[start:end], late), *refs[end:])

    return pl.pallas_call(
        kernel,
        name="mixer_post",
        out_shape=(struct((mp, width, 2 * width // mp), BF), struct((count, width), BF), struct((16, width), F32)),
        in_specs=[IN_SMEM] + [IN_VMEM] * len(first) + [IN_HBM] * len(late),
        out_specs=(IN_VMEM,) * 3,
        scratch_shapes=post_scratch(late, offsets, count, width),
        compiler_params=pltpu.CompilerParams(vmem_limit_bytes=ROOM),
    )(lengths, *first, *[v for v, _ in late])


def features(length, feature_count, count):
    step = np.arange(count)
    band = np.arange(1, (feature_count - 1) // 2 + 1)
    phase = ((step[:, None] * band[None, :]) % length).astype(np.float32) * np.float32(2.0 * math.pi / length)
    position = (step / length).astype(np.float32)
    table = np.concatenate([position[:, None], np.cos(phase), np.sin(phase)], axis=1)
    return table.astype(np.float32), position


def product(left, right):
    return jnp.dot(left, right, precision=FULL_PRECISION, preferred_element_type=F32)


def norm_parts(values):
    centred = values - jnp.mean(values, axis=-1, keepdims=True)
    inverse_std = lax.rsqrt(jnp.mean(centred * centred, axis=-1, keepdims=True) + EPS_NORM)
    return centred * inverse_std, inverse_std


def norm_back(grad, gain, normed, inverse_std):
    scaled = grad * gain
    mean = jnp.mean(scaled, axis=-1, keepdims=True)
    along = jnp.mean(scaled * normed, axis=-1, keepdims=True)
    return (scaled - mean - normed * along) * inverse_std


def to_parts(values, mp):
    count, width = values.shape
    near = width // mp // HALVES
    cut = values.reshape(FOLD, count // FOLD, mp, HALVES, near).transpose(3, 2, 1, 0, 4)
    return cut.reshape(HALVES, mp, count // FOLD, FOLD * near)


def forward_fallback(lengths, tokens, weights, gain_own, channel_own, taps, table, step_col, f_in, f_out, tables):
    mp, m = lax.axis_size("mp"), lax.axis_index("mp")
    count, width = tokens.shape
    own, shard = width // mp, weights[1].shape[0]
    first_shard = jnp.concatenate([*weights[0], weights[1]], axis=1)
    chunks = [v.astype(BF) for v in (first_shard, weights[2], weights[3])]
    gains = jnp.pad(gain_own.astype(BF), ((0, 14), (0, 128 - shard)))
    channel = jnp.pad(channel_own, ((0, 16 - channel_own.shape[0]), (0, 0)))
    edges = jnp.stack([tokens[count - EDGE :], tokens[:EDGE]])
    first, up, down, gains_all, channel_all, edges_all = gather_fallback(chunks, gains, channel, edges)
    first = first.reshape(mp, width, width)
    w_in = first[:, :, : 3 * own].reshape(mp, width, 3, own).transpose(1, 2, 0, 3).reshape(width, 3 * width)
    w_out = first[:, :, 3 * own :].transpose(1, 0, 2).reshape(width, width)
    gain_rows = gains_all[:, 0:8, :shard].transpose(1, 0, 2).reshape(8, width).astype(F32)
    chan_rows = channel_all.transpose(1, 0, 2).reshape(-1, width)
    position = m * count - EDGE + jnp.arange(count + 2 * EDGE, dtype=jnp.int32)
    doc = jnp.sum((position[:, None] >= jnp.cumsum(lengths[0])[None, :]).astype(jnp.int32), axis=1)
    doc = jnp.where(position < 0, -1, doc)
    n1, inv1 = norm_parts(jnp.concatenate([edges_all[0], tokens, edges_all[1]]).astype(F32))
    a = (n1 * gain_rows[0]).astype(BF)
    z = jnp.dot(a, w_in, preferred_element_type=F32)
    s = []
    for j in range(3):
        stream, total = z[:, j * width : (j + 1) * width], None
        for k in range(taps):
            part = stream[EDGE - k : stream.shape[0] - k]
            if k:
                part = jnp.where((doc[EDGE:] == doc[EDGE - k : doc.shape[0] - k])[:, None], part, 0.0)
            term = chan_rows[3 * k + j] * part
            total = term if total is None else total + term
        s.append(total)
    w_own = s[2][:count] * s[1][:count]
    phase = product(table, f_in)
    hidden = jnp.sin(phase)
    lane = (m * own + jnp.arange(own, dtype=jnp.int32)).astype(F32)
    decay = jnp.exp(-step_col * (FAST_DECAY + (SLOW_DECAY - FAST_DECAY) * lane / (width - 1)))
    w_parts = exchange([*to_parts(w_own.astype(BF), mp)], None, 3)
    filters = jnp.split(product(hidden, f_out) * decay, HALVES, axis=1)
    halves = [conv_forward(w_parts[i], lengths, filters[i], tables) for i in range(HALVES)]
    y_back = jnp.stack(exchange([v[0] for v in halves], None, 4))
    w_parts, spectrum = jnp.stack(w_parts), jnp.stack([v[1] for v in halves])
    return (
        w_parts, y_back, spectrum, hidden, phase, decay, gain_rows, chan_rows,
        z.reshape(-1, 3, width).transpose(1, 0, 2), s[0][:count], s[1], s[2], w_own, a, n1,
        jnp.broadcast_to(inv1, (inv1.shape[0], 128)), w_in.reshape(width, 3, width).transpose(1, 0, 2), w_out, up, down,
    )


def per_device(
    tokens, cotangent, doc_lengths, in_weight, out_weight, up_weight, down_weight, gains, channel_weight,
    filter_in, filter_out, in_rows, in_cols, out_rows, out_cols, up_rows, up_cols, down_rows, down_cols,
    gain_moment, channel_moment, filter_in_moment, filter_out_moment,
):
    dp, mp = lax.axis_size("dp"), lax.axis_size("mp")
    count, width = tokens.shape
    length = count * mp
    own = channel_weight.shape[1]
    rows = in_weight.shape[0]
    hidden = up_weight.shape[1]
    taps = (channel_weight.shape[0] - 1) // 3
    most = length // 2

    in_weight, gains, gain_moment = in_weight.transpose(1, 0, 2), gains.T, gain_moment.T

    table, step = features(length, filter_in.shape[0], most)
    tables = tuple(jnp.asarray(t) for t in transform_tables(count // 2))
    run = mixer_forward if dp == 8 else forward_fallback
    (
        w_parts, y_back, spectrum, hidden_filter, phase, decay, gain_rows, chan_rows, z, s0, s1, s2, w_own,
        a, n1, inv1, w_in, w_out, whole_up, whole_down,
    ) = run(
        doc_lengths, tokens, (in_weight, out_weight, up_weight, down_weight), gains, channel_weight, taps,
        table, step[:, None], filter_in, filter_out, tables,
    )
    whole_up = whole_up.reshape(mp, width, hidden)
    whole_down = whole_down.reshape(mp, width, hidden)

    activations, up_part, down_part, out_part, gy_parts, g_y, g_s0, g_x2, feed_sums, g_s0_own = feed(
        y_back, w_own, s0, tokens, cotangent, w_out, gain_rows, chan_rows, 3 * taps, whole_up, whole_down
    )

    up_part, down_part = [p.reshape(mp, dp, rows, hidden) for p in (up_part, down_part)]
    gw_back, gw_edge, sums, g_a0, fin_part, fout_part, *partials, first_part = mixer_backward(
        doc_lengths, taps, gy_parts, g_s0_own, channel_weight, feed_sums, up_part, down_part, g_s0, z, a, w_in,
        chan_rows, out_part, w_parts, tables, spectrum, decay, hidden_filter, filter_out, phase, table,
    )

    results = finish(
        doc_lengths, taps, (gw_back, gw_edge, chan_rows, gain_rows, sums),
        post_late(g_y, s1, s2, z, a, w_in, g_a0, n1, inv1, g_x2), partials, first_part, fin_part, fout_part,
        (
            in_weight, out_weight, in_rows, out_rows, up_rows, down_rows,
            in_cols, out_cols, up_cols, down_cols, gains, gain_moment,
        ),
        up_weight, down_weight,
        (channel_weight, channel_moment, filter_in, filter_in_moment, filter_out, filter_out_moment),
    )
    (
        input_grad, norm, in_g, out_g, up_g, down_g, gain_g, in_n, out_n, up_n, down_n, gain_n, gain_m,
        in_r, out_r, up_r, down_r, in_c, out_c, up_c, down_c,
        chan_g, chan_n, chan_m, fin_g, fin_n, fin_m, fout_g, fout_n, fout_m,
    ) = hand_out(results, own)
    return (
        activations, input_grad, norm.reshape(()),
        in_g.transpose(1, 0, 2), out_g, up_g, down_g, gain_g.T, chan_g, fin_g, fout_g,
        in_n.transpose(1, 0, 2), out_n, up_n, down_n, gain_n.T, chan_n, fin_n, fout_n,
        in_r, in_c, out_r, out_c, up_r, up_c, down_r, down_c, gain_m.T, chan_m, fin_m, fout_m,
    )


def solution(mesh):
    tokens, by_rows, by_cols, both = P(("dp", "mp"), None), P("dp", None), P(None, "mp"), P("dp", "mp")
    cube, vec_dp, vec_mp = P("dp", None, "mp"), P("dp"), P("mp")
    moments = (vec_dp, by_cols, vec_dp, vec_mp, vec_dp, vec_mp, vec_dp, vec_mp)
    weights = (cube, both, both, both, by_rows, by_cols, P(), by_cols)
    small = (by_rows, by_cols, P(), by_cols)
    return jax.shard_map(
        per_device,
        mesh=mesh,
        in_specs=(tokens, tokens, by_rows) + weights + moments + small,
        out_specs=(tokens, tokens, P()) + weights + weights + moments + small,
        check_vma=False,
    )
```

```python
import functools
import math

import jax
import jax.numpy as jnp
import ml_dtypes
import numpy as np
from jax import lax
from jax.experimental import pallas as pl
from jax.experimental.pallas import tpu as pltpu
from jax.sharding import PartitionSpec as P

EPS_NORM = 1e-05
MOMENT_DECAY = 0.5
CLIP_NORM = 1.0
CLIP_STEP = 0.25
STEP_RATE = 2.0
FAST_DECAY = 15.35
SLOW_DECAY = 3.07
FULL_PRECISION = lax.Precision.HIGHEST
BF = jnp.bfloat16
F32 = jnp.float32
MESH = pl.DeviceIdType.MESH
BLOCK = 256
EDGE = 16
HALVES = 2
FOLD = 4
ROOM = 62 << 20
IN_VMEM = pl.BlockSpec(memory_space=pltpu.VMEM)
IN_HBM = pl.BlockSpec(memory_space=pl.ANY)
IN_SMEM = pl.BlockSpec(memory_space=pltpu.SMEM)


def struct(shape, dtype):
    return jax.ShapeDtypeStruct(tuple(shape), dtype)


def transform_tables(block):
    freq = 2 * np.arange(block)[:, None] + 1
    angle = np.pi * (freq * np.arange(block)[None, :] % (4 * block)) / (2 * block)
    table = np.concatenate([np.cos(angle), -np.sin(angle)], axis=0).astype(np.float32)
    high = table.astype(ml_dtypes.bfloat16)
    low = (table - high.astype(np.float32)).astype(ml_dtypes.bfloat16)
    return high, low, np.ascontiguousarray(high.T), np.ascontiguousarray(low.T)


def mm(left, right):
    return lax.dot_general(left, right, (((1,), (0,)), ((), ())), preferred_element_type=F32)


def split(values):
    high = values.astype(BF)
    return high, (values - high.astype(F32)).astype(BF)


def load_rows(ref, start, count, lead=()):
    odd = lax.rem(start, 8)
    tile = ref[lead + (pl.ds(lax.div(start, 8), count // 8 + 1),)]
    width = tile.shape[-1]
    tile = pltpu.roll(tile, lax.rem(8 - odd, 8), axis=1)
    first = lax.broadcasted_iota(jnp.int32, (count // 8, 8, width), 1) < 8 - odd
    return jnp.where(first, tile[:-1], tile[1:]).reshape(count, width)


def tiles(values):
    return values.reshape(values.shape[0] // 8, 8, values.shape[1])


def unpack(target, source, channels):
    parts, rows, width = source.shape
    fold, count = width // channels, rows // 8
    for part in range(parts):
        for piece in range(fold):
            values = source[part, :, piece * channels : (piece + 1) * channels].astype(F32)
            target[pl.ds((part * fold + piece) * count, count), :, 0:channels] = tiles(values)


def pack_block(target, index, values, channels):
    rows = target.shape[1]
    fold, pieces = target.shape[2] // channels, values.shape[0] // rows
    for i in range(pieces):
        part, piece = divmod(index * pieces + i, fold)
        source = values[i * rows : (i + 1) * rows, 0:channels]
        target[part, :, pl.ds(piece * channels, channels)] = source.astype(target.dtype)


def beside(values):
    return [jnp.concatenate(values[i : i + 2], axis=1) for i in range(0, len(values), 2)]


def apart(values, lanes):
    return [v[:, i : i + lanes] for v in values for i in range(0, v.shape[1], lanes)]


def pair_rows(index, block, size):
    first = pl.multiple_of(index * size, size)
    return pl.ds(first, size), pl.ds(pl.multiple_of(block + first, size), size)


def signs(size, width, scale):
    odd = lax.broadcasted_iota(jnp.int32, (size, width), 0) % 2
    return jnp.where(odd == 0, scale, -scale).astype(F32)


def filter_spectrum(filter_ref, spectrum, raw, tables, block):
    count, lanes = raw.shape[0], raw.shape[2]
    high, low = tables[0][...], tables[1][...]
    terms = [split(filter_ref[pl.ds(lag * block, block), :]) for lag in range(count)]
    tops, rests = beside([t[0] for t in terms]), beside([t[1] for t in terms])
    done = [mm(high, t) + mm(high, r) + mm(low, t) for t, r in zip(tops, rests)]
    for lag, values in enumerate(apart(done, lanes)):
        raw[lag] = values
    scale = 1.0 / block

    def body(index, carry):
        re_rows, im_rows = pair_rows(index, block, 8)
        sign = signs(8, raw.shape[2], scale)
        for lag in range(count):
            re, im = raw[lag, re_rows, :] * scale, raw[lag, im_rows, :] * scale
            if lag:
                re = re - sign * raw[lag - 1, im_rows, :]
                im = im + sign * raw[lag - 1, re_rows, :]
            spectrum[lag, re_rows, :] = re
            spectrum[lag, im_rows, :] = im
        return carry

    lax.fori_loop(0, block // 8, body, 0)


def slot_blocks(source, target, tables, start, length, block):
    high, low = tables[0][...], tables[1][...]
    blocks = []
    for index in range(target.shape[0]):
        values = load_rows(source, start + index * block, block)
        inside = lax.broadcasted_iota(jnp.int32, values.shape, 0) + index * block < length
        blocks.append(jnp.where(inside, values, 0.0).astype(BF))
    done = [mm(high, values) + mm(low, values) for values in beside(blocks)]
    for index, values in enumerate(apart(done, target.shape[2])):
        target[index] = values


def inverse(top, rest, tables):
    high, low = tables[2][...], tables[3][...]
    count, lanes = top.shape[0], top.shape[2]
    tops, rests = beside([top[i] for i in range(count)]), beside([rest[i] for i in range(count)])
    return apart([mm(high, t) + mm(high, r) + mm(low, t) for t, r in zip(tops, rests)], lanes)


def document_starts(len_ref, count):
    starts, at = [], jnp.int32(0)
    for slot in range(count):
        starts.append(at)
        at = at + len_ref[0, slot]
    return starts


def merge_slots(slots, starts, put, total, block, most):
    for index in range(total // block):
        first = index * block
        merged = None
        for slot, start in enumerate(starts):
            at = jnp.clip(first - start, -block, most) + block
            values = load_rows(slots, at, block, (slot,))
            if merged is None:
                merged = values
            else:
                inside = lax.broadcasted_iota(jnp.int32, values.shape, 0) + first >= start
                merged = jnp.where(inside, values, merged)
        put(index, merged)


def forward_products(spectrum, raw, top, rest, block):
    count = raw.shape[0]

    def body(index, carry):
        re_rows, im_rows = pair_rows(index, block, 16)
        hr = [spectrum[i, re_rows, :] for i in range(count)]
        hi = [spectrum[i, im_rows, :] for i in range(count)]
        xr = [raw[i, re_rows, :] for i in range(count)]
        xi = [raw[i, im_rows, :] for i in range(count)]
        for out in range(count):
            re = hr[0] * xr[out] - hi[0] * xi[out]
            im = hr[0] * xi[out] + hi[0] * xr[out]
            for lag in range(1, out + 1):
                re = re + (hr[lag] * xr[out - lag] - hi[lag] * xi[out - lag])
                im = im + (hr[lag] * xi[out - lag] + hi[lag] * xr[out - lag])
            top[out, re_rows, :], rest[out, re_rows, :] = split(re)
            top[out, im_rows, :], rest[out, im_rows, :] = split(im)
        return carry

    lax.fori_loop(0, block // 16, body, 0)


def backward_products(spectrum, grad, raw, total, top, rest, block, first_slot):
    count = raw.shape[0]

    def body(index, carry):
        re_rows, im_rows = pair_rows(index, block, 16)
        gr = [grad[i, re_rows, :] for i in range(count)]
        gi = [grad[i, im_rows, :] for i in range(count)]
        hr = [spectrum[i, re_rows, :] for i in range(count)]
        hi = [spectrum[i, im_rows, :] for i in range(count)]
        for out in range(count):
            re = hr[0] * gr[out] + hi[0] * gi[out]
            im = hr[0] * gi[out] - hi[0] * gr[out]
            for later in range(out + 1, count):
                lag = later - out
                re = re + (hr[lag] * gr[later] + hi[lag] * gi[later])
                im = im + (hr[lag] * gi[later] - hi[lag] * gr[later])
            top[out, re_rows, :], rest[out, re_rows, :] = split(re)
            top[out, im_rows, :], rest[out, im_rows, :] = split(im)
        xr = [raw[i, re_rows, :] for i in range(count)]
        xi = [raw[i, im_rows, :] for i in range(count)]
        for lag in range(count):
            re = im = None
            for at in range(count - lag):
                a = xr[at] * gr[at + lag] + xi[at] * gi[at + lag]
                b = xr[at] * gi[at + lag] - xi[at] * gr[at + lag]
                re = a if re is None else re + a
                im = b if im is None else im + b
            if not first_slot:
                re = re + total[lag, re_rows, :]
                im = im + total[lag, im_rows, :]
            total[lag, re_rows, :] = re
            total[lag, im_rows, :] = im
        return carry

    lax.fori_loop(0, block // 16, body, 0)


def filter_gradient(total, top, rest, tables, out_ref, lanes, channels, block):
    count, width = total.shape[0], total.shape[2]
    scale = 1.0 / block

    def body(index, carry):
        re_rows, im_rows = pair_rows(index, block, 16)
        sign = signs(16, width, 1.0)
        for lag in range(count):
            re, im = total[lag, re_rows, :], total[lag, im_rows, :]
            if lag + 1 < count:
                re = re + sign * total[lag + 1, im_rows, :]
                im = im - sign * total[lag + 1, re_rows, :]
            top[lag, re_rows, :], rest[lag, re_rows, :] = split(re * scale)
            top[lag, im_rows, :], rest[lag, im_rows, :] = split(im * scale)
        return carry

    lax.fori_loop(0, block // 16, body, 0)
    for lag, values in enumerate(inverse(top, rest, tables)):
        out_ref[pl.ds(lag * block, block), lanes] = values[:, 0:channels]


def conv_forward_steps(doc_count, len_ref, x_ref, tables, y_ref, spectrum, full, raw, top, rest, slots, between):
    block, blocks = spectrum.shape[1] // 2, spectrum.shape[0]
    channels = x_ref.shape[2] // FOLD
    unpack(full, x_ref, channels)
    starts = document_starts(len_ref, doc_count)
    for slot in range(doc_count):
        slot_blocks(full, raw, tables, starts[slot], len_ref[0, slot], block)
        forward_products(spectrum, raw, top, rest, block)
        for out, values in enumerate(inverse(top, rest, tables)):
            slots[slot, pl.ds((1 + out) * block // 8, block // 8)] = tiles(values)
        between(slot)

    def put(index, values):
        pack_block(y_ref, index, values, channels)

    tokens = math.prod(x_ref.shape) // channels
    merge_slots(slots, starts, put, tokens, block, blocks * block)


def conv_backward_steps(
    doc_count, len_ref, g_ref, x_ref, spectrum, skip, tables, gw_ref, edge_ref, gf_ref, lanes,
    g_full, x_full, grad, raw, top, rest, total, slots, between,
):
    block, blocks, channels = spectrum.shape[1] // 2, spectrum.shape[0], x_ref.shape[2] // FOLD
    unpack(g_full, g_ref, channels)
    unpack(x_full, x_ref, channels)
    starts = document_starts(len_ref, doc_count)
    for slot in range(doc_count):
        slot_blocks(g_full, grad, tables, starts[slot], len_ref[0, slot], block)
        slot_blocks(x_full, raw, tables, starts[slot], len_ref[0, slot], block)
        backward_products(spectrum, grad, raw, total, top, rest, block, slot == 0)
        for out, values in enumerate(inverse(top, rest, tables)):
            slots[slot, pl.ds((1 + out) * block // 8, block // 8)] = tiles(values)
        between(slot)
    edge_ref[...] = jnp.zeros(edge_ref.shape, edge_ref.dtype)
    parts = x_ref.shape[0]
    tokens = math.prod(x_ref.shape) // channels
    each = tokens // parts // block

    def put(index, values):
        pack_block(gw_ref, index, values, channels)
        if index % each == 0 and index:
            own = g_full[pl.ds(index * block // 8, EDGE // 8)].reshape(values[0:EDGE].shape)[:, 0:channels] * skip
            edge_ref[index // each - 1, :, 0:channels] = (values[0:EDGE, 0:channels] + own).astype(edge_ref.dtype)

    merge_slots(slots, starts, put, tokens, block, blocks * block)
    between(doc_count)
    filter_gradient(total, top, rest, tables, gf_ref, lanes, channels, block)


def lanes_for(channels):
    return -(-channels // 128) * 128


def conv_scratch(x_shape, blocks, block, docs):
    channels = x_shape[2] // FOLD
    tokens, lanes = math.prod(x_shape) // channels, lanes_for(channels)
    wide = (blocks, 2 * block, lanes)
    full = pltpu.VMEM(((tokens + blocks * block) // 8 + 1, 8, lanes), F32)
    slots = pltpu.VMEM((docs, (blocks + 2) * block // 8 + 1, 8, lanes), F32)
    return full, pltpu.VMEM(wide, F32), pltpu.VMEM(wide, BF), slots


def conv_forward_kernel(doc_count, len_ref, x_ref, filter_ref, t0, t1, t2, t3, y_ref, spectrum, full, raw, top, rest, slots):
    tables = (t0, t1, t2, t3)
    filter_spectrum(filter_ref, spectrum, raw, tables, spectrum.shape[1] // 2)
    conv_forward_steps(
        doc_count, len_ref, x_ref, tables, y_ref, spectrum, full, raw, top, rest, slots, lambda slot: None
    )


def conv_forward(x, lengths, filters, tables):
    docs, block = lengths.shape[1], tables[0].shape[1]
    blocks, channels = filters.shape[0] // block, filters.shape[1]
    filters = jnp.pad(filters, ((0, 0), (0, lanes_for(channels) - channels)))
    full, raw, low, slots = conv_scratch(x.shape, blocks, block, docs)
    return pl.pallas_call(
        functools.partial(conv_forward_kernel, docs),
        name="conv_forward",
        out_shape=(struct(x.shape, BF), struct((blocks, 2 * block, filters.shape[1]), F32)),
        in_specs=[IN_SMEM] + [IN_VMEM] * 6,
        out_specs=(IN_VMEM, IN_VMEM),
        scratch_shapes=[full, raw, low, low, slots],
        compiler_params=pltpu.CompilerParams(vmem_limit_bytes=ROOM),
    )(lengths, x, filters, *tables)


def conv_backward_kernel(doc_count, len_ref, g_ref, x_ref, spectrum, skip_ref, t0, t1, t2, t3, gw_ref, edge_ref, gf_ref, *work):
    conv_backward_steps(
        doc_count, len_ref, g_ref, x_ref, spectrum, skip_ref[...], (t0, t1, t2, t3), gw_ref, edge_ref, gf_ref,
        slice(None), *work, lambda slot: None,
    )


def conv_backward(g, x, lengths, spectrum, skip_gain, tables):
    blocks, block, channels = spectrum.shape[0], spectrum.shape[1] // 2, x.shape[2] // FOLD
    docs = lengths.shape[1]
    full, raw, low, slots = conv_scratch(x.shape, blocks, block, docs)
    return pl.pallas_call(
        functools.partial(conv_backward_kernel, docs),
        name="conv_backward",
        out_shape=(
            struct(x.shape, BF),
            struct((x.shape[0], EDGE, lanes_for(channels)), BF),
            struct((blocks * block, channels), F32),
        ),
        in_specs=[IN_SMEM] + [IN_VMEM] * 8,
        out_specs=(IN_VMEM,) * 3,
        scratch_shapes=[full, full, raw, raw, low, low, raw, slots],
        compiler_params=pltpu.CompilerParams(vmem_limit_bytes=ROOM),
    )(lengths, g, x, spectrum, skip_gain, *tables)


def turned(value, bit):
    return value + bit - 2 * bit * ((value // bit) % 2)


def send(source, target, send_sem, recv_sem, device):
    copy = pltpu.make_async_remote_copy(
        src_ref=source,
        dst_ref=target,
        send_sem=send_sem,
        recv_sem=recv_sem,
        device_id=device,
        device_id_type=MESH,
    )
    copy.start()
    return copy


def greet(peers):
    barrier = pltpu.get_barrier_semaphore()
    for peer in peers:
        pl.semaphore_signal(barrier, inc=1, device_id=peer, device_id_type=MESH)
    pl.semaphore_wait(barrier, len(peers))


def ring(me, count):
    return [lax.rem(me + step, count) for step in range(1, count)]


def dma(*shape):
    return pltpu.SemaphoreType.DMA(shape)


def gather_fallback(chunks, gains, channel, edges):
    mp = lax.axis_size("mp")
    down = [(i, (i + 1) % mp) for i in range(mp)]
    up = [(i, (i - 1) % mp) for i in range(mp)]
    spread = [lax.all_gather(lax.all_gather(c, "dp"), "mp") for c in chunks]
    return (
        *spread,
        lax.all_gather(gains, "dp"),
        lax.all_gather(channel, "mp"),
        jnp.stack([lax.ppermute(edges[0], "mp", down), lax.ppermute(edges[1], "mp", up)]),
    )


def exchange_kernel(count, has_edge, *refs):
    sources, refs = refs[: count + has_edge], refs[count + has_edge :]
    targets, refs = refs[: count + has_edge], refs[count + has_edge :]
    send_sem, recv_sem, edge_send, edge_recv = refs
    d, m, mp = lax.axis_index("dp"), lax.axis_index("mp"), lax.axis_size("mp")
    greet([(d, e) for e in ring(m, mp)])
    copies = []
    for step, e in reversed(list(enumerate(ring(m, mp)))):
        for i in range(count):
            copies.append(
                send(sources[i].at[e], targets[i].at[m], send_sem.at[i, step], recv_sem.at[i, step], (d, e))
            )
    if has_edge:
        before = lax.rem(m + mp - 1, mp)
        copies.append(send(sources[count], targets[count], edge_send.at[0], edge_recv.at[0], (d, before)))
    for i in range(count):
        targets[i][m] = sources[i][m]
    for copy in copies:
        copy.wait()


def exchange(arrays, edge, collective_id):
    mp, count = lax.axis_size("mp"), len(arrays)
    inputs = list(arrays) + ([] if edge is None else [edge])
    return pl.pallas_call(
        functools.partial(exchange_kernel, count, int(edge is not None)),
        name="exchange_%d" % collective_id,
        out_shape=tuple(struct(a.shape, a.dtype) for a in inputs),
        in_specs=[IN_VMEM] * len(inputs),
        out_specs=(IN_VMEM,) * len(inputs),
        scratch_shapes=[dma(count, mp - 1), dma(count, mp - 1), dma(1), dma(1)],
        compiler_params=pltpu.CompilerParams(
            collective_id=collective_id, has_side_effects=True, vmem_limit_bytes=ROOM
        ),
    )(*inputs)


class Flow:
    def __init__(self, part, refs, lanes=slice(None)):
        self.part, self.lanes = part, lanes
        (self.own, self.from_core, self.from_y2, self.from_x2, self.from_x1, self.from_y1, self.from_z) = refs[:7]
        self.own_sem, self.p_send, self.p_recv, self.z_send, self.z_recv = refs[7:]
        self.d, self.m, self.mp = lax.axis_index("dp"), lax.axis_index("mp"), lax.axis_size("mp")
        self.half = self.mp // 2
        self.y, self.x, self.core = self.d // 4, (self.d // 2) % 2, self.d % 2
        self.pending = []

    def push(self, slot, source, target, bit):
        peer = (turned(self.d, bit), self.m)
        copy = send(source, target, self.p_send.at[slot], self.p_recv.at[slot], peer)
        self.pending.append(copy)
        return copy

    def start(self):
        self.copy = self.push(0, self.part.at[:, :, :, 1 - self.core, :, self.lanes], self.from_core, 1)
        self.local = pltpu.make_async_copy(self.part.at[:, :, :, self.core, :, self.lanes], self.own, self.own_sem.at[0])
        self.local.start()

    def core_stage(self):
        own, half, y, x = self.own, self.half, self.y, self.x
        self.local.wait()
        self.copy.wait_recv()

        def body(i, carry):
            at = (i // 4, (i // 2) % 2, i % 2)
            own[at] = own[at] + self.from_core[at]
            return carry

        lax.fori_loop(0, self.mp * 4, body, 0)
        low, high = pl.ds(0, half), pl.ds(half, self.mp - half)
        self.copies = [
            self.push(1, own.at[low, 1 - y], self.from_y2, 4),
            self.push(2, own.at[high, :, 1 - x], self.from_x2, 2),
        ]

    def second_sum(self):
        own, half, y, x = self.own, self.half, self.y, self.x
        for copy in self.copies:
            copy.wait_recv()

        def body(i, carry):
            a, b = i // 2, i % 2
            own[a, y, b] = own[a, y, b] + self.from_y2[a, b]
            own[half + a, b, x] = own[half + a, b, x] + self.from_x2[a, b]
            return carry

        lax.fori_loop(0, half * 2, body, 0)

    def second_stage(self):
        own, half, y, x = self.own, self.half, self.y, self.x
        self.second_sum()
        low, high = pl.ds(0, half), pl.ds(half, self.mp - half)
        self.copies = [
            self.push(3, own.at[low, y, 1 - x], self.from_x1, 2),
            self.push(4, own.at[high, 1 - y, x], self.from_y1, 4),
        ]

    def third_stage(self):
        own, half, y, x = self.own, self.half, self.y, self.x
        for copy in self.copies:
            copy.wait_recv()

        def body(a, carry):
            own[a, y, x] = own[a, y, x] + self.from_x1[a]
            own[half + a, y, x] = own[half + a, y, x] + self.from_y1[a]
            return carry

        lax.fori_loop(0, half, body, 0)

    def send_z(self):
        self.copies = [
            send(
                self.own.at[e, self.y, self.x], self.from_z.at[step], self.z_send.at[step], self.z_recv.at[step],
                (self.d, e),
            )
            for step, e in enumerate(ring(self.m, self.mp))
        ]
        self.pending.extend(self.copies)

    def finish(self, out):
        for copy in self.copies:
            copy.wait_recv()
        total = self.own[self.m, self.y, self.x].astype(F32)
        for step in range(self.mp - 1):
            total = total + self.from_z[step].astype(F32)
        out[:, self.lanes] = total

    def drain(self):
        for copy in self.pending:
            copy.wait_send()


FLOW_REFS = 12


def flow_scratch(mp, block, over_z=True):
    half = mp // 2
    leads = ((mp, 2, 2), (mp, 2, 2), (half, 2), (mp - half, 2), (half,), (mp - half,))
    last = (mp - 1,) + block if over_z else (1, 16, 128)
    return [pltpu.VMEM(lead + block, BF) for lead in leads] + [pltpu.VMEM(last, BF)] + [dma(1), dma(5), dma(5), dma(mp - 1), dma(mp - 1)]


class SmallSums:
    def __init__(self, small, outs, wide, refs):
        count = len(small)
        self.small, self.outs, self.wide = small, outs, wide
        self.running, self.from_dp, self.from_mp = [refs[i * count : (i + 1) * count] for i in range(3)]
        self.s_send, self.s_recv = refs[3 * count :]
        self.pending = []

    def start(self, stage):
        bit = (1, 2, 4)[stage]
        d, m = lax.axis_index("dp"), lax.axis_index("mp")
        if stage == 0:
            for i, ref in enumerate(self.small):
                self.running[i][0] = ref[...]
        self.copies = []
        for i in range(len(self.small)):
            at = i * 8 + stage
            self.copies.append(
                send(
                    self.running[i].at[stage], self.from_dp[i].at[stage], self.s_send.at[at], self.s_recv.at[at],
                    (turned(d, bit), m),
                )
            )
        self.pending.extend(self.copies)

    def end(self, stage):
        for i, copy in enumerate(self.copies):
            copy.wait_recv()
            self.running[i][stage + 1] = self.running[i][stage] + self.from_dp[i][stage]

    def start_mp(self):
        d, m, mp = lax.axis_index("dp"), lax.axis_index("mp"), lax.axis_size("mp")
        self.copies = []
        for i, wide in enumerate(self.wide):
            if wide:
                for step, e in enumerate(ring(m, mp)):
                    at = i * 8 + 3 + step
                    self.copies.append(
                        send(
                            self.running[i].at[3], self.from_mp[i].at[m], self.s_send.at[at], self.s_recv.at[at],
                            (d, e),
                        )
                    )
                self.from_mp[i][m] = self.running[i][3]
        self.pending.extend(self.copies)

    def end_mp(self):
        for copy in self.copies:
            copy.wait_recv()
        for i, wide in enumerate(self.wide):
            if wide:
                total = self.from_mp[i][0]
                for e in range(1, lax.axis_size("mp")):
                    total = total + self.from_mp[i][e]
                self.outs[i][...] = total
            else:
                self.outs[i][...] = self.running[i][3]

    def drain(self):
        for copy in self.pending:
            copy.wait_send()


def small_scratch(small, mp):
    scratch = []
    for lead in (4, 3, mp):
        scratch += [pltpu.VMEM((lead,) + s.shape, F32) for s in small]
    return scratch + [dma(8 * len(small)), dma(8 * len(small))]


def scatter_fallback(part):
    over_mp = lax.psum_scatter(part, "mp", scatter_dimension=0)
    return lax.psum_scatter(over_mp, "dp", scatter_dimension=0).astype(F32)


def cored(part):
    return part.reshape((part.shape[0], 2, 2, 2) + part.shape[2:])


class Blocks:
    def __init__(self, pairs, send_sem, recv_sem):
        self.pairs, self.send_sem, self.recv_sem = pairs, send_sem, recv_sem
        self.d, self.m, self.mp = lax.axis_index("dp"), lax.axis_index("mp"), lax.axis_size("mp")

    def start(self):
        self.copies = []
        for step, e in reversed(list(enumerate(ring(self.m, self.mp)))):
            for i, (source, target) in enumerate(self.pairs):
                sems = self.send_sem.at[i, step], self.recv_sem.at[i, step]
                self.copies.append(send(source.at[e], target.at[self.m], *sems, (self.d, e)))
        for source, target in self.pairs:
            target[self.m] = source[self.m]

    def arrive(self):
        for copy in self.copies:
            copy.wait_recv()

    def drain(self):
        for copy in self.copies:
            copy.wait_send()


def stream_zero(offsets, edge, gs, z, w, channel, marks, sums, feed_sums):
    count = gs.shape[0] - EDGE
    same = [None] + [marks[k - 1, :, 0:1] > 0.0 for k in range(1, offsets)]
    gs[pl.ds(count, EDGE), :] = edge[...].astype(F32)
    sums[...] = jnp.zeros(sums.shape, F32)
    g_z = short_backward(0, gs, z, channel, same, offsets, count, sums).astype(BF)
    sums[pl.ds(3 * offsets, 1), :] = feed_sums[1:2, :]
    sums[pl.ds(3 * offsets + 2, 1), :] = feed_sums[0:1, :]
    return g_z, dot_nt(g_z, w[...])


def mixer_backward_kernel(doc_count, offsets, len_ref, g_parts, edge, channel_own, feed_sums, part_a, part_b, *refs):
    late_refs, refs = refs[:17], refs[17:]
    gw_back, gw_edge_back, sums, ga0_out, fin_part, fout_part, partial_a, b_low, b_high, part_c_out, refs = *refs[:10], refs[10:]
    held, refs = refs[:16], refs[16:]
    (
        late_sem, ga0, part_c, save_sem, edge_back, gs, marks, gf_ref, g_in, gw, gw_edge, g_full, x_full, grad, raw,
        top, rest, total, slots, b_send, b_recv, c_send, c_recv, e_sem, *refs,
    ) = refs
    a_refs, b_refs = refs[:FLOW_REFS], refs[FLOW_REFS:]
    z, acts, w, channel, out_part, x_ref, t0, t1, t2, t3, spectrum, decay, hidden, f_out, phase, table = held
    tables = (t0, t1, t2, t3)
    parts = x_ref.shape[1]
    near = x_ref.shape[3] // FOLD
    half = near * HALVES
    own_count = ga0.shape[0]
    d, m, mp = lax.axis_index("dp"), lax.axis_index("mp"), lax.axis_size("mp")
    a, b = Flow(part_a, a_refs), Flow(part_b, b_refs)
    incoming, outgoing = [], []
    for side in range(HALVES):
        incoming.append(Blocks([(g_parts.at[side], g_in.at[side])], b_send.at[side], b_recv.at[side]))
        pairs = [(gw.at[side], gw_back.at[side]), (gw_edge.at[side], gw_edge_back.at[side])]
        outgoing.append(Blocks(pairs, c_send.at[side], c_recv.at[side]))
    late = Late(late_refs, (gs.at[pl.ds(0, own_count)],) + tuple(held), late_sem)
    greet([(turned(d, bit), m) for bit in (1, 2, 4)] + [(d, e) for e in ring(m, mp)])
    edge_copy = send(edge, edge_back, e_sem.at[0], e_sem.at[1], (d, lax.rem(m + mp - 1, mp)))
    for copies in incoming:
        copies.start()
    a.start()
    mark_same(marks, len_ref, doc_count, m * own_count - EDGE)
    a.core_stage()
    b.start()
    late.need(0, 1, 2, 3, 4, 5)
    edge_copy.wait_recv()
    g_z, back = stream_zero(offsets, edge_back, gs, z, w, channel, marks, sums, feed_sums)
    ga0[...] = back
    size = part_c.shape[4]
    for first in range(0, parts, 2):
        in_grad = dot_tn(acts[pl.ds(EDGE, own_count), :], g_z[:, first * half : (first + 2) * half])
        for part in range(first, first + 2):
            cols = slice((part - first) * half, (part - first + 1) * half)
            for owner in range(8):
                at = (part, owner // 4, owner // 2 % 2, owner % 2, slice(None))
                rows = slice(owner * size, (owner + 1) * size)
                part_c[at + (pl.ds(0, half),)] = in_grad[rows, cols].astype(BF)
                part_c[at + (pl.ds(half, half),)] = out_part[part, rows]
    saves = Late((ga0, part_c), (ga0_out, part_c_out), save_sem)
    late.need(*range(6, 17))
    skip = channel_own[channel_own.shape[0] - 1 :, :]

    def first_side(step):
        if step == 0:
            b.core_stage()
        if step == 2:
            a.second_stage()

    def last_side(step):
        if step == doc_count:
            a.third_stage()

    for side in range(HALVES):
        incoming[side].arrive()
        between = (first_side, last_side)[side]
        lanes = pl.ds(side * near, near)

        def after(step, side=side, between=between):
            if step == doc_count:
                outgoing[side].start()
            between(step)

        conv_backward_steps(
            doc_count, len_ref, g_in.at[side], x_ref.at[side], spectrum.at[side], skip[:, side * near : (side + 1) * near],
            tables, gw.at[side], gw_edge.at[side], gf_ref, lanes, g_full, x_full, grad, raw, top, rest, total, slots, after,
        )
    g_raw = gf_ref[...] * decay[...]
    fout_part[...] = near_product(hidden[...], g_raw, dot_tn)
    fin_part[...] = near_product(table[...], near_product(g_raw, f_out[...], dot_nt) * jnp.cos(phase[...]), dot_tn)
    for e in range(parts):
        partial_a[e] = a.own[e, a.y, a.x]
    b.second_sum()
    for e in range(parts // 2):
        for other in range(2):
            b_low[e, other] = b.own[e, b.y, other]
            b_high[e, other] = b.own[parts // 2 + e, other, b.x]
    for copies in outgoing:
        copies.arrive()
    edge_copy.wait_send()
    saves.need(0, 1)
    for copies in incoming + outgoing:
        copies.drain()
    for flow in (a, b):
        flow.drain()


def mixer_backward(
    lengths, offsets, g_parts, edge, channel_own, feed_sums, part_a, part_b, g_s0, z, a, w_in, channel, out_part, x,
    tables, spectrum, decay, hidden, f_out, phase, table,
):
    dp, mp = lax.axis_size("dp"), lax.axis_size("mp")
    parts, docs = x.shape[1], lengths.shape[1]
    blocks, block, near = spectrum.shape[1], spectrum.shape[2] // 2, x.shape[3] // FOLD
    half, width = HALVES * near, 2 * HALVES * near
    size = part_a.shape[2]
    full = channel.shape[1]
    if dp != 8:
        g_in = exchange([*g_parts], edge, 5)
        edge_back = g_in[HALVES]
        halves = []
        for side in range(HALVES):
            skip = channel_own[-1:, side * near : (side + 1) * near]
            halves.append(conv_backward(g_in[side], x[side], lengths, spectrum[side], skip, tables))
        g_raw = jnp.concatenate([v[2] for v in halves], axis=1) * decay
        fin, fout = product(table.T, product(g_raw, f_out.T) * jnp.cos(phase)), product(hidden.T, g_raw)
        backs = exchange([v[i] for i in range(2) for v in halves], None, 6)
        gw_back, gw_edge_back = jnp.stack(backs[:HALVES]), jnp.stack(backs[HALVES:])
        count = g_s0.shape[0]
        gs = jnp.concatenate([g_s0, edge_back.astype(F32)])
        position = lax.axis_index("mp") * count - EDGE + jnp.arange(count + 2 * EDGE, dtype=jnp.int32)
        doc = jnp.sum((position[:, None] >= jnp.cumsum(lengths[0])[None, :]).astype(jnp.int32), axis=1)
        doc = jnp.where(position < 0, -1, doc)
        same = [None] + [(doc[EDGE:] == doc[EDGE - k : doc.shape[0] - k])[:, None] for k in range(1, offsets)]
        g_z, sums = None, jnp.zeros((16, full), F32)
        for k in range(offsets):
            later, before = gs[k : count + k], z[0, EDGE - k : EDGE - k + count]
            if k:
                later, before = jnp.where(same[k][k : count + k], later, 0.0), jnp.where(same[k][:count], before, 0.0)
            g_z = channel[3 * k] * later if g_z is None else g_z + channel[3 * k] * later
            sums = sums.at[3 * k].set(jnp.sum(gs[:count] * before, axis=0))
        sums = sums.at[3 * offsets].set(feed_sums[1]).at[3 * offsets + 2].set(feed_sums[0])
        g_z = g_z.astype(BF)
        grad = dot_tn(a[EDGE : EDGE + count], g_z).reshape(full, mp, half).transpose(1, 0, 2).astype(BF)
        part_c = jnp.concatenate([grad, out_part], axis=2).reshape(mp, dp, size, width)
        over_dp = [lax.psum_scatter(p, "dp", scatter_dimension=1) for p in (part_a, part_b)]
        return (
            gw_back, gw_edge_back, sums, dot_nt(g_z, w_in[0]), fin, fout, *over_dp, None, part_c,
        )
    edge_shape = (HALVES, parts, EDGE, lanes_for(near))
    own, own_c = part_a.shape[2:], (size, width)
    rows, raw, low, slots = conv_scratch(x.shape[1:], blocks, block, docs)
    first = (g_parts, edge, channel_own, feed_sums)
    late = [
        (g_s0, None), (z, 0), (a, None), (w_in, 0), (channel, None), (out_part, None), (x, None),
        *[(t, None) for t in tables], (spectrum, None), (decay, None), (hidden, None), (f_out, None), (phase, None),
        (table, None),
    ]
    fin, fout = struct((table.shape[1], hidden.shape[1]), F32), struct((hidden.shape[1], half), F32)
    longer = (g_s0.shape[0] + EDGE, full)

    def kernel(*refs):
        start = 3 + len(first)
        chosen = [r if i is None else r.at[i] for r, (_, i) in zip(refs[start : start + len(late)], late)]
        mixer_backward_kernel(docs, offsets, *refs[:start], *chosen, *refs[start + len(late) :])

    return pl.pallas_call(
        kernel,
        name="mixer_backward",
        out_shape=(
            struct(x.shape, BF), struct(edge_shape, BF), struct((16, full), F32), struct(g_s0.shape, F32), fin, fout,
            struct((mp,) + own, BF), *[struct((mp // 2, 2) + own, BF)] * 2, struct((mp, 2, 2, 2) + own_c, BF),
        ),
        in_specs=[IN_SMEM] + [IN_VMEM] * len(first) + [IN_HBM] * (2 + len(late)),
        out_specs=(*[IN_VMEM] * 3, IN_HBM, *[IN_VMEM] * 5, IN_HBM),
        scratch_shapes=[
            *[pltpu.VMEM(v.shape if i is None else v.shape[1:], v.dtype) for v, i in late[1:]],
            dma(len(late)), pltpu.VMEM(g_s0.shape, F32), pltpu.VMEM((mp, 2, 2, 2) + own_c, BF), dma(2),
            pltpu.VMEM(edge.shape, BF), pltpu.VMEM(longer, F32),
            pltpu.VMEM((offsets - 1, longer[0], 128), F32),
            pltpu.VMEM((blocks * block, half), F32), pltpu.VMEM(x.shape, BF), pltpu.VMEM(x.shape, BF),
            pltpu.VMEM(edge_shape, BF), rows, rows, raw, raw, low, low, raw, slots,
            dma(HALVES, 1, mp - 1), dma(HALVES, 1, mp - 1), dma(HALVES, 2, mp - 1), dma(HALVES, 2, mp - 1), dma(2),
            *flow_scratch(mp, own, False), *flow_scratch(mp, own, False),
        ],
        compiler_params=pltpu.CompilerParams(collective_id=5, has_side_effects=True, vmem_limit_bytes=ROOM),
    )(lengths, *first, cored(part_a), cored(part_b), *[v for v, _ in late])


def spread_sum(block, slots, send_sem, recv_sem, axis, first):
    d, m = lax.axis_index("dp"), lax.axis_index("mp")
    count = lax.axis_size(axis)
    me = d if axis == "dp" else m
    copies = []
    for step, e in enumerate(ring(me, count)):
        peer = (e, m) if axis == "dp" else (d, e)
        copies.append(send(block, slots.at[me], send_sem.at[first + step], recv_sem.at[first + step], peer))
    slots[me] = block[...]
    for copy in copies:
        copy.wait()
    total = slots[0]
    for e in range(1, count):
        total = total + slots[e]
    return total


def total_of(values):
    return jnp.sum(jnp.sum(values, axis=1, keepdims=True), axis=0, keepdims=True)


def lanes_of(items):
    lane = lax.broadcasted_iota(jnp.int32, (1, 128), 1)
    row = jnp.zeros((1, 128), F32)
    for index, item in enumerate(items):
        row = row + jnp.where(lane == index, item, 0.0)
    return row


def update_body(
    taps, g0, g1, g2, w0, w1, w2, rows, cols, vec_sum, own_gain, gain, gain_mom, chan, chan_mom,
    fin_sum, fin, fin_mom, fout_sum, fout, fout_mom,
    norm_out, c0, c1, c2, n0, n1, n2, rows_out, cols_out, gain_g, gain_n, gain_m,
    chan_g, chan_n, chan_m, fin_g, fin_n, fin_m, fout_g, fout_n, fout_m,
    turn, mp_block, dp_block, mp_slots, dp_slots, last_block, mp_last, dp_last, send_sem, recv_sem,
):
    d, m = lax.axis_index("dp"), lax.axis_index("mp")
    dp, mp = lax.axis_size("dp"), lax.axis_size("mp")
    size, width = g0.shape
    in_width = 3 * (width // 4)
    is_in = lax.broadcasted_iota(jnp.int32, (size, width), 1) < in_width

    def four(v0, v1, v2, reduce_fn):
        return [
            reduce_fn(jnp.where(is_in, v0, 0.0)),
            reduce_fn(jnp.where(is_in, 0.0, v0)),
            reduce_fn(v1),
            reduce_fn(v2),
        ]

    def row_sum(v):
        return jnp.sum(v, axis=1, keepdims=True)

    def col_sum(v):
        return jnp.sum(v, axis=0, keepdims=True)

    s0, s1, s2 = g0[...] * g0[...], g1[...] * g1[...], g2[...] * g2[...]
    lane = lax.broadcasted_iota(jnp.int32, (size, 128), 1)
    row_parts = four(s0, s1, s2, row_sum)
    packed = jnp.zeros((size, 128), F32)
    for index, part in enumerate(row_parts):
        packed = packed + jnp.where(lane == index, part, 0.0)
    turn[...] = jnp.zeros(turn.shape, F32)
    dp_block[...] = jnp.zeros(dp_block.shape, F32)
    turn[pl.ds(0, size), :] = packed
    mp_block[pl.ds(0, 8), :] = jnp.transpose(turn[...])[0:8]
    old = rows[...]
    old_parts = [total_of(old[:, i : i + 1]) / mp for i in range(4)]
    weight_parts = four(w0[...] * w0[...], w1[...] * w1[...], w2[...] * w2[...], total_of)
    scalars = (
        [total_of(p) for p in row_parts]
        + old_parts
        + weight_parts
        + [
            total_of(gain[...] * gain[...]) / mp,
            total_of(chan[...] * chan[...]) / dp,
            total_of(fout[...] * fout[...]) / dp,
            total_of(fout_sum[...] * fout_sum[...]) / dp,
        ]
    )
    mp_block[pl.ds(8, 8), :] = jnp.broadcast_to(lanes_of(scalars), (8, 128))
    over_mp = spread_sum(mp_block, mp_slots, send_sem, recv_sem, "mp", 0)
    pieces = width // 128
    for index, values in enumerate((s0, s1, s2)):
        sums = col_sum(values)
        for piece in range(pieces):
            dp_block[pl.ds(index * pieces + piece, 1), :] = sums[:, piece * 128 : (piece + 1) * 128]
    dp_block[pl.ds(3 * pieces, 1), :] = over_mp[8:9]
    over_dp = spread_sum(dp_block, dp_slots, send_sem, recv_sem, "dp", mp)
    turn[pl.ds(0, 8), :] = over_mp[0:8]
    row_totals = jnp.transpose(turn[...])[0:size]
    shared = over_dp[3 * pieces : 3 * pieces + 1]

    def scalar(index):
        return shared[:, index : index + 1]

    last = 3 * taps + 1
    vec_sq = total_of(vec_sum[0 : last + 2, :] * vec_sum[0 : last + 2, :])
    fin_sq = total_of(fin_sum[...] * fin_sum[...])
    norm = jnp.sqrt(
        scalar(0) + scalar(1) + scalar(2) + scalar(3) + vec_sq + scalar(15) + fin_sq
    )
    norm_out[...] = norm
    clip = 1.0 / jnp.maximum(1.0, norm / CLIP_NORM)
    square = clip * clip
    fresh = 1.0 - MOMENT_DECAY
    all_rows = size * dp
    wide = [in_width * mp, (width - in_width) * mp, width * mp, width * mp]
    ratio = []
    fresh_rows = jnp.zeros((size, 128), F32)
    for index in range(4):
        row_new = (
            MOMENT_DECAY * old[:, index : index + 1]
            + fresh * square * row_totals[:, index : index + 1] / wide[index]
        )
        mean = MOMENT_DECAY * scalar(4 + index) / all_rows + fresh * square * scalar(index) / (
            all_rows * wide[index]
        )
        ratio.append(row_new / mean)
        fresh_rows = fresh_rows + jnp.where(lane == index, row_new, 0.0)
    turn[pl.ds(0, size), :] = fresh_rows
    rows_out[...] = jnp.transpose(turn[...])[0:8]
    for index in range(3):
        for piece in range(pieces):
            at = pl.ds(piece * 128, 128)
            row = index * pieces + piece
            cols_out[pl.ds(index, 1), at] = (
                MOMENT_DECAY * cols[pl.ds(index, 1), at]
                + fresh * square * over_dp[row : row + 1] / all_rows
            )
    first_ratio = jnp.where(is_in, ratio[0], ratio[1])
    steps = []
    for grad, out, factor, index in ((g0, c0, first_ratio, 0), (g1, c1, ratio[2], 1), (g2, c2, ratio[3], 2)):
        clipped = grad[...] * clip
        out[...] = clipped
        steps.append(clipped * lax.rsqrt(factor * cols_out[pl.ds(index, 1), :]))
    u0, u1, u2 = steps

    def plain(clipped, moment, grad_out, moment_out):
        fresh_moment = MOMENT_DECAY * moment + fresh * clipped * clipped
        grad_out[...] = clipped
        moment_out[...] = fresh_moment
        return clipped * lax.rsqrt(fresh_moment)

    picked = vec_sum[last : last + 2, 0:size]
    for e in range(1, dp):
        picked = jnp.where(d == e, vec_sum[last : last + 2, e * size : (e + 1) * size], picked)
    own_gain[...] = jnp.zeros(own_gain.shape, F32)
    own_gain[:, pl.ds(0, size)] = picked
    own = width // mp
    own_chan = vec_sum[0:last, 0:own]
    for e in range(1, mp):
        own_chan = jnp.where(m == e, vec_sum[0:last, e * own : (e + 1) * own], own_chan)
    u_gain = plain(own_gain[...] * clip, gain_mom[...], gain_g, gain_m)
    u_chan = plain(own_chan * clip, chan_mom[...], chan_g, chan_m)
    u_fin = plain(fin_sum[...] * clip, fin_mom[...], fin_g, fin_m)
    u_fout = plain(fout_sum[...] * clip, fout_mom[...], fout_g, fout_m)
    step_parts = four(u0 * u0, u1 * u1, u2 * u2, total_of) + [
        total_of(u_gain * u_gain) / mp,
        total_of(u_chan * u_chan) / dp,
        total_of(u_fout * u_fout) / dp,
    ]
    last_block[...] = jnp.broadcast_to(lanes_of(step_parts), (8, 128))
    half_way = spread_sum(last_block, mp_last, send_sem, recv_sem, "mp", mp + dp)
    mp_block[pl.ds(0, 8), :] = half_way
    step_sums = spread_sum(mp_block.at[pl.ds(0, 8)], dp_last, send_sem, recv_sem, "dp", 2 * mp + dp)[0:1]

    def factors(step_total, weight_total, entries):
        shrink = 1.0 / jnp.maximum(1.0, jnp.sqrt(step_total / entries) / CLIP_STEP)
        return STEP_RATE * jnp.sqrt(weight_total / entries) * shrink

    def step_sum(index):
        return step_sums[:, index : index + 1]

    rate = [factors(step_sum(i), scalar(8 + i), all_rows * wide[i]) for i in range(4)]
    n0[...] = w0[...] - jnp.where(is_in, rate[0], rate[1]) * u0
    n1[...] = w1[...] - rate[2] * u1
    n2[...] = w2[...] - rate[3] * u2
    gain_n[...] = gain[...] - factors(step_sum(4), scalar(12), 2 * all_rows) * u_gain
    chan_n[...] = chan[...] - factors(step_sum(5), scalar(13), chan.shape[0] * chan.shape[1] * mp) * u_chan
    fout_n[...] = fout[...] - factors(step_sum(6), scalar(14), fout.shape[0] * fout.shape[1] * mp) * u_fout
    fin_count = fin.shape[0] * fin.shape[1]
    fin_rate = factors(total_of(u_fin * u_fin), total_of(fin[...] * fin[...]), fin_count)
    fin_n[...] = fin[...] - fin_rate * u_fin


def greet_all():
    d, m = lax.axis_index("dp"), lax.axis_index("mp")
    greet([(e, m) for e in ring(d, lax.axis_size("dp"))] + [(d, e) for e in ring(m, lax.axis_size("mp"))])


def prepare(raw, ready, turn):
    in_w, out_w, in_rows, out_rows, up_rows, down_rows, in_cols, out_cols, up_cols, down_cols, gain_own, gain_mom_own = raw
    w0, rows, cols, gain, gain_mom = ready
    size, own = out_w.shape
    for j in range(3):
        w0[:, pl.ds(j * own, own)] = in_w[j]
        cols[0:1, pl.ds(j * own, own)] = in_cols[j : j + 1, :]
    w0[:, pl.ds(3 * own, own)] = out_w[...]
    cols[0:1, pl.ds(3 * own, own)] = out_cols[...].reshape(1, own)
    cols[1:2, :] = up_cols[...].reshape(1, -1)
    cols[2:3, :] = down_cols[...].reshape(1, -1)
    turn[...] = jnp.zeros(turn.shape, F32)
    for index, source in enumerate((in_rows, out_rows, up_rows, down_rows)):
        turn[pl.ds(index, 1), pl.ds(0, size)] = source[...].reshape(1, size)
    rows[...] = jnp.transpose(turn[...])[0:size]
    for source, target, fill in ((gain_own, gain, 0.0), (gain_mom_own, gain_mom, 1.0)):
        target[...] = jnp.full(target.shape, fill, F32)
        target[:, pl.ds(0, size)] = source[...]


def prepare_scratch(size, width):
    return [
        pltpu.VMEM((size, width), F32), pltpu.VMEM((size, 128), F32), pltpu.VMEM((8, width), F32),
        pltpu.VMEM((2, 128), F32), pltpu.VMEM((2, 128), F32),
    ]


OUTS = 21


def run_update(taps, grads, sums, w1, w2, ready, own_gain, old, outs, work):
    w0, rows, cols, gain, gain_mom = ready
    chan, chan_mom, fin, fin_mom, fout, fout_mom = old
    update_body(
        taps, *grads, w0, w1, w2, rows, cols, sums[0], own_gain, gain, gain_mom, chan, chan_mom,
        sums[1], fin, fin_mom, sums[2], fout, fout_mom, *outs, *work,
    )


def update_kernel(taps, *refs):
    grads, sums, refs = refs[:3], refs[3:6], refs[6:]
    raw, w1, w2, old, refs = refs[:12], refs[12], refs[13], refs[14:20], refs[20:]
    outs, ready, own_gain, work = refs[:OUTS], refs[OUTS : OUTS + 5], refs[OUTS + 5], refs[OUTS + 6 :]
    prepare(raw, ready, work[0])
    greet_all()
    run_update(taps, grads, sums, w1, w2, ready, own_gain, old, outs, work)


def place_first(g0, zero_and_out, one_and_two):
    own = g0.shape[1] // 4
    g0[:, pl.ds(0, own)] = zero_and_out[:, 0:own]
    g0[:, pl.ds(own, 2 * own)] = one_and_two
    g0[:, pl.ds(3 * own, own)] = zero_and_out[:, own : 2 * own]


class LastOverDp:
    def __init__(self, low, high, from_low, from_high, send_sem, recv_sem):
        self.low, self.high, self.from_low, self.from_high = low, high, from_low, from_high
        d, m = lax.axis_index("dp"), lax.axis_index("mp")
        self.y, self.x = d // 4, (d // 2) % 2
        self.copies = [
            send(low.at[:, 1 - self.x], from_low, send_sem.at[0], recv_sem.at[0], (turned(d, 2), m)),
            send(high.at[:, 1 - self.y], from_high, send_sem.at[1], recv_sem.at[1], (turned(d, 4), m)),
        ]

    def finish(self, partial):
        for copy in self.copies:
            copy.wait()
        half = self.from_low.shape[0]
        for e in range(half):
            partial[e] = self.low[e, self.x] + self.from_low[e]
            partial[half + e] = self.high[e, self.y] + self.from_high[e]


class OverMp:
    def __init__(self, partial, arrived, passed, send_sem, recv_sem):
        self.partial, self.arrived, self.passed = partial, arrived, passed
        self.send_sem, self.recv_sem = send_sem, recv_sem
        self.d, self.m = lax.axis_index("dp"), lax.axis_index("mp")
        near = turned(self.m, 1)
        self.far = turned(self.m, 2)
        self.copies = [self.push(partial.at[e], slot, near) for slot, e in enumerate((near, turned(near, 2)))]

    def push(self, source, slot, peer):
        sems = self.send_sem.at[slot], self.recv_sem.at[slot]
        return send(source, self.arrived.at[slot], *sems, (self.d, peer))

    def step(self):
        for copy in self.copies:
            copy.wait()
        self.passed[...] = self.partial[self.far] + self.arrived[1]
        self.copies = [self.push(self.passed, 2, self.far)]

    def total(self):
        self.copies[0].wait()
        return self.partial[self.m].astype(F32) + self.arrived[0].astype(F32) + self.arrived[2].astype(F32)


def end_kernel(doc_count, taps, len_ref, gw_ref, gw_edge, channel, gains, sums_in, *refs):
    late_refs, partial_a, b_low, b_high, part_c, fin_part, fout_part, refs = refs[:12], *refs[12:18], refs[18:]
    raw, w1, w2, old, refs = refs[:12], refs[12], refs[13], refs[14:20], refs[20:]
    input_grad, outs, refs = refs[0], refs[1 : OUTS + 1], refs[OUTS + 1 :]
    held, late_sem, work, refs = refs[:12], refs[12], refs[13:17], refs[17:]
    ready, own_gain, refs = refs[:5], refs[5], refs[6:]
    g0, g1, g2, g_late, vec, vec_sum, fin_sum, fout_sum, part, refs = *refs[:9], refs[9:]
    update_work, refs = refs[:10], refs[10:]
    arrived, passed, z_send, z_recv, refs = refs[:2], refs[2:4], refs[4], refs[5], refs[6:]
    g_c, partial_b, from_low, from_high, l_send, l_recv, refs = *refs[:6], refs[6:]
    partials = (partial_a, partial_b)
    mp = lax.axis_size("mp")
    own = gw_ref.shape[3] // FOLD * HALVES
    size = g0.shape[0]
    lanes = g_late.shape[1] // FLOWS
    flows = []
    for i in range(FLOWS):
        flows.append(Flow(part, refs[i * FLOW_REFS : (i + 1) * FLOW_REFS], pl.ds(i * lanes, lanes)))
    refs = refs[FLOWS * FLOW_REFS :]
    flow_c, refs = Flow(part_c, refs[:FLOW_REFS]), refs[FLOW_REFS:]
    early = SmallSums((fin_part, fout_part), (fin_sum, fout_sum), (True, False), refs[:8])
    final = SmallSums((vec,), (vec_sum,), (True,), refs[8:])
    late = Late(late_refs, held, late_sem)
    vec[...] = sums_in[...]
    greet_all()
    last_b = LastOverDp(b_low, b_high, from_low, from_high, l_send, l_recv)
    flow_c.start()

    def start_mp(i):
        return OverMp(partials[i], arrived[i], passed[i], z_send.at[i], z_recv.at[i])

    over_mp = [start_mp(0)]
    early.start(0)

    def stream_done(j, grad):
        for e in range(mp):
            for owner in range(8):
                at = (e, owner // 4, owner // 2 % 2, owner % 2, slice(None), pl.ds((j - 1) * own, own))
                part[at] = grad[owner * size : (owner + 1) * size, e * own : (e + 1) * own].astype(BF)
        if j == 1:
            flows[0].start()
            flow_c.core_stage()
            early.end(0)
            early.start(1)
            over_mp[0].step()
            last_b.finish(partial_b)
            over_mp.append(start_mp(1))
        else:
            flows[1].start()
            flows[2].start()
            flow_c.second_stage()
            early.end(1)
            early.start(2)
            over_mp[1].step()

    total = post_steps(
        doc_count, taps, len_ref, gw_ref, gw_edge, channel, gains, vec, held, late, work, stream_done
    )
    final.start(0)
    flows[0].core_stage()
    flow_c.third_stage()
    flow_c.send_z()
    final.end(0)
    final.start(1)
    flows[1].core_stage()
    flows[2].core_stage()
    early.end(2)
    early.start_mp()
    post_end(total, gains, held, input_grad)
    final.end(1)
    final.start(2)
    for flow in flows:
        flow.second_stage()
    final.end(2)
    final.start_mp()
    prepare(raw, ready, update_work[0])
    for flow in flows:
        flow.third_stage()
        flow.send_z()
    g1[...] = over_mp[0].total()
    g2[...] = over_mp[1].total()
    flow_c.finish(g_c)
    early.end_mp()
    final.end_mp()
    for flow in flows:
        flow.finish(g_late)
    place_first(g0, g_c[...], g_late[...])
    for flow in (*flows, flow_c):
        flow.drain()
    early.drain()
    final.drain()
    run_update(taps, (g0, g1, g2), (vec_sum, fin_sum, fout_sum), w1, w2, ready, own_gain, old, outs, update_work)


def update_scratch(dp, mp, width):
    pieces = 3 * width // 128 + 1
    tall = -(-pieces // 8) * 8
    sems = 2 * (dp + mp)
    return [
        pltpu.VMEM((128, 128), F32),
        pltpu.VMEM((16, 128), F32),
        pltpu.VMEM((tall, 128), F32),
        pltpu.VMEM((mp, 16, 128), F32),
        pltpu.VMEM((dp, tall, 128), F32),
        pltpu.VMEM((8, 128), F32),
        pltpu.VMEM((mp, 8, 128), F32),
        pltpu.VMEM((dp, 8, 128), F32),
        dma(sems),
        dma(sems),
    ]


def hand_out_kernel(*refs):
    input_grad, norm, c0, c1, c2, n0, n1, n2, rows, cols, gain_g, gain_n, gain_m, *small = refs[: OUTS + 1]
    (
        input_grad_out, norm_out, in_g, out_g, up_g, down_g, gain_g_out, in_n, out_n, up_n, down_n, gain_n_out, gain_m_out,
        in_r, out_r, up_r, down_r, in_c, out_c, up_c, down_c, *small_out,
    ) = refs[OUTS + 1 :]
    size, own = out_g.shape
    input_grad_out[...] = input_grad[...]
    norm_out[...] = norm[...]
    for source, first, last in ((c0, in_g, out_g), (n0, in_n, out_n)):
        for j in range(3):
            first[j] = source[:, j * own : (j + 1) * own]
        last[...] = source[:, 3 * own : 4 * own]
    for source, target in ((c1, up_g), (c2, down_g), (n1, up_n), (n2, down_n)):
        target[...] = source[...]
    for source, target in ((gain_g, gain_g_out), (gain_n, gain_n_out), (gain_m, gain_m_out)):
        target[...] = source[:, 0:size]
    for index, target in enumerate((in_r, out_r, up_r, down_r)):
        target[...] = rows[index : index + 1, 0:size].reshape(size)
    for j in range(3):
        in_c[j : j + 1, :] = cols[0:1, j * own : (j + 1) * own]
    out_c[...] = cols[0:1, 3 * own : 4 * own].reshape(own)
    up_c[...] = cols[1:2, :].reshape(-1)
    down_c[...] = cols[2:3, :].reshape(-1)
    for source, target in zip(small, small_out):
        target[...] = source[...]


def hand_out(results, own):
    size, width = results[2].shape
    cube, part, full = (3, size, own), (size, own), (size, width)
    column, row, wide = (2, size), (size,), (width,)
    shapes = [(1, 1), cube, part, full, full, column, cube, part, full, full, column, column, row, row, row, row]
    shapes += [(3, own), (own,), wide, wide] + [v.shape for v in results[13:]]
    return pl.pallas_call(
        hand_out_kernel,
        name="hand_out",
        out_shape=(struct(results[0].shape, BF), *[struct(s, F32) for s in shapes]),
        in_specs=[IN_VMEM] * len(results),
        out_specs=(IN_VMEM,) * (1 + len(shapes)),
        compiler_params=pltpu.CompilerParams(vmem_limit_bytes=ROOM),
    )(*results)


FLOWS = 3


def finish(lengths, taps, first, late, partials, part_c, fin_part, fout_part, raw, w1, w2, old):
    dp, mp = lax.axis_size("dp"), lax.axis_size("mp")
    size, own = raw[1].shape
    width = w1.shape[1]
    count = late[0][0].shape[0]
    docs = lengths.shape[1]
    big = struct((size, width), F32)
    flat = [(2, 128), old[0].shape, old[2].shape, old[4].shape]
    outs = [struct((1, 1), F32)] + [big] * 6 + [struct((8, 128), F32), struct((3, width), F32)]
    outs += [struct(s, F32) for s in flat for _ in range(3)]
    params = pltpu.CompilerParams(collective_id=2, has_side_effects=True, vmem_limit_bytes=ROOM)
    tail = [*raw, w1, w2, *old]
    own_gain = pltpu.VMEM((2, 128), F32)
    if dp != 8:
        last_part, input_grad, vec = post(lengths, taps, *first, late)
        over_mp = [lax.psum_scatter(p, "mp").astype(F32) for p in partials[:2]]
        grad = scatter_fallback(last_part.reshape(mp, dp, size, 2 * own))
        first_grad = scatter_fallback(part_c)
        grad = jnp.concatenate([first_grad[:, :own], grad, first_grad[:, own:]], axis=1)
        sums = [lax.psum(vec, ("dp", "mp")), lax.psum(fin_part, ("dp", "mp")), lax.psum(fout_part, "dp")]
        inputs = [grad, *over_mp, *sums, *tail]
        results = pl.pallas_call(
            functools.partial(update_kernel, taps),
            name="clip_and_update",
            out_shape=tuple(outs),
            in_specs=[IN_VMEM] * len(inputs),
            out_specs=(IN_VMEM,) * len(outs),
            scratch_shapes=prepare_scratch(size, width) + [own_gain] + update_scratch(dp, mp, width),
            compiler_params=params,
        )(*inputs)
        return (input_grad, *results)
    flows = []
    for _ in range(FLOWS):
        flows += flow_scratch(mp, (size, 2 * own // FLOWS))
    vec = struct((16, width), F32)
    after = [fin_part, fout_part, *tail]

    def kernel(*refs):
        start = 1 + len(first)
        end = start + len(late)
        end_kernel(docs, taps, *refs[:start], *choose(refs[start:end], late), *refs[end:])

    return pl.pallas_call(
        kernel,
        name="sum_clip_update",
        out_shape=(struct((count, width), BF), *outs),
        in_specs=[IN_SMEM] + [IN_VMEM] * len(first) + [IN_HBM] * len(late) + [IN_VMEM] * 3 + [IN_HBM] + [IN_VMEM] * len(after),
        out_specs=(IN_VMEM,) * (1 + len(outs)),
        scratch_shapes=[
            *post_scratch(late, taps, count, width),
            *prepare_scratch(size, width),
            own_gain,
            *[pltpu.VMEM((size, width), F32)] * 3,
            pltpu.VMEM((size, 2 * own), F32),
            *[pltpu.VMEM(v.shape, F32) for v in (vec, vec, fin_part, fout_part)],
            pltpu.VMEM((mp, 2, 2, 2, size, 2 * own), BF),
            *update_scratch(dp, mp, width),
            *[pltpu.VMEM((mp - 1, size, width), BF)] * 2,
            *[pltpu.VMEM((size, width), BF)] * 2,
            dma(2, mp - 1),
            dma(2, mp - 1),
            pltpu.VMEM((size, 2 * own), F32),
            pltpu.VMEM((mp, size, width), BF),
            *[pltpu.VMEM((mp // 2, size, width), BF)] * 2,
            dma(2),
            dma(2),
            *flows,
            *flow_scratch(mp, (size, 2 * own)),
            *small_scratch((fin_part, fout_part), mp),
            *small_scratch((vec,), mp),
        ],
        compiler_params=params,
    )(lengths, *first, *[v for v, _ in late], *partials, part_c, *after)


class Spread:
    def __init__(self, own, whole, lanes, refs, direct):
        self.whole, self.lanes, self.direct = whole, lanes, direct
        self.source = own.at[:, lanes]
        self.own_sem, self.z_send, self.z_recv, self.p_send, self.p_recv = refs
        self.d, self.m, self.mp = lax.axis_index("dp"), lax.axis_index("mp"), lax.axis_size("mp")
        d = self.d
        self.dx, self.dy, self.dc = turned(d, 2), turned(d, 4), turned(d, 1)
        half = self.mp // 2
        self.low, self.high, self.all = pl.ds(0, half), pl.ds(half, self.mp - half), pl.ds(0, self.mp)

    def start(self):
        target = self.whole.at[self.m, self.d, :, self.lanes]
        self.copy = pltpu.make_async_copy(self.source, target, self.own_sem.at[0])
        self.copy.start()
        self.z = []
        if self.direct:
            for step, e in enumerate(ring(self.m, self.mp)):
                sems = self.z_send.at[step], self.z_recv.at[step]
                self.z.append(send(self.source, target, *sems, (self.d, e)))
        else:
            self.blocks, self.bit = [self.m], self.mp // 2
            self.send_blocks()

    def send_blocks(self):
        self.stepped = []
        for block in self.blocks:
            slot = len(self.z)
            target = self.whole.at[block, self.d, :, self.lanes]
            source = self.source if slot == 0 else target
            peer = (self.d, turned(self.m, self.bit))
            copy = send(source, target, self.z_send.at[slot], self.z_recv.at[slot], peer)
            self.stepped.append(copy)
            self.z.append(copy)

    def z_step(self):
        if self.bit == self.mp // 2:
            self.copy.wait()
        for copy in self.stepped:
            copy.wait_recv()
        self.blocks = self.blocks + [turned(block, self.bit) for block in self.blocks]
        self.bit //= 2
        self.send_blocks()

    def push(self, slot, rows, owner, peer):
        block = self.whole.at[rows, owner, :, self.lanes]
        return send(block, block, self.p_send.at[slot], self.p_recv.at[slot], (peer, self.m))

    def stage_one(self):
        if self.direct:
            self.copy.wait()
        for copy in self.z if self.direct else self.stepped:
            copy.wait_recv()
        d, dx, dy = self.d, self.dx, self.dy
        self.first = [self.push(0, self.low, d, dx), self.push(1, self.high, d, dy)]
        self.last = [self.push(2, self.all, d, self.dc)]

    def stage_two(self):
        for copy in self.first:
            copy.wait_recv()
        d, dx, dy = self.d, self.dx, self.dy
        self.second = [
            self.push(3, self.low, d, dy),
            self.push(4, self.high, d, dx),
            self.push(5, self.low, dx, dy),
            self.push(6, self.high, dy, dx),
        ]

    def stage_three(self):
        for copy in self.second:
            copy.wait_recv()
        for slot, owner in enumerate((self.dx, self.dy, turned(self.dx, 4))):
            self.last.append(self.push(7 + slot, self.all, owner, self.dc))

    def arrive(self):
        for copy in self.last:
            copy.wait_recv()

    def drain(self):
        for copy in self.z + self.first + self.second + self.last:
            copy.wait_send()


SPREAD_REFS = 5


def spread_scratch(mp):
    return [dma(1), dma(mp - 1), dma(mp - 1), dma(10), dma(10)]


def mark_same(same, len_ref, doc_count, first):
    tail = same.shape[1]
    position = lax.broadcasted_iota(jnp.int32, (tail + EDGE, 128), 0) + first
    doc = jnp.zeros(position.shape, jnp.int32)
    end = jnp.int32(0)
    for slot in range(doc_count):
        end = end + len_ref[0, slot]
        doc = doc + (position >= end).astype(jnp.int32)
    doc = jnp.where(position < 0, -1, doc)
    for k in range(1, same.shape[0] + 1):
        same[k - 1] = jnp.where(doc[EDGE:] == doc[EDGE - k : EDGE - k + tail], 1.0, 0.0)


def near_product(left, right, dot=mm):
    l_top, l_rest = split(left)
    r_top, r_rest = split(right)
    return dot(l_top, r_top) + dot(l_top, r_rest) + dot(l_rest, r_top)


def mixer_forward_kernel(
    doc_count, taps, len_ref, tok, in_w, out_w, up_w, down_w, gains_own, channel_own, table, step_col, f_in, f_out,
    t0, t1, t2, t3,
    w_parts, y_back, gain_rows, chan_rows, spectrum_out, hidden_out, phase_out, decay_out,
    z_out, s0_out, s1_out, s2_out, w_out_own, a_out, n1_out, inv1_out, w_in_out, w_out_out, whole_up, whole_down,
    spectrum, hidden, phase, decay, chunk_first, chunk_up, chunk_down, gains, channel, turn, whole_first, gains_all, channel_all, edges_all, filters, w_send, y_parts, full, raw, top, rest, slots,
    ext, n1, inv1, a, z, s0, s1, s2, w_own, w_in, w_out, same,
    s_send, s_recv, save_sem, b_send, b_recv, c_send, c_recv, *spread_refs,
):
    tables = (t0, t1, t2, t3)
    d, m = lax.axis_index("dp"), lax.axis_index("mp")
    dp, mp = lax.axis_size("dp"), lax.axis_size("mp")
    count, width = tok.shape
    rows = chunk_first.shape[0]
    own = width // mp
    block = count // 2
    blocks = raw.shape[0]

    place = (2, 0, 1)
    for j in range(3):
        chunk_first[:, pl.ds(place[j] * own, own)] = in_w[j].astype(BF)
    chunk_first[:, pl.ds(3 * own, own)] = out_w[...].astype(BF)
    chunk_up[...] = up_w[...].astype(BF)
    chunk_down[...] = down_w[...].astype(BF)
    turn[...] = jnp.zeros(turn.shape, F32)
    turn[pl.ds(0, 2), pl.ds(0, rows)] = gains_own[...]
    gains[...] = turn[...].astype(BF)
    channel[...] = jnp.zeros(channel.shape, F32)
    channel[pl.ds(0, channel_own.shape[0]), :] = channel_own[...]
    greet_all()

    small = []
    for step, e in enumerate(ring(d, dp)):
        small.append(send(gains, gains_all.at[d], s_send.at[step], s_recv.at[step], (e, m)))
    for step, e in enumerate(ring(m, mp)):
        at = dp + step
        small.append(send(channel, channel_all.at[m], s_send.at[at], s_recv.at[at], (d, e)))
    at = dp + mp
    for index, first, peer in ((0, count - EDGE, lax.rem(m + 1, mp)), (1, 0, lax.rem(m + mp - 1, mp))):
        sems = s_send.at[at + index], s_recv.at[at + index]
        small.append(send(tok.at[pl.ds(first, EDGE)], edges_all.at[index], *sems, (d, peer)))
    gains_all[d] = gains[...]
    channel_all[m] = channel[...]

    half = width // 2
    plan = [
        (chunk_first, whole_first, pl.ds(0, half)),
        (chunk_first, whole_first, pl.ds(half, width - half)),
        (chunk_up, whole_up, pl.ds(0, chunk_up.shape[1])),
        (chunk_down, whole_down, pl.ds(0, chunk_down.shape[1])),
    ]
    flows = [
        Spread(*p, spread_refs[i * SPREAD_REFS : (i + 1) * SPREAD_REFS], direct=i == 0) for i, p in enumerate(plan)
    ]
    left, right, up, down = flows
    left.start()
    right.start()

    phase[...] = near_product(table[...], f_in[...])
    hidden[...] = jnp.sin(phase[...])
    lane = (m * own + lax.broadcasted_iota(jnp.int32, (1, own), 1)).astype(F32)
    rate = FAST_DECAY + (SLOW_DECAY - FAST_DECAY) * lane / (width - 1)
    decay[...] = jnp.exp(-step_col[...] * rate)
    near = own // HALVES
    values = near_product(hidden[...], f_out[...]) * decay[...]
    for side in range(HALVES):
        filters[side, :, 0:near] = values[:, side * near : (side + 1) * near]

    mark_same(same, len_ref, doc_count, m * count - EDGE)

    left.stage_one()
    right.z_step()
    up.start()
    down.start()
    for copy in small:
        copy.wait()
    for e in range(dp):
        gain_rows[0:2, pl.ds(e * rows, rows)] = gains_all[e, 0:2, 0:rows].astype(F32)
    for e in range(mp):
        chan_rows[:, pl.ds(e * own, own)] = channel_all[e]
    ext[pl.ds(0, EDGE), :] = edges_all[0].astype(F32)
    ext[pl.ds(EDGE, count), :] = tok[...].astype(F32)
    ext[pl.ds(EDGE + count, EDGE), :] = edges_all[1].astype(F32)

    def norm_body(i, carry):
        at = pl.ds(pl.multiple_of(i * 32, 32), 32)
        normed, inverse_std = norm_parts(ext[at, :])
        n1[at, :] = normed
        inv1[at, :] = jnp.broadcast_to(inverse_std, (32, 128))
        a[at, :] = (normed * gain_rows[0:1, :]).astype(BF)
        return carry

    def stream_weights(j):
        for e in range(mp):
            part = whole_first[e, :, :, pl.ds(place[j] * own, own)].reshape(dp * rows, own)
            w_in[:, pl.ds(j * width + e * own, own)] = part

    def project(j):
        cols = pl.ds(j * width, width)
        z[:, cols] = mm(a[...], w_in[:, cols])

    def short(first, size, j):
        part = z[pl.ds(first + 8, size + 8), pl.ds(j * width, width)]
        total = chan_rows[j : j + 1, :] * part[8 : size + 8]
        for k in range(1, taps):
            keep = same[k - 1, pl.ds(first, size), 0:1] > 0.0
            moved = jnp.where(keep, part[8 - k : size + 8 - k], 0.0)
            total = total + chan_rows[3 * k + j : 3 * k + j + 1, :] * moved
        return total

    def value_body(i, carry):
        first = pl.multiple_of(i * 48, 16)
        at = pl.ds(first, 48)
        one, two = short(first, 48, 1), short(first, 48, 2)
        s1[at, :], s2[at, :] = one, two
        w_own[at, :] = two * one
        return carry

    def gate_body(i, carry):
        first = pl.multiple_of(i * 48, 16)
        s0[pl.ds(first, 48), :] = short(first, 48, 0)
        return carry

    lax.fori_loop(0, ext.shape[0] // 32, norm_body, 0)
    left.stage_two()
    right.stage_one()
    up.z_step()
    for side in range(HALVES):
        filter_spectrum(filters.at[side], spectrum.at[side], raw, tables, block)
    left.stage_three()
    right.stage_two()
    down.z_step()
    left.arrive()
    for j in (1, 2):
        stream_weights(j)
        project(j)
    up.stage_one()
    lax.fori_loop(0, s0.shape[0] // 48, value_body, 0)
    piece = count // FOLD
    for side in range(HALVES):
        for part in range(mp):
            for i in range(FOLD):
                values = w_own[pl.ds(i * piece, piece), pl.ds(part * own + side * near, near)]
                w_send[side, part, :, pl.ds(i * near, near)] = values.astype(BF)
    going, back = [], []
    for side in range(HALVES):
        going.append(Blocks([(w_send.at[side], w_parts.at[side])], b_send.at[side], b_recv.at[side]))
        back.append(Blocks([(y_parts.at[side], y_back.at[side])], c_send.at[side], c_recv.at[side]))
        going[side].start()
    right.stage_three()
    down.stage_one()
    right.arrive()
    stream_weights(0)
    project(0)
    lax.fori_loop(0, s0.shape[0] // 48, gate_body, 0)
    saves = []

    def save(source, target):
        copy = pltpu.make_async_copy(source, target, save_sem.at[len(saves)])
        copy.start()
        saves.append(copy)

    own_rows = pl.ds(0, count)
    for source, target in (
        *[(z.at[:, pl.ds(j * width, width)], z_out.at[j]) for j in range(3)], (s0.at[own_rows], s0_out), (s1, s1_out), (s2, s2_out), (w_own.at[own_rows], w_out_own),
        (a, a_out), (n1, n1_out), (inv1, inv1_out), (spectrum, spectrum_out), (hidden, hidden_out), (phase, phase_out),
        (decay, decay_out),
        *[(w_in.at[:, pl.ds(j * width, width)], w_in_out.at[j]) for j in range(3)],
    ):
        save(source, target)
    for e in range(mp):
        part = whole_first[e, :, :, pl.ds(3 * own, own)].reshape(dp * rows, own)
        w_out[:, pl.ds(e * own, own)] = part
    save(w_out, w_out_out)
    def between(slot):
        if slot == 2:
            down.stage_two()

    up.stage_two()
    for side in range(HALVES):
        going[side].arrive()
        conv_forward_steps(
            doc_count, len_ref, w_parts.at[side], tables, y_parts.at[side], spectrum.at[side], full, raw, top, rest,
            slots, between if side == 0 else lambda slot: None,
        )
        back[side].start()
    up.stage_three()
    down.stage_three()
    up.arrive()
    down.arrive()
    for side in range(HALVES):
        back[side].arrive()
    for copy in saves:
        copy.wait()
    for copies in going + back:
        copies.drain()
    for flow in flows:
        flow.drain()


def mixer_forward(lengths, tokens, weights, gains, channel, taps, table, step_col, f_in, f_out, tables):
    mp, dp = lax.axis_size("mp"), lax.axis_size("dp")
    count, width = tokens.shape
    own, block, docs = width // mp, count // 2, lengths.shape[1]
    lags = table.shape[0]
    blocks = lags // block
    near = own // HALVES
    rows = weights[1].shape[0]
    shards = [(rows, 4 * own), weights[2].shape, weights[3].shape]
    whole = [(mp, dp) + s for s in shards]
    longer, later = (count + 2 * EDGE, width), (count + EDGE, width)
    parts = (HALVES, mp, count // FOLD, FOLD * near)
    full, raw, low, slots = conv_scratch(parts[1:], blocks, block, docs)
    net = [
        ((HALVES, blocks, 2 * block, lanes_for(near)), F32), ((lags, f_in.shape[1]), F32), ((lags, f_in.shape[1]), F32),
        ((lags, own), F32),
    ]
    vmem_outs = [(parts, BF), (parts, BF), ((8, width), F32), ((16, width), F32)]
    hbm_outs = net + [
        ((3,) + longer, F32), ((count, width), F32), (later, F32), (later, F32), ((count, width), F32),
        (longer, BF), (longer, F32), ((longer[0], 128), F32), ((3, width, width), BF), ((width, width), BF),
        (whole[1], BF), (whole[2], BF),
    ]
    inputs = (lengths, tokens, *weights, gains, channel, table, step_col, f_in, f_out, *tables)
    results = pl.pallas_call(
        functools.partial(mixer_forward_kernel, docs, taps),
        name="mixer_forward",
        out_shape=tuple(struct(*o) for o in vmem_outs + hbm_outs),
        in_specs=[IN_SMEM] + [IN_VMEM] * (len(inputs) - 1),
        out_specs=(IN_VMEM,) * len(vmem_outs) + (IN_HBM,) * len(hbm_outs),
        scratch_shapes=[
            *[pltpu.VMEM(*v) for v in net], *[pltpu.VMEM(s, BF) for s in shards], pltpu.VMEM((16, 128), BF), pltpu.VMEM((16, own), F32),
            pltpu.VMEM((16, 128), F32),
            pltpu.VMEM(whole[0], BF), pltpu.VMEM((dp, 16, 128), BF), pltpu.VMEM((mp, 16, own), F32),
            pltpu.VMEM((2, EDGE, width), BF),
            pltpu.VMEM((HALVES, lags, lanes_for(near)), F32), pltpu.VMEM(parts, BF), pltpu.VMEM(parts, BF),
            full, raw, low, low, slots,
            pltpu.VMEM(longer, F32), pltpu.VMEM(longer, F32), pltpu.VMEM((longer[0], 128), F32), pltpu.VMEM(longer, BF),
            pltpu.VMEM((longer[0], 3 * width), F32), pltpu.VMEM(later, F32), pltpu.VMEM(later, F32),
            pltpu.VMEM(later, F32), pltpu.VMEM(later, F32), pltpu.VMEM((width, 3 * width), BF),
            pltpu.VMEM((width, width), BF), pltpu.VMEM((taps - 1, later[0], 128), F32),
            dma(dp + mp + 2), dma(dp + mp + 2), dma(24), *([dma(HALVES, 1, mp - 1)] * 4),
            *(spread_scratch(mp) * 4),
        ],
        compiler_params=pltpu.CompilerParams(collective_id=0, has_side_effects=True, vmem_limit_bytes=ROOM),
    )(*inputs)
    return (*results[:2], *results[4:8], *results[2:4], *results[8:])


def dot_nt(left, right):
    return lax.dot_general(left, right, (((1,), (1,)), ((), ())), preferred_element_type=F32)


def dot_tn(left, right):
    return lax.dot_general(left, right, (((0,), (0,)), ((), ())), preferred_element_type=F32)


def pieces(parts, count, width):
    near, rows = width // parts // HALVES, count // FOLD
    for side in range(HALVES):
        for part in range(parts):
            for i in range(FOLD):
                cols = pl.ds((part * HALVES + side) * near, near)
                yield pl.ds(i * rows, rows), cols, side, part, pl.ds(i * near, near)


def gelu_parts(x):
    scale, cubic = math.sqrt(2.0 / math.pi), 0.044715
    square = x * x
    t = jnp.tanh(x * (scale + (scale * cubic) * square))
    half = 0.5 + 0.5 * t
    value = x * half
    return value, half + value * (1.0 - t) * (scale + (3.0 * scale * cubic) * square)


COLS = 768


def feed_kernel(
    skip_row, y_ref, w_ref, s0_ref, tok, cot, w_out, gains, channel, up, down,
    act_out, up_part, down_part, out_part, g_parts, gy_out, gs0_out, gx2_out, sums, edge_out,
    y, o, x2, n2, inv2, b, b_t, cot_t, mix, acc_out, acc_b,
):
    step, steps = pl.program_id(0), pl.num_programs(0)
    parts = y_ref.shape[1]
    count, width = tok.shape
    tile = 128
    gain, skip = gains.at[1:2], channel.at[skip_row : skip_row + 1]

    @pl.when(step == 0)
    def _():
        for rows, cols, side, part, lanes in pieces(parts, count, width):
            y[rows, cols] = y_ref[side, part, :, lanes].astype(F32)

        def body(index, carry):
            rows = pl.ds(pl.multiple_of(index * tile, tile), tile)
            values = y[rows, :] + skip[...] * w_ref[rows, :]
            y[rows, :] = values
            mixed = (values * s0_ref[rows, :]).astype(BF)
            o[rows, :] = mixed
            residual = tok[rows, :].astype(F32) + dot_nt(mixed, w_out[...])
            x2[rows, :] = residual
            normed, inverse_std = norm_parts(residual)
            n2[rows, :] = normed
            inv2[rows, :] = jnp.broadcast_to(inverse_std, (tile, 128))
            b[rows, :] = (normed * gain[...]).astype(BF)
            return carry

        lax.fori_loop(0, count // tile, body, 0)
        b_t[...] = b[...].T
        cot_t[...] = cot[...].T
        acc_out[...] = jnp.zeros(acc_out.shape, F32)
        acc_b[...] = jnp.zeros(acc_b.shape, F32)

    up_w, down_w = up[0], down[0]
    value, slope = gelu_parts(mm(b[...], up_w))
    act = value.astype(BF)
    g_hpre = (mm(cot[...], down_w) * slope).astype(BF)
    up_part[0] = mm(b_t[...], g_hpre).astype(BF)
    down_part[0] = mm(cot_t[...], act).astype(BF)
    acc_out[...] += dot_nt(act, down_w)
    acc_b[...] += dot_nt(g_hpre, up_w)

    @pl.when(step == steps - 1)
    def _():
        sums[...] = jnp.zeros(sums.shape, F32)

        def body(index, carry):
            rows = pl.ds(pl.multiple_of(index * tile, tile), tile)
            act_out[rows, :] = (x2[rows, :] + acc_out[rows, :]).astype(BF)
            g_b, normed = acc_b[rows, :], n2[rows, :]
            sums[0:1, :] += jnp.sum(g_b * normed, axis=0, keepdims=True)
            g_x2 = cot[rows, :].astype(F32) + norm_back(g_b, gain[...], normed, inv2[rows, 0:1])
            gx2_out[rows, :] = g_x2
            low = g_x2.astype(BF)
            mix[rows, :] = low
            g_o = mm(low, w_out[...])
            g_y = g_o * s0_ref[rows, :]
            gy_out[rows, :] = g_y
            gs0_out[rows, :] = g_o * y[rows, :]
            sums[1:2, :] += jnp.sum(g_y * w_ref[rows, :], axis=0, keepdims=True)
            return carry

        lax.fori_loop(0, count // tile, body, 0)
        for rows, cols, side, part, lanes in pieces(parts, count, width):
            g_parts[side, part, :, lanes] = gy_out[rows, cols].astype(BF)
        edge_out[...] = gs0_out[pl.ds(0, EDGE), :].astype(BF)
        grad = dot_tn(mix[...], o[...])
        own = width // parts
        for part in range(parts):
            out_part[part] = grad[:, part * own : (part + 1) * own].astype(BF)


def feed(y_parts, w_own, s0, tokens, cotangent, w_out, gains, channel, skip_row, whole_up, whole_down):
    mp, width, hidden = whole_up.shape
    count = tokens.shape[0]
    own, cols = width // mp, COLS
    each = hidden // cols
    once = pl.Buffered(1)

    def fixed(shape):
        return pl.BlockSpec(shape, lambda i: (0,) * len(shape), pipeline_mode=once)

    def moving():
        return pl.BlockSpec((1, width, cols), lambda i: (i // each, 0, i % each))

    full, half = (count, width), y_parts.shape
    outs = [
        (full, BF), (whole_up.shape, BF), (whole_up.shape, BF), ((mp, width, own), BF), (half, BF),
        (full, F32), (full, F32), (full, F32), ((8, width), F32), ((EDGE, width), BF),
    ]
    out_specs = [moving() if i in (1, 2) else fixed(s) for i, (s, _) in enumerate(outs)]
    inputs = (y_parts, w_own, s0, tokens, cotangent, w_out, gains, channel)
    return pl.pallas_call(
        functools.partial(feed_kernel, skip_row),
        name="feed_forward",
        grid=(mp * each,),
        out_shape=tuple(struct(s, t) for s, t in outs),
        in_specs=[fixed(v.shape) for v in inputs] + [moving(), moving()],
        out_specs=tuple(out_specs),
        scratch_shapes=[
            pltpu.VMEM(full, F32), pltpu.VMEM(full, BF), pltpu.VMEM(full, F32), pltpu.VMEM(full, F32),
            pltpu.VMEM((count, 128), F32), pltpu.VMEM(full, BF), pltpu.VMEM((width, count), BF),
            pltpu.VMEM((width, count), BF), pltpu.VMEM(full, BF), pltpu.VMEM(full, F32), pltpu.VMEM(full, F32),
        ],
        compiler_params=pltpu.CompilerParams(vmem_limit_bytes=ROOM),
    )(*inputs, whole_up, whole_down)


class Late:
    def __init__(self, sources, targets, sem):
        self.copies = []
        for i, (source, target) in enumerate(zip(sources, targets)):
            copy = pltpu.make_async_copy(source, target, sem.at[i])
            copy.start()
            self.copies.append(copy)

    def need(self, *indices):
        for i in indices:
            self.copies[i].wait()


def short_backward(j, gs, z, channel, same, offsets, count, sums):
    tap_rows = [channel[3 * k + j : 3 * k + j + 1, :] for k in range(offsets)]
    g_z = None
    for k in range(offsets):
        later = gs[pl.ds(k, count), :]
        before = z[pl.ds(EDGE - k, count), :]
        if k:
            later = jnp.where(same[k][k : count + k], later, 0.0)
            before = jnp.where(same[k][:count], before, 0.0)
        g_z = tap_rows[k] * later if g_z is None else g_z + tap_rows[k] * later
        sums[pl.ds(3 * k + j, 1), :] = jnp.sum(gs[pl.ds(0, count), :] * before, axis=0, keepdims=True)
    return g_z


def post_steps(doc_count, offsets, len_ref, gw_ref, gw_edge, channel, gains, sums, held, late, work, stream_done):
    gy_ref, s2_ref, z1, a_ref, w1, s1_ref, z2, w2, ga0, n1_ref, inv1_ref, gx2_ref = held
    gw, gs, gz, marks = work
    parts = gw_ref.shape[1]
    count, width = gy_ref.shape
    near = width // parts // HALVES
    skip = channel[3 * offsets : 3 * offsets + 1, :]
    for rows, cols, side, part, lanes in pieces(parts, count, width):
        gw[rows, cols] = gw_ref[side, part, :, lanes].astype(F32)
    for side in range(HALVES):
        for part in range(parts):
            at = pl.ds((part * HALVES + side) * near, near)
            gw[pl.ds(count, EDGE), at] = gw_edge[side, part, :, 0:near].astype(F32)
    mark_same(marks, len_ref, doc_count, lax.axis_index("mp") * count - EDGE)
    same = [None] + [marks[k - 1, :, 0:1] > 0.0 for k in range(1, offsets)]
    late.need(0)
    gw[pl.ds(0, count), :] += skip * gy_ref[...]
    total = None
    for j, other, z, w, order in ((1, s2_ref, z1, w1, (1, 2, 3, 4)), (2, s1_ref, z2, w2, (5, 6, 7))):
        late.need(*order)
        gs[...] = gw[...] * other[...]
        gz[...] = short_backward(j, gs, z, channel, same, offsets, count, sums).astype(BF)
        stream_done(j, dot_tn(a_ref[pl.ds(EDGE, count), :], gz[...]))
        term = dot_nt(gz[...], w[...])
        total = term if total is None else total + term
    late.need(8, 9, 10, 11)
    total = total + ga0[...]
    sums[pl.ds(3 * offsets + 1, 1), :] = jnp.sum(total * n1_ref[pl.ds(EDGE, count), :], axis=0, keepdims=True)
    return total


def post_end(total, gains, held, input_grad):
    n1_ref, inv1_ref, gx2_ref = held[9:]
    count = gx2_ref.shape[0]
    normed, inverse_std = n1_ref[pl.ds(EDGE, count), :], inv1_ref[pl.ds(EDGE, count), 0:1]
    input_grad[...] = (gx2_ref[...] + norm_back(total, gains[0:1, :], normed, inverse_std)).astype(BF)


def post_kernel(doc_count, offsets, len_ref, gw_ref, gw_edge, channel, gains, sums_in, *refs):
    late_refs, refs = refs[:12], refs[12:]
    last_part, input_grad, sums, refs = refs[0], refs[1], refs[2], refs[3:]
    held, late_sem, work = refs[:12], refs[12], refs[13:]
    late = Late(late_refs, held, late_sem)
    parts, own = gw_ref.shape[1], last_part.shape[2] // 2
    sums[...] = sums_in[...]

    def stream_done(j, grad):
        for part in range(parts):
            last_part[part, :, pl.ds((j - 1) * own, own)] = grad[:, part * own : (part + 1) * own].astype(BF)

    total = post_steps(
        doc_count, offsets, len_ref, gw_ref, gw_edge, channel, gains, sums, held, late, work, stream_done
    )
    post_end(total, gains, held, input_grad)


def post_late(g_y, s1, s2, z, a, w_in, ga0, n1, inv1, g_x2):
    return [
        (g_y, None), (s2, None), (z, 1), (a, None), (w_in, 1), (s1, None), (z, 2), (w_in, 2), (ga0, None), (n1, None),
        (inv1, None), (g_x2, None),
    ]


def post_scratch(late, offsets, count, width):
    return [
        *[pltpu.VMEM(v.shape if i is None else v.shape[1:], v.dtype) for v, i in late],
        dma(len(late)),
        pltpu.VMEM((count + EDGE, width), F32),
        pltpu.VMEM((count + EDGE, width), F32),
        pltpu.VMEM((count, width), BF),
        pltpu.VMEM((offsets - 1, count + EDGE, 128), F32),
    ]


def choose(refs, late):
    return [r if i is None else r.at[i] for r, (_, i) in zip(refs, late)]


def post(lengths, offsets, gw_parts, gw_edge, channel, gains, sums_in, late):
    mp = gw_parts.shape[1]
    count, width = late[0][0].shape
    first = (gw_parts, gw_edge, channel, gains, sums_in)

    def kernel(*refs):
        start = 1 + len(first)
        end = start + len(late)
        post_kernel(lengths.shape[1], offsets, *refs[:start], *choose(refs[start:end], late), *refs[end:])

    return pl.pallas_call(
        kernel,
        name="mixer_post",
        out_shape=(struct((mp, width, 2 * width // mp), BF), struct((count, width), BF), struct((16, width), F32)),
        in_specs=[IN_SMEM] + [IN_VMEM] * len(first) + [IN_HBM] * len(late),
        out_specs=(IN_VMEM,) * 3,
        scratch_shapes=post_scratch(late, offsets, count, width),
        compiler_params=pltpu.CompilerParams(vmem_limit_bytes=ROOM),
    )(lengths, *first, *[v for v, _ in late])


def features(length, feature_count, count):
    step = np.arange(count)
    band = np.arange(1, (feature_count - 1) // 2 + 1)
    phase = ((step[:, None] * band[None, :]) % length).astype(np.float32) * np.float32(2.0 * math.pi / length)
    position = (step / length).astype(np.float32)
    table = np.concatenate([position[:, None], np.cos(phase), np.sin(phase)], axis=1)
    return table.astype(np.float32), position


def product(left, right):
    return jnp.dot(left, right, precision=FULL_PRECISION, preferred_element_type=F32)


def norm_parts(values):
    centred = values - jnp.mean(values, axis=-1, keepdims=True)
    inverse_std = lax.rsqrt(jnp.mean(centred * centred, axis=-1, keepdims=True) + EPS_NORM)
    return centred * inverse_std, inverse_std


def norm_back(grad, gain, normed, inverse_std):
    scaled = grad * gain
    mean = jnp.mean(scaled, axis=-1, keepdims=True)
    along = jnp.mean(scaled * normed, axis=-1, keepdims=True)
    return (scaled - mean - normed * along) * inverse_std


def to_parts(values, mp):
    count, width = values.shape
    near = width // mp // HALVES
    cut = values.reshape(FOLD, count // FOLD, mp, HALVES, near).transpose(3, 2, 1, 0, 4)
    return cut.reshape(HALVES, mp, count // FOLD, FOLD * near)


def forward_fallback(lengths, tokens, weights, gain_own, channel_own, taps, table, step_col, f_in, f_out, tables):
    mp, m = lax.axis_size("mp"), lax.axis_index("mp")
    count, width = tokens.shape
    own, shard = width // mp, weights[1].shape[0]
    first_shard = jnp.concatenate([*weights[0], weights[1]], axis=1)
    chunks = [v.astype(BF) for v in (first_shard, weights[2], weights[3])]
    gains = jnp.pad(gain_own.astype(BF), ((0, 14), (0, 128 - shard)))
    channel = jnp.pad(channel_own, ((0, 16 - channel_own.shape[0]), (0, 0)))
    edges = jnp.stack([tokens[count - EDGE :], tokens[:EDGE]])
    first, up, down, gains_all, channel_all, edges_all = gather_fallback(chunks, gains, channel, edges)
    first = first.reshape(mp, width, width)
    w_in = first[:, :, : 3 * own].reshape(mp, width, 3, own).transpose(1, 2, 0, 3).reshape(width, 3 * width)
    w_out = first[:, :, 3 * own :].transpose(1, 0, 2).reshape(width, width)
    gain_rows = gains_all[:, 0:8, :shard].transpose(1, 0, 2).reshape(8, width).astype(F32)
    chan_rows = channel_all.transpose(1, 0, 2).reshape(-1, width)
    position = m * count - EDGE + jnp.arange(count + 2 * EDGE, dtype=jnp.int32)
    doc = jnp.sum((position[:, None] >= jnp.cumsum(lengths[0])[None, :]).astype(jnp.int32), axis=1)
    doc = jnp.where(position < 0, -1, doc)
    n1, inv1 = norm_parts(jnp.concatenate([edges_all[0], tokens, edges_all[1]]).astype(F32))
    a = (n1 * gain_rows[0]).astype(BF)
    z = jnp.dot(a, w_in, preferred_element_type=F32)
    s = []
    for j in range(3):
        stream, total = z[:, j * width : (j + 1) * width], None
        for k in range(taps):
            part = stream[EDGE - k : stream.shape[0] - k]
            if k:
                part = jnp.where((doc[EDGE:] == doc[EDGE - k : doc.shape[0] - k])[:, None], part, 0.0)
            term = chan_rows[3 * k + j] * part
            total = term if total is None else total + term
        s.append(total)
    w_own = s[2][:count] * s[1][:count]
    phase = product(table, f_in)
    hidden = jnp.sin(phase)
    lane = (m * own + jnp.arange(own, dtype=jnp.int32)).astype(F32)
    decay = jnp.exp(-step_col * (FAST_DECAY + (SLOW_DECAY - FAST_DECAY) * lane / (width - 1)))
    w_parts = exchange([*to_parts(w_own.astype(BF), mp)], None, 3)
    filters = jnp.split(product(hidden, f_out) * decay, HALVES, axis=1)
    halves = [conv_forward(w_parts[i], lengths, filters[i], tables) for i in range(HALVES)]
    y_back = jnp.stack(exchange([v[0] for v in halves], None, 4))
    w_parts, spectrum = jnp.stack(w_parts), jnp.stack([v[1] for v in halves])
    return (
        w_parts, y_back, spectrum, hidden, phase, decay, gain_rows, chan_rows,
        z.reshape(-1, 3, width).transpose(1, 0, 2), s[0][:count], s[1], s[2], w_own, a, n1,
        jnp.broadcast_to(inv1, (inv1.shape[0], 128)), w_in.reshape(width, 3, width).transpose(1, 0, 2), w_out, up, down,
    )


def per_device(
    tokens, cotangent, doc_lengths, in_weight, out_weight, up_weight, down_weight, gains, channel_weight,
    filter_in, filter_out, in_rows, in_cols, out_rows, out_cols, up_rows, up_cols, down_rows, down_cols,
    gain_moment, channel_moment, filter_in_moment, filter_out_moment,
):
    dp, mp = lax.axis_size("dp"), lax.axis_size("mp")
    count, width = tokens.shape
    length = count * mp
    own = channel_weight.shape[1]
    rows = in_weight.shape[0]
    hidden = up_weight.shape[1]
    taps = (channel_weight.shape[0] - 1) // 3
    most = length // 2

    in_weight, gains, gain_moment = in_weight.transpose(1, 0, 2), gains.T, gain_moment.T

    table, step = features(length, filter_in.shape[0], most)
    tables = tuple(jnp.asarray(t) for t in transform_tables(count // 2))
    run = mixer_forward if dp == 8 else forward_fallback
    (
        w_parts, y_back, spectrum, hidden_filter, phase, decay, gain_rows, chan_rows, z, s0, s1, s2, w_own,
        a, n1, inv1, w_in, w_out, whole_up, whole_down,
    ) = run(
        doc_lengths, tokens, (in_weight, out_weight, up_weight, down_weight), gains, channel_weight, taps,
        table, step[:, None], filter_in, filter_out, tables,
    )
    whole_up = whole_up.reshape(mp, width, hidden)
    whole_down = whole_down.reshape(mp, width, hidden)

    activations, up_part, down_part, out_part, gy_parts, g_y, g_s0, g_x2, feed_sums, g_s0_own = feed(
        y_back, w_own, s0, tokens, cotangent, w_out, gain_rows, chan_rows, 3 * taps, whole_up, whole_down
    )

    up_part, down_part = [p.reshape(mp, dp, rows, hidden) for p in (up_part, down_part)]
    gw_back, gw_edge, sums, g_a0, fin_part, fout_part, *partials, first_part = mixer_backward(
        doc_lengths, taps, gy_parts, g_s0_own, channel_weight, feed_sums, up_part, down_part, g_s0, z, a, w_in,
        chan_rows, out_part, w_parts, tables, spectrum, decay, hidden_filter, filter_out, phase, table,
    )

    results = finish(
        doc_lengths, taps, (gw_back, gw_edge, chan_rows, gain_rows, sums),
        post_late(g_y, s1, s2, z, a, w_in, g_a0, n1, inv1, g_x2), partials, first_part, fin_part, fout_part,
        (
            in_weight, out_weight, in_rows, out_rows, up_rows, down_rows,
            in_cols, out_cols, up_cols, down_cols, gains, gain_moment,
        ),
        up_weight, down_weight,
        (channel_weight, channel_moment, filter_in, filter_in_moment, filter_out, filter_out_moment),
    )
    (
        input_grad, norm, in_g, out_g, up_g, down_g, gain_g, in_n, out_n, up_n, down_n, gain_n, gain_m,
        in_r, out_r, up_r, down_r, in_c, out_c, up_c, down_c,
        chan_g, chan_n, chan_m, fin_g, fin_n, fin_m, fout_g, fout_n, fout_m,
    ) = hand_out(results, own)
    return (
        activations, input_grad, norm.reshape(()),
        in_g.transpose(1, 0, 2), out_g, up_g, down_g, gain_g.T, chan_g, fin_g, fout_g,
        in_n.transpose(1, 0, 2), out_n, up_n, down_n, gain_n.T, chan_n, fin_n, fout_n,
        in_r, in_c, out_r, out_c, up_r, up_c, down_r, down_c, gain_m.T, chan_m, fin_m, fout_m,
    )


def solution(mesh):
    tokens, by_rows, by_cols, both = P(("dp", "mp"), None), P("dp", None), P(None, "mp"), P("dp", "mp")
    cube, vec_dp, vec_mp = P("dp", None, "mp"), P("dp"), P("mp")
    moments = (vec_dp, by_cols, vec_dp, vec_mp, vec_dp, vec_mp, vec_dp, vec_mp)
    weights = (cube, both, both, both, by_rows, by_cols, P(), by_cols)
    small = (by_rows, by_cols, P(), by_cols)
    return jax.shard_map(
        per_device,
        mesh=mesh,
        in_specs=(tokens, tokens, by_rows) + weights + moments + small,
        out_specs=(tokens, tokens, P()) + weights + weights + moments + small,
        check_vma=False,
    )
```

```python
import functools
import math

import jax
import jax.numpy as jnp
import ml_dtypes
import numpy as np
from jax import lax
from jax.experimental import pallas as pl
from jax.experimental.pallas import tpu as pltpu
from jax.sharding import PartitionSpec as P

EPS_NORM = 1e-05
MOMENT_DECAY = 0.5
CLIP_NORM = 1.0
CLIP_STEP = 0.25
STEP_RATE = 2.0
FAST_DECAY = 15.35
SLOW_DECAY = 3.07
FULL_PRECISION = lax.Precision.HIGHEST
BF = jnp.bfloat16
F32 = jnp.float32
MESH = pl.DeviceIdType.MESH
BLOCK = 256
EDGE = 16
HALVES = 2
FOLD = 4
ROOM = 62 << 20
IN_VMEM = pl.BlockSpec(memory_space=pltpu.VMEM)
IN_HBM = pl.BlockSpec(memory_space=pl.ANY)
IN_SMEM = pl.BlockSpec(memory_space=pltpu.SMEM)


def struct(shape, dtype):
    return jax.ShapeDtypeStruct(tuple(shape), dtype)


def transform_tables(block):
    freq = 2 * np.arange(block)[:, None] + 1
    angle = np.pi * (freq * np.arange(block)[None, :] % (4 * block)) / (2 * block)
    table = np.concatenate([np.cos(angle), -np.sin(angle)], axis=0).astype(np.float32)
    high = table.astype(ml_dtypes.bfloat16)
    low = (table - high.astype(np.float32)).astype(ml_dtypes.bfloat16)
    return high, low, np.ascontiguousarray(high.T), np.ascontiguousarray(low.T)


def mm(left, right):
    return lax.dot_general(left, right, (((1,), (0,)), ((), ())), preferred_element_type=F32)


def split(values):
    high = values.astype(BF)
    return high, (values - high.astype(F32)).astype(BF)


def load_rows(ref, start, count, lead=()):
    odd = lax.rem(start, 8)
    tile = ref[lead + (pl.ds(lax.div(start, 8), count // 8 + 1),)]
    width = tile.shape[-1]
    tile = pltpu.roll(tile, lax.rem(8 - odd, 8), axis=1)
    first = lax.broadcasted_iota(jnp.int32, (count // 8, 8, width), 1) < 8 - odd
    return jnp.where(first, tile[:-1], tile[1:]).reshape(count, width)


def tiles(values):
    return values.reshape(values.shape[0] // 8, 8, values.shape[1])


def unpack(target, source, channels):
    parts, rows, width = source.shape
    fold, count = width // channels, rows // 8
    for part in range(parts):
        for piece in range(fold):
            values = source[part, :, piece * channels : (piece + 1) * channels].astype(F32)
            target[pl.ds((part * fold + piece) * count, count), :, 0:channels] = tiles(values)


def pack_block(target, index, values, channels):
    rows = target.shape[1]
    fold, pieces = target.shape[2] // channels, values.shape[0] // rows
    for i in range(pieces):
        part, piece = divmod(index * pieces + i, fold)
        source = values[i * rows : (i + 1) * rows, 0:channels]
        target[part, :, pl.ds(piece * channels, channels)] = source.astype(target.dtype)


def beside(values):
    return [jnp.concatenate(values[i : i + 2], axis=1) for i in range(0, len(values), 2)]


def apart(values, lanes):
    return [v[:, i : i + lanes] for v in values for i in range(0, v.shape[1], lanes)]


def pair_rows(index, block, size):
    first = pl.multiple_of(index * size, size)
    return pl.ds(first, size), pl.ds(pl.multiple_of(block + first, size), size)


def signs(size, width, scale):
    odd = lax.broadcasted_iota(jnp.int32, (size, width), 0) % 2
    return jnp.where(odd == 0, scale, -scale).astype(F32)


def filter_spectrum(filter_ref, spectrum, raw, tables, block):
    count, lanes = raw.shape[0], raw.shape[2]
    high, low = tables[0][...], tables[1][...]
    terms = [split(filter_ref[pl.ds(lag * block, block), :]) for lag in range(count)]
    tops, rests = beside([t[0] for t in terms]), beside([t[1] for t in terms])
    done = [mm(high, t) + mm(high, r) + mm(low, t) for t, r in zip(tops, rests)]
    for lag, values in enumerate(apart(done, lanes)):
        raw[lag] = values
    scale = 1.0 / block

    def body(index, carry):
        re_rows, im_rows = pair_rows(index, block, 8)
        sign = signs(8, raw.shape[2], scale)
        for lag in range(count):
            re, im = raw[lag, re_rows, :] * scale, raw[lag, im_rows, :] * scale
            if lag:
                re = re - sign * raw[lag - 1, im_rows, :]
                im = im + sign * raw[lag - 1, re_rows, :]
            spectrum[lag, re_rows, :] = re
            spectrum[lag, im_rows, :] = im
        return carry

    lax.fori_loop(0, block // 8, body, 0)


def slot_blocks(source, target, tables, start, length, block):
    high, low = tables[0][...], tables[1][...]
    blocks = []
    for index in range(target.shape[0]):
        values = load_rows(source, start + index * block, block)
        inside = lax.broadcasted_iota(jnp.int32, values.shape, 0) + index * block < length
        blocks.append(jnp.where(inside, values, 0.0).astype(BF))
    done = [mm(high, values) + mm(low, values) for values in beside(blocks)]
    for index, values in enumerate(apart(done, target.shape[2])):
        target[index] = values


def inverse(top, rest, tables):
    high, low = tables[2][...], tables[3][...]
    count, lanes = top.shape[0], top.shape[2]
    tops, rests = beside([top[i] for i in range(count)]), beside([rest[i] for i in range(count)])
    return apart([mm(high, t) + mm(high, r) + mm(low, t) for t, r in zip(tops, rests)], lanes)


def document_starts(len_ref, count):
    starts, at = [], jnp.int32(0)
    for slot in range(count):
        starts.append(at)
        at = at + len_ref[0, slot]
    return starts


def merge_slots(slots, starts, put, total, block, most):
    for index in range(total // block):
        first = index * block
        merged = None
        for slot, start in enumerate(starts):
            at = jnp.clip(first - start, -block, most) + block
            values = load_rows(slots, at, block, (slot,))
            if merged is None:
                merged = values
            else:
                inside = lax.broadcasted_iota(jnp.int32, values.shape, 0) + first >= start
                merged = jnp.where(inside, values, merged)
        put(index, merged)


def forward_products(spectrum, raw, top, rest, block):
    count = raw.shape[0]

    def body(index, carry):
        re_rows, im_rows = pair_rows(index, block, 16)
        hr = [spectrum[i, re_rows, :] for i in range(count)]
        hi = [spectrum[i, im_rows, :] for i in range(count)]
        xr = [raw[i, re_rows, :] for i in range(count)]
        xi = [raw[i, im_rows, :] for i in range(count)]
        for out in range(count):
            re = hr[0] * xr[out] - hi[0] * xi[out]
            im = hr[0] * xi[out] + hi[0] * xr[out]
            for lag in range(1, out + 1):
                re = re + (hr[lag] * xr[out - lag] - hi[lag] * xi[out - lag])
                im = im + (hr[lag] * xi[out - lag] + hi[lag] * xr[out - lag])
            top[out, re_rows, :], rest[out, re_rows, :] = split(re)
            top[out, im_rows, :], rest[out, im_rows, :] = split(im)
        return carry

    lax.fori_loop(0, block // 16, body, 0)


def backward_products(spectrum, grad, raw, total, top, rest, block, first_slot):
    count = raw.shape[0]

    def body(index, carry):
        re_rows, im_rows = pair_rows(index, block, 16)
        gr = [grad[i, re_rows, :] for i in range(count)]
        gi = [grad[i, im_rows, :] for i in range(count)]
        hr = [spectrum[i, re_rows, :] for i in range(count)]
        hi = [spectrum[i, im_rows, :] for i in range(count)]
        for out in range(count):
            re = hr[0] * gr[out] + hi[0] * gi[out]
            im = hr[0] * gi[out] - hi[0] * gr[out]
            for later in range(out + 1, count):
                lag = later - out
                re = re + (hr[lag] * gr[later] + hi[lag] * gi[later])
                im = im + (hr[lag] * gi[later] - hi[lag] * gr[later])
            top[out, re_rows, :], rest[out, re_rows, :] = split(re)
            top[out, im_rows, :], rest[out, im_rows, :] = split(im)
        xr = [raw[i, re_rows, :] for i in range(count)]
        xi = [raw[i, im_rows, :] for i in range(count)]
        for lag in range(count):
            re = im = None
            for at in range(count - lag):
                a = xr[at] * gr[at + lag] + xi[at] * gi[at + lag]
                b = xr[at] * gi[at + lag] - xi[at] * gr[at + lag]
                re = a if re is None else re + a
                im = b if im is None else im + b
            if not first_slot:
                re = re + total[lag, re_rows, :]
                im = im + total[lag, im_rows, :]
            total[lag, re_rows, :] = re
            total[lag, im_rows, :] = im
        return carry

    lax.fori_loop(0, block // 16, body, 0)


def filter_gradient(total, top, rest, tables, out_ref, lanes, channels, block):
    count, width = total.shape[0], total.shape[2]
    scale = 1.0 / block

    def body(index, carry):
        re_rows, im_rows = pair_rows(index, block, 16)
        sign = signs(16, width, 1.0)
        for lag in range(count):
            re, im = total[lag, re_rows, :], total[lag, im_rows, :]
            if lag + 1 < count:
                re = re + sign * total[lag + 1, im_rows, :]
                im = im - sign * total[lag + 1, re_rows, :]
            top[lag, re_rows, :], rest[lag, re_rows, :] = split(re * scale)
            top[lag, im_rows, :], rest[lag, im_rows, :] = split(im * scale)
        return carry

    lax.fori_loop(0, block // 16, body, 0)
    for lag, values in enumerate(inverse(top, rest, tables)):
        out_ref[pl.ds(lag * block, block), lanes] = values[:, 0:channels]


def conv_forward_steps(doc_count, len_ref, x_ref, tables, y_ref, spectrum, full, raw, top, rest, slots, between):
    block, blocks = spectrum.shape[1] // 2, spectrum.shape[0]
    channels = x_ref.shape[2] // FOLD
    unpack(full, x_ref, channels)
    starts = document_starts(len_ref, doc_count)
    for slot in range(doc_count):
        slot_blocks(full, raw, tables, starts[slot], len_ref[0, slot], block)
        forward_products(spectrum, raw, top, rest, block)
        for out, values in enumerate(inverse(top, rest, tables)):
            slots[slot, pl.ds((1 + out) * block // 8, block // 8)] = tiles(values)
        between(slot)

    def put(index, values):
        pack_block(y_ref, index, values, channels)

    tokens = math.prod(x_ref.shape) // channels
    merge_slots(slots, starts, put, tokens, block, blocks * block)


def conv_backward_steps(
    doc_count, len_ref, g_ref, x_ref, spectrum, skip, tables, gw_ref, edge_ref, gf_ref, lanes,
    g_full, x_full, grad, raw, top, rest, total, slots, between,
):
    block, blocks, channels = spectrum.shape[1] // 2, spectrum.shape[0], x_ref.shape[2] // FOLD
    unpack(g_full, g_ref, channels)
    unpack(x_full, x_ref, channels)
    starts = document_starts(len_ref, doc_count)
    for slot in range(doc_count):
        slot_blocks(g_full, grad, tables, starts[slot], len_ref[0, slot], block)
        slot_blocks(x_full, raw, tables, starts[slot], len_ref[0, slot], block)
        backward_products(spectrum, grad, raw, total, top, rest, block, slot == 0)
        for out, values in enumerate(inverse(top, rest, tables)):
            slots[slot, pl.ds((1 + out) * block // 8, block // 8)] = tiles(values)
        between(slot)
    edge_ref[...] = jnp.zeros(edge_ref.shape, edge_ref.dtype)
    parts = x_ref.shape[0]
    tokens = math.prod(x_ref.shape) // channels
    each = tokens // parts // block

    def put(index, values):
        pack_block(gw_ref, index, values, channels)
        if index % each == 0 and index:
            own = g_full[pl.ds(index * block // 8, EDGE // 8)].reshape(values[0:EDGE].shape)[:, 0:channels] * skip
            edge_ref[index // each - 1, :, 0:channels] = (values[0:EDGE, 0:channels] + own).astype(edge_ref.dtype)

    merge_slots(slots, starts, put, tokens, block, blocks * block)
    between(doc_count)
    filter_gradient(total, top, rest, tables, gf_ref, lanes, channels, block)


def lanes_for(channels):
    return -(-channels // 128) * 128


def conv_scratch(x_shape, blocks, block, docs):
    channels = x_shape[2] // FOLD
    tokens, lanes = math.prod(x_shape) // channels, lanes_for(channels)
    wide = (blocks, 2 * block, lanes)
    full = pltpu.VMEM(((tokens + blocks * block) // 8 + 1, 8, lanes), F32)
    slots = pltpu.VMEM((docs, (blocks + 2) * block // 8 + 1, 8, lanes), F32)
    return full, pltpu.VMEM(wide, F32), pltpu.VMEM(wide, BF), slots


def conv_forward_kernel(doc_count, len_ref, x_ref, filter_ref, t0, t1, t2, t3, y_ref, spectrum, full, raw, top, rest, slots):
    tables = (t0, t1, t2, t3)
    filter_spectrum(filter_ref, spectrum, raw, tables, spectrum.shape[1] // 2)
    conv_forward_steps(
        doc_count, len_ref, x_ref, tables, y_ref, spectrum, full, raw, top, rest, slots, lambda slot: None
    )


def conv_forward(x, lengths, filters, tables):
    docs, block = lengths.shape[1], tables[0].shape[1]
    blocks, channels = filters.shape[0] // block, filters.shape[1]
    filters = jnp.pad(filters, ((0, 0), (0, lanes_for(channels) - channels)))
    full, raw, low, slots = conv_scratch(x.shape, blocks, block, docs)
    return pl.pallas_call(
        functools.partial(conv_forward_kernel, docs),
        name="conv_forward",
        out_shape=(struct(x.shape, BF), struct((blocks, 2 * block, filters.shape[1]), F32)),
        in_specs=[IN_SMEM] + [IN_VMEM] * 6,
        out_specs=(IN_VMEM, IN_VMEM),
        scratch_shapes=[full, raw, low, low, slots],
        compiler_params=pltpu.CompilerParams(vmem_limit_bytes=ROOM),
    )(lengths, x, filters, *tables)


def conv_backward_kernel(doc_count, len_ref, g_ref, x_ref, spectrum, skip_ref, t0, t1, t2, t3, gw_ref, edge_ref, gf_ref, *work):
    conv_backward_steps(
        doc_count, len_ref, g_ref, x_ref, spectrum, skip_ref[...], (t0, t1, t2, t3), gw_ref, edge_ref, gf_ref,
        slice(None), *work, lambda slot: None,
    )


def conv_backward(g, x, lengths, spectrum, skip_gain, tables):
    blocks, block, channels = spectrum.shape[0], spectrum.shape[1] // 2, x.shape[2] // FOLD
    docs = lengths.shape[1]
    full, raw, low, slots = conv_scratch(x.shape, blocks, block, docs)
    return pl.pallas_call(
        functools.partial(conv_backward_kernel, docs),
        name="conv_backward",
        out_shape=(
            struct(x.shape, BF),
            struct((x.shape[0], EDGE, lanes_for(channels)), BF),
            struct((blocks * block, channels), F32),
        ),
        in_specs=[IN_SMEM] + [IN_VMEM] * 8,
        out_specs=(IN_VMEM,) * 3,
        scratch_shapes=[full, full, raw, raw, low, low, raw, slots],
        compiler_params=pltpu.CompilerParams(vmem_limit_bytes=ROOM),
    )(lengths, g, x, spectrum, skip_gain, *tables)


def turned(value, bit):
    return value + bit - 2 * bit * ((value // bit) % 2)


def send(source, target, send_sem, recv_sem, device):
    copy = pltpu.make_async_remote_copy(
        src_ref=source,
        dst_ref=target,
        send_sem=send_sem,
        recv_sem=recv_sem,
        device_id=device,
        device_id_type=MESH,
    )
    copy.start()
    return copy


def greet(peers):
    barrier = pltpu.get_barrier_semaphore()
    for peer in peers:
        pl.semaphore_signal(barrier, inc=1, device_id=peer, device_id_type=MESH)
    pl.semaphore_wait(barrier, len(peers))


def ring(me, count):
    return [lax.rem(me + step, count) for step in range(1, count)]


def dma(*shape):
    return pltpu.SemaphoreType.DMA(shape)


def gather_fallback(chunks, gains, channel, edges):
    mp = lax.axis_size("mp")
    down = [(i, (i + 1) % mp) for i in range(mp)]
    up = [(i, (i - 1) % mp) for i in range(mp)]
    spread = [lax.all_gather(lax.all_gather(c, "dp"), "mp") for c in chunks]
    return (
        *spread,
        lax.all_gather(gains, "dp"),
        lax.all_gather(channel, "mp"),
        jnp.stack([lax.ppermute(edges[0], "mp", down), lax.ppermute(edges[1], "mp", up)]),
    )


def exchange_kernel(count, has_edge, *refs):
    sources, refs = refs[: count + has_edge], refs[count + has_edge :]
    targets, refs = refs[: count + has_edge], refs[count + has_edge :]
    send_sem, recv_sem, edge_send, edge_recv = refs
    d, m, mp = lax.axis_index("dp"), lax.axis_index("mp"), lax.axis_size("mp")
    greet([(d, e) for e in ring(m, mp)])
    copies = []
    for step, e in reversed(list(enumerate(ring(m, mp)))):
        for i in range(count):
            copies.append(
                send(sources[i].at[e], targets[i].at[m], send_sem.at[i, step], recv_sem.at[i, step], (d, e))
            )
    if has_edge:
        before = lax.rem(m + mp - 1, mp)
        copies.append(send(sources[count], targets[count], edge_send.at[0], edge_recv.at[0], (d, before)))
    for i in range(count):
        targets[i][m] = sources[i][m]
    for copy in copies:
        copy.wait()


def exchange(arrays, edge, collective_id):
    mp, count = lax.axis_size("mp"), len(arrays)
    inputs = list(arrays) + ([] if edge is None else [edge])
    return pl.pallas_call(
        functools.partial(exchange_kernel, count, int(edge is not None)),
        name="exchange_%d" % collective_id,
        out_shape=tuple(struct(a.shape, a.dtype) for a in inputs),
        in_specs=[IN_VMEM] * len(inputs),
        out_specs=(IN_VMEM,) * len(inputs),
        scratch_shapes=[dma(count, mp - 1), dma(count, mp - 1), dma(1), dma(1)],
        compiler_params=pltpu.CompilerParams(
            collective_id=collective_id, has_side_effects=True, vmem_limit_bytes=ROOM
        ),
    )(*inputs)


class Flow:
    def __init__(self, part, refs, lanes=slice(None)):
        self.part, self.lanes = part, lanes
        (self.own, self.from_core, self.from_y2, self.from_x2, self.from_x1, self.from_y1, self.from_z) = refs[:7]
        self.own_sem, self.p_send, self.p_recv, self.z_send, self.z_recv = refs[7:]
        self.d, self.m, self.mp = lax.axis_index("dp"), lax.axis_index("mp"), lax.axis_size("mp")
        self.half = self.mp // 2
        self.y, self.x, self.core = self.d // 4, (self.d // 2) % 2, self.d % 2
        self.pending = []

    def push(self, slot, source, target, bit):
        peer = (turned(self.d, bit), self.m)
        copy = send(source, target, self.p_send.at[slot], self.p_recv.at[slot], peer)
        self.pending.append(copy)
        return copy

    def start(self):
        self.copy = self.push(0, self.part.at[:, :, :, 1 - self.core, :, self.lanes], self.from_core, 1)
        self.local = pltpu.make_async_copy(self.part.at[:, :, :, self.core, :, self.lanes], self.own, self.own_sem.at[0])
        self.local.start()

    def core_stage(self):
        own, half, y, x = self.own, self.half, self.y, self.x
        self.local.wait()
        self.copy.wait_recv()

        def body(i, carry):
            at = (i // 4, (i // 2) % 2, i % 2)
            own[at] = own[at] + self.from_core[at]
            return carry

        lax.fori_loop(0, self.mp * 4, body, 0)
        low, high = pl.ds(0, half), pl.ds(half, self.mp - half)
        self.copies = [
            self.push(1, own.at[low, 1 - y], self.from_y2, 4),
            self.push(2, own.at[high, :, 1 - x], self.from_x2, 2),
        ]

    def second_sum(self):
        own, half, y, x = self.own, self.half, self.y, self.x
        for copy in self.copies:
            copy.wait_recv()

        def body(i, carry):
            a, b = i // 2, i % 2
            own[a, y, b] = own[a, y, b] + self.from_y2[a, b]
            own[half + a, b, x] = own[half + a, b, x] + self.from_x2[a, b]
            return carry

        lax.fori_loop(0, half * 2, body, 0)

    def second_stage(self):
        own, half, y, x = self.own, self.half, self.y, self.x
        self.second_sum()
        low, high = pl.ds(0, half), pl.ds(half, self.mp - half)
        self.copies = [
            self.push(3, own.at[low, y, 1 - x], self.from_x1, 2),
            self.push(4, own.at[high, 1 - y, x], self.from_y1, 4),
        ]

    def third_stage(self):
        own, half, y, x = self.own, self.half, self.y, self.x
        for copy in self.copies:
            copy.wait_recv()

        def body(a, carry):
            own[a, y, x] = own[a, y, x] + self.from_x1[a]
            own[half + a, y, x] = own[half + a, y, x] + self.from_y1[a]
            return carry

        lax.fori_loop(0, half, body, 0)

    def send_z(self):
        self.copies = [
            send(
                self.own.at[e, self.y, self.x], self.from_z.at[step], self.z_send.at[step], self.z_recv.at[step],
                (self.d, e),
            )
            for step, e in enumerate(ring(self.m, self.mp))
        ]
        self.pending.extend(self.copies)

    def finish(self, out):
        for copy in self.copies:
            copy.wait_recv()
        total = self.own[self.m, self.y, self.x].astype(F32)
        for step in range(self.mp - 1):
            total = total + self.from_z[step].astype(F32)
        out[:, self.lanes] = total

    def drain(self):
        for copy in self.pending:
            copy.wait_send()


FLOW_REFS = 12


def flow_scratch(mp, block, over_z=True):
    half = mp // 2
    leads = ((mp, 2, 2), (mp, 2, 2), (half, 2), (mp - half, 2), (half,), (mp - half,))
    last = (mp - 1,) + block if over_z else (1, 16, 128)
    return [pltpu.VMEM(lead + block, BF) for lead in leads] + [pltpu.VMEM(last, BF)] + [dma(1), dma(5), dma(5), dma(mp - 1), dma(mp - 1)]


class SmallSums:
    def __init__(self, small, outs, wide, refs):
        count = len(small)
        self.small, self.outs, self.wide = small, outs, wide
        self.running, self.from_dp, self.from_mp = [refs[i * count : (i + 1) * count] for i in range(3)]
        self.s_send, self.s_recv = refs[3 * count :]
        self.pending = []

    def start(self, stage):
        bit = (1, 2, 4)[stage]
        d, m = lax.axis_index("dp"), lax.axis_index("mp")
        if stage == 0:
            for i, ref in enumerate(self.small):
                self.running[i][0] = ref[...]
        self.copies = []
        for i in range(len(self.small)):
            at = i * 8 + stage
            self.copies.append(
                send(
                    self.running[i].at[stage], self.from_dp[i].at[stage], self.s_send.at[at], self.s_recv.at[at],
                    (turned(d, bit), m),
                )
            )
        self.pending.extend(self.copies)

    def end(self, stage):
        for i, copy in enumerate(self.copies):
            copy.wait_recv()
            self.running[i][stage + 1] = self.running[i][stage] + self.from_dp[i][stage]

    def start_mp(self):
        d, m, mp = lax.axis_index("dp"), lax.axis_index("mp"), lax.axis_size("mp")
        self.copies = []
        for i, wide in enumerate(self.wide):
            if wide:
                for step, e in enumerate(ring(m, mp)):
                    at = i * 8 + 3 + step
                    self.copies.append(
                        send(
                            self.running[i].at[3], self.from_mp[i].at[m], self.s_send.at[at], self.s_recv.at[at],
                            (d, e),
                        )
                    )
                self.from_mp[i][m] = self.running[i][3]
        self.pending.extend(self.copies)

    def end_mp(self):
        for copy in self.copies:
            copy.wait_recv()
        for i, wide in enumerate(self.wide):
            if wide:
                total = self.from_mp[i][0]
                for e in range(1, lax.axis_size("mp")):
                    total = total + self.from_mp[i][e]
                self.outs[i][...] = total
            else:
                self.outs[i][...] = self.running[i][3]

    def drain(self):
        for copy in self.pending:
            copy.wait_send()


def small_scratch(small, mp):
    scratch = []
    for lead in (4, 3, mp):
        scratch += [pltpu.VMEM((lead,) + s.shape, F32) for s in small]
    return scratch + [dma(8 * len(small)), dma(8 * len(small))]


def scatter_fallback(part):
    over_mp = lax.psum_scatter(part, "mp", scatter_dimension=0)
    return lax.psum_scatter(over_mp, "dp", scatter_dimension=0).astype(F32)


def cored(part):
    return part.reshape((part.shape[0], 2, 2, 2) + part.shape[2:])


class Blocks:
    def __init__(self, pairs, send_sem, recv_sem):
        self.pairs, self.send_sem, self.recv_sem = pairs, send_sem, recv_sem
        self.d, self.m, self.mp = lax.axis_index("dp"), lax.axis_index("mp"), lax.axis_size("mp")

    def start(self):
        self.copies = []
        for step, e in reversed(list(enumerate(ring(self.m, self.mp)))):
            for i, (source, target) in enumerate(self.pairs):
                sems = self.send_sem.at[i, step], self.recv_sem.at[i, step]
                self.copies.append(send(source.at[e], target.at[self.m], *sems, (self.d, e)))
        for source, target in self.pairs:
            target[self.m] = source[self.m]

    def arrive(self):
        for copy in self.copies:
            copy.wait_recv()

    def drain(self):
        for copy in self.copies:
            copy.wait_send()


def stream_zero(offsets, edge, gs, z, w, channel, marks, sums, feed_sums):
    count = gs.shape[0] - EDGE
    same = [None] + [marks[k - 1, :, 0:1] > 0.0 for k in range(1, offsets)]
    gs[pl.ds(count, EDGE), :] = edge[...].astype(F32)
    sums[...] = jnp.zeros(sums.shape, F32)
    g_z = short_backward(0, gs, z, channel, same, offsets, count, sums).astype(BF)
    sums[pl.ds(3 * offsets, 1), :] = feed_sums[1:2, :]
    sums[pl.ds(3 * offsets + 2, 1), :] = feed_sums[0:1, :]
    return g_z, dot_nt(g_z, w[...])


def mixer_backward_kernel(doc_count, offsets, len_ref, g_parts, edge, channel_own, feed_sums, part_a, part_b, *refs):
    late_refs, refs = refs[:17], refs[17:]
    gw_back, gw_edge_back, sums, ga0_out, fin_part, fout_part, partial_a, b_low, b_high, part_c_out, refs = *refs[:10], refs[10:]
    held, refs = refs[:16], refs[16:]
    (
        late_sem, ga0, part_c, save_sem, edge_back, gs, marks, gf_ref, g_in, gw, gw_edge, g_full, x_full, grad, raw,
        top, rest, total, slots, b_send, b_recv, c_send, c_recv, e_sem, *refs,
    ) = refs
    a_refs, b_refs = refs[:FLOW_REFS], refs[FLOW_REFS:]
    z, acts, w, channel, out_part, x_ref, t0, t1, t2, t3, spectrum, decay, hidden, f_out, phase, table = held
    tables = (t0, t1, t2, t3)
    parts = x_ref.shape[1]
    near = x_ref.shape[3] // FOLD
    half = near * HALVES
    own_count = ga0.shape[0]
    d, m, mp = lax.axis_index("dp"), lax.axis_index("mp"), lax.axis_size("mp")
    a, b = Flow(part_a, a_refs), Flow(part_b, b_refs)
    incoming, outgoing = [], []
    for side in range(HALVES):
        incoming.append(Blocks([(g_parts.at[side], g_in.at[side])], b_send.at[side], b_recv.at[side]))
        pairs = [(gw.at[side], gw_back.at[side]), (gw_edge.at[side], gw_edge_back.at[side])]
        outgoing.append(Blocks(pairs, c_send.at[side], c_recv.at[side]))
    late = Late(late_refs, (gs.at[pl.ds(0, own_count)],) + tuple(held), late_sem)
    greet([(turned(d, bit), m) for bit in (1, 2, 4)] + [(d, e) for e in ring(m, mp)])
    edge_copy = send(edge, edge_back, e_sem.at[0], e_sem.at[1], (d, lax.rem(m + mp - 1, mp)))
    for copies in incoming:
        copies.start()
    a.start()
    mark_same(marks, len_ref, doc_count, m * own_count - EDGE)
    a.core_stage()
    b.start()
    late.need(0, 1, 2, 3, 4, 5)
    edge_copy.wait_recv()
    g_z, back = stream_zero(offsets, edge_back, gs, z, w, channel, marks, sums, feed_sums)
    ga0[...] = back
    size = part_c.shape[4]
    for first in range(0, parts, 2):
        in_grad = dot_tn(acts[pl.ds(EDGE, own_count), :], g_z[:, first * half : (first + 2) * half])
        for part in range(first, first + 2):
            cols = slice((part - first) * half, (part - first + 1) * half)
            for owner in range(8):
                at = (part, owner // 4, owner // 2 % 2, owner % 2, slice(None))
                rows = slice(owner * size, (owner + 1) * size)
                part_c[at + (pl.ds(0, half),)] = in_grad[rows, cols].astype(BF)
                part_c[at + (pl.ds(half, half),)] = out_part[part, rows]
    saves = Late((ga0, part_c), (ga0_out, part_c_out), save_sem)
    late.need(*range(6, 17))
    skip = channel_own[channel_own.shape[0] - 1 :, :]

    def first_side(step):
        if step == 0:
            b.core_stage()
        if step == 2:
            a.second_stage()

    def last_side(step):
        if step == doc_count:
            a.third_stage()

    for side in range(HALVES):
        incoming[side].arrive()
        between = (first_side, last_side)[side]
        lanes = pl.ds(side * near, near)

        def after(step, side=side, between=between):
            if step == doc_count:
                outgoing[side].start()
            between(step)

        conv_backward_steps(
            doc_count, len_ref, g_in.at[side], x_ref.at[side], spectrum.at[side], skip[:, side * near : (side + 1) * near],
            tables, gw.at[side], gw_edge.at[side], gf_ref, lanes, g_full, x_full, grad, raw, top, rest, total, slots, after,
        )
    g_raw = gf_ref[...] * decay[...]
    fout_part[...] = near_product(hidden[...], g_raw, dot_tn)
    fin_part[...] = near_product(table[...], near_product(g_raw, f_out[...], dot_nt) * jnp.cos(phase[...]), dot_tn)
    for e in range(parts):
        partial_a[e] = a.own[e, a.y, a.x]
    b.second_sum()
    for e in range(parts // 2):
        for other in range(2):
            b_low[e, other] = b.own[e, b.y, other]
            b_high[e, other] = b.own[parts // 2 + e, other, b.x]
    for copies in outgoing:
        copies.arrive()
    edge_copy.wait_send()
    saves.need(0, 1)
    for copies in incoming + outgoing:
        copies.drain()
    for flow in (a, b):
        flow.drain()


def mixer_backward(
    lengths, offsets, g_parts, edge, channel_own, feed_sums, part_a, part_b, g_s0, z, a, w_in, channel, out_part, x,
    tables, spectrum, decay, hidden, f_out, phase, table,
):
    dp, mp = lax.axis_size("dp"), lax.axis_size("mp")
    parts, docs = x.shape[1], lengths.shape[1]
    blocks, block, near = spectrum.shape[1], spectrum.shape[2] // 2, x.shape[3] // FOLD
    half, width = HALVES * near, 2 * HALVES * near
    size = part_a.shape[2]
    full = channel.shape[1]
    if dp != 8:
        g_in = exchange([*g_parts], edge, 5)
        edge_back = g_in[HALVES]
        halves = []
        for side in range(HALVES):
            skip = channel_own[-1:, side * near : (side + 1) * near]
            halves.append(conv_backward(g_in[side], x[side], lengths, spectrum[side], skip, tables))
        g_raw = jnp.concatenate([v[2] for v in halves], axis=1) * decay
        fin, fout = product(table.T, product(g_raw, f_out.T) * jnp.cos(phase)), product(hidden.T, g_raw)
        backs = exchange([v[i] for i in range(2) for v in halves], None, 6)
        gw_back, gw_edge_back = jnp.stack(backs[:HALVES]), jnp.stack(backs[HALVES:])
        count = g_s0.shape[0]
        gs = jnp.concatenate([g_s0, edge_back.astype(F32)])
        position = lax.axis_index("mp") * count - EDGE + jnp.arange(count + 2 * EDGE, dtype=jnp.int32)
        doc = jnp.sum((position[:, None] >= jnp.cumsum(lengths[0])[None, :]).astype(jnp.int32), axis=1)
        doc = jnp.where(position < 0, -1, doc)
        same = [None] + [(doc[EDGE:] == doc[EDGE - k : doc.shape[0] - k])[:, None] for k in range(1, offsets)]
        g_z, sums = None, jnp.zeros((16, full), F32)
        for k in range(offsets):
            later, before = gs[k : count + k], z[0, EDGE - k : EDGE - k + count]
            if k:
                later, before = jnp.where(same[k][k : count + k], later, 0.0), jnp.where(same[k][:count], before, 0.0)
            g_z = channel[3 * k] * later if g_z is None else g_z + channel[3 * k] * later
            sums = sums.at[3 * k].set(jnp.sum(gs[:count] * before, axis=0))
        sums = sums.at[3 * offsets].set(feed_sums[1]).at[3 * offsets + 2].set(feed_sums[0])
        g_z = g_z.astype(BF)
        grad = dot_tn(a[EDGE : EDGE + count], g_z).reshape(full, mp, half).transpose(1, 0, 2).astype(BF)
        part_c = jnp.concatenate([grad, out_part], axis=2).reshape(mp, dp, size, width)
        over_dp = [lax.psum_scatter(p, "dp", scatter_dimension=1) for p in (part_a, part_b)]
        return (
            gw_back, gw_edge_back, sums, dot_nt(g_z, w_in[0]), fin, fout, *over_dp, None, part_c,
        )
    edge_shape = (HALVES, parts, EDGE, lanes_for(near))
    own, own_c = part_a.shape[2:], (size, width)
    rows, raw, low, slots = conv_scratch(x.shape[1:], blocks, block, docs)
    first = (g_parts, edge, channel_own, feed_sums)
    late = [
        (g_s0, None), (z, 0), (a, None), (w_in, 0), (channel, None), (out_part, None), (x, None),
        *[(t, None) for t in tables], (spectrum, None), (decay, None), (hidden, None), (f_out, None), (phase, None),
        (table, None),
    ]
    fin, fout = struct((table.shape[1], hidden.shape[1]), F32), struct((hidden.shape[1], half), F32)
    longer = (g_s0.shape[0] + EDGE, full)

    def kernel(*refs):
        start = 3 + len(first)
        chosen = [r if i is None else r.at[i] for r, (_, i) in zip(refs[start : start + len(late)], late)]
        mixer_backward_kernel(docs, offsets, *refs[:start], *chosen, *refs[start + len(late) :])

    return pl.pallas_call(
        kernel,
        name="mixer_backward",
        out_shape=(
            struct(x.shape, BF), struct(edge_shape, BF), struct((16, full), F32), struct(g_s0.shape, F32), fin, fout,
            struct((mp,) + own, BF), *[struct((mp // 2, 2) + own, BF)] * 2, struct((mp, 2, 2, 2) + own_c, BF),
        ),
        in_specs=[IN_SMEM] + [IN_VMEM] * len(first) + [IN_HBM] * (2 + len(late)),
        out_specs=(*[IN_VMEM] * 3, IN_HBM, *[IN_VMEM] * 5, IN_HBM),
        scratch_shapes=[
            *[pltpu.VMEM(v.shape if i is None else v.shape[1:], v.dtype) for v, i in late[1:]],
            dma(len(late)), pltpu.VMEM(g_s0.shape, F32), pltpu.VMEM((mp, 2, 2, 2) + own_c, BF), dma(2),
            pltpu.VMEM(edge.shape, BF), pltpu.VMEM(longer, F32),
            pltpu.VMEM((offsets - 1, longer[0], 128), F32),
            pltpu.VMEM((blocks * block, half), F32), pltpu.VMEM(x.shape, BF), pltpu.VMEM(x.shape, BF),
            pltpu.VMEM(edge_shape, BF), rows, rows, raw, raw, low, low, raw, slots,
            dma(HALVES, 1, mp - 1), dma(HALVES, 1, mp - 1), dma(HALVES, 2, mp - 1), dma(HALVES, 2, mp - 1), dma(2),
            *flow_scratch(mp, own, False), *flow_scratch(mp, own, False),
        ],
        compiler_params=pltpu.CompilerParams(collective_id=5, has_side_effects=True, vmem_limit_bytes=ROOM),
    )(lengths, *first, cored(part_a), cored(part_b), *[v for v, _ in late])


def spread_sum(block, slots, send_sem, recv_sem, axis, first):
    d, m = lax.axis_index("dp"), lax.axis_index("mp")
    count = lax.axis_size(axis)
    me = d if axis == "dp" else m
    copies = []
    for step, e in enumerate(ring(me, count)):
        peer = (e, m) if axis == "dp" else (d, e)
        copies.append(send(block, slots.at[me], send_sem.at[first + step], recv_sem.at[first + step], peer))
    slots[me] = block[...]
    for copy in copies:
        copy.wait()
    total = slots[0]
    for e in range(1, count):
        total = total + slots[e]
    return total


def total_of(values):
    return jnp.sum(jnp.sum(values, axis=1, keepdims=True), axis=0, keepdims=True)


def lanes_of(items):
    lane = lax.broadcasted_iota(jnp.int32, (1, 128), 1)
    row = jnp.zeros((1, 128), F32)
    for index, item in enumerate(items):
        row = row + jnp.where(lane == index, item, 0.0)
    return row


def update_body(
    taps, g0, g1, g2, w0, w1, w2, rows, cols, vec_sum, own_gain, gain, gain_mom, chan, chan_mom,
    fin_sum, fin, fin_mom, fout_sum, fout, fout_mom,
    norm_out, c0, c1, c2, n0, n1, n2, rows_out, cols_out, gain_g, gain_n, gain_m,
    chan_g, chan_n, chan_m, fin_g, fin_n, fin_m, fout_g, fout_n, fout_m,
    turn, mp_block, dp_block, mp_slots, dp_slots, last_block, mp_last, dp_last, send_sem, recv_sem,
):
    d, m = lax.axis_index("dp"), lax.axis_index("mp")
    dp, mp = lax.axis_size("dp"), lax.axis_size("mp")
    size, width = g0.shape
    in_width = 3 * (width // 4)
    is_in = lax.broadcasted_iota(jnp.int32, (size, width), 1) < in_width

    def four(v0, v1, v2, reduce_fn):
        return [
            reduce_fn(jnp.where(is_in, v0, 0.0)),
            reduce_fn(jnp.where(is_in, 0.0, v0)),
            reduce_fn(v1),
            reduce_fn(v2),
        ]

    def row_sum(v):
        return jnp.sum(v, axis=1, keepdims=True)

    def col_sum(v):
        return jnp.sum(v, axis=0, keepdims=True)

    s0, s1, s2 = g0[...] * g0[...], g1[...] * g1[...], g2[...] * g2[...]
    lane = lax.broadcasted_iota(jnp.int32, (size, 128), 1)
    row_parts = four(s0, s1, s2, row_sum)
    packed = jnp.zeros((size, 128), F32)
    for index, part in enumerate(row_parts):
        packed = packed + jnp.where(lane == index, part, 0.0)
    turn[...] = jnp.zeros(turn.shape, F32)
    dp_block[...] = jnp.zeros(dp_block.shape, F32)
    turn[pl.ds(0, size), :] = packed
    mp_block[pl.ds(0, 8), :] = jnp.transpose(turn[...])[0:8]
    old = rows[...]
    old_parts = [total_of(old[:, i : i + 1]) / mp for i in range(4)]
    weight_parts = four(w0[...] * w0[...], w1[...] * w1[...], w2[...] * w2[...], total_of)
    scalars = (
        [total_of(p) for p in row_parts]
        + old_parts
        + weight_parts
        + [
            total_of(gain[...] * gain[...]) / mp,
            total_of(chan[...] * chan[...]) / dp,
            total_of(fout[...] * fout[...]) / dp,
            total_of(fout_sum[...] * fout_sum[...]) / dp,
        ]
    )
    mp_block[pl.ds(8, 8), :] = jnp.broadcast_to(lanes_of(scalars), (8, 128))
    over_mp = spread_sum(mp_block, mp_slots, send_sem, recv_sem, "mp", 0)
    pieces = width // 128
    for index, values in enumerate((s0, s1, s2)):
        sums = col_sum(values)
        for piece in range(pieces):
            dp_block[pl.ds(index * pieces + piece, 1), :] = sums[:, piece * 128 : (piece + 1) * 128]
    dp_block[pl.ds(3 * pieces, 1), :] = over_mp[8:9]
    over_dp = spread_sum(dp_block, dp_slots, send_sem, recv_sem, "dp", mp)
    turn[pl.ds(0, 8), :] = over_mp[0:8]
    row_totals = jnp.transpose(turn[...])[0:size]
    shared = over_dp[3 * pieces : 3 * pieces + 1]

    def scalar(index):
        return shared[:, index : index + 1]

    last = 3 * taps + 1
    vec_sq = total_of(vec_sum[0 : last + 2, :] * vec_sum[0 : last + 2, :])
    fin_sq = total_of(fin_sum[...] * fin_sum[...])
    norm = jnp.sqrt(
        scalar(0) + scalar(1) + scalar(2) + scalar(3) + vec_sq + scalar(15) + fin_sq
    )
    norm_out[...] = norm
    clip = 1.0 / jnp.maximum(1.0, norm / CLIP_NORM)
    square = clip * clip
    fresh = 1.0 - MOMENT_DECAY
    all_rows = size * dp
    wide = [in_width * mp, (width - in_width) * mp, width * mp, width * mp]
    ratio = []
    fresh_rows = jnp.zeros((size, 128), F32)
    for index in range(4):
        row_new = (
            MOMENT_DECAY * old[:, index : index + 1]
            + fresh * square * row_totals[:, index : index + 1] / wide[index]
        )
        mean = MOMENT_DECAY * scalar(4 + index) / all_rows + fresh * square * scalar(index) / (
            all_rows * wide[index]
        )
        ratio.append(row_new / mean)
        fresh_rows = fresh_rows + jnp.where(lane == index, row_new, 0.0)
    turn[pl.ds(0, size), :] = fresh_rows
    rows_out[...] = jnp.transpose(turn[...])[0:8]
    for index in range(3):
        for piece in range(pieces):
            at = pl.ds(piece * 128, 128)
            row = index * pieces + piece
            cols_out[pl.ds(index, 1), at] = (
                MOMENT_DECAY * cols[pl.ds(index, 1), at]
                + fresh * square * over_dp[row : row + 1] / all_rows
            )
    first_ratio = jnp.where(is_in, ratio[0], ratio[1])
    steps = []
    for grad, out, factor, index in ((g0, c0, first_ratio, 0), (g1, c1, ratio[2], 1), (g2, c2, ratio[3], 2)):
        clipped = grad[...] * clip
        out[...] = clipped
        steps.append(clipped * lax.rsqrt(factor * cols_out[pl.ds(index, 1), :]))
    u0, u1, u2 = steps

    def plain(clipped, moment, grad_out, moment_out):
        fresh_moment = MOMENT_DECAY * moment + fresh * clipped * clipped
        grad_out[...] = clipped
        moment_out[...] = fresh_moment
        return clipped * lax.rsqrt(fresh_moment)

    picked = vec_sum[last : last + 2, 0:size]
    for e in range(1, dp):
        picked = jnp.where(d == e, vec_sum[last : last + 2, e * size : (e + 1) * size], picked)
    own_gain[...] = jnp.zeros(own_gain.shape, F32)
    own_gain[:, pl.ds(0, size)] = picked
    own = width // mp
    own_chan = vec_sum[0:last, 0:own]
    for e in range(1, mp):
        own_chan = jnp.where(m == e, vec_sum[0:last, e * own : (e + 1) * own], own_chan)
    u_gain = plain(own_gain[...] * clip, gain_mom[...], gain_g, gain_m)
    u_chan = plain(own_chan * clip, chan_mom[...], chan_g, chan_m)
    u_fin = plain(fin_sum[...] * clip, fin_mom[...], fin_g, fin_m)
    u_fout = plain(fout_sum[...] * clip, fout_mom[...], fout_g, fout_m)
    step_parts = four(u0 * u0, u1 * u1, u2 * u2, total_of) + [
        total_of(u_gain * u_gain) / mp,
        total_of(u_chan * u_chan) / dp,
        total_of(u_fout * u_fout) / dp,
    ]
    last_block[...] = jnp.broadcast_to(lanes_of(step_parts), (8, 128))
    half_way = spread_sum(last_block, mp_last, send_sem, recv_sem, "mp", mp + dp)
    mp_block[pl.ds(0, 8), :] = half_way
    step_sums = spread_sum(mp_block.at[pl.ds(0, 8)], dp_last, send_sem, recv_sem, "dp", 2 * mp + dp)[0:1]

    def factors(step_total, weight_total, entries):
        shrink = 1.0 / jnp.maximum(1.0, jnp.sqrt(step_total / entries) / CLIP_STEP)
        return STEP_RATE * jnp.sqrt(weight_total / entries) * shrink

    def step_sum(index):
        return step_sums[:, index : index + 1]

    rate = [factors(step_sum(i), scalar(8 + i), all_rows * wide[i]) for i in range(4)]
    n0[...] = w0[...] - jnp.where(is_in, rate[0], rate[1]) * u0
    n1[...] = w1[...] - rate[2] * u1
    n2[...] = w2[...] - rate[3] * u2
    gain_n[...] = gain[...] - factors(step_sum(4), scalar(12), 2 * all_rows) * u_gain
    chan_n[...] = chan[...] - factors(step_sum(5), scalar(13), chan.shape[0] * chan.shape[1] * mp) * u_chan
    fout_n[...] = fout[...] - factors(step_sum(6), scalar(14), fout.shape[0] * fout.shape[1] * mp) * u_fout
    fin_count = fin.shape[0] * fin.shape[1]
    fin_rate = factors(total_of(u_fin * u_fin), total_of(fin[...] * fin[...]), fin_count)
    fin_n[...] = fin[...] - fin_rate * u_fin


def greet_all():
    d, m = lax.axis_index("dp"), lax.axis_index("mp")
    greet([(e, m) for e in ring(d, lax.axis_size("dp"))] + [(d, e) for e in ring(m, lax.axis_size("mp"))])


def prepare(raw, ready, turn):
    in_w, out_w, in_rows, out_rows, up_rows, down_rows, in_cols, out_cols, up_cols, down_cols, gain_own, gain_mom_own = raw
    w0, rows, cols, gain, gain_mom = ready
    size, own = out_w.shape
    for j in range(3):
        w0[:, pl.ds(j * own, own)] = in_w[j]
        cols[0:1, pl.ds(j * own, own)] = in_cols[j : j + 1, :]
    w0[:, pl.ds(3 * own, own)] = out_w[...]
    cols[0:1, pl.ds(3 * own, own)] = out_cols[...].reshape(1, own)
    cols[1:2, :] = up_cols[...].reshape(1, -1)
    cols[2:3, :] = down_cols[...].reshape(1, -1)
    turn[...] = jnp.zeros(turn.shape, F32)
    for index, source in enumerate((in_rows, out_rows, up_rows, down_rows)):
        turn[pl.ds(index, 1), pl.ds(0, size)] = source[...].reshape(1, size)
    rows[...] = jnp.transpose(turn[...])[0:size]
    for source, target, fill in ((gain_own, gain, 0.0), (gain_mom_own, gain_mom, 1.0)):
        target[...] = jnp.full(target.shape, fill, F32)
        target[:, pl.ds(0, size)] = source[...]


def prepare_scratch(size, width):
    return [
        pltpu.VMEM((size, width), F32), pltpu.VMEM((size, 128), F32), pltpu.VMEM((8, width), F32),
        pltpu.VMEM((2, 128), F32), pltpu.VMEM((2, 128), F32),
    ]


OUTS = 21


def run_update(taps, grads, sums, w1, w2, ready, own_gain, old, outs, work):
    w0, rows, cols, gain, gain_mom = ready
    chan, chan_mom, fin, fin_mom, fout, fout_mom = old
    update_body(
        taps, *grads, w0, w1, w2, rows, cols, sums[0], own_gain, gain, gain_mom, chan, chan_mom,
        sums[1], fin, fin_mom, sums[2], fout, fout_mom, *outs, *work,
    )


def update_kernel(taps, *refs):
    grads, sums, refs = refs[:3], refs[3:6], refs[6:]
    raw, w1, w2, old, refs = refs[:12], refs[12], refs[13], refs[14:20], refs[20:]
    outs, ready, own_gain, work = refs[:OUTS], refs[OUTS : OUTS + 5], refs[OUTS + 5], refs[OUTS + 6 :]
    prepare(raw, ready, work[0])
    greet_all()
    run_update(taps, grads, sums, w1, w2, ready, own_gain, old, outs, work)


def place_first(g0, zero_and_out, one_and_two):
    own = g0.shape[1] // 4
    g0[:, pl.ds(0, own)] = zero_and_out[:, 0:own]
    g0[:, pl.ds(own, 2 * own)] = one_and_two
    g0[:, pl.ds(3 * own, own)] = zero_and_out[:, own : 2 * own]


class LastOverDp:
    def __init__(self, low, high, from_low, from_high, send_sem, recv_sem):
        self.low, self.high, self.from_low, self.from_high = low, high, from_low, from_high
        d, m = lax.axis_index("dp"), lax.axis_index("mp")
        self.y, self.x = d // 4, (d // 2) % 2
        self.copies = [
            send(low.at[:, 1 - self.x], from_low, send_sem.at[0], recv_sem.at[0], (turned(d, 2), m)),
            send(high.at[:, 1 - self.y], from_high, send_sem.at[1], recv_sem.at[1], (turned(d, 4), m)),
        ]

    def finish(self, partial):
        for copy in self.copies:
            copy.wait()
        half = self.from_low.shape[0]
        for e in range(half):
            partial[e] = self.low[e, self.x] + self.from_low[e]
            partial[half + e] = self.high[e, self.y] + self.from_high[e]


class OverMp:
    def __init__(self, partial, arrived, passed, send_sem, recv_sem):
        self.partial, self.arrived, self.passed = partial, arrived, passed
        self.send_sem, self.recv_sem = send_sem, recv_sem
        self.d, self.m = lax.axis_index("dp"), lax.axis_index("mp")
        near = turned(self.m, 1)
        self.far = turned(self.m, 2)
        self.copies = [self.push(partial.at[e], slot, near) for slot, e in enumerate((near, turned(near, 2)))]

    def push(self, source, slot, peer):
        sems = self.send_sem.at[slot], self.recv_sem.at[slot]
        return send(source, self.arrived.at[slot], *sems, (self.d, peer))

    def step(self):
        for copy in self.copies:
            copy.wait()
        self.passed[...] = self.partial[self.far] + self.arrived[1]
        self.copies = [self.push(self.passed, 2, self.far)]

    def total(self):
        self.copies[0].wait()
        return self.partial[self.m].astype(F32) + self.arrived[0].astype(F32) + self.arrived[2].astype(F32)


def end_kernel(doc_count, taps, len_ref, gw_ref, gw_edge, channel, gains, sums_in, *refs):
    late_refs, partial_a, b_low, b_high, part_c, fin_part, fout_part, refs = refs[:12], *refs[12:18], refs[18:]
    raw, w1, w2, old, refs = refs[:12], refs[12], refs[13], refs[14:20], refs[20:]
    input_grad, outs, refs = refs[0], refs[1 : OUTS + 1], refs[OUTS + 1 :]
    held, late_sem, work, refs = refs[:12], refs[12], refs[13:17], refs[17:]
    ready, own_gain, refs = refs[:5], refs[5], refs[6:]
    g0, g1, g2, g_late, vec, vec_sum, fin_sum, fout_sum, part, refs = *refs[:9], refs[9:]
    update_work, refs = refs[:10], refs[10:]
    arrived, passed, z_send, z_recv, refs = refs[:2], refs[2:4], refs[4], refs[5], refs[6:]
    g_c, partial_b, from_low, from_high, l_send, l_recv, refs = *refs[:6], refs[6:]
    partials = (partial_a, partial_b)
    mp = lax.axis_size("mp")
    own = gw_ref.shape[3] // FOLD * HALVES
    size = g0.shape[0]
    lanes = g_late.shape[1] // FLOWS
    flows = []
    for i in range(FLOWS):
        flows.append(Flow(part, refs[i * FLOW_REFS : (i + 1) * FLOW_REFS], pl.ds(i * lanes, lanes)))
    refs = refs[FLOWS * FLOW_REFS :]
    flow_c, refs = Flow(part_c, refs[:FLOW_REFS]), refs[FLOW_REFS:]
    early = SmallSums((fin_part, fout_part), (fin_sum, fout_sum), (True, False), refs[:8])
    final = SmallSums((vec,), (vec_sum,), (True,), refs[8:])
    late = Late(late_refs, held, late_sem)
    vec[...] = sums_in[...]
    greet_all()
    last_b = LastOverDp(b_low, b_high, from_low, from_high, l_send, l_recv)
    flow_c.start()

    def start_mp(i):
        return OverMp(partials[i], arrived[i], passed[i], z_send.at[i], z_recv.at[i])

    over_mp = [start_mp(0)]
    early.start(0)

    def stream_done(j, grad):
        for e in range(mp):
            for owner in range(8):
                at = (e, owner // 4, owner // 2 % 2, owner % 2, slice(None), pl.ds((j - 1) * own, own))
                part[at] = grad[owner * size : (owner + 1) * size, e * own : (e + 1) * own].astype(BF)
        if j == 1:
            flows[0].start()
            flow_c.core_stage()
            early.end(0)
            early.start(1)
            over_mp[0].step()
            last_b.finish(partial_b)
            over_mp.append(start_mp(1))
        else:
            flows[1].start()
            flows[2].start()
            flow_c.second_stage()
            early.end(1)
            early.start(2)
            over_mp[1].step()

    total = post_steps(
        doc_count, taps, len_ref, gw_ref, gw_edge, channel, gains, vec, held, late, work, stream_done
    )
    final.start(0)
    flows[0].core_stage()
    flow_c.third_stage()
    flow_c.send_z()
    final.end(0)
    final.start(1)
    flows[1].core_stage()
    flows[2].core_stage()
    early.end(2)
    early.start_mp()
    post_end(total, gains, held, input_grad)
    final.end(1)
    final.start(2)
    for flow in flows:
        flow.second_stage()
    final.end(2)
    final.start_mp()
    prepare(raw, ready, update_work[0])
    for flow in flows:
        flow.third_stage()
        flow.send_z()
    g1[...] = over_mp[0].total()
    g2[...] = over_mp[1].total()
    flow_c.finish(g_c)
    early.end_mp()
    final.end_mp()
    for flow in flows:
        flow.finish(g_late)
    place_first(g0, g_c[...], g_late[...])
    for flow in (*flows, flow_c):
        flow.drain()
    early.drain()
    final.drain()
    run_update(taps, (g0, g1, g2), (vec_sum, fin_sum, fout_sum), w1, w2, ready, own_gain, old, outs, update_work)


def update_scratch(dp, mp, width):
    pieces = 3 * width // 128 + 1
    tall = -(-pieces // 8) * 8
    sems = 2 * (dp + mp)
    return [
        pltpu.VMEM((128, 128), F32),
        pltpu.VMEM((16, 128), F32),
        pltpu.VMEM((tall, 128), F32),
        pltpu.VMEM((mp, 16, 128), F32),
        pltpu.VMEM((dp, tall, 128), F32),
        pltpu.VMEM((8, 128), F32),
        pltpu.VMEM((mp, 8, 128), F32),
        pltpu.VMEM((dp, 8, 128), F32),
        dma(sems),
        dma(sems),
    ]


def hand_out_kernel(*refs):
    input_grad, norm, c0, c1, c2, n0, n1, n2, rows, cols, gain_g, gain_n, gain_m, *small = refs[: OUTS + 1]
    (
        input_grad_out, norm_out, in_g, out_g, up_g, down_g, gain_g_out, in_n, out_n, up_n, down_n, gain_n_out, gain_m_out,
        in_r, out_r, up_r, down_r, in_c, out_c, up_c, down_c, *small_out,
    ) = refs[OUTS + 1 :]
    size, own = out_g.shape
    input_grad_out[...] = input_grad[...]
    norm_out[...] = norm[...]
    for source, first, last in ((c0, in_g, out_g), (n0, in_n, out_n)):
        for j in range(3):
            first[j] = source[:, j * own : (j + 1) * own]
        last[...] = source[:, 3 * own : 4 * own]
    for source, target in ((c1, up_g), (c2, down_g), (n1, up_n), (n2, down_n)):
        target[...] = source[...]
    for source, target in ((gain_g, gain_g_out), (gain_n, gain_n_out), (gain_m, gain_m_out)):
        target[...] = source[:, 0:size]
    for index, target in enumerate((in_r, out_r, up_r, down_r)):
        target[...] = rows[index : index + 1, 0:size].reshape(size)
    for j in range(3):
        in_c[j : j + 1, :] = cols[0:1, j * own : (j + 1) * own]
    out_c[...] = cols[0:1, 3 * own : 4 * own].reshape(own)
    up_c[...] = cols[1:2, :].reshape(-1)
    down_c[...] = cols[2:3, :].reshape(-1)
    for source, target in zip(small, small_out):
        target[...] = source[...]


def hand_out(results, own):
    size, width = results[2].shape
    cube, part, full = (3, size, own), (size, own), (size, width)
    column, row, wide = (2, size), (size,), (width,)
    shapes = [(1, 1), cube, part, full, full, column, cube, part, full, full, column, column, row, row, row, row]
    shapes += [(3, own), (own,), wide, wide] + [v.shape for v in results[13:]]
    return pl.pallas_call(
        hand_out_kernel,
        name="hand_out",
        out_shape=(struct(results[0].shape, BF), *[struct(s, F32) for s in shapes]),
        in_specs=[IN_VMEM] * len(results),
        out_specs=(IN_VMEM,) * (1 + len(shapes)),
        compiler_params=pltpu.CompilerParams(vmem_limit_bytes=ROOM),
    )(*results)


FLOWS = 3


def finish(lengths, taps, first, late, partials, part_c, fin_part, fout_part, raw, w1, w2, old):
    dp, mp = lax.axis_size("dp"), lax.axis_size("mp")
    size, own = raw[1].shape
    width = w1.shape[1]
    count = late[0][0].shape[0]
    docs = lengths.shape[1]
    big = struct((size, width), F32)
    flat = [(2, 128), old[0].shape, old[2].shape, old[4].shape]
    outs = [struct((1, 1), F32)] + [big] * 6 + [struct((8, 128), F32), struct((3, width), F32)]
    outs += [struct(s, F32) for s in flat for _ in range(3)]
    params = pltpu.CompilerParams(collective_id=2, has_side_effects=True, vmem_limit_bytes=ROOM)
    tail = [*raw, w1, w2, *old]
    own_gain = pltpu.VMEM((2, 128), F32)
    if dp != 8:
        last_part, input_grad, vec = post(lengths, taps, *first, late)
        over_mp = [lax.psum_scatter(p, "mp").astype(F32) for p in partials[:2]]
        grad = scatter_fallback(last_part.reshape(mp, dp, size, 2 * own))
        first_grad = scatter_fallback(part_c)
        grad = jnp.concatenate([first_grad[:, :own], grad, first_grad[:, own:]], axis=1)
        sums = [lax.psum(vec, ("dp", "mp")), lax.psum(fin_part, ("dp", "mp")), lax.psum(fout_part, "dp")]
        inputs = [grad, *over_mp, *sums, *tail]
        results = pl.pallas_call(
            functools.partial(update_kernel, taps),
            name="clip_and_update",
            out_shape=tuple(outs),
            in_specs=[IN_VMEM] * len(inputs),
            out_specs=(IN_VMEM,) * len(outs),
            scratch_shapes=prepare_scratch(size, width) + [own_gain] + update_scratch(dp, mp, width),
            compiler_params=params,
        )(*inputs)
        return (input_grad, *results)
    flows = []
    for _ in range(FLOWS):
        flows += flow_scratch(mp, (size, 2 * own // FLOWS))
    vec = struct((16, width), F32)
    after = [fin_part, fout_part, *tail]

    def kernel(*refs):
        start = 1 + len(first)
        end = start + len(late)
        end_kernel(docs, taps, *refs[:start], *choose(refs[start:end], late), *refs[end:])

    return pl.pallas_call(
        kernel,
        name="sum_clip_update",
        out_shape=(struct((count, width), BF), *outs),
        in_specs=[IN_SMEM] + [IN_VMEM] * len(first) + [IN_HBM] * len(late) + [IN_VMEM] * 3 + [IN_HBM] + [IN_VMEM] * len(after),
        out_specs=(IN_VMEM,) * (1 + len(outs)),
        scratch_shapes=[
            *post_scratch(late, taps, count, width),
            *prepare_scratch(size, width),
            own_gain,
            *[pltpu.VMEM((size, width), F32)] * 3,
            pltpu.VMEM((size, 2 * own), F32),
            *[pltpu.VMEM(v.shape, F32) for v in (vec, vec, fin_part, fout_part)],
            pltpu.VMEM((mp, 2, 2, 2, size, 2 * own), BF),
            *update_scratch(dp, mp, width),
            *[pltpu.VMEM((mp - 1, size, width), BF)] * 2,
            *[pltpu.VMEM((size, width), BF)] * 2,
            dma(2, mp - 1),
            dma(2, mp - 1),
            pltpu.VMEM((size, 2 * own), F32),
            pltpu.VMEM((mp, size, width), BF),
            *[pltpu.VMEM((mp // 2, size, width), BF)] * 2,
            dma(2),
            dma(2),
            *flows,
            *flow_scratch(mp, (size, 2 * own)),
            *small_scratch((fin_part, fout_part), mp),
            *small_scratch((vec,), mp),
        ],
        compiler_params=params,
    )(lengths, *first, *[v for v, _ in late], *partials, part_c, *after)


class Spread:
    def __init__(self, own, whole, lanes, refs, direct):
        self.whole, self.lanes, self.direct = whole, lanes, direct
        self.source = own.at[:, lanes]
        self.own_sem, self.z_send, self.z_recv, self.p_send, self.p_recv = refs
        self.d, self.m, self.mp = lax.axis_index("dp"), lax.axis_index("mp"), lax.axis_size("mp")
        d = self.d
        self.dx, self.dy, self.dc = turned(d, 2), turned(d, 4), turned(d, 1)
        half = self.mp // 2
        self.low, self.high, self.all = pl.ds(0, half), pl.ds(half, self.mp - half), pl.ds(0, self.mp)

    def start(self):
        target = self.whole.at[self.m, self.d, :, self.lanes]
        self.copy = pltpu.make_async_copy(self.source, target, self.own_sem.at[0])
        self.copy.start()
        self.z = []
        if self.direct:
            for step, e in enumerate(ring(self.m, self.mp)):
                sems = self.z_send.at[step], self.z_recv.at[step]
                self.z.append(send(self.source, target, *sems, (self.d, e)))
        else:
            self.blocks, self.bit = [self.m], self.mp // 2
            self.send_blocks()

    def send_blocks(self):
        self.stepped = []
        for block in self.blocks:
            slot = len(self.z)
            target = self.whole.at[block, self.d, :, self.lanes]
            source = self.source if slot == 0 else target
            peer = (self.d, turned(self.m, self.bit))
            copy = send(source, target, self.z_send.at[slot], self.z_recv.at[slot], peer)
            self.stepped.append(copy)
            self.z.append(copy)

    def z_step(self):
        if self.bit == self.mp // 2:
            self.copy.wait()
        for copy in self.stepped:
            copy.wait_recv()
        self.blocks = self.blocks + [turned(block, self.bit) for block in self.blocks]
        self.bit //= 2
        self.send_blocks()

    def push(self, slot, rows, owner, peer):
        block = self.whole.at[rows, owner, :, self.lanes]
        return send(block, block, self.p_send.at[slot], self.p_recv.at[slot], (peer, self.m))

    def stage_one(self):
        if self.direct:
            self.copy.wait()
        for copy in self.z if self.direct else self.stepped:
            copy.wait_recv()
        d, dx, dy = self.d, self.dx, self.dy
        self.first = [self.push(0, self.low, d, dx), self.push(1, self.high, d, dy)]
        self.last = [self.push(2, self.all, d, self.dc)]

    def stage_two(self):
        for copy in self.first:
            copy.wait_recv()
        d, dx, dy = self.d, self.dx, self.dy
        self.second = [
            self.push(3, self.low, d, dy),
            self.push(4, self.high, d, dx),
            self.push(5, self.low, dx, dy),
            self.push(6, self.high, dy, dx),
        ]

    def stage_three(self):
        for copy in self.second:
            copy.wait_recv()
        for slot, owner in enumerate((self.dx, self.dy, turned(self.dx, 4))):
            self.last.append(self.push(7 + slot, self.all, owner, self.dc))

    def arrive(self):
        for copy in self.last:
            copy.wait_recv()

    def drain(self):
        for copy in self.z + self.first + self.second + self.last:
            copy.wait_send()


SPREAD_REFS = 5


def spread_scratch(mp):
    return [dma(1), dma(mp - 1), dma(mp - 1), dma(10), dma(10)]


def mark_same(same, len_ref, doc_count, first):
    tail = same.shape[1]
    position = lax.broadcasted_iota(jnp.int32, (tail + EDGE, 128), 0) + first
    doc = jnp.zeros(position.shape, jnp.int32)
    end = jnp.int32(0)
    for slot in range(doc_count):
        end = end + len_ref[0, slot]
        doc = doc + (position >= end).astype(jnp.int32)
    doc = jnp.where(position < 0, -1, doc)
    for k in range(1, same.shape[0] + 1):
        same[k - 1] = jnp.where(doc[EDGE:] == doc[EDGE - k : EDGE - k + tail], 1.0, 0.0)


def near_product(left, right, dot=mm):
    l_top, l_rest = split(left)
    r_top, r_rest = split(right)
    return dot(l_top, r_top) + dot(l_top, r_rest) + dot(l_rest, r_top)


def mixer_forward_kernel(
    doc_count, taps, len_ref, tok, in_w, out_w, up_w, down_w, gains_own, channel_own, table, step_col, f_in, f_out,
    t0, t1, t2, t3,
    w_parts, y_back, gain_rows, chan_rows, spectrum_out, hidden_out, phase_out, decay_out,
    z_out, s0_out, s1_out, s2_out, w_out_own, a_out, n1_out, inv1_out, w_in_out, w_out_out, whole_up, whole_down,
    spectrum, hidden, phase, decay, chunk_first, chunk_up, chunk_down, gains, channel, turn, whole_first, gains_all, channel_all, edges_all, filters, w_send, y_parts, full, raw, top, rest, slots,
    ext, n1, inv1, a, z, s0, s1, s2, w_own, w_in, w_out, same,
    s_send, s_recv, save_sem, b_send, b_recv, c_send, c_recv, *spread_refs,
):
    tables = (t0, t1, t2, t3)
    d, m = lax.axis_index("dp"), lax.axis_index("mp")
    dp, mp = lax.axis_size("dp"), lax.axis_size("mp")
    count, width = tok.shape
    rows = chunk_first.shape[0]
    own = width // mp
    block = count // 2
    blocks = raw.shape[0]

    place = (2, 0, 1)
    for j in range(3):
        chunk_first[:, pl.ds(place[j] * own, own)] = in_w[j].astype(BF)
    chunk_first[:, pl.ds(3 * own, own)] = out_w[...].astype(BF)
    chunk_up[...] = up_w[...].astype(BF)
    chunk_down[...] = down_w[...].astype(BF)
    turn[...] = jnp.zeros(turn.shape, F32)
    turn[pl.ds(0, 2), pl.ds(0, rows)] = gains_own[...]
    gains[...] = turn[...].astype(BF)
    channel[...] = jnp.zeros(channel.shape, F32)
    channel[pl.ds(0, channel_own.shape[0]), :] = channel_own[...]
    greet_all()

    small = []
    for step, e in enumerate(ring(d, dp)):
        small.append(send(gains, gains_all.at[d], s_send.at[step], s_recv.at[step], (e, m)))
    for step, e in enumerate(ring(m, mp)):
        at = dp + step
        small.append(send(channel, channel_all.at[m], s_send.at[at], s_recv.at[at], (d, e)))
    at = dp + mp
    for index, first, peer in ((0, count - EDGE, lax.rem(m + 1, mp)), (1, 0, lax.rem(m + mp - 1, mp))):
        sems = s_send.at[at + index], s_recv.at[at + index]
        small.append(send(tok.at[pl.ds(first, EDGE)], edges_all.at[index], *sems, (d, peer)))
    gains_all[d] = gains[...]
    channel_all[m] = channel[...]

    half = width // 2
    plan = [
        (chunk_first, whole_first, pl.ds(0, half)),
        (chunk_first, whole_first, pl.ds(half, width - half)),
        (chunk_up, whole_up, pl.ds(0, chunk_up.shape[1])),
        (chunk_down, whole_down, pl.ds(0, chunk_down.shape[1])),
    ]
    flows = [
        Spread(*p, spread_refs[i * SPREAD_REFS : (i + 1) * SPREAD_REFS], direct=i == 0) for i, p in enumerate(plan)
    ]
    left, right, up, down = flows
    left.start()
    right.start()

    phase[...] = near_product(table[...], f_in[...])
    hidden[...] = jnp.sin(phase[...])
    lane = (m * own + lax.broadcasted_iota(jnp.int32, (1, own), 1)).astype(F32)
    rate = FAST_DECAY + (SLOW_DECAY - FAST_DECAY) * lane / (width - 1)
    decay[...] = jnp.exp(-step_col[...] * rate)
    near = own // HALVES
    values = near_product(hidden[...], f_out[...]) * decay[...]
    for side in range(HALVES):
        filters[side, :, 0:near] = values[:, side * near : (side + 1) * near]

    mark_same(same, len_ref, doc_count, m * count - EDGE)

    left.stage_one()
    right.z_step()
    up.start()
    down.start()
    for copy in small:
        copy.wait()
    for e in range(dp):
        gain_rows[0:2, pl.ds(e * rows, rows)] = gains_all[e, 0:2, 0:rows].astype(F32)
    for e in range(mp):
        chan_rows[:, pl.ds(e * own, own)] = channel_all[e]
    ext[pl.ds(0, EDGE), :] = edges_all[0].astype(F32)
    ext[pl.ds(EDGE, count), :] = tok[...].astype(F32)
    ext[pl.ds(EDGE + count, EDGE), :] = edges_all[1].astype(F32)

    def norm_body(i, carry):
        at = pl.ds(pl.multiple_of(i * 32, 32), 32)
        normed, inverse_std = norm_parts(ext[at, :])
        n1[at, :] = normed
        inv1[at, :] = jnp.broadcast_to(inverse_std, (32, 128))
        a[at, :] = (normed * gain_rows[0:1, :]).astype(BF)
        return carry

    def stream_weights(j):
        for e in range(mp):
            part = whole_first[e, :, :, pl.ds(place[j] * own, own)].reshape(dp * rows, own)
            w_in[:, pl.ds(j * width + e * own, own)] = part

    def project(j):
        cols = pl.ds(j * width, width)
        z[:, cols] = mm(a[...], w_in[:, cols])

    def short(first, size, j):
        part = z[pl.ds(first + 8, size + 8), pl.ds(j * width, width)]
        total = chan_rows[j : j + 1, :] * part[8 : size + 8]
        for k in range(1, taps):
            keep = same[k - 1, pl.ds(first, size), 0:1] > 0.0
            moved = jnp.where(keep, part[8 - k : size + 8 - k], 0.0)
            total = total + chan_rows[3 * k + j : 3 * k + j + 1, :] * moved
        return total

    def value_body(i, carry):
        first = pl.multiple_of(i * 48, 16)
        at = pl.ds(first, 48)
        one, two = short(first, 48, 1), short(first, 48, 2)
        s1[at, :], s2[at, :] = one, two
        w_own[at, :] = two * one
        return carry

    def gate_body(i, carry):
        first = pl.multiple_of(i * 48, 16)
        s0[pl.ds(first, 48), :] = short(first, 48, 0)
        return carry

    lax.fori_loop(0, ext.shape[0] // 32, norm_body, 0)
    left.stage_two()
    right.stage_one()
    up.z_step()
    for side in range(HALVES):
        filter_spectrum(filters.at[side], spectrum.at[side], raw, tables, block)
    left.stage_three()
    right.stage_two()
    down.z_step()
    left.arrive()
    for j in (1, 2):
        stream_weights(j)
        project(j)
    lax.fori_loop(0, s0.shape[0] // 48, value_body, 0)
    piece = count // FOLD
    for side in range(HALVES):
        for part in range(mp):
            for i in range(FOLD):
                values = w_own[pl.ds(i * piece, piece), pl.ds(part * own + side * near, near)]
                w_send[side, part, :, pl.ds(i * near, near)] = values.astype(BF)
    going, back = [], []
    for side in range(HALVES):
        going.append(Blocks([(w_send.at[side], w_parts.at[side])], b_send.at[side], b_recv.at[side]))
        back.append(Blocks([(y_parts.at[side], y_back.at[side])], c_send.at[side], c_recv.at[side]))
        going[side].start()
    up.stage_one()
    right.stage_three()
    down.stage_one()
    right.arrive()
    stream_weights(0)
    project(0)
    lax.fori_loop(0, s0.shape[0] // 48, gate_body, 0)
    saves = []

    def save(source, target):
        copy = pltpu.make_async_copy(source, target, save_sem.at[len(saves)])
        copy.start()
        saves.append(copy)

    own_rows = pl.ds(0, count)
    for source, target in (
        *[(z.at[:, pl.ds(j * width, width)], z_out.at[j]) for j in range(3)], (s0.at[own_rows], s0_out), (s1, s1_out), (s2, s2_out), (w_own.at[own_rows], w_out_own),
        (a, a_out), (n1, n1_out), (inv1, inv1_out), (spectrum, spectrum_out), (hidden, hidden_out), (phase, phase_out),
        (decay, decay_out),
        *[(w_in.at[:, pl.ds(j * width, width)], w_in_out.at[j]) for j in range(3)],
    ):
        save(source, target)
    for e in range(mp):
        part = whole_first[e, :, :, pl.ds(3 * own, own)].reshape(dp * rows, own)
        w_out[:, pl.ds(e * own, own)] = part
    save(w_out, w_out_out)
    def between(slot):
        if slot == 2:
            down.stage_two()

    up.stage_two()
    for side in range(HALVES):
        going[side].arrive()
        conv_forward_steps(
            doc_count, len_ref, w_parts.at[side], tables, y_parts.at[side], spectrum.at[side], full, raw, top, rest,
            slots, between if side == 0 else lambda slot: None,
        )
        back[side].start()
    up.stage_three()
    down.stage_three()
    up.arrive()
    down.arrive()
    for side in range(HALVES):
        back[side].arrive()
    for copy in saves:
        copy.wait()
    for copies in going + back:
        copies.drain()
    for flow in flows:
        flow.drain()


def mixer_forward(lengths, tokens, weights, gains, channel, taps, table, step_col, f_in, f_out, tables):
    mp, dp = lax.axis_size("mp"), lax.axis_size("dp")
    count, width = tokens.shape
    own, block, docs = width // mp, count // 2, lengths.shape[1]
    lags = table.shape[0]
    blocks = lags // block
    near = own // HALVES
    rows = weights[1].shape[0]
    shards = [(rows, 4 * own), weights[2].shape, weights[3].shape]
    whole = [(mp, dp) + s for s in shards]
    longer, later = (count + 2 * EDGE, width), (count + EDGE, width)
    parts = (HALVES, mp, count // FOLD, FOLD * near)
    full, raw, low, slots = conv_scratch(parts[1:], blocks, block, docs)
    net = [
        ((HALVES, blocks, 2 * block, lanes_for(near)), F32), ((lags, f_in.shape[1]), F32), ((lags, f_in.shape[1]), F32),
        ((lags, own), F32),
    ]
    vmem_outs = [(parts, BF), (parts, BF), ((8, width), F32), ((16, width), F32)]
    hbm_outs = net + [
        ((3,) + longer, F32), ((count, width), F32), (later, F32), (later, F32), ((count, width), F32),
        (longer, BF), (longer, F32), ((longer[0], 128), F32), ((3, width, width), BF), ((width, width), BF),
        (whole[1], BF), (whole[2], BF),
    ]
    inputs = (lengths, tokens, *weights, gains, channel, table, step_col, f_in, f_out, *tables)
    results = pl.pallas_call(
        functools.partial(mixer_forward_kernel, docs, taps),
        name="mixer_forward",
        out_shape=tuple(struct(*o) for o in vmem_outs + hbm_outs),
        in_specs=[IN_SMEM] + [IN_VMEM] * (len(inputs) - 1),
        out_specs=(IN_VMEM,) * len(vmem_outs) + (IN_HBM,) * len(hbm_outs),
        scratch_shapes=[
            *[pltpu.VMEM(*v) for v in net], *[pltpu.VMEM(s, BF) for s in shards], pltpu.VMEM((16, 128), BF), pltpu.VMEM((16, own), F32),
            pltpu.VMEM((16, 128), F32),
            pltpu.VMEM(whole[0], BF), pltpu.VMEM((dp, 16, 128), BF), pltpu.VMEM((mp, 16, own), F32),
            pltpu.VMEM((2, EDGE, width), BF),
            pltpu.VMEM((HALVES, lags, lanes_for(near)), F32), pltpu.VMEM(parts, BF), pltpu.VMEM(parts, BF),
            full, raw, low, low, slots,
            pltpu.VMEM(longer, F32), pltpu.VMEM(longer, F32), pltpu.VMEM((longer[0], 128), F32), pltpu.VMEM(longer, BF),
            pltpu.VMEM((longer[0], 3 * width), F32), pltpu.VMEM(later, F32), pltpu.VMEM(later, F32),
            pltpu.VMEM(later, F32), pltpu.VMEM(later, F32), pltpu.VMEM((width, 3 * width), BF),
            pltpu.VMEM((width, width), BF), pltpu.VMEM((taps - 1, later[0], 128), F32),
            dma(dp + mp + 2), dma(dp + mp + 2), dma(24), *([dma(HALVES, 1, mp - 1)] * 4),
            *(spread_scratch(mp) * 4),
        ],
        compiler_params=pltpu.CompilerParams(collective_id=0, has_side_effects=True, vmem_limit_bytes=ROOM),
    )(*inputs)
    return (*results[:2], *results[4:8], *results[2:4], *results[8:])


def dot_nt(left, right):
    return lax.dot_general(left, right, (((1,), (1,)), ((), ())), preferred_element_type=F32)


def dot_tn(left, right):
    return lax.dot_general(left, right, (((0,), (0,)), ((), ())), preferred_element_type=F32)


def pieces(parts, count, width):
    near, rows = width // parts // HALVES, count // FOLD
    for side in range(HALVES):
        for part in range(parts):
            for i in range(FOLD):
                cols = pl.ds((part * HALVES + side) * near, near)
                yield pl.ds(i * rows, rows), cols, side, part, pl.ds(i * near, near)


def gelu_parts(x):
    scale, cubic = math.sqrt(2.0 / math.pi), 0.044715
    square = x * x
    t = jnp.tanh(x * (scale + (scale * cubic) * square))
    half = 0.5 + 0.5 * t
    value = x * half
    return value, half + value * (1.0 - t) * (scale + (3.0 * scale * cubic) * square)


COLS = 768


def feed_kernel(
    skip_row, y_ref, w_ref, s0_ref, tok, cot, w_out, gains, channel, up, down,
    act_out, up_part, down_part, out_part, g_parts, gy_out, gs0_out, gx2_out, sums, edge_out,
    y, o, x2, n2, inv2, b, b_t, cot_t, mix, acc_out, acc_b,
):
    step, steps = pl.program_id(0), pl.num_programs(0)
    parts = y_ref.shape[1]
    count, width = tok.shape
    tile = 128
    gain, skip = gains.at[1:2], channel.at[skip_row : skip_row + 1]

    @pl.when(step == 0)
    def _():
        for rows, cols, side, part, lanes in pieces(parts, count, width):
            y[rows, cols] = y_ref[side, part, :, lanes].astype(F32)

        def body(index, carry):
            rows = pl.ds(pl.multiple_of(index * tile, tile), tile)
            values = y[rows, :] + skip[...] * w_ref[rows, :]
            y[rows, :] = values
            mixed = (values * s0_ref[rows, :]).astype(BF)
            o[rows, :] = mixed
            residual = tok[rows, :].astype(F32) + dot_nt(mixed, w_out[...])
            x2[rows, :] = residual
            normed, inverse_std = norm_parts(residual)
            n2[rows, :] = normed
            inv2[rows, :] = jnp.broadcast_to(inverse_std, (tile, 128))
            b[rows, :] = (normed * gain[...]).astype(BF)
            return carry

        lax.fori_loop(0, count // tile, body, 0)
        b_t[...] = b[...].T
        cot_t[...] = cot[...].T
        acc_out[...] = jnp.zeros(acc_out.shape, F32)
        acc_b[...] = jnp.zeros(acc_b.shape, F32)

    up_w, down_w = up[0], down[0]
    value, slope = gelu_parts(mm(b[...], up_w))
    act = value.astype(BF)
    g_hpre = (mm(cot[...], down_w) * slope).astype(BF)
    up_part[0] = mm(b_t[...], g_hpre).astype(BF)
    down_part[0] = mm(cot_t[...], act).astype(BF)
    acc_out[...] += dot_nt(act, down_w)
    acc_b[...] += dot_nt(g_hpre, up_w)

    @pl.when(step == steps - 1)
    def _():
        sums[...] = jnp.zeros(sums.shape, F32)

        def body(index, carry):
            rows = pl.ds(pl.multiple_of(index * tile, tile), tile)
            act_out[rows, :] = (x2[rows, :] + acc_out[rows, :]).astype(BF)
            g_b, normed = acc_b[rows, :], n2[rows, :]
            sums[0:1, :] += jnp.sum(g_b * normed, axis=0, keepdims=True)
            g_x2 = cot[rows, :].astype(F32) + norm_back(g_b, gain[...], normed, inv2[rows, 0:1])
            gx2_out[rows, :] = g_x2
            low = g_x2.astype(BF)
            mix[rows, :] = low
            g_o = mm(low, w_out[...])
            g_y = g_o * s0_ref[rows, :]
            gy_out[rows, :] = g_y
            gs0_out[rows, :] = g_o * y[rows, :]
            sums[1:2, :] += jnp.sum(g_y * w_ref[rows, :], axis=0, keepdims=True)
            return carry

        lax.fori_loop(0, count // tile, body, 0)
        for rows, cols, side, part, lanes in pieces(parts, count, width):
            g_parts[side, part, :, lanes] = gy_out[rows, cols].astype(BF)
        edge_out[...] = gs0_out[pl.ds(0, EDGE), :].astype(BF)
        grad = dot_tn(mix[...], o[...])
        own = width // parts
        for part in range(parts):
            out_part[part] = grad[:, part * own : (part + 1) * own].astype(BF)


def feed(y_parts, w_own, s0, tokens, cotangent, w_out, gains, channel, skip_row, whole_up, whole_down):
    mp, width, hidden = whole_up.shape
    count = tokens.shape[0]
    own, cols = width // mp, COLS
    each = hidden // cols
    once = pl.Buffered(1)

    def fixed(shape):
        return pl.BlockSpec(shape, lambda i: (0,) * len(shape), pipeline_mode=once)

    def moving():
        return pl.BlockSpec((1, width, cols), lambda i: (i // each, 0, i % each))

    full, half = (count, width), y_parts.shape
    outs = [
        (full, BF), (whole_up.shape, BF), (whole_up.shape, BF), ((mp, width, own), BF), (half, BF),
        (full, F32), (full, F32), (full, F32), ((8, width), F32), ((EDGE, width), BF),
    ]
    out_specs = [moving() if i in (1, 2) else fixed(s) for i, (s, _) in enumerate(outs)]
    inputs = (y_parts, w_own, s0, tokens, cotangent, w_out, gains, channel)
    return pl.pallas_call(
        functools.partial(feed_kernel, skip_row),
        name="feed_forward",
        grid=(mp * each,),
        out_shape=tuple(struct(s, t) for s, t in outs),
        in_specs=[fixed(v.shape) for v in inputs] + [moving(), moving()],
        out_specs=tuple(out_specs),
        scratch_shapes=[
            pltpu.VMEM(full, F32), pltpu.VMEM(full, BF), pltpu.VMEM(full, F32), pltpu.VMEM(full, F32),
            pltpu.VMEM((count, 128), F32), pltpu.VMEM(full, BF), pltpu.VMEM((width, count), BF),
            pltpu.VMEM((width, count), BF), pltpu.VMEM(full, BF), pltpu.VMEM(full, F32), pltpu.VMEM(full, F32),
        ],
        compiler_params=pltpu.CompilerParams(vmem_limit_bytes=ROOM),
    )(*inputs, whole_up, whole_down)


class Late:
    def __init__(self, sources, targets, sem):
        self.copies = []
        for i, (source, target) in enumerate(zip(sources, targets)):
            copy = pltpu.make_async_copy(source, target, sem.at[i])
            copy.start()
            self.copies.append(copy)

    def need(self, *indices):
        for i in indices:
            self.copies[i].wait()


def short_backward(j, gs, z, channel, same, offsets, count, sums):
    tap_rows = [channel[3 * k + j : 3 * k + j + 1, :] for k in range(offsets)]
    g_z = None
    for k in range(offsets):
        later = gs[pl.ds(k, count), :]
        before = z[pl.ds(EDGE - k, count), :]
        if k:
            later = jnp.where(same[k][k : count + k], later, 0.0)
            before = jnp.where(same[k][:count], before, 0.0)
        g_z = tap_rows[k] * later if g_z is None else g_z + tap_rows[k] * later
        sums[pl.ds(3 * k + j, 1), :] = jnp.sum(gs[pl.ds(0, count), :] * before, axis=0, keepdims=True)
    return g_z


def post_steps(doc_count, offsets, len_ref, gw_ref, gw_edge, channel, gains, sums, held, late, work, stream_done):
    gy_ref, s2_ref, z1, a_ref, w1, s1_ref, z2, w2, ga0, n1_ref, inv1_ref, gx2_ref = held
    gw, gs, gz, marks = work
    parts = gw_ref.shape[1]
    count, width = gy_ref.shape
    near = width // parts // HALVES
    skip = channel[3 * offsets : 3 * offsets + 1, :]
    for rows, cols, side, part, lanes in pieces(parts, count, width):
        gw[rows, cols] = gw_ref[side, part, :, lanes].astype(F32)
    for side in range(HALVES):
        for part in range(parts):
            at = pl.ds((part * HALVES + side) * near, near)
            gw[pl.ds(count, EDGE), at] = gw_edge[side, part, :, 0:near].astype(F32)
    mark_same(marks, len_ref, doc_count, lax.axis_index("mp") * count - EDGE)
    same = [None] + [marks[k - 1, :, 0:1] > 0.0 for k in range(1, offsets)]
    late.need(0)
    gw[pl.ds(0, count), :] += skip * gy_ref[...]
    total = None
    for j, other, z, w, order in ((1, s2_ref, z1, w1, (1, 2, 3, 4)), (2, s1_ref, z2, w2, (5, 6, 7))):
        late.need(*order)
        gs[...] = gw[...] * other[...]
        gz[...] = short_backward(j, gs, z, channel, same, offsets, count, sums).astype(BF)
        stream_done(j, dot_tn(a_ref[pl.ds(EDGE, count), :], gz[...]))
        term = dot_nt(gz[...], w[...])
        total = term if total is None else total + term
    late.need(8, 9, 10, 11)
    total = total + ga0[...]
    sums[pl.ds(3 * offsets + 1, 1), :] = jnp.sum(total * n1_ref[pl.ds(EDGE, count), :], axis=0, keepdims=True)
    return total


def post_end(total, gains, held, input_grad):
    n1_ref, inv1_ref, gx2_ref = held[9:]
    count = gx2_ref.shape[0]
    normed, inverse_std = n1_ref[pl.ds(EDGE, count), :], inv1_ref[pl.ds(EDGE, count), 0:1]
    input_grad[...] = (gx2_ref[...] + norm_back(total, gains[0:1, :], normed, inverse_std)).astype(BF)


def post_kernel(doc_count, offsets, len_ref, gw_ref, gw_edge, channel, gains, sums_in, *refs):
    late_refs, refs = refs[:12], refs[12:]
    last_part, input_grad, sums, refs = refs[0], refs[1], refs[2], refs[3:]
    held, late_sem, work = refs[:12], refs[12], refs[13:]
    late = Late(late_refs, held, late_sem)
    parts, own = gw_ref.shape[1], last_part.shape[2] // 2
    sums[...] = sums_in[...]

    def stream_done(j, grad):
        for part in range(parts):
            last_part[part, :, pl.ds((j - 1) * own, own)] = grad[:, part * own : (part + 1) * own].astype(BF)

    total = post_steps(
        doc_count, offsets, len_ref, gw_ref, gw_edge, channel, gains, sums, held, late, work, stream_done
    )
    post_end(total, gains, held, input_grad)


def post_late(g_y, s1, s2, z, a, w_in, ga0, n1, inv1, g_x2):
    return [
        (g_y, None), (s2, None), (z, 1), (a, None), (w_in, 1), (s1, None), (z, 2), (w_in, 2), (ga0, None), (n1, None),
        (inv1, None), (g_x2, None),
    ]


def post_scratch(late, offsets, count, width):
    return [
        *[pltpu.VMEM(v.shape if i is None else v.shape[1:], v.dtype) for v, i in late],
        dma(len(late)),
        pltpu.VMEM((count + EDGE, width), F32),
        pltpu.VMEM((count + EDGE, width), F32),
        pltpu.VMEM((count, width), BF),
        pltpu.VMEM((offsets - 1, count + EDGE, 128), F32),
    ]


def choose(refs, late):
    return [r if i is None else r.at[i] for r, (_, i) in zip(refs, late)]


def post(lengths, offsets, gw_parts, gw_edge, channel, gains, sums_in, late):
    mp = gw_parts.shape[1]
    count, width = late[0][0].shape
    first = (gw_parts, gw_edge, channel, gains, sums_in)

    def kernel(*refs):
        start = 1 + len(first)
        end = start + len(late)
        post_kernel(lengths.shape[1], offsets, *refs[:start], *choose(refs[start:end], late), *refs[end:])

    return pl.pallas_call(
        kernel,
        name="mixer_post",
        out_shape=(struct((mp, width, 2 * width // mp), BF), struct((count, width), BF), struct((16, width), F32)),
        in_specs=[IN_SMEM] + [IN_VMEM] * len(first) + [IN_HBM] * len(late),
        out_specs=(IN_VMEM,) * 3,
        scratch_shapes=post_scratch(late, offsets, count, width),
        compiler_params=pltpu.CompilerParams(vmem_limit_bytes=ROOM),
    )(lengths, *first, *[v for v, _ in late])


def features(length, feature_count, count):
    step = np.arange(count)
    band = np.arange(1, (feature_count - 1) // 2 + 1)
    phase = ((step[:, None] * band[None, :]) % length).astype(np.float32) * np.float32(2.0 * math.pi / length)
    position = (step / length).astype(np.float32)
    table = np.concatenate([position[:, None], np.cos(phase), np.sin(phase)], axis=1)
    return table.astype(np.float32), position


def product(left, right):
    return jnp.dot(left, right, precision=FULL_PRECISION, preferred_element_type=F32)


def norm_parts(values):
    centred = values - jnp.mean(values, axis=-1, keepdims=True)
    inverse_std = lax.rsqrt(jnp.mean(centred * centred, axis=-1, keepdims=True) + EPS_NORM)
    return centred * inverse_std, inverse_std


def norm_back(grad, gain, normed, inverse_std):
    scaled = grad * gain
    mean = jnp.mean(scaled, axis=-1, keepdims=True)
    along = jnp.mean(scaled * normed, axis=-1, keepdims=True)
    return (scaled - mean - normed * along) * inverse_std


def to_parts(values, mp):
    count, width = values.shape
    near = width // mp // HALVES
    cut = values.reshape(FOLD, count // FOLD, mp, HALVES, near).transpose(3, 2, 1, 0, 4)
    return cut.reshape(HALVES, mp, count // FOLD, FOLD * near)


def forward_fallback(lengths, tokens, weights, gain_own, channel_own, taps, table, step_col, f_in, f_out, tables):
    mp, m = lax.axis_size("mp"), lax.axis_index("mp")
    count, width = tokens.shape
    own, shard = width // mp, weights[1].shape[0]
    first_shard = jnp.concatenate([*weights[0], weights[1]], axis=1)
    chunks = [v.astype(BF) for v in (first_shard, weights[2], weights[3])]
    gains = jnp.pad(gain_own.astype(BF), ((0, 14), (0, 128 - shard)))
    channel = jnp.pad(channel_own, ((0, 16 - channel_own.shape[0]), (0, 0)))
    edges = jnp.stack([tokens[count - EDGE :], tokens[:EDGE]])
    first, up, down, gains_all, channel_all, edges_all = gather_fallback(chunks, gains, channel, edges)
    first = first.reshape(mp, width, width)
    w_in = first[:, :, : 3 * own].reshape(mp, width, 3, own).transpose(1, 2, 0, 3).reshape(width, 3 * width)
    w_out = first[:, :, 3 * own :].transpose(1, 0, 2).reshape(width, width)
    gain_rows = gains_all[:, 0:8, :shard].transpose(1, 0, 2).reshape(8, width).astype(F32)
    chan_rows = channel_all.transpose(1, 0, 2).reshape(-1, width)
    position = m * count - EDGE + jnp.arange(count + 2 * EDGE, dtype=jnp.int32)
    doc = jnp.sum((position[:, None] >= jnp.cumsum(lengths[0])[None, :]).astype(jnp.int32), axis=1)
    doc = jnp.where(position < 0, -1, doc)
    n1, inv1 = norm_parts(jnp.concatenate([edges_all[0], tokens, edges_all[1]]).astype(F32))
    a = (n1 * gain_rows[0]).astype(BF)
    z = jnp.dot(a, w_in, preferred_element_type=F32)
    s = []
    for j in range(3):
        stream, total = z[:, j * width : (j + 1) * width], None
        for k in range(taps):
            part = stream[EDGE - k : stream.shape[0] - k]
            if k:
                part = jnp.where((doc[EDGE:] == doc[EDGE - k : doc.shape[0] - k])[:, None], part, 0.0)
            term = chan_rows[3 * k + j] * part
            total = term if total is None else total + term
        s.append(total)
    w_own = s[2][:count] * s[1][:count]
    phase = product(table, f_in)
    hidden = jnp.sin(phase)
    lane = (m * own + jnp.arange(own, dtype=jnp.int32)).astype(F32)
    decay = jnp.exp(-step_col * (FAST_DECAY + (SLOW_DECAY - FAST_DECAY) * lane / (width - 1)))
    w_parts = exchange([*to_parts(w_own.astype(BF), mp)], None, 3)
    filters = jnp.split(product(hidden, f_out) * decay, HALVES, axis=1)
    halves = [conv_forward(w_parts[i], lengths, filters[i], tables) for i in range(HALVES)]
    y_back = jnp.stack(exchange([v[0] for v in halves], None, 4))
    w_parts, spectrum = jnp.stack(w_parts), jnp.stack([v[1] for v in halves])
    return (
        w_parts, y_back, spectrum, hidden, phase, decay, gain_rows, chan_rows,
        z.reshape(-1, 3, width).transpose(1, 0, 2), s[0][:count], s[1], s[2], w_own, a, n1,
        jnp.broadcast_to(inv1, (inv1.shape[0], 128)), w_in.reshape(width, 3, width).transpose(1, 0, 2), w_out, up, down,
    )


def per_device(
    tokens, cotangent, doc_lengths, in_weight, out_weight, up_weight, down_weight, gains, channel_weight,
    filter_in, filter_out, in_rows, in_cols, out_rows, out_cols, up_rows, up_cols, down_rows, down_cols,
    gain_moment, channel_moment, filter_in_moment, filter_out_moment,
):
    dp, mp = lax.axis_size("dp"), lax.axis_size("mp")
    count, width = tokens.shape
    length = count * mp
    own = channel_weight.shape[1]
    rows = in_weight.shape[0]
    hidden = up_weight.shape[1]
    taps = (channel_weight.shape[0] - 1) // 3
    most = length // 2

    in_weight, gains, gain_moment = in_weight.transpose(1, 0, 2), gains.T, gain_moment.T

    table, step = features(length, filter_in.shape[0], most)
    tables = tuple(jnp.asarray(t) for t in transform_tables(count // 2))
    run = mixer_forward if dp == 8 else forward_fallback
    (
        w_parts, y_back, spectrum, hidden_filter, phase, decay, gain_rows, chan_rows, z, s0, s1, s2, w_own,
        a, n1, inv1, w_in, w_out, whole_up, whole_down,
    ) = run(
        doc_lengths, tokens, (in_weight, out_weight, up_weight, down_weight), gains, channel_weight, taps,
        table, step[:, None], filter_in, filter_out, tables,
    )
    whole_up = whole_up.reshape(mp, width, hidden)
    whole_down = whole_down.reshape(mp, width, hidden)

    activations, up_part, down_part, out_part, gy_parts, g_y, g_s0, g_x2, feed_sums, g_s0_own = feed(
        y_back, w_own, s0, tokens, cotangent, w_out, gain_rows, chan_rows, 3 * taps, whole_up, whole_down
    )

    up_part, down_part = [p.reshape(mp, dp, rows, hidden) for p in (up_part, down_part)]
    gw_back, gw_edge, sums, g_a0, fin_part, fout_part, *partials, first_part = mixer_backward(
        doc_lengths, taps, gy_parts, g_s0_own, channel_weight, feed_sums, up_part, down_part, g_s0, z, a, w_in,
        chan_rows, out_part, w_parts, tables, spectrum, decay, hidden_filter, filter_out, phase, table,
    )

    results = finish(
        doc_lengths, taps, (gw_back, gw_edge, chan_rows, gain_rows, sums),
        post_late(g_y, s1, s2, z, a, w_in, g_a0, n1, inv1, g_x2), partials, first_part, fin_part, fout_part,
        (
            in_weight, out_weight, in_rows, out_rows, up_rows, down_rows,
            in_cols, out_cols, up_cols, down_cols, gains, gain_moment,
        ),
        up_weight, down_weight,
        (channel_weight, channel_moment, filter_in, filter_in_moment, filter_out, filter_out_moment),
    )
    (
        input_grad, norm, in_g, out_g, up_g, down_g, gain_g, in_n, out_n, up_n, down_n, gain_n, gain_m,
        in_r, out_r, up_r, down_r, in_c, out_c, up_c, down_c,
        chan_g, chan_n, chan_m, fin_g, fin_n, fin_m, fout_g, fout_n, fout_m,
    ) = hand_out(results, own)
    return (
        activations, input_grad, norm.reshape(()),
        in_g.transpose(1, 0, 2), out_g, up_g, down_g, gain_g.T, chan_g, fin_g, fout_g,
        in_n.transpose(1, 0, 2), out_n, up_n, down_n, gain_n.T, chan_n, fin_n, fout_n,
        in_r, in_c, out_r, out_c, up_r, up_c, down_r, down_c, gain_m.T, chan_m, fin_m, fout_m,
    )


def solution(mesh):
    tokens, by_rows, by_cols, both = P(("dp", "mp"), None), P("dp", None), P(None, "mp"), P("dp", "mp")
    cube, vec_dp, vec_mp = P("dp", None, "mp"), P("dp"), P("mp")
    moments = (vec_dp, by_cols, vec_dp, vec_mp, vec_dp, vec_mp, vec_dp, vec_mp)
    weights = (cube, both, both, both, by_rows, by_cols, P(), by_cols)
    small = (by_rows, by_cols, P(), by_cols)
    return jax.shard_map(
        per_device,
        mesh=mesh,
        in_specs=(tokens, tokens, by_rows) + weights + moments + small,
        out_specs=(tokens, tokens, P()) + weights + weights + moments + small,
        check_vma=False,
    )
```
